32 devices in a mesh: expert: 8 (over z, y), head: 4 (over x, core).
Axes of the slice: x: 2, y: 2, z: 4, core: 2. Of those that a mesh axis runs over, the one named last changes fastest.
Arguments:
- hidden_in: bfloat16 [2048, 2048], P('expert'), may hold values from -6 to 6
- norm1_gain: float32 [2048], replicated, may hold values from 0.1 to 1.9
- w_query: bfloat16 [2048, 2048], P(None, 'head'), may hold values from -0.125 to 0.125
- w_key: bfloat16 [2048, 2048], P(None, 'head'), may hold values from -0.125 to 0.125
- w_value: bfloat16 [2048, 2048], P(None, 'head'), may hold values from -0.125 to 0.125
- w_out: bfloat16 [2048, 2048], P('head'), may hold values from -0.75 to 0.75
- query_gain: float32 [2048], P('head'), may hold values from 0.1 to 1.9
- key_gain: float32 [2048], P('head'), may hold values from 0.1 to 1.9
- norm2_gain: float32 [2048], replicated, may hold values from 0.1 to 1.9
- w_router: bfloat16 [2048, 16], replicated, may hold values from -0.0625 to 0.0625
- w_gate: bfloat16 [16, 2048, 1024], P('expert', None, 'head'), may hold values from -0.125 to 0.125
- w_up: bfloat16 [16, 2048, 1024], P('expert', None, 'head'), may hold values from -0.125 to 0.125
- w_down: bfloat16 [16, 1024, 2048], P('expert', 'head'), may hold values from -0.75 to 0.75
- routes: int32 [2048, 8], P('expert'), may hold values from 0 to 15, all different within a row; in each aligned block of 256 rows (0 to 255, 256 to 511, ...) at most 256 rows name the same one
- segments: int32 [2048], replicated, may hold values from 0 to 2, as said below
- cotangent: bfloat16 [2048, 2048], P('expert'), may hold values from -6 to 6
Outputs:
- output: bfloat16 [2048, 2048], P('expert')
- grad_input: float32 [2048, 2048], P('expert')
- grad_norm1: float32 [2048], replicated
- grad_query: float32 [2048, 2048], P('expert', 'head')
- grad_key: float32 [2048, 2048], P('expert', 'head')
- grad_value: float32 [2048, 2048], P('expert', 'head')
- grad_w_out: float32 [2048, 2048], P('head', 'expert')
- grad_query_gain: float32 [2048], P('head')
- grad_key_gain: float32 [2048], P('head')
- grad_norm2: float32 [2048], replicated
- grad_router: float32 [2048, 16], replicated
- grad_gate: float32 [16, 2048, 1024], P('expert', None, 'head')
- grad_up: float32 [16, 2048, 1024], P('expert', None, 'head')
- grad_down: float32 [16, 1024, 2048], P('expert', 'head')
The draws below stay inside these ranges and needn't reach their ends.
Inputs may be any that keep to these rules, and one draw needn't show every extreme that they name: `routes`: each token names 8 different experts. Among the rows of one device, no expert is named more than 256 times, and in every draw some expert is named exactly 256 times by one device's rows. `segments`: never falling along the tokens; no document spans two sequences of 2048 tokens.
All inputs are finite; a program needn't handle non-finite values.
Results may differ from the reference program's by a relative error of at most 0.024.
Values may be sent and summed in bfloat16 or wider, within the bound.
A program may use at most 320 MiB of HBM per device.

```python
import math
import jax
import jax.numpy as jnp
import numpy as np
from jax import lax

D = 2048
HEADS = 16
HEAD_DIM = 128
FF = 1024
TOP = 8
EXPERTS = 16
SEQ = 2048
TOK_DEV = 256
TOKENS = 2048
CAP = 256
N_EXPERT = 8


def draw_segments(key, part):
    key = jax.random.fold_in(key, 11)
    seq_count = TOKENS // SEQ
    first_key, second_key = jax.random.split(key)
    leading = jax.random.randint(first_key, (seq_count,), 1, TOK_DEV // 2 + 1, dtype=jnp.int32)
    trailing = jax.random.randint(second_key, (seq_count,), 1, TOK_DEV // 2 + 1, dtype=jnp.int32)
    places = jnp.arange(TOKENS, dtype=jnp.int32)
    which = places // SEQ
    inner = places % SEQ
    past_lead = (inner >= leading[which]).astype(jnp.int32)
    past_main = (inner >= SEQ - trailing[which]).astype(jnp.int32)
    return (3 * which + past_lead + past_main).astype(jnp.int32)


def level_of(rng, dims, cuts, low, largest):
    loudness = 1.0
    for dim, blocks in cuts:
        draws = jax.random.uniform(jax.random.fold_in(jax.random.fold_in(rng, 6), dim), (blocks,), jnp.float32, low / len(cuts), largest / len(cuts))
        loudness = loudness * jnp.repeat(jnp.exp(draws), dims[dim] // blocks).reshape((-1,) + (1,) * (len(dims) - 1 - dim))
    return loudness


def shared_out(own_key, own, number, rows, amount, top, limit, slope):
    order = jax.random.permutation(own_key, amount)
    crowded, usual = load_shares(amount, rows * top, limit, slope, True), load_shares(amount, rows * top, limit, slope, False)
    places = jnp.arange(amount)

    def named(sizes, offset_by):
        used = int((sizes > 0).sum())
        fixed = max(1, used // 4)
        passed = fixed + (places - fixed + offset_by * (used - fixed)) % max(1, amount - fixed)
        return jnp.zeros((amount,), jnp.int32).at[order[jnp.where(places < fixed, places, passed)]].set(jnp.asarray(sizes, jnp.int32))

    sizes = jnp.where(number % 4 == 0, named(crowded, number // 4), named(usual, number - number // 4 - 1))
    mixed = jax.random.permutation(jax.random.fold_in(own, 3), amount)
    source_of, taker = mixed[0:amount // 2 * 2:2], mixed[1:amount // 2 * 2:2]
    margin = jnp.minimum(sizes[source_of] - 1, limit - sizes[taker]) // 2
    margin = jnp.where((source_of == order[0]) | (taker == order[0]) | (sizes[taker] == 0), 0, jnp.maximum(margin, 0))
    passed = jax.random.randint(jax.random.fold_in(own, 4), (amount // 2,), 0, 1 << 20) % (margin + 1)
    sizes = sizes.at[source_of].add(-passed).at[taker].add(passed)
    labels = jnp.searchsorted(jnp.cumsum(sizes), jnp.arange(rows * top), side="right").astype(jnp.int32)
    table = labels.reshape(top, rows).T
    table = table[jax.random.permutation(jax.random.fold_in(own, 1), rows)]
    offset_by = jax.random.randint(jax.random.fold_in(own, 2), (rows, 1), 0, top)
    return jnp.take_along_axis(table, (jnp.arange(top)[None, :] + offset_by) % top, axis=1)


def load_shares(amount, total, bound, skew, full):
    loads = [(1 << 20) // math.isqrt(grade ** skew) + 1 for grade in range(1, amount + 1)]
    largest = bound if full else min(bound, max(-(-total // amount), total * loads[0] // sum(loads)))
    least = 1 if total - largest >= amount - 1 else 0
    given, spare = [largest] + [least] * (amount - 1), total - largest - least * (amount - 1)
    while spare > 0:
        movable = [i for i in range(1, amount) if given[i] < largest] or [i for i in range(1, amount) if given[i] < bound]
        mass, budget = sum([loads[i] for i in movable]), spare
        for i in movable:
            extra = min(bound - given[i], max(1, budget * loads[i] // mass), spare)
            given[i] = given[i] + extra
            spare = spare - extra
    return np.array(given)


def scatter_about(stream_key, extent, spread, limit, cuts=(), kind=jnp.bfloat16):
    values = spread * jax.random.normal(stream_key, extent, jnp.float32)
    if cuts:
        values = values * level_of(stream_key, extent, cuts, -0.22, 0.18)
    return jnp.clip(values, -limit, limit).astype(kind)


def setup_inputs(seed: int = 0) -> dict:
    seeds = jax.random.split(jax.random.key(seed), 17)
    hidden_in = scatter_about(seeds[0], (TOKENS, D), 1.0, 6.0, ((0, 8),))
    norm1_gain = jnp.clip(1.0 + 0.18 * jax.random.normal(seeds[1], (D,), jnp.float32), 0.1, 1.9)
    w_query = scatter_about(seeds[2], (D, D), D ** -0.5, 0.125, ((1, 4),))
    w_key = scatter_about(seeds[3], (D, D), D ** -0.5, 0.125, ((1, 4),))
    w_value = scatter_about(seeds[4], (D, D), D ** -0.5, 0.125, ((1, 4),))
    w_out = scatter_about(seeds[5], (D, D), (D // 32) ** -0.5, 0.75, ((0, 4),))
    query_gain = jnp.clip(1.0 + 0.18 * jax.random.normal(seeds[6], (D,), jnp.float32), 0.1, 1.9)
    key_gain = jnp.clip(1.0 + 0.18 * jax.random.normal(seeds[7], (D,), jnp.float32), 0.1, 1.9)
    norm2_gain = jnp.clip(1.0 + 0.18 * jax.random.normal(seeds[8], (D,), jnp.float32), 0.1, 1.9)
    w_router = scatter_about(seeds[9], (D, EXPERTS), (4 * D) ** -0.5, 0.0625)
    w_gate = scatter_about(seeds[10], (EXPERTS, D, FF), D ** -0.5, 0.125, ((0, 8), (2, 4)))
    w_up = scatter_about(seeds[11], (EXPERTS, D, FF), D ** -0.5, 0.125, ((0, 8), (2, 4)))
    w_down = scatter_about(seeds[12], (EXPERTS, FF, D), (FF // 16) ** -0.5, 0.75, ((0, 8), (1, 4)))
    routes_keys = jax.random.split(jax.random.fold_in(seeds[13], 1), TOKENS // TOK_DEV)
    routes_turns = jax.random.permutation(jax.random.fold_in(seeds[13], 3), TOKENS // TOK_DEV)
    routes = jax.vmap(lambda own, number: shared_out(jax.random.fold_in(seeds[13], 2), own, number, TOK_DEV, EXPERTS, TOP, CAP, 1))(routes_keys, routes_turns).reshape((TOKENS, TOP))
    segments = draw_segments(jax.random.fold_in(seeds[16], 71), 0)
    cotangent = scatter_about(seeds[15], (TOKENS, D), 1.0, 6.0, ((0, 8),))
    return {"hidden_in": hidden_in, "norm1_gain": norm1_gain, "w_query": w_query, "w_key": w_key, "w_value": w_value, "w_out": w_out, "query_gain": query_gain, "key_gain": key_gain, "norm2_gain": norm2_gain, "w_router": w_router, "w_gate": w_gate, "w_up": w_up, "w_down": w_down, "routes": routes, "segments": segments, "cotangent": cotangent}


EPSILON = 1e-05
ROPE_BASE = 10000.0
MASKED = -1000000000.0
PRECISE = lax.Precision.HIGHEST

@jax.custom_vjp
def low(v):
    return lax.optimization_barrier(v.astype(jnp.bfloat16)).astype(jnp.float32)

@jax.custom_vjp
def low_back(v):
    return v

def low_keep(v):
    return (low(v), None)

def low_pass(kept, grad):
    return (grad,)

def back_keep(v):
    return (v, None)

def back_low(kept, grad):
    return (low(grad),)
low.defvjp(low_keep, low_pass)
low_back.defvjp(back_keep, back_low)

def norm_rows(values, gain_row):
    return values * lax.rsqrt(lax.optimization_barrier(jnp.mean(values * values, -1, keepdims=True)) + EPSILON) * gain_row

def rotate(values):
    seq_len = values.shape[0]
    half_dim = values.shape[-1] // 2
    places = jnp.arange(seq_len, dtype=jnp.int32).astype(jnp.float32)
    inv_freq = ROPE_BASE ** (-jnp.arange(half_dim, dtype=jnp.int32).astype(jnp.float32) / half_dim)
    angles = places[:, None] * inv_freq[None, :]
    cosine = jnp.cos(angles)[:, None, :]
    sine_part = jnp.sin(angles)[:, None, :]
    first_half = values[..., :half_dim]
    second_half = values[..., half_dim:]
    return jnp.concatenate([first_half * cosine - second_half * sine_part, second_half * cosine + first_half * sine_part], -1)

def attend(seq_input, seq_segments, w_query, w_key, w_value, query_gain, key_gain):
    seq_len = seq_input.shape[0]

    def split_heads(values):
        return values.reshape(seq_len, HEADS, HEAD_DIM)
    q_raw = low_back(jnp.dot(seq_input, w_query, precision=PRECISE))
    k_raw = low_back(jnp.dot(seq_input, w_key, precision=PRECISE))
    v_heads = low(low_back(jnp.dot(seq_input, w_value, precision=PRECISE)))
    queries = low(rotate(norm_rows(split_heads(q_raw), query_gain.reshape(HEADS, HEAD_DIM))))
    key_rot = low(rotate(norm_rows(split_heads(k_raw), key_gain.reshape(HEADS, HEAD_DIM))))
    scores = low_back(jnp.einsum('thd,shd->hts', queries, key_rot, precision=PRECISE) * HEAD_DIM ** (-0.5))
    places = jnp.arange(seq_len, dtype=jnp.int32)
    allowed = (places[:, None] >= places[None, :]) & (seq_segments[:, None] == seq_segments[None, :])
    scores = jnp.where(allowed[None], scores, MASKED)
    row_max = lax.optimization_barrier(jnp.max(scores, -1, keepdims=True))
    raised = jnp.exp(scores - row_max)
    attn_probs = low(raised / lax.optimization_barrier(jnp.sum(raised, -1, keepdims=True)))
    context = jnp.einsum('hts,shd->thd', attn_probs, split_heads(v_heads), precision=PRECISE)
    return low(low_back(context.reshape(seq_len, D)))

def expert_rows(seq_input, seq_gates, seq_routes, w_gate, w_up, w_down):
    seq_len = seq_input.shape[0]
    catalog = jnp.arange(EXPERTS, dtype=jnp.int32)
    token_hot = lax.optimization_barrier(jnp.sum((seq_routes[:, :, None] == catalog).astype(jnp.int32), 1, dtype=jnp.int32))
    earlier = (jnp.cumsum(token_hot, 0, dtype=jnp.int32) - token_hot).astype(jnp.int32)
    slot_rank = jnp.take_along_axis(earlier, seq_routes, 1).astype(jnp.int32)
    position = (seq_routes * CAP + slot_rank).astype(jnp.int32)
    owners = jnp.full((EXPERTS * CAP,), seq_len, jnp.int32)
    owners = owners.at[position.reshape(-1)].set(jnp.repeat(jnp.arange(seq_len, dtype=jnp.int32), TOP))
    padded = jnp.concatenate([seq_input, jnp.zeros((1, D), jnp.float32)], 0)
    rows_in = low_back(padded[owners].reshape(EXPERTS, CAP, D))
    gate_act = low_back(jnp.einsum('ecd,edf->ecf', rows_in, w_gate, precision=PRECISE))
    up_act = low_back(jnp.einsum('ecd,edf->ecf', rows_in, w_up, precision=PRECISE))
    hidden = low(jax.nn.silu(gate_act) * up_act)
    rows_out = low_back(low(jnp.einsum('ecf,efd->ecd', hidden, w_down, precision=PRECISE)))
    picked = rows_out.reshape(EXPERTS * CAP, D)[position]
    return lax.optimization_barrier(jnp.sum(seq_gates[:, :, None] * picked, 1))

def forward(hidden_in, norm1_gain, w_query, w_key, w_value, w_out, query_gain, key_gain, norm2_gain, w_router, w_gate, w_up, w_down, routes, segments):
    attn_input = low(norm_rows(hidden_in, norm1_gain))
    attend_one = jax.checkpoint(lambda pair: attend(pair[0], pair[1], w_query, w_key, w_value, query_gain, key_gain))
    seq_count = TOKENS // SEQ
    context = lax.map(attend_one, (attn_input.reshape(seq_count, SEQ, D), segments.reshape(seq_count, SEQ)))
    attn_out = low_back(jnp.dot(context.reshape(TOKENS, D), w_out, precision=PRECISE))
    middle = hidden_in + attn_out
    moe_input = low(norm_rows(middle, norm2_gain))
    logits = low_back(jnp.dot(moe_input, w_router, precision=PRECISE))
    chosen = jnp.take_along_axis(logits, routes, 1)
    raised = jnp.exp(chosen - lax.optimization_barrier(jnp.max(chosen, -1, keepdims=True)))
    gate_weights = raised / lax.optimization_barrier(jnp.sum(raised, -1, keepdims=True))
    expert_one = jax.checkpoint(lambda triple: expert_rows(triple[0], triple[1], triple[2], w_gate, w_up, w_down))
    moe_out = lax.map(expert_one, (moe_input.reshape(N_EXPERT, TOK_DEV, D), gate_weights.reshape(N_EXPERT, TOK_DEV, TOP), routes.reshape(N_EXPERT, TOK_DEV, TOP)))
    return middle + moe_out.reshape(TOKENS, D)

def reference(hidden_in, norm1_gain, w_query, w_key, w_value, w_out, query_gain, key_gain, norm2_gain, w_router, w_gate, w_up, w_down, routes, segments, cotangent):
    floats = tuple((member.astype(jnp.float32) for member in (hidden_in, norm1_gain, w_query, w_key, w_value, w_out, query_gain, key_gain, norm2_gain, w_router, w_gate, w_up, w_down)))

    def apply_layer(*weights):
        return forward(*weights, routes, segments)
    result, pullback = jax.vjp(apply_layer, *floats)
    grads = pullback(cotangent.astype(jnp.float32))
    return (result.astype(jnp.bfloat16), grads[0], grads[1], grads[2], grads[3], grads[4], grads[5], grads[6], grads[7], grads[8], grads[9], grads[10], grads[11], grads[12])
```

```python
import jax
import jax.numpy as jnp
from jax import lax
from jax.experimental import pallas as pl
from jax.experimental.pallas import tpu as pltpu
from jax.sharding import PartitionSpec as P

HEAD_DIM = 128
TOP = 8
SEQ = 2048
MESH = pl.DeviceIdType.MESH
bf16 = jnp.bfloat16
f32 = jnp.float32


EPSILON = 1e-05
ROPE_BASE = 10000.0
MASKED = -1000000000.0


def from_behind(shard, axis, by):
    size = lax.axis_size(axis)
    pairs = [(i, i + by) for i in range(size) if 0 <= i + by < size]
    return lax.ppermute(shard, axis, pairs)


def inverse_rms(values):
    return lax.rsqrt(jnp.mean(values * values, -1, keepdims=True) + EPSILON)


def norm_back(grad_normed, normed, inverse):
    return inverse * (grad_normed - normed * jnp.mean(grad_normed * normed, -1, keepdims=True))


def rope_tables(places, half_dim):
    inv_freq = ROPE_BASE ** (-lax.iota(jnp.int32, half_dim).astype(jnp.float32) / half_dim)
    angles = places[:, None] * inv_freq[None, :]
    return (jnp.cos(angles)[:, None, :], jnp.sin(angles)[:, None, :])


def rotate(values, cosine, sine_part, direction):
    half_dim = values.shape[-1] // 2
    first_half = values[..., :half_dim]
    second_half = values[..., half_dim:]
    turned = direction * sine_part
    return jnp.concatenate(
        [first_half * cosine - second_half * turned, second_half * cosine + first_half * turned], -1
    )


def place():
    block = lax.axis_index("expert")
    lane = lax.axis_index("head")
    return block // 2, block % 2, lane // 2, lane % 2


def device(z, y, x, core):
    return (z * 2 + y, x * 2 + core)


def greet(z, y, x, core):
    barrier = pltpu.get_barrier_semaphore()

    def signal(target):
        pl.semaphore_signal(barrier, inc=1, device_id=target, device_id_type=MESH)

    signal(device(z, 1 - y, x, core))
    signal(device(z, y, 1 - x, core))
    signal(device(z, y, x, 1 - core))

    @pl.when(z > 0)
    def _():
        signal(device(z - 1, y, x, core))

    @pl.when(z < 3)
    def _():
        signal(device(z + 1, y, x, core))

    pl.semaphore_wait(barrier, 3 + (z > 0).astype(jnp.int32) + (z < 3).astype(jnp.int32))


def gather_kernel(own, whole, local_sem, send, recv):
    z, y, x, core = place()
    rows = own.shape[0]
    eighth = rows // 8
    me = z * 2 + y
    slab = pl.ds(pl.multiple_of(core * 4 * eighth + x * eighth, eighth), 3 * eighth)
    mine = pl.ds(pl.multiple_of(core * 4 * eighth + x * 3 * eighth, eighth), eighth)
    theirs = pl.ds(pl.multiple_of(core * 4 * eighth + (1 - x) * 3 * eighth, eighth), eighth)
    UP, DOWN, Y, X, CORE, CORE_X = range(6)

    def copy(kind, block, part, target, from_own=False):
        source = own.at[part] if from_own else whole.at[block, part]
        return pltpu.make_async_remote_copy(
            src_ref=source, dst_ref=whole.at[block, part],
            send_sem=send.at[kind, block], recv_sem=recv.at[kind, block],
            device_id=target, device_id_type=MESH)

    up = lambda b, o=False: copy(UP, b, slab, device(z + 1, y, x, core), o)
    down = lambda b, o=False: copy(DOWN, b, slab, device(z - 1, y, x, core), o)
    over = lambda b, o=False: copy(Y, b, slab, device(z, 1 - y, x, core), o)
    side = lambda b: copy(X, b, mine, device(z, y, 1 - x, core))
    twin = lambda b: copy(CORE, b, slab, device(z, y, x, 1 - core))
    twin_x = lambda b: copy(CORE_X, b, theirs, device(z, y, x, 1 - core))

    greet(z, y, x, core)
    keep = pltpu.make_async_copy(own, whole.at[me], local_sem)
    keep.start()

    @pl.when(z < 3)
    def _():
        up(me, True).start()

    @pl.when(z > 0)
    def _():
        down(me, True).start()

    over(me, True).start()

    def spread(b):
        side(b).start()
        twin(b).start()

    def from_y(zb):
        b = zb * 2 + 1 - y
        over(b).wait_recv()
        spread(b)

    for d in range(1, 4):
        @pl.when(z >= d)
        def _():
            b = (z - d) * 2 + y
            up(b).wait_recv()

            @pl.when(z < 3)
            def _():
                up(b).start()
            over(b).start()
            spread(b)

        @pl.when(z + d <= 3)
        def _():
            b = (z + d) * 2 + y
            down(b).wait_recv()

            @pl.when(z > 0)
            def _():
                down(b).start()
            over(b).start()
            spread(b)

        if d == 1:
            from_y(z)
        else:
            @pl.when(z >= d - 1)
            def _():
                from_y(z - (d - 1))

            @pl.when(z + d - 1 <= 3)
            def _():
                from_y(z + d - 1)

    @pl.when(z >= 3)
    def _():
        from_y(z - 3)

    @pl.when(z <= 0)
    def _():
        from_y(z + 3)

    for d in range(0, 4):
        def through(zb):
            for yb in (y, 1 - y):
                b = zb * 2 + yb

                def move():
                    side_in = copy(X, b, theirs, device(z, y, 1 - x, core))
                    side_in.wait_recv()
                    twin_x(b).start()
                if d == 0 and yb is y:
                    continue
                move()
        if d == 0:
            through(z)
        else:
            @pl.when(z >= d)
            def _():
                through(z - d)

            @pl.when(z + d <= 3)
            def _():
                through(z + d)

    other = pl.ds(pl.multiple_of((1 - core) * 4 * eighth + x * eighth, eighth), 3 * eighth)
    other_x = pl.ds(pl.multiple_of((1 - core) * 4 * eighth + (1 - x) * 3 * eighth, eighth), eighth)
    for b in range(8):
        zb, yb = b // 2, b % 2

        @pl.when(me != b)
        def _():
            copy(CORE, b, other, device(z, y, x, 1 - core)).wait_recv()
            copy(CORE_X, b, other_x, device(z, y, x, 1 - core)).wait_recv()
            side(b).wait_send()
            twin(b).wait_send()
            twin_x(b).wait_send()

        @pl.when(yb == y)
        def _():
            over(b).wait_send()

        @pl.when((yb == y) & (zb <= z) & (z < 3))
        def _():
            up(b).wait_send()

        @pl.when((yb == y) & (zb >= z) & (z > 0))
        def _():
            down(b).wait_send()
    keep.wait()


def gather_all(own, number):
    rows, width = own.shape
    return pl.pallas_call(
        gather_kernel,
        out_shape=jax.ShapeDtypeStruct((8, rows, width), own.dtype),
        in_specs=[pl.BlockSpec(memory_space=pl.ANY)],
        out_specs=pl.BlockSpec(memory_space=pl.ANY),
        scratch_shapes=[pltpu.SemaphoreType.DMA, pltpu.SemaphoreType.DMA((6, 8)), pltpu.SemaphoreType.DMA((6, 8))],
        compiler_params=pltpu.CompilerParams(collective_id=number, has_side_effects=True),
    )(own)


def add_rows(target, source, rows):
    step = 16

    @pl.loop(0, rows // step)
    def _(i):
        part = pl.ds(pl.multiple_of(i * step, step), step)
        target[part] = (target[part].astype(f32) + source[part].astype(f32)).astype(bf16)


def scatter_kernel(parts, total, held, from_core, from_x, from_y, from_below, from_above, shared_in,
                   load_sem, send, recv, end_send, end_recv):
    z, y, x, core = place()
    half = parts.shape[1] // 2
    piece = half // 4
    me = z * 2 + y
    ahead = z // 2
    order = (3 - 3 * ahead, 2 - ahead, z + 1 - 2 * (z % 2), z)
    my_half = pl.ds(pl.multiple_of(core * half, half), half)
    other_half = pl.ds(pl.multiple_of((1 - core) * half, half), half)
    slab = pl.ds(pl.multiple_of(x * piece, piece), 3 * piece)
    mine = pl.ds(pl.multiple_of(x * 3 * piece, piece), piece)
    theirs = pl.ds(pl.multiple_of((1 - x) * 3 * piece, piece), piece)
    shared = pl.ds(piece, 2 * piece)
    CORE, X, Y, UP, DOWN = range(5)

    def remote(kind, number, source, target, where):
        return pltpu.make_async_remote_copy(
            src_ref=source, dst_ref=target, send_sem=send.at[kind, number],
            recv_sem=recv.at[kind, number], device_id=where, device_id_type=MESH)

    def load(b):
        return pltpu.make_async_copy(parts.at[b, my_half], held.at[b], load_sem.at[b])

    def to_core(b):
        return remote(CORE, b, parts.at[b, other_half], from_core.at[b], device(z, y, x, 1 - core))

    def to_x(b):
        return remote(X, b, held.at[b, theirs], from_x.at[b], device(z, y, 1 - x, core))

    def to_y(zb):
        return remote(Y, zb, held.at[zb * 2 + 1 - y, slab], from_y.at[zb], device(z, 1 - y, x, core))

    def to_above(zb):
        return remote(UP, zb, held.at[zb * 2 + y, slab], from_below.at[zb], device(z + 1, y, x, core))

    def to_below(zb):
        return remote(DOWN, zb, held.at[zb * 2 + y, slab], from_above.at[zb], device(z - 1, y, x, core))

    greet(z, y, x, core)
    for zb in order:
        for yb in (1 - y, y):
            load(zb * 2 + yb).start()
            to_core(zb * 2 + yb).start()

    def stage_core(zb, yb):
        b = zb * 2 + yb
        load(b).wait()
        to_core(b).wait_recv()
        add_rows(held.at[b], from_core.at[b], half)
        to_x(b).start()

    def stage_x(zb, yb):
        b = zb * 2 + yb
        to_x(b).wait_recv()
        add_rows(held.at[b, mine], from_x.at[b], piece)

    def stage_y(zb):
        stage_x(zb, 1 - y)
        to_y(zb).start()

    def climb(zb):
        @pl.when(z > 0)
        def _():
            to_above(zb).wait_recv()
            add_rows(held.at[zb * 2 + y, slab], from_below.at[zb], 3 * piece)
        to_above(zb).start()

    def descend(zb):
        @pl.when(z < 3)
        def _():
            to_below(zb).wait_recv()
            add_rows(held.at[zb * 2 + y, slab], from_above.at[zb], 3 * piece)
        to_below(zb).start()

    def stage_z(i):
        zb = order[i]
        to_y(zb).wait_recv()
        add_rows(held.at[zb * 2 + y, slab], from_y.at[zb], 3 * piece)
        rises = (ahead == 0) if i < 2 else (z % 2 == 0)

        @pl.when(rises)
        def _():
            climb(zb)

        @pl.when(jnp.logical_not(rises))
        def _():
            descend(zb)

    stage_core(order[0], 1 - y)
    stage_core(order[0], y)
    for i in range(4):
        if i < 3:
            stage_core(order[i + 1], 1 - y)
        stage_y(order[i])
        if i < 3:
            stage_core(order[i + 1], y)
        stage_x(order[i], y)
        if i > 0:
            stage_z(i - 1)

    own = held.at[me]
    to_y(z).wait_recv()
    add_rows(own.at[slab], from_y.at[z], 3 * piece)

    @pl.when(z > 0)
    def _():
        to_above(z).wait_recv()
        add_rows(own.at[slab], from_below.at[z], 3 * piece)

    @pl.when(z < 3)
    def _():
        to_below(z).wait_recv()
        add_rows(own.at[slab], from_above.at[z], 3 * piece)

    def at_end(number, source, target, where):
        return pltpu.make_async_remote_copy(
            src_ref=source, dst_ref=target, send_sem=end_send.at[number],
            recv_sem=end_recv.at[number], device_id=where, device_id_type=MESH)

    base = core * half
    out_mine = pl.ds(pl.multiple_of(base + x * 3 * piece, piece), piece)
    out_theirs = pl.ds(pl.multiple_of(base + (1 - x) * 3 * piece, piece), piece)
    sums = at_end(0, held.at[me, shared], shared_in, device(z, y, 1 - x, core))
    ready = at_end(1, held.at[me, mine], total.at[out_mine], device(z, y, 1 - x, core))
    sums.start()
    ready.start()
    total[out_mine] = held[me, mine]
    sums.wait_recv()
    out_shared = pl.ds(pl.multiple_of(base + piece, piece), 2 * piece)
    total[out_shared] = (held[me, shared].astype(f32) + shared_in[...].astype(f32)).astype(bf16)
    at_end(1, held.at[me, mine], total.at[out_theirs], device(z, y, 1 - x, core)).wait_recv()
    finished = at_end(2, total.at[my_half], total.at[my_half], device(z, y, x, 1 - core))
    finished.start()
    at_end(2, total.at[my_half], total.at[other_half], device(z, y, x, 1 - core)).wait_recv()
    sums.wait_send()
    ready.wait_send()
    finished.wait_send()

    for b in range(8):
        zb, yb = b // 2, b % 2
        to_core(b).wait_send()
        to_x(b).wait_send()
        if yb == 0:
            to_y(zb).wait_send()

            @pl.when(zb > z)
            def _():
                to_above(zb).wait_send()

            @pl.when(zb < z)
            def _():
                to_below(zb).wait_send()


def scatter_sum(parts, number):
    _, rows, width = parts.shape
    half, piece = rows // 2, rows // 8
    return pl.pallas_call(
        scatter_kernel,
        out_shape=jax.ShapeDtypeStruct((rows, width), bf16),
        in_specs=[pl.BlockSpec(memory_space=pl.ANY)],
        out_specs=pl.BlockSpec(memory_space=pltpu.VMEM),
        scratch_shapes=[
            pltpu.VMEM((8, half, width), bf16),
            pltpu.VMEM((8, half, width), bf16),
            pltpu.VMEM((8, piece, width), bf16),
            pltpu.VMEM((4, 3 * piece, width), bf16),
            pltpu.VMEM((4, 3 * piece, width), bf16),
            pltpu.VMEM((4, 3 * piece, width), bf16),
            pltpu.VMEM((2 * piece, width), bf16),
            pltpu.SemaphoreType.DMA((8,)),
            pltpu.SemaphoreType.DMA((5, 8)),
            pltpu.SemaphoreType.DMA((5, 8)),
            pltpu.SemaphoreType.DMA((3,)),
            pltpu.SemaphoreType.DMA((3,)),
        ],
        compiler_params=pltpu.CompilerParams(collective_id=number, has_side_effects=True, vmem_limit_bytes=48 * 2**20),
    )(parts)
def dot(a,b): return jnp.dot(a,b,preferred_element_type=f32)
def dot_nt(a,b): return lax.dot_general(a,b,(((1,),(1,)),((),())),preferred_element_type=f32)
def dot_tn(a,b): return lax.dot_general(a,b,(((0,),(0,)),((),())),preferred_element_type=f32)

def moe_kernel(first, x_ref, g_ref, mask_ref, wr_ref, wg_ref, wu_ref, wd_ref, hg_ref, da_ref, gg_ref, out_ref, gx_ref):
    x = x_ref[...]
    g = g_ref[...]
    logits = dot(x, wr_ref[...])
    mask = mask_ref[...] > 0
    top = jnp.max(jnp.where(mask, logits, -jnp.inf), -1, keepdims=True)
    raised = jnp.where(mask, jnp.exp(jnp.where(mask, logits - top, 0.0)), 0.0)
    gates = raised / jnp.sum(raised, -1, keepdims=True)
    lanes = lax.broadcasted_iota(jnp.int32, gates.shape, 1)
    ff = wg_ref.shape[2]
    gx = None
    out = None
    gg = jnp.zeros(gates.shape, f32)
    for j in range(wg_ref.shape[0]):
        here = lanes == first[0] + j
        gate = jnp.sum(jnp.where(here, gates, 0.0), -1, keepdims=True)
        ga = dot(x, wg_ref[j])
        ua = dot(x, wu_ref[j])
        gw = dot_nt(g, wd_ref[j])
        s = 1.0 / (1.0 + jnp.exp(-ga))
        silu = ga * s
        h = (silu * ua).astype(bf16).astype(f32)
        gg = gg + jnp.where(here, jnp.sum(h * gw, -1, keepdims=True), 0.0)
        gh = gw * gate
        hg = (h * gate).astype(bf16)
        du = (gh * silu).astype(bf16)
        dg = (gh * ua * s * (1.0 + ga * (1.0 - s))).astype(bf16)
        hg_ref[:, j * ff:(j + 1) * ff] = hg
        da_ref[:, 2 * j * ff:(2 * j + 1) * ff] = dg
        da_ref[:, (2 * j + 1) * ff:(2 * j + 2) * ff] = du
        o = dot(hg, wd_ref[j])
        b = dot_nt(dg, wg_ref[j]) + dot_nt(du, wu_ref[j])
        out = o if out is None else out + o
        gx = b if gx is None else gx + b
    gg_ref[...] = gg
    out_ref[...] = out.astype(bf16)
    gx_ref[...] = gx.astype(bf16)

def moe(first, X, G, mask, wr, wg, wu, wd, bt=256):
    T, D = X.shape
    E = mask.shape[1]
    J, _, F = wg.shape
    blk = lambda w: pl.BlockSpec((bt, w), lambda i, s: (i, 0))
    full = lambda *shp: pl.BlockSpec(shp, lambda i, s: (0,) * len(shp))
    return pl.pallas_call(moe_kernel,
        grid_spec=pltpu.PrefetchScalarGridSpec(num_scalar_prefetch=1, grid=(T // bt,),
        in_specs=[blk(D), blk(D), blk(E), full(D, E), full(J, D, F), full(J, D, F), full(J, F, D)],
        out_specs=[blk(J * F), blk(2 * J * F), blk(E), blk(D), blk(D)]),
        out_shape=[jax.ShapeDtypeStruct((T, J * F), bf16), jax.ShapeDtypeStruct((T, 2 * J * F), bf16), jax.ShapeDtypeStruct((T, E), f32),
                   jax.ShapeDtypeStruct((T, D), bf16), jax.ShapeDtypeStruct((T, D), bf16)],
        compiler_params=pltpu.CompilerParams(vmem_limit_bytes=56 * 2**20),
    )(first, X, G, mask, wr, wg, wu, wd)

def tn_kernel(a_ref, b_ref, o_ref):
    o_ref[...] = dot_tn(a_ref[...], b_ref[...])

def tn(a, b, bm=256, bn=None, fuse=False):
    T, M = a.shape
    N = b.shape[1]
    bn = bn or N
    return pl.pallas_call(tn_kernel, grid=(M // bm, N // bn),
        in_specs=[pl.BlockSpec((T, bm), lambda i, j: (0, i)), pl.BlockSpec((T, bn), lambda i, j: (0, j))],
        out_specs=pl.BlockSpec((bm, bn), lambda i, j: (i, j)),
        out_shape=jax.ShapeDtypeStruct((M, N), f32),
        compiler_params=pltpu.CompilerParams(vmem_limit_bytes=56 * 2**20, fuse_transposed_lhs_in_matmul=fuse))(a, b)


def on_device(
    hidden_in,
    norm1_gain,
    w_query,
    w_key,
    w_value,
    w_out,
    query_gain,
    key_gain,
    norm2_gain,
    w_router,
    w_gate,
    w_up,
    w_down,
    routes,
    segments,
    cotangent,
):
    seq_len, width = hidden_in.shape
    local_width = w_query.shape[1]
    head_count = local_width // HEAD_DIM
    expert_devs = lax.axis_size("expert")
    local_experts = w_gate.shape[0]
    expert_total = w_router.shape[1]
    capacity = 2 * seq_len * TOP // expert_total
    slab_rows = local_experts * capacity
    my_index = lax.axis_index("expert")
    group = SEQ // seq_len
    rank = my_index % group
    f32 = jnp.float32
    bf16 = jnp.bfloat16

    def split_heads(values):
        return values.reshape(seq_len, head_count, HEAD_DIM)

    inputs = hidden_in.astype(f32)
    inverse_attn = inverse_rms(inputs)
    normed_attn = inputs * inverse_attn
    attn_input = (normed_attn * norm1_gain).astype(bf16)
    q_raw = split_heads(jnp.dot(attn_input, w_query, preferred_element_type=f32))
    k_raw = split_heads(jnp.dot(attn_input, w_key, preferred_element_type=f32))
    v_heads = split_heads(jnp.dot(attn_input, w_value, preferred_element_type=f32).astype(bf16))
    q_gains = query_gain.reshape(head_count, HEAD_DIM)
    k_gains = key_gain.reshape(head_count, HEAD_DIM)
    q_inverse = inverse_rms(q_raw)
    q_normed = q_raw * q_inverse
    k_inverse = inverse_rms(k_raw)
    k_normed = k_raw * k_inverse
    local_places = lax.iota(jnp.int32, seq_len)
    query_places = rank * seq_len + local_places
    cosine, sine_part = rope_tables(query_places.astype(f32), HEAD_DIM // 2)
    queries = rotate(q_normed * q_gains, cosine, sine_part, 1.0).astype(bf16)
    key_rot = rotate(k_normed * k_gains, cosine, sine_part, 1.0).astype(bf16)
    score_scale = HEAD_DIM ** (-0.5)
    keys_values = jnp.stack([key_rot, v_heads])
    pieces = [keys_values]
    for offset in range(1, group):
        keys_values = from_behind(keys_values, "expert", 1)
        pieces.append(keys_values)
    stacked = jnp.stack(pieces, 1).reshape(2, group * seq_len, head_count, HEAD_DIM)
    keys_all = stacked[0]
    values_all = stacked[1]
    query_segs = lax.dynamic_slice_in_dim(segments, my_index * seq_len, seq_len, 0)
    key_segs = jnp.concatenate(
        [
            lax.dynamic_slice_in_dim(
                segments, jnp.maximum(my_index - offset, 0) * seq_len, seq_len, 0
            )
            for offset in range(group)
        ],
        0,
    )
    offsets = lax.iota(jnp.int32, group)
    key_places = ((rank - offsets)[:, None] * seq_len + local_places[None, :]).reshape(-1)
    key_valid = jnp.repeat(rank - offsets >= 0, seq_len)
    allowed = (
        key_valid[None, :]
        & (query_places[:, None] >= key_places[None, :])
        & (query_segs[:, None] == key_segs[None, :])
    )

    def scores_of():
        raw_scores = (
            jnp.einsum("thd,shd->hts", queries, keys_all, preferred_element_type=f32) * score_scale
        )
        return jnp.where(allowed[None], raw_scores, MASKED)

    scores = scores_of()
    row_max = jnp.max(scores, -1, keepdims=True)
    raised = jnp.exp(scores - row_max)
    exp_total = jnp.sum(raised, -1, keepdims=True)
    log_total = row_max + jnp.log(exp_total)
    attn_probs = (raised / exp_total).astype(bf16)
    context = (
        jnp.einsum("hts,shd->thd", attn_probs, values_all, preferred_element_type=f32)
        .reshape(seq_len, local_width)
        .astype(bf16)
    )
    attn_part = jnp.dot(context, w_out, preferred_element_type=f32)
    middle = inputs + lax.psum(attn_part, "head")
    inverse_moe = inverse_rms(middle)
    normed_moe = middle * inverse_moe
    moe_input = (normed_moe * norm2_gain).astype(bf16)
    logits = jnp.dot(moe_input, w_router, preferred_element_type=f32)
    chosen = jnp.take_along_axis(logits, routes, 1)
    raised_gate = jnp.exp(chosen - jnp.max(chosen, -1, keepdims=True))
    gate_weights = raised_gate / jnp.sum(raised_gate, -1, keepdims=True)
    catalog = lax.iota(jnp.int32, expert_total)
    route_hot = (routes[:, :, None] == catalog).astype(jnp.int32)
    token_hot = jnp.sum(route_hot, 1, dtype=jnp.int32)
    earlier = jnp.cumsum(token_hot, 0, dtype=jnp.int32) - token_hot
    position = routes * capacity + jnp.take_along_axis(earlier, routes, 1)
    flat_pos = position.reshape(-1)
    owners = (
        jnp.full((expert_total * capacity,), seq_len, jnp.int32)
        .at[flat_pos]
        .set(jnp.repeat(lax.iota(jnp.int32, seq_len), TOP))
    )
    padded = jnp.concatenate([moe_input, jnp.zeros((1, width), bf16)], 0)
    outgoing = padded[owners].reshape(expert_devs, slab_rows, width)
    arrived = lax.all_to_all(outgoing, "expert", split_axis=0, concat_axis=0, tiled=True)
    rows_in = arrived.reshape(expert_devs, local_experts, capacity, width)
    gate_act = jnp.einsum("sjcd,jdf->sjcf", rows_in, w_gate, preferred_element_type=f32)
    up_act = jnp.einsum("sjcd,jdf->sjcf", rows_in, w_up, preferred_element_type=f32)
    hidden = (jax.nn.silu(gate_act) * up_act).astype(bf16)
    partial_out = jnp.einsum("sjcf,jfd->sjcd", hidden, w_down, preferred_element_type=f32).reshape(
        expert_devs, slab_rows, width
    )
    rows_out = (
        lax.psum_scatter(partial_out.astype(jnp.bfloat16), "head", scatter_dimension=2, tiled=True)
        .astype(jnp.float32)
        .astype(bf16)
    )
    leaving = lax.all_gather(rows_out, "head", axis=2, tiled=True)
    returned = lax.all_to_all(leaving, "expert", split_axis=0, concat_axis=0, tiled=True)
    picked = returned.reshape(expert_total * capacity, width)[position]
    moe_out = jnp.einsum("tk,tkd->td", gate_weights, picked, preferred_element_type=f32)
    output = (middle + moe_out).astype(bf16)
    grad_final = cotangent.astype(f32)
    grad_gates = jnp.einsum("td,tkd->tk", grad_final, picked, preferred_element_type=f32)
    grad_chosen = gate_weights * (
        grad_gates - jnp.sum(grad_gates * gate_weights, -1, keepdims=True)
    )
    grad_logits = jnp.einsum("tk,tke->te", grad_chosen, route_hot.astype(f32)).astype(bf16)
    grad_router = jnp.dot(moe_input.T, grad_logits, preferred_element_type=f32)
    grad_moe_input = jnp.dot(grad_logits, w_router.T, preferred_element_type=f32)
    grad_expert_out = (gate_weights[:, :, None] * grad_final[:, None, :]).astype(bf16)
    grad_slab = (
        jnp.zeros((expert_total * capacity, width), bf16)
        .at[flat_pos]
        .set(grad_expert_out.reshape(seq_len * TOP, width))
    )
    grad_slab = grad_slab.reshape(expert_devs, slab_rows, width)
    grad_arrived = lax.all_to_all(grad_slab, "expert", split_axis=0, concat_axis=0, tiled=True)
    grad_rows_out = grad_arrived.reshape(expert_devs, local_experts, capacity, width)
    grad_hidden = jnp.einsum("sjcd,jfd->sjcf", grad_rows_out, w_down, preferred_element_type=f32)
    grad_down = jnp.einsum("sjcf,sjcd->jfd", hidden, grad_rows_out, preferred_element_type=f32)
    sigmoid = jax.nn.sigmoid(gate_act)
    grad_up_act = (grad_hidden * gate_act * sigmoid).astype(bf16)
    grad_gate_act = (grad_hidden * up_act * sigmoid * (1.0 + gate_act * (1.0 - sigmoid))).astype(
        bf16
    )
    grad_gate = jnp.einsum("sjcd,sjcf->jdf", rows_in, grad_gate_act, preferred_element_type=f32)
    grad_up = jnp.einsum("sjcd,sjcf->jdf", rows_in, grad_up_act, preferred_element_type=f32)
    grad_rows_in = jnp.einsum("sjcf,jdf->sjcd", grad_gate_act, w_gate, preferred_element_type=f32)
    grad_rows_in = grad_rows_in + jnp.einsum(
        "sjcf,jdf->sjcd", grad_up_act, w_up, preferred_element_type=f32
    )
    grad_back = (
        lax.psum_scatter(
            grad_rows_in.reshape(expert_devs, slab_rows, width).astype(jnp.bfloat16),
            "head",
            scatter_dimension=2,
            tiled=True,
        )
        .astype(jnp.float32)
        .astype(bf16)
    )
    leaving_grad = lax.all_gather(grad_back, "head", axis=2, tiled=True)
    grad_home = lax.all_to_all(leaving_grad, "expert", split_axis=0, concat_axis=0, tiled=True)
    grad_moe_input = grad_moe_input + jnp.sum(
        grad_home.reshape(expert_total * capacity, width)[position], 1, dtype=f32
    )
    grad_norm2 = jnp.sum(grad_moe_input * normed_moe, 0)
    grad_middle = grad_final + norm_back(grad_moe_input * norm2_gain, normed_moe, inverse_moe)
    grad_attn = grad_middle.astype(bf16)
    grad_out_turned = jnp.dot(grad_attn.T, context, preferred_element_type=f32)
    grad_context = split_heads(jnp.dot(grad_attn, w_out.T, preferred_element_type=f32).astype(bf16))
    attn_full = jnp.exp(scores_of() - log_total)
    attn_low = attn_full.astype(bf16)
    grad_values_all = jnp.einsum("hts,thd->shd", attn_low, grad_context, preferred_element_type=f32)
    grad_probs = jnp.einsum("thd,shd->hts", grad_context, values_all, preferred_element_type=f32)
    grad_scores = (
        attn_full * (grad_probs - jnp.sum(grad_probs * attn_full, -1, keepdims=True))
    ).astype(bf16)
    grad_queries = (
        jnp.einsum("hts,shd->thd", grad_scores, keys_all, preferred_element_type=f32) * score_scale
    )
    grad_keys_all = (
        jnp.einsum("hts,thd->shd", grad_scores, queries, preferred_element_type=f32) * score_scale
    )
    kv_terms = jnp.stack([grad_keys_all, grad_values_all]).reshape(
        2, group, seq_len, head_count, HEAD_DIM
    )
    kv_total = kv_terms[:, 0]
    for offset in range(1, group):
        kv_total = kv_total + from_behind(
            kv_terms[:, offset].astype(jnp.bfloat16), "expert", -offset
        ).astype(jnp.float32)
    grad_keys = kv_total[0]
    grad_values = kv_total[1]
    grad_q_normed = rotate(grad_queries, cosine, sine_part, -1.0)
    grad_k_normed = rotate(grad_keys, cosine, sine_part, -1.0)
    grad_query_gain = jnp.sum(grad_q_normed * q_normed, 0).reshape(local_width)
    grad_key_gain = jnp.sum(grad_k_normed * k_normed, 0).reshape(local_width)
    grad_q_raw = (
        norm_back(grad_q_normed * q_gains, q_normed, q_inverse)
        .reshape(seq_len, local_width)
        .astype(bf16)
    )
    grad_k_raw = (
        norm_back(grad_k_normed * k_gains, k_normed, k_inverse)
        .reshape(seq_len, local_width)
        .astype(bf16)
    )
    grad_v_raw = grad_values.reshape(seq_len, local_width).astype(bf16)
    grad_query = jnp.dot(attn_input.T, grad_q_raw, preferred_element_type=f32)
    grad_key = jnp.dot(attn_input.T, grad_k_raw, preferred_element_type=f32)
    grad_value = jnp.dot(attn_input.T, grad_v_raw, preferred_element_type=f32)
    input_part = jnp.dot(grad_q_raw, w_query.T, preferred_element_type=f32)
    input_part = input_part + jnp.dot(grad_k_raw, w_key.T, preferred_element_type=f32)
    input_part = input_part + jnp.dot(grad_v_raw, w_value.T, preferred_element_type=f32)
    grad_attn_input = lax.psum(input_part.astype(jnp.bfloat16), "head").astype(jnp.float32)
    grad_norm1 = jnp.sum(grad_attn_input * normed_attn, 0)
    grad_input = grad_middle + norm_back(grad_attn_input * norm1_gain, normed_attn, inverse_attn)
    grad_query, grad_key, grad_value, grad_out_turned = (
        lax.psum_scatter(
            grad_query.astype(jnp.bfloat16), "expert", scatter_dimension=0, tiled=True
        ).astype(jnp.float32),
        lax.psum_scatter(
            grad_key.astype(jnp.bfloat16), "expert", scatter_dimension=0, tiled=True
        ).astype(jnp.float32),
        lax.psum_scatter(
            grad_value.astype(jnp.bfloat16), "expert", scatter_dimension=0, tiled=True
        ).astype(jnp.float32),
        lax.psum_scatter(
            grad_out_turned.astype(jnp.bfloat16), "expert", scatter_dimension=0, tiled=True
        ).astype(jnp.float32),
    )
    grad_router, grad_norm1, grad_norm2, grad_query_gain, grad_key_gain = (
        lax.psum(grad_router.astype(jnp.bfloat16), "expert").astype(jnp.float32),
        lax.psum(grad_norm1.astype(jnp.bfloat16), "expert").astype(jnp.float32),
        lax.psum(grad_norm2.astype(jnp.bfloat16), "expert").astype(jnp.float32),
        lax.psum(grad_query_gain.astype(jnp.bfloat16), "expert").astype(jnp.float32),
        lax.psum(grad_key_gain.astype(jnp.bfloat16), "expert").astype(jnp.float32),
    )
    return (
        output,
        grad_input,
        grad_norm1,
        grad_query,
        grad_key,
        grad_value,
        grad_out_turned.T,
        grad_query_gain,
        grad_key_gain,
        grad_norm2,
        grad_router,
        grad_gate,
        grad_up,
        grad_down,
    )


def on_device_dense(
    hidden_in,
    norm1_gain,
    w_query,
    w_key,
    w_value,
    w_out,
    query_gain,
    key_gain,
    norm2_gain,
    w_router,
    w_gate,
    w_up,
    w_down,
    routes,
    segments,
    cotangent,
):
    seq_len, width = hidden_in.shape
    local_width = w_query.shape[1]
    head_count = local_width // HEAD_DIM
    expert_devs = lax.axis_size("expert")
    local_experts = w_gate.shape[0]
    expert_total = w_router.shape[1]
    capacity = 2 * seq_len * TOP // expert_total
    slab_rows = local_experts * capacity
    my_index = lax.axis_index("expert")
    group = SEQ // seq_len
    rank = my_index % group
    f32 = jnp.float32
    bf16 = jnp.bfloat16

    def split_heads(values):
        return values.reshape(seq_len, head_count, HEAD_DIM)

    inputs = hidden_in.astype(f32)
    inverse_attn = inverse_rms(inputs)
    normed_attn = inputs * inverse_attn
    attn_input = (normed_attn * norm1_gain).astype(bf16)
    q_raw = split_heads(jnp.dot(attn_input, w_query, preferred_element_type=f32))
    k_raw = split_heads(jnp.dot(attn_input, w_key, preferred_element_type=f32))
    v_heads = split_heads(jnp.dot(attn_input, w_value, preferred_element_type=f32).astype(bf16))
    q_gains = query_gain.reshape(head_count, HEAD_DIM)
    k_gains = key_gain.reshape(head_count, HEAD_DIM)
    q_inverse = inverse_rms(q_raw)
    q_normed = q_raw * q_inverse
    k_inverse = inverse_rms(k_raw)
    k_normed = k_raw * k_inverse
    local_places = lax.iota(jnp.int32, seq_len)
    query_places = rank * seq_len + local_places
    cosine, sine_part = rope_tables(query_places.astype(f32), HEAD_DIM // 2)
    queries = rotate(q_normed * q_gains, cosine, sine_part, 1.0).astype(bf16)
    key_rot = rotate(k_normed * k_gains, cosine, sine_part, 1.0).astype(bf16)
    score_scale = HEAD_DIM ** (-0.5)
    keys_values = jnp.stack([key_rot, v_heads])
    pieces = [keys_values]
    for offset in range(1, group):
        keys_values = from_behind(keys_values, "expert", 1)
        pieces.append(keys_values)
    stacked = jnp.stack(pieces, 1).reshape(2, group * seq_len, head_count, HEAD_DIM)
    keys_all = stacked[0]
    values_all = stacked[1]
    query_segs = lax.dynamic_slice_in_dim(segments, my_index * seq_len, seq_len, 0)
    key_segs = jnp.concatenate(
        [
            lax.dynamic_slice_in_dim(
                segments, jnp.maximum(my_index - offset, 0) * seq_len, seq_len, 0
            )
            for offset in range(group)
        ],
        0,
    )
    offsets = lax.iota(jnp.int32, group)
    key_places = ((rank - offsets)[:, None] * seq_len + local_places[None, :]).reshape(-1)
    key_valid = jnp.repeat(rank - offsets >= 0, seq_len)
    allowed = (
        key_valid[None, :]
        & (query_places[:, None] >= key_places[None, :])
        & (query_segs[:, None] == key_segs[None, :])
    )

    def scores_of():
        raw_scores = (
            jnp.einsum("thd,shd->hts", queries, keys_all, preferred_element_type=f32) * score_scale
        )
        return jnp.where(allowed[None], raw_scores, MASKED)

    scores = scores_of()
    row_max = jnp.max(scores, -1, keepdims=True)
    raised = jnp.exp(scores - row_max)
    exp_total = jnp.sum(raised, -1, keepdims=True)
    log_total = row_max + jnp.log(exp_total)
    attn_probs = (raised / exp_total).astype(bf16)
    context = (
        jnp.einsum("hts,shd->thd", attn_probs, values_all, preferred_element_type=f32)
        .reshape(seq_len, local_width)
        .astype(bf16)
    )
    attn_part = jnp.dot(context, w_out, preferred_element_type=f32)
    middle = inputs + lax.psum(attn_part, "head")
    inverse_moe = inverse_rms(middle)
    normed_moe = middle * inverse_moe
    moe_input = (normed_moe * norm2_gain).astype(bf16)
    everyone = gather_all(moe_input, 1).reshape(expert_devs * seq_len, width)
    all_grads = gather_all(cotangent, 2).reshape(expert_devs * seq_len, width)
    all_routes = lax.all_gather(routes, "expert", axis=0, tiled=True)
    catalog = lax.iota(jnp.int32, expert_total)
    mask = jnp.sum((all_routes[:, :, None] == catalog).astype(f32), 1)
    first = jnp.full((1,), local_experts, jnp.int32) * my_index
    weighted, grad_acts, grad_gates, out_part, grad_part = moe(
        first, everyone, all_grads, mask, w_router, w_gate, w_up, w_down
    )
    ff = w_gate.shape[2]
    grad_down = tn(weighted, all_grads, 512, 512).reshape(local_experts, ff, width)
    acts = tn(everyone, grad_acts, 512, 1024).reshape(width, local_experts, 2, ff)
    grad_gate = acts[:, :, 0].transpose(1, 0, 2)
    grad_up = acts[:, :, 1].transpose(1, 0, 2)
    shape = (expert_devs, seq_len, width)
    moe_out = scatter_sum(out_part.reshape(shape), 3)
    home = scatter_sum(grad_part.reshape(shape), 4)
    output = (middle + moe_out.astype(f32)).astype(bf16)
    grad_final = cotangent.astype(f32)
    grad_gates = lax.psum(grad_gates, ("expert", "head"))
    grad_gates = lax.dynamic_slice_in_dim(grad_gates, my_index * seq_len, seq_len, 0)
    own_mask = lax.dynamic_slice_in_dim(mask, my_index * seq_len, seq_len, 0) > 0
    logits = jnp.where(own_mask, jnp.dot(moe_input, w_router, preferred_element_type=f32), -jnp.inf)
    raised_gate = jnp.exp(logits - jnp.max(logits, -1, keepdims=True))
    gate_weights = raised_gate / jnp.sum(raised_gate, -1, keepdims=True)
    grad_logits = (
        gate_weights * (grad_gates - jnp.sum(grad_gates * gate_weights, -1, keepdims=True))
    ).astype(bf16)
    grad_router = jnp.dot(moe_input.T, grad_logits, preferred_element_type=f32)
    grad_moe_input = jnp.dot(grad_logits, w_router.T, preferred_element_type=f32) + home.astype(f32)
    grad_norm2 = jnp.sum(grad_moe_input * normed_moe, 0)
    grad_middle = grad_final + norm_back(grad_moe_input * norm2_gain, normed_moe, inverse_moe)
    grad_attn = grad_middle.astype(bf16)
    grad_out_turned = jnp.dot(grad_attn.T, context, preferred_element_type=f32)
    grad_context = split_heads(jnp.dot(grad_attn, w_out.T, preferred_element_type=f32).astype(bf16))
    attn_full = jnp.exp(scores_of() - log_total)
    attn_low = attn_full.astype(bf16)
    grad_values_all = jnp.einsum("hts,thd->shd", attn_low, grad_context, preferred_element_type=f32)
    grad_probs = jnp.einsum("thd,shd->hts", grad_context, values_all, preferred_element_type=f32)
    grad_scores = (
        attn_full * (grad_probs - jnp.sum(grad_probs * attn_full, -1, keepdims=True))
    ).astype(bf16)
    grad_queries = (
        jnp.einsum("hts,shd->thd", grad_scores, keys_all, preferred_element_type=f32) * score_scale
    )
    grad_keys_all = (
        jnp.einsum("hts,thd->shd", grad_scores, queries, preferred_element_type=f32) * score_scale
    )
    kv_terms = jnp.stack([grad_keys_all, grad_values_all]).reshape(
        2, group, seq_len, head_count, HEAD_DIM
    )
    kv_total = kv_terms[:, 0]
    for offset in range(1, group):
        kv_total = kv_total + from_behind(
            kv_terms[:, offset].astype(jnp.bfloat16), "expert", -offset
        ).astype(jnp.float32)
    grad_keys = kv_total[0]
    grad_values = kv_total[1]
    grad_q_normed = rotate(grad_queries, cosine, sine_part, -1.0)
    grad_k_normed = rotate(grad_keys, cosine, sine_part, -1.0)
    grad_query_gain = jnp.sum(grad_q_normed * q_normed, 0).reshape(local_width)
    grad_key_gain = jnp.sum(grad_k_normed * k_normed, 0).reshape(local_width)
    grad_q_raw = (
        norm_back(grad_q_normed * q_gains, q_normed, q_inverse)
        .reshape(seq_len, local_width)
        .astype(bf16)
    )
    grad_k_raw = (
        norm_back(grad_k_normed * k_gains, k_normed, k_inverse)
        .reshape(seq_len, local_width)
        .astype(bf16)
    )
    grad_v_raw = grad_values.reshape(seq_len, local_width).astype(bf16)
    grad_query = jnp.dot(attn_input.T, grad_q_raw, preferred_element_type=f32)
    grad_key = jnp.dot(attn_input.T, grad_k_raw, preferred_element_type=f32)
    grad_value = jnp.dot(attn_input.T, grad_v_raw, preferred_element_type=f32)
    input_part = jnp.dot(grad_q_raw, w_query.T, preferred_element_type=f32)
    input_part = input_part + jnp.dot(grad_k_raw, w_key.T, preferred_element_type=f32)
    input_part = input_part + jnp.dot(grad_v_raw, w_value.T, preferred_element_type=f32)
    grad_attn_input = lax.psum(input_part.astype(jnp.bfloat16), "head").astype(jnp.float32)
    grad_norm1 = jnp.sum(grad_attn_input * normed_attn, 0)
    grad_input = grad_middle + norm_back(grad_attn_input * norm1_gain, normed_attn, inverse_attn)
    grad_query, grad_key, grad_value, grad_out_turned = (
        lax.psum_scatter(
            grad_query.astype(jnp.bfloat16), "expert", scatter_dimension=0, tiled=True
        ).astype(jnp.float32),
        lax.psum_scatter(
            grad_key.astype(jnp.bfloat16), "expert", scatter_dimension=0, tiled=True
        ).astype(jnp.float32),
        lax.psum_scatter(
            grad_value.astype(jnp.bfloat16), "expert", scatter_dimension=0, tiled=True
        ).astype(jnp.float32),
        lax.psum_scatter(
            grad_out_turned.astype(jnp.bfloat16), "expert", scatter_dimension=0, tiled=True
        ).astype(jnp.float32),
    )
    grad_router, grad_norm1, grad_norm2, grad_query_gain, grad_key_gain = (
        lax.psum(grad_router.astype(jnp.bfloat16), "expert").astype(jnp.float32),
        lax.psum(grad_norm1.astype(jnp.bfloat16), "expert").astype(jnp.float32),
        lax.psum(grad_norm2.astype(jnp.bfloat16), "expert").astype(jnp.float32),
        lax.psum(grad_query_gain.astype(jnp.bfloat16), "expert").astype(jnp.float32),
        lax.psum(grad_key_gain.astype(jnp.bfloat16), "expert").astype(jnp.float32),
    )
    return (
        output,
        grad_input,
        grad_norm1,
        grad_query,
        grad_key,
        grad_value,
        grad_out_turned.T,
        grad_query_gain,
        grad_key_gain,
        grad_norm2,
        grad_router,
        grad_gate,
        grad_up,
        grad_down,
    )


def solution(mesh):
    experts, heads = mesh.shape["expert"], mesh.shape["head"]
    form = on_device_dense if (experts, heads) == (8, 4) else on_device
    return jax.shard_map(
        form,
        mesh=mesh,
        in_specs=(
            P("expert", None),
            P(),
            P(None, "head"),
            P(None, "head"),
            P(None, "head"),
            P("head", None),
            P("head"),
            P("head"),
            P(),
            P(),
            P("expert", None, "head"),
            P("expert", None, "head"),
            P("expert", "head", None),
            P("expert", None),
            P(),
            P("expert", None),
        ),
        out_specs=(
            P("expert", None),
            P("expert", None),
            P(),
            P("expert", "head"),
            P("expert", "head"),
            P("expert", "head"),
            P("head", "expert"),
            P("head"),
            P("head"),
            P(),
            P(),
            P("expert", None, "head"),
            P("expert", None, "head"),
            P("expert", "head", None),
        ),
        check_vma=False,
    )
```

```python
import functools

import jax
import jax.numpy as jnp
from jax import lax
from jax.experimental import pallas as pl
from jax.experimental.pallas import tpu as pltpu
from jax.sharding import PartitionSpec as P

HEAD_DIM = 128
TOP = 8
SEQ = 2048
MESH = pl.DeviceIdType.MESH
bf16 = jnp.bfloat16
f32 = jnp.float32


EPSILON = 1e-05
ROPE_BASE = 10000.0
MASKED = -1000000000.0


def from_behind(shard, axis, by):
    size = lax.axis_size(axis)
    pairs = [(i, i + by) for i in range(size) if 0 <= i + by < size]
    return lax.ppermute(shard, axis, pairs)


def inverse_rms(values):
    return lax.rsqrt(jnp.mean(values * values, -1, keepdims=True) + EPSILON)


def norm_back(grad_normed, normed, inverse):
    return inverse * (grad_normed - normed * jnp.mean(grad_normed * normed, -1, keepdims=True))


def rope_tables(places, half_dim):
    inv_freq = ROPE_BASE ** (-lax.iota(jnp.int32, half_dim).astype(jnp.float32) / half_dim)
    angles = places[:, None] * inv_freq[None, :]
    return (jnp.cos(angles)[:, None, :], jnp.sin(angles)[:, None, :])


def rotate(values, cosine, sine_part, direction):
    half_dim = values.shape[-1] // 2
    first_half = values[..., :half_dim]
    second_half = values[..., half_dim:]
    turned = direction * sine_part
    return jnp.concatenate(
        [first_half * cosine - second_half * turned, second_half * cosine + first_half * turned], -1
    )


def place():
    block = lax.axis_index("expert")
    lane = lax.axis_index("head")
    return block // 2, block % 2, lane // 2, lane % 2


def device(z, y, x, core):
    return (z * 2 + y, x * 2 + core)


def greet(z, y, x, core):
    barrier = pltpu.get_barrier_semaphore()

    def signal(target):
        pl.semaphore_signal(barrier, inc=1, device_id=target, device_id_type=MESH)

    signal(device(z, 1 - y, x, core))
    signal(device(z, y, 1 - x, core))
    signal(device(z, y, x, 1 - core))

    @pl.when(z > 0)
    def _():
        signal(device(z - 1, y, x, core))

    @pl.when(z < 3)
    def _():
        signal(device(z + 1, y, x, core))

    pl.semaphore_wait(barrier, 3 + (z > 0).astype(jnp.int32) + (z < 3).astype(jnp.int32))


def gather_kernel(own, whole, local_sem, send, recv):
    z, y, x, core = place()
    rows = own.shape[0]
    eighth = rows // 8
    me = z * 2 + y
    slab = pl.ds(pl.multiple_of(core * 4 * eighth + x * eighth, eighth), 3 * eighth)
    mine = pl.ds(pl.multiple_of(core * 4 * eighth + x * 3 * eighth, eighth), eighth)
    theirs = pl.ds(pl.multiple_of(core * 4 * eighth + (1 - x) * 3 * eighth, eighth), eighth)
    UP, DOWN, Y, X, CORE, CORE_X = range(6)

    def copy(kind, block, part, target, from_own=False):
        source = own.at[part] if from_own else whole.at[block, part]
        return pltpu.make_async_remote_copy(
            src_ref=source, dst_ref=whole.at[block, part],
            send_sem=send.at[kind, block], recv_sem=recv.at[kind, block],
            device_id=target, device_id_type=MESH)

    up = lambda b, o=False: copy(UP, b, slab, device(z + 1, y, x, core), o)
    down = lambda b, o=False: copy(DOWN, b, slab, device(z - 1, y, x, core), o)
    over = lambda b, o=False: copy(Y, b, slab, device(z, 1 - y, x, core), o)
    side = lambda b: copy(X, b, mine, device(z, y, 1 - x, core))
    twin = lambda b: copy(CORE, b, slab, device(z, y, x, 1 - core))
    twin_x = lambda b: copy(CORE_X, b, theirs, device(z, y, x, 1 - core))

    greet(z, y, x, core)
    keep = pltpu.make_async_copy(own, whole.at[me], local_sem)
    keep.start()

    @pl.when(z < 3)
    def _():
        up(me, True).start()

    @pl.when(z > 0)
    def _():
        down(me, True).start()

    over(me, True).start()

    def spread(b):
        side(b).start()
        twin(b).start()

    def from_y(zb):
        b = zb * 2 + 1 - y
        over(b).wait_recv()
        spread(b)

    for d in range(1, 4):
        @pl.when(z >= d)
        def _():
            b = (z - d) * 2 + y
            up(b).wait_recv()

            @pl.when(z < 3)
            def _():
                up(b).start()
            over(b).start()
            spread(b)

        @pl.when(z + d <= 3)
        def _():
            b = (z + d) * 2 + y
            down(b).wait_recv()

            @pl.when(z > 0)
            def _():
                down(b).start()
            over(b).start()
            spread(b)

        if d == 1:
            from_y(z)
        else:
            @pl.when(z >= d - 1)
            def _():
                from_y(z - (d - 1))

            @pl.when(z + d - 1 <= 3)
            def _():
                from_y(z + d - 1)

    @pl.when(z >= 3)
    def _():
        from_y(z - 3)

    @pl.when(z <= 0)
    def _():
        from_y(z + 3)

    for d in range(0, 4):
        def through(zb):
            for yb in (y, 1 - y):
                b = zb * 2 + yb

                def move():
                    side_in = copy(X, b, theirs, device(z, y, 1 - x, core))
                    side_in.wait_recv()
                    twin_x(b).start()
                if d == 0 and yb is y:
                    continue
                move()
        if d == 0:
            through(z)
        else:
            @pl.when(z >= d)
            def _():
                through(z - d)

            @pl.when(z + d <= 3)
            def _():
                through(z + d)

    other = pl.ds(pl.multiple_of((1 - core) * 4 * eighth + x * eighth, eighth), 3 * eighth)
    other_x = pl.ds(pl.multiple_of((1 - core) * 4 * eighth + (1 - x) * 3 * eighth, eighth), eighth)
    for b in range(8):
        zb, yb = b // 2, b % 2

        @pl.when(me != b)
        def _():
            copy(CORE, b, other, device(z, y, x, 1 - core)).wait_recv()
            copy(CORE_X, b, other_x, device(z, y, x, 1 - core)).wait_recv()
            side(b).wait_send()
            twin(b).wait_send()
            twin_x(b).wait_send()

        @pl.when(yb == y)
        def _():
            over(b).wait_send()

        @pl.when((yb == y) & (zb <= z) & (z < 3))
        def _():
            up(b).wait_send()

        @pl.when((yb == y) & (zb >= z) & (z > 0))
        def _():
            down(b).wait_send()
    keep.wait()


def gather_all(own, number):
    rows, width = own.shape
    return pl.pallas_call(
        gather_kernel,
        out_shape=jax.ShapeDtypeStruct((8, rows, width), own.dtype),
        in_specs=[pl.BlockSpec(memory_space=pl.ANY)],
        out_specs=pl.BlockSpec(memory_space=pl.ANY),
        scratch_shapes=[pltpu.SemaphoreType.DMA, pltpu.SemaphoreType.DMA((6, 8)), pltpu.SemaphoreType.DMA((6, 8))],
        compiler_params=pltpu.CompilerParams(collective_id=number, has_side_effects=True),
    )(own)


def add_split(a, b):
    pair = a.astype(f32) + b.astype(f32)
    lanes = lax.broadcasted_iota(jnp.int32, pair.shape, 1)
    whole = jnp.where(lanes < 16, pair + pltpu.roll(pair, 112, 1), 0.0)
    high = whole.astype(bf16).astype(f32)
    return (high + pltpu.roll(whole - high, 16, 1)).astype(bf16)


def sum_of(a, b):
    width = a.shape[-1]
    main = width - width % 2048
    total = (a[:, :main].astype(f32) + b[:, :main].astype(f32)).astype(bf16)
    if main == width:
        return total
    return jnp.concatenate([total, add_split(a[:, main:], b[:, main:])], 1)


def add_rows(target, source, rows):
    step = 16

    @pl.loop(0, rows // step)
    def _(i):
        part = pl.ds(pl.multiple_of(i * step, step), step)
        target[part] = sum_of(target[part], source[part])


def scatter_kernel(parts, total, held, from_core, from_x, from_y, from_below, from_above, shared_in,
                   load_sem, send, recv, end_send, end_recv):
    z, y, x, core = place()
    half = parts.shape[1] // 2
    piece = half // 4
    me = z * 2 + y
    ahead = z // 2
    order = (3 - 3 * ahead, 2 - ahead, z + 1 - 2 * (z % 2), z)
    my_half = pl.ds(pl.multiple_of(core * half, half), half)
    other_half = pl.ds(pl.multiple_of((1 - core) * half, half), half)
    slab = pl.ds(pl.multiple_of(x * piece, piece), 3 * piece)
    mine = pl.ds(pl.multiple_of(x * 3 * piece, piece), piece)
    theirs = pl.ds(pl.multiple_of((1 - x) * 3 * piece, piece), piece)
    shared = pl.ds(piece, 2 * piece)
    CORE, X, Y, UP, DOWN = range(5)

    def remote(kind, number, source, target, where):
        return pltpu.make_async_remote_copy(
            src_ref=source, dst_ref=target, send_sem=send.at[kind, number],
            recv_sem=recv.at[kind, number], device_id=where, device_id_type=MESH)

    def load(b):
        return pltpu.make_async_copy(parts.at[b, my_half], held.at[b], load_sem.at[b])

    def to_core(b):
        return remote(CORE, b, parts.at[b, other_half], from_core.at[b], device(z, y, x, 1 - core))

    def to_x(b):
        return remote(X, b, held.at[b, theirs], from_x.at[b], device(z, y, 1 - x, core))

    def to_y(zb):
        return remote(Y, zb, held.at[zb * 2 + 1 - y, slab], from_y.at[zb], device(z, 1 - y, x, core))

    def to_above(zb):
        return remote(UP, zb, held.at[zb * 2 + y, slab], from_below.at[zb], device(z + 1, y, x, core))

    def to_below(zb):
        return remote(DOWN, zb, held.at[zb * 2 + y, slab], from_above.at[zb], device(z - 1, y, x, core))

    greet(z, y, x, core)
    for zb in order:
        for yb in (1 - y, y):
            load(zb * 2 + yb).start()
            to_core(zb * 2 + yb).start()

    def stage_core(zb, yb):
        b = zb * 2 + yb
        load(b).wait()
        to_core(b).wait_recv()
        add_rows(held.at[b], from_core.at[b], half)
        to_x(b).start()

    def stage_x(zb, yb):
        b = zb * 2 + yb
        to_x(b).wait_recv()
        add_rows(held.at[b, mine], from_x.at[b], piece)

    def stage_y(zb):
        stage_x(zb, 1 - y)
        to_y(zb).start()

    def climb(zb):
        @pl.when(z > 0)
        def _():
            to_above(zb).wait_recv()
            add_rows(held.at[zb * 2 + y, slab], from_below.at[zb], 3 * piece)
        to_above(zb).start()

    def descend(zb):
        @pl.when(z < 3)
        def _():
            to_below(zb).wait_recv()
            add_rows(held.at[zb * 2 + y, slab], from_above.at[zb], 3 * piece)
        to_below(zb).start()

    def stage_z(i):
        zb = order[i]
        to_y(zb).wait_recv()
        add_rows(held.at[zb * 2 + y, slab], from_y.at[zb], 3 * piece)
        rises = (ahead == 0) if i < 2 else (z % 2 == 0)

        @pl.when(rises)
        def _():
            climb(zb)

        @pl.when(jnp.logical_not(rises))
        def _():
            descend(zb)

    stage_core(order[0], 1 - y)
    stage_core(order[0], y)
    for i in range(4):
        if i < 3:
            stage_core(order[i + 1], 1 - y)
        stage_y(order[i])
        if i < 3:
            stage_core(order[i + 1], y)
        stage_x(order[i], y)
        if i > 0:
            stage_z(i - 1)

    own = held.at[me]
    to_y(z).wait_recv()
    add_rows(own.at[slab], from_y.at[z], 3 * piece)

    @pl.when(z > 0)
    def _():
        to_above(z).wait_recv()
        add_rows(own.at[slab], from_below.at[z], 3 * piece)

    @pl.when(z < 3)
    def _():
        to_below(z).wait_recv()
        add_rows(own.at[slab], from_above.at[z], 3 * piece)

    def at_end(number, source, target, where):
        return pltpu.make_async_remote_copy(
            src_ref=source, dst_ref=target, send_sem=end_send.at[number],
            recv_sem=end_recv.at[number], device_id=where, device_id_type=MESH)

    base = core * half
    out_mine = pl.ds(pl.multiple_of(base + x * 3 * piece, piece), piece)
    out_theirs = pl.ds(pl.multiple_of(base + (1 - x) * 3 * piece, piece), piece)
    sums = at_end(0, held.at[me, shared], shared_in, device(z, y, 1 - x, core))
    ready = at_end(1, held.at[me, mine], total.at[out_mine], device(z, y, 1 - x, core))
    sums.start()
    ready.start()
    total[out_mine] = held[me, mine]
    sums.wait_recv()
    out_shared = pl.ds(pl.multiple_of(base + piece, piece), 2 * piece)
    total[out_shared] = sum_of(held[me, shared], shared_in[...])
    at_end(1, held.at[me, mine], total.at[out_theirs], device(z, y, 1 - x, core)).wait_recv()
    finished = at_end(2, total.at[my_half], total.at[my_half], device(z, y, x, 1 - core))
    finished.start()
    at_end(2, total.at[my_half], total.at[other_half], device(z, y, x, 1 - core)).wait_recv()
    sums.wait_send()
    ready.wait_send()
    finished.wait_send()

    for b in range(8):
        zb, yb = b // 2, b % 2
        to_core(b).wait_send()
        to_x(b).wait_send()
        if yb == 0:
            to_y(zb).wait_send()

            @pl.when(zb > z)
            def _():
                to_above(zb).wait_send()

            @pl.when(zb < z)
            def _():
                to_below(zb).wait_send()


def scatter_sum(parts, number):
    _, rows, width = parts.shape
    half, piece = rows // 2, rows // 8
    return pl.pallas_call(
        scatter_kernel,
        out_shape=jax.ShapeDtypeStruct((rows, width), bf16),
        in_specs=[pl.BlockSpec(memory_space=pl.ANY)],
        out_specs=pl.BlockSpec(memory_space=pltpu.VMEM),
        scratch_shapes=[
            pltpu.VMEM((8, half, width), bf16),
            pltpu.VMEM((8, half, width), bf16),
            pltpu.VMEM((8, piece, width), bf16),
            pltpu.VMEM((4, 3 * piece, width), bf16),
            pltpu.VMEM((4, 3 * piece, width), bf16),
            pltpu.VMEM((4, 3 * piece, width), bf16),
            pltpu.VMEM((2 * piece, width), bf16),
            pltpu.SemaphoreType.DMA((8,)),
            pltpu.SemaphoreType.DMA((5, 8)),
            pltpu.SemaphoreType.DMA((5, 8)),
            pltpu.SemaphoreType.DMA((3,)),
            pltpu.SemaphoreType.DMA((3,)),
        ],
        compiler_params=pltpu.CompilerParams(collective_id=number, has_side_effects=True, vmem_limit_bytes=48 * 2**20),
    )(parts)
def dot(a,b): return jnp.dot(a,b,preferred_element_type=f32)
def dot_nt(a,b): return lax.dot_general(a,b,(((1,),(1,)),((),())),preferred_element_type=f32)
def dot_tn(a,b): return lax.dot_general(a,b,(((0,),(0,)),((),())),preferred_element_type=f32)

def moe_kernel(first, x_ref, g_ref, mask_ref, wr_ref, wg_ref, wu_ref, wd_ref, hg_ref, da_ref, parts_ref):
    x = x_ref[...]
    g = g_ref[...]
    logits = dot(x, wr_ref[...])
    mask = mask_ref[:, :wr_ref.shape[1]].astype(f32) > 0
    top = jnp.max(jnp.where(mask, logits, -jnp.inf), -1, keepdims=True)
    raised = jnp.where(mask, jnp.exp(jnp.where(mask, logits - top, 0.0)), 0.0)
    gates = raised / jnp.sum(raised, -1, keepdims=True)
    lanes = lax.broadcasted_iota(jnp.int32, gates.shape, 1)
    ff = wg_ref.shape[2]
    gx = None
    out = None
    gg = jnp.zeros(gates.shape, f32)
    for j in range(wg_ref.shape[0]):
        here = lanes == first[0] + j
        gate = jnp.sum(jnp.where(here, gates, 0.0), -1, keepdims=True)
        ga = dot(x, wg_ref[j])
        ua = dot(x, wu_ref[j])
        gw = dot_nt(g, wd_ref[j])
        s = 1.0 / (1.0 + jnp.exp(-ga))
        silu = ga * s
        h = (silu * ua).astype(bf16).astype(f32)
        gg = gg + jnp.where(here, jnp.sum(h * gw, -1, keepdims=True), 0.0)
        gh = gw * gate
        hg = (h * gate).astype(bf16)
        du = (gh * silu).astype(bf16)
        dg = (gh * ua * s * (1.0 + ga * (1.0 - s))).astype(bf16)
        hg_ref[:, j * ff:(j + 1) * ff] = hg
        da_ref[:, 2 * j * ff:(2 * j + 1) * ff] = dg
        da_ref[:, (2 * j + 1) * ff:(2 * j + 2) * ff] = du
        o = dot(hg, wd_ref[j])
        b = dot_nt(dg, wg_ref[j]) + dot_nt(du, wu_ref[j])
        out = o if out is None else out + o
        gx = b if gx is None else gx + b
    D = x.shape[1]
    parts_ref[:, :D] = out.astype(bf16)
    parts_ref[:, D:2 * D] = gx.astype(bf16)
    high = gg.astype(bf16)
    low = (gg - high.astype(f32)).astype(bf16)
    spare = jnp.zeros((gg.shape[0], 128 - 2 * gg.shape[1]), bf16)
    parts_ref[:, 2 * D:] = jnp.concatenate([high, low, spare], 1)

def moe(first, X, G, wr, wg, wu, wd, bt=512):
    T, D = X.shape
    E = wr.shape[1]
    J, _, F = wg.shape
    blk = lambda w: pl.BlockSpec((bt, w), lambda i, s: (i, 0))
    full = lambda *shp: pl.BlockSpec(shp, lambda i, s: (0,) * len(shp))
    return pl.pallas_call(moe_kernel,
        grid_spec=pltpu.PrefetchScalarGridSpec(num_scalar_prefetch=1, grid=(T // bt,),
        in_specs=[blk(D), blk(D), pl.BlockSpec((bt, 128), lambda i, s: (i, D // 128)), full(D, E), full(J, D, F), full(J, D, F), full(J, F, D)],
        out_specs=[blk(J * F), blk(2 * J * F), blk(2 * D + 128)]),
        out_shape=[jax.ShapeDtypeStruct((T, J * F), bf16), jax.ShapeDtypeStruct((T, 2 * J * F), bf16),
                   jax.ShapeDtypeStruct((T, 2 * D + 128), bf16)],
        compiler_params=pltpu.CompilerParams(vmem_limit_bytes=56 * 2**20),
    )(first, X, G, G, wr, wg, wu, wd)

def tn_kernel(a_ref, b_ref, o_ref):
    o_ref[...] = dot_tn(a_ref[...], b_ref[...])

def tn(a, b, bm, bn, N):
    T, M = a.shape
    return pl.pallas_call(tn_kernel, grid=(M // bm, N // bn),
        in_specs=[pl.BlockSpec((T, bm), lambda i, j: (0, i)), pl.BlockSpec((T, bn), lambda i, j: (0, j))],
        out_specs=pl.BlockSpec((bm, bn), lambda i, j: (i, j)),
        out_shape=jax.ShapeDtypeStruct((M, N), f32),
        compiler_params=pltpu.CompilerParams(vmem_limit_bytes=56 * 2**20))(a, b)


def expert_grads_kernel(a_ref, b_ref, gate_ref, up_ref):
    both = dot_tn(a_ref[...], b_ref[...])
    ff = gate_ref.shape[2]
    for j in range(gate_ref.shape[0]):
        gate_ref[j] = both[:, 2 * j * ff:(2 * j + 1) * ff]
        up_ref[j] = both[:, (2 * j + 1) * ff:(2 * j + 2) * ff]


def expert_grads(a, b, J, bm=512):
    T, D = a.shape
    F = b.shape[1] // (2 * J)
    spec = pl.BlockSpec((J, bm, F), lambda i: (0, i, 0))
    shape = jax.ShapeDtypeStruct((J, D, F), f32)
    return pl.pallas_call(expert_grads_kernel, grid=(D // bm,),
        in_specs=[pl.BlockSpec((T, bm), lambda i: (0, i)), pl.BlockSpec((T, 2 * J * F), lambda i: (0, 0))],
        out_specs=[spec, spec], out_shape=[shape, shape],
        compiler_params=pltpu.CompilerParams(vmem_limit_bytes=56 * 2**20))(a, b)


EPS = 1e-05
HD = 128
BLOCK = 256


def block_of(r, parity):
    return 2 * r + (parity if r % 2 == 0 else 1 - parity)


def norm_factor(v):
    return lax.rsqrt(jnp.mean(v * v, -1, keepdims=True) + EPS)


def project_kernel(x_ref, gain_ref, w_ref, qg_ref, kg_ref, cos_ref, sin_ref, a_ref, q_ref, k_ref, v_ref, qr_ref, kr_ref):
    x = x_ref[...].astype(f32)
    a = (x * norm_factor(x) * gain_ref[...]).astype(bf16)
    a_ref[...] = a
    raw = dot(a, w_ref[...])
    cosine, sine = cos_ref[...], sin_ref[...]

    def turned(part, gain):
        n = part * norm_factor(part) * gain
        return (n * cosine + pltpu.roll(n, HD // 2, 1) * sine).astype(bf16)

    q_raw, k_raw = raw[:, :HD], raw[:, HD:2 * HD]
    qr_ref[...] = q_raw
    kr_ref[...] = k_raw
    q_ref[...] = turned(q_raw, qg_ref[...])
    k_ref[...] = turned(k_raw, kg_ref[...])
    v_ref[...] = raw[:, 2 * HD:].astype(bf16)


def project(x, gain, w, qg, kg, cosine, sine, bt=256):
    T, D = x.shape
    blk = lambda n: pl.BlockSpec((bt, n), lambda i: (i, 0))
    full = lambda *s: pl.BlockSpec(s, lambda i: (0,) * len(s))
    sd = jax.ShapeDtypeStruct
    return pl.pallas_call(
        project_kernel, grid=(T // bt,),
        in_specs=[blk(D), full(1, D), full(D, 3 * HD), full(1, HD), full(1, HD), blk(HD), blk(HD)],
        out_specs=[blk(D)] + [blk(HD)] * 5,
        out_shape=[sd((T, D), bf16)] + [sd((T, HD), bf16)] * 3 + [sd((T, HD), f32)] * 2,
        compiler_params=pltpu.CompilerParams(vmem_limit_bytes=40 * 2**20),
    )(x, gain, w, qg, kg, cosine, sine)


def probabilities(r, start, q, k_ref, segc_ref, segr_ref):
    keys = (2 * r + 2) * BLOCK
    scores = dot_nt(q, k_ref[:keys]) * (HD ** -0.5)
    rows = start + lax.broadcasted_iota(jnp.int32, scores.shape, 0)
    columns = lax.broadcasted_iota(jnp.int32, scores.shape, 1)
    same = segc_ref[pl.ds(start, BLOCK)] == segr_ref[:, :keys]
    scores = jnp.where((rows >= columns) & same, scores, -1000000000.0)
    raised = jnp.exp(scores - jnp.max(scores, -1, keepdims=True))
    return raised / jnp.sum(raised, -1, keepdims=True)


def attend_kernel(q_ref, k_ref, v_ref, segc_ref, segr_ref, out_ref):
    parity = lax.axis_index("expert") % 2
    for r in range(4):
        start = pl.multiple_of(block_of(r, parity) * BLOCK, BLOCK)
        probs = probabilities(r, start, q_ref[pl.ds(start, BLOCK)], k_ref, segc_ref, segr_ref)
        out_ref[r] = dot(probs.astype(bf16), v_ref[:(2 * r + 2) * BLOCK]).astype(bf16)


VM = pl.BlockSpec(memory_space=pltpu.VMEM)


def attend(q, k, v, segc, segr):
    return pl.pallas_call(
        attend_kernel, in_specs=[VM] * 5, out_specs=VM,
        out_shape=jax.ShapeDtypeStruct((4, BLOCK, HD), bf16),
        compiler_params=pltpu.CompilerParams(vmem_limit_bytes=40 * 2**20),
    )(q, k, v, segc, segr)


def attend_back_kernel(q_ref, k_ref, v_ref, segc_ref, segr_ref, g_ref, dq_ref, own_ref, other_ref, dk, dv):
    parity = lax.axis_index("expert") % 2
    for r in (3, 2, 1, 0):
        keys = (2 * r + 2) * BLOCK
        start = pl.multiple_of(block_of(r, parity) * BLOCK, BLOCK)
        q = q_ref[pl.ds(start, BLOCK)]
        g = g_ref[r]
        probs = probabilities(r, start, q, k_ref, segc_ref, segr_ref)
        gv = dot_tn(probs.astype(bf16), g)
        gp = dot_nt(g, v_ref[:keys])
        gs = (probs * (gp - jnp.sum(gp * probs, -1, keepdims=True))).astype(bf16)
        dq_ref[r] = dot(gs, k_ref[:keys]) * (HD ** -0.5)
        gk = dot_tn(gs, q) * (HD ** -0.5)
        if r == 3:
            dv[...] = gv
            dk[...] = gk
        else:
            dv[:keys] += gv
            dk[:keys] += gk
    for r in range(4):
        mine = pl.ds(pl.multiple_of(block_of(r, parity) * BLOCK, BLOCK), BLOCK)
        other = pl.ds(pl.multiple_of(block_of(r, 1 - parity) * BLOCK, BLOCK), BLOCK)
        own_ref[r, :, :HD] = dk[mine]
        own_ref[r, :, HD:] = dv[mine]
        other_ref[r, :, :HD] = dk[other].astype(bf16)
        other_ref[r, :, HD:] = dv[other].astype(bf16)


def attend_back(q, k, v, segc, segr, g):
    T = q.shape[0]
    sd = jax.ShapeDtypeStruct
    return pl.pallas_call(
        attend_back_kernel, in_specs=[VM] * 6, out_specs=[VM] * 3,
        out_shape=[sd((4, BLOCK, HD), f32), sd((4, BLOCK, 2 * HD), f32), sd((4, BLOCK, 2 * HD), bf16)],
        scratch_shapes=[pltpu.VMEM((T, HD), f32), pltpu.VMEM((T, HD), f32)],
        compiler_params=pltpu.CompilerParams(vmem_limit_bytes=48 * 2**20),
    )(q, k, v, segc, segr, g)


def settle_kernel(dq_ref, own_ref, other_ref, qr_ref, kr_ref, qg_ref, kg_ref, cos_ref, sin_ref,
                  raw_ref, gains_ref, arrived, send, recv):
    z, y, x, core = place()
    barrier = pltpu.get_barrier_semaphore()
    partner = device(z, 1 - y, x, core)
    pl.semaphore_signal(barrier, inc=1, device_id=partner, device_id_type=MESH)
    pl.semaphore_wait(barrier, 1)
    copies = []
    for r in range(4):
        copy = pltpu.make_async_remote_copy(
            src_ref=other_ref.at[r], dst_ref=arrived.at[r], send_sem=send.at[r], recv_sem=recv.at[r],
            device_id=partner, device_id_type=MESH)
        copy.start()
        copies.append(copy)
    gain_sums = [jnp.zeros((1, HD), f32), jnp.zeros((1, HD), f32)]

    def back(turned, raw, gain, which, cosine, sine):
        g = turned * cosine - pltpu.roll(turned, HD // 2, 1) * sine
        factor = norm_factor(raw)
        n = raw * factor
        gain_sums[which] = gain_sums[which] + jnp.sum(g * n, 0, keepdims=True)
        g = g * gain
        return (factor * (g - n * jnp.mean(g * n, -1, keepdims=True))).astype(bf16)

    for r in range(4):
        rows = pl.ds(pl.multiple_of(block_of(r, y) * BLOCK, BLOCK), BLOCK)
        raw_ref[r, :, :HD] = back(dq_ref[r], qr_ref[rows], qg_ref[...], 0, cos_ref[rows], sin_ref[rows])
    for r in range(4):
        rows = pl.ds(pl.multiple_of(block_of(r, y) * BLOCK, BLOCK), BLOCK)
        copies[r].wait_recv()
        dk = own_ref[r, :, :HD] + arrived[r, :, :HD].astype(f32)
        raw_ref[r, :, HD:2 * HD] = back(dk, kr_ref[rows], kg_ref[...], 1, cos_ref[rows], sin_ref[rows])
        raw_ref[r, :, 2 * HD:] = (own_ref[r, :, HD:] + arrived[r, :, HD:].astype(f32)).astype(bf16)
    gains_ref[0:1] = gain_sums[0]
    gains_ref[1:2] = gain_sums[1]
    for copy in copies:
        copy.wait_send()


def settle(dq, own, other, qr, kr, qg, kg, cosine, sine, number):
    sd = jax.ShapeDtypeStruct
    return pl.pallas_call(
        settle_kernel, in_specs=[VM] * 9, out_specs=[VM] * 2,
        out_shape=[sd((4, BLOCK, 3 * HD), bf16), sd((2, HD), f32)],
        scratch_shapes=[pltpu.VMEM((4, BLOCK, 2 * HD), bf16), pltpu.SemaphoreType.DMA((4,)), pltpu.SemaphoreType.DMA((4,))],
        compiler_params=pltpu.CompilerParams(collective_id=number, has_side_effects=True, vmem_limit_bytes=48 * 2**20),
    )(dq, own, other, qr, kr, qg, kg, cosine, sine)


def greet_owners(z, y, x, core, sources):
    barrier = pltpu.get_barrier_semaphore()
    for r in range(4):
        target = device(r, sources(r), x, core)

        def signal():
            pl.semaphore_signal(barrier, inc=1, device_id=target, device_id_type=MESH)
        pl.when((z != r) | (z % 2 == 1))(signal)
    return barrier


def blend_kernel(parts, groups, multiply, part_ref, *refs):
    weights = refs[:groups]
    total, gathered, out_half, in_half, kept, held, from_x, send, recv, pair_send, pair_recv, local = refs[groups:]
    z, y, x, core = place()
    targets = lambda r: (y if r % 2 == 0 else 1 - y)
    source_y = (y + z) % 2
    barrier = greet_owners(z, y, x, core, lambda r: source_y)
    for where in (device(z, y, 1 - x, core), device(z, y, x, 1 - core)):
        pl.semaphore_signal(barrier, inc=1, device_id=where, device_id_type=MESH)
    pl.semaphore_wait(barrier, 5 + z % 2)
    width = HD * 4

    def lanes(g, n):
        return pl.ds(pl.multiple_of(g * width + n * HD, HD), HD)

    def remote(r, g):
        return pltpu.make_async_remote_copy(
            src_ref=part_ref.at[r, :, pl.ds(g * HD, HD)], dst_ref=gathered.at[:, lanes(g, z)],
            send_sem=send.at[r, g], recv_sem=recv.at[z, g],
            device_id=device(r, targets(r), x, core), device_id_type=MESH)

    def arriving(n, g):
        return pltpu.make_async_remote_copy(
            src_ref=part_ref.at[n, :, pl.ds(g * HD, HD)], dst_ref=gathered.at[:, lanes(g, n)],
            send_sem=send.at[n, g], recv_sem=recv.at[n, g],
            device_id=device(n, source_y, x, core), device_id_type=MESH)

    def own(r, g):
        return pltpu.make_async_copy(
            part_ref.at[r, :, pl.ds(g * HD, HD)], gathered.at[:, lanes(g, r)], local.at[g])

    for r in range(4):
        here = (z == r) & (z % 2 == 0)

        @pl.when(here)
        def _():
            for g in range(groups):
                own(r, g).start()

        @pl.when(jnp.logical_not(here))
        def _():
            for g in range(groups):
                remote(r, g).start()
    for r in range(4):
        here = (z == r) & (z % 2 == 0)

        @pl.when(here)
        def _():
            for g in range(groups):
                own(r, g).wait()

        @pl.when(jnp.logical_not(here))
        def _():
            for g in range(groups):
                arriving(r, g).wait_recv()

    rows = total.shape[0]
    half = rows // 2
    chunk = half // 2
    my_half = core * half
    other_half = (1 - core) * half

    def pair(kind, c, source, target, where):
        return pltpu.make_async_remote_copy(
            src_ref=source, dst_ref=target, send_sem=pair_send.at[kind, c], recv_sem=pair_recv.at[kind, c],
            device_id=where, device_id_type=MESH)

    twin = device(z, y, x, 1 - core)
    across = device(z, y, 1 - x, core)
    piece = lambda c: pl.ds(c * chunk, chunk)
    first = [pair(0, c, out_half.at[piece(c)], in_half.at[piece(c)], twin) for c in range(2)]
    second = [pair(1, c, held.at[piece(c)], from_x.at[piece(c)], across) for c in range(2)]
    at = lambda base, c: pl.ds(pl.multiple_of(base + c * chunk, chunk), chunk)
    third = [pair(2, c, total.at[at(my_half, c)], total.at[at(my_half, c)], twin) for c in range(2)]
    for c in range(2):
        out_half[piece(c)] = multiply(gathered[at(other_half, c)], weights).astype(bf16)
        first[c].start()
    for c in range(2):
        kept[...] = multiply(gathered[at(my_half, c)], weights)
        first[c].wait_recv()
        held[piece(c)] = (kept[...] + in_half[piece(c)].astype(f32)).astype(bf16)
        second[c].start()
    for c in range(2):
        second[c].wait_recv()
        total[at(my_half, c)] = (held[piece(c)].astype(f32) + from_x[piece(c)].astype(f32)).astype(bf16)
        third[c].start()
    for c in range(2):
        pair(2, c, total.at[at(my_half, c)], total.at[at(other_half, c)], twin).wait_recv()
        first[c].wait_send()
        second[c].wait_send()
        third[c].wait_send()
    for r in range(4):
        here = (z == r) & (z % 2 == 0)

        @pl.when(jnp.logical_not(here))
        def _():
            for g in range(groups):
                remote(r, g).wait_send()


def blend(parts, weights, multiply, number):
    groups = parts.shape[2] // HD
    rows, width = BLOCK, 2048
    sd = jax.ShapeDtypeStruct
    half = rows // 2
    return pl.pallas_call(
        functools.partial(blend_kernel, 4, groups, multiply),
        in_specs=[VM] * (1 + groups), out_specs=[VM] * 2,
        out_shape=[sd((rows, width), bf16), sd((rows, 4 * groups * HD), bf16)],
        scratch_shapes=[
            pltpu.VMEM((half, width), bf16), pltpu.VMEM((half, width), bf16), pltpu.VMEM((half // 2, width), f32),
            pltpu.VMEM((half, width), bf16), pltpu.VMEM((half, width), bf16),
            pltpu.SemaphoreType.DMA((4, groups)), pltpu.SemaphoreType.DMA((4, groups)),
            pltpu.SemaphoreType.DMA((3, 2)), pltpu.SemaphoreType.DMA((3, 2)), pltpu.SemaphoreType.DMA((groups,)),
        ],
        compiler_params=pltpu.CompilerParams(collective_id=number, has_side_effects=True, vmem_limit_bytes=48 * 2**20),
    )(parts, *weights)


def hand_back_kernel(g_ref, out_ref, send, recv, local):
    z, y, x, core = place()
    source_y = (y + z) % 2
    barrier = pltpu.get_barrier_semaphore()
    for r in range(4):
        def signal():
            pl.semaphore_signal(barrier, inc=1, device_id=device(r, y if r % 2 == 0 else 1 - y, x, core), device_id_type=MESH)
        pl.when((z != r) | (z % 2 == 1))(signal)
    pl.semaphore_wait(barrier, 3 + z % 2)

    def remote(n):
        return pltpu.make_async_remote_copy(
            src_ref=g_ref.at[:, pl.ds(n * HD, HD)], dst_ref=out_ref.at[z], send_sem=send.at[n], recv_sem=recv.at[z],
            device_id=device(n, source_y, x, core), device_id_type=MESH)

    def arriving(r):
        return pltpu.make_async_remote_copy(
            src_ref=g_ref.at[:, pl.ds(r * HD, HD)], dst_ref=out_ref.at[r], send_sem=send.at[r], recv_sem=recv.at[r],
            device_id=device(r, y if r % 2 == 0 else 1 - y, x, core), device_id_type=MESH)

    def own(n):
        return pltpu.make_async_copy(g_ref.at[:, pl.ds(n * HD, HD)], out_ref.at[n], local)

    for n in range(4):
        here = (z == n) & (z % 2 == 0)
        pl.when(here)(lambda: own(n).start())
        pl.when(jnp.logical_not(here))(lambda: remote(n).start())
    for n in range(4):
        here = (z == n) & (z % 2 == 0)
        pl.when(here)(lambda: own(n).wait())
        pl.when(jnp.logical_not(here))(lambda: arriving(n).wait_recv())
        pl.when(jnp.logical_not(here))(lambda: remote(n).wait_send())


def hand_back(g, number):
    return pl.pallas_call(
        hand_back_kernel, in_specs=[VM], out_specs=VM,
        out_shape=jax.ShapeDtypeStruct((4, BLOCK, HD), bf16),
        scratch_shapes=[pltpu.SemaphoreType.DMA((4,)), pltpu.SemaphoreType.DMA((4,)), pltpu.SemaphoreType.DMA],
        compiler_params=pltpu.CompilerParams(collective_id=number, has_side_effects=True),
    )(g)


def grad_weight_kernel(parity, a_ref, raw_ref, out_ref, acc):
    r = pl.program_id(0)
    part = dot_tn(a_ref[...], raw_ref[0])

    @pl.when(r == 0)
    def _():
        acc[...] = part

    @pl.when(r > 0)
    def _():
        acc[...] += part

    @pl.when(r == 3)
    def _():
        out_ref[...] = acc[...].astype(bf16)


def grad_weight(parity, a, raw):
    T, D = a.shape
    W = raw.shape[2]
    return pl.pallas_call(
        grad_weight_kernel,
        grid_spec=pltpu.PrefetchScalarGridSpec(
            num_scalar_prefetch=1, grid=(4,),
            in_specs=[pl.BlockSpec((BLOCK, D), lambda r, p: (2 * r + (r + p[0]) % 2, 0)),
                      pl.BlockSpec((1, BLOCK, W), lambda r, p: (r, 0, 0))],
            out_specs=pl.BlockSpec((D, W), lambda r, p: (0, 0)),
            scratch_shapes=[pltpu.VMEM((D, W), f32)]),
        out_shape=jax.ShapeDtypeStruct((D, W), bf16),
        compiler_params=pltpu.CompilerParams(vmem_limit_bytes=40 * 2**20),
    )(parity, a, raw)


def deliver_kernel(add_up, part_ref, out_ref, held, from_y, from_z, send, recv, local):
    z, y, x, core = place()
    barrier = pltpu.get_barrier_semaphore()
    partner = device(z, 1 - y, x, core)
    pl.semaphore_signal(barrier, inc=1, device_id=partner, device_id_type=MESH)
    for n in range(4):
        pl.when(z != n)(lambda: pl.semaphore_signal(barrier, inc=1, device_id=device(n, y, x, core), device_id_type=MESH))
    pl.semaphore_wait(barrier, 4)

    def pair(n):
        return pltpu.make_async_remote_copy(
            src_ref=part_ref.at[n * 2 + 1 - y], dst_ref=from_y.at[n], send_sem=send.at[0, n], recv_sem=recv.at[0, n],
            device_id=partner, device_id_type=MESH)

    def along(n):
        return pltpu.make_async_remote_copy(
            src_ref=held.at[n], dst_ref=from_z.at[z], send_sem=send.at[1, n], recv_sem=recv.at[1, z],
            device_id=device(n, y, x, core), device_id_type=MESH)

    def arriving(n):
        return pltpu.make_async_remote_copy(
            src_ref=held.at[n], dst_ref=from_z.at[n], send_sem=send.at[1, n], recv_sem=recv.at[1, n],
            device_id=device(n, y, x, core), device_id_type=MESH)

    ahead = z // 2
    order = (3 - 3 * ahead, 2 - ahead, z + 1 - 2 * (z % 2), z)
    for n in order:
        pair(n).start()
    for i, n in enumerate(order):
        pair(n).wait_recv()
        held[n] = (part_ref[n * 2 + y].astype(f32) + from_y[n].astype(f32)).astype(bf16)
        if i < 3:
            along(n).start()
    from_z[z] = held[z]
    for n in range(4):
        pl.when(z != n)(lambda: arriving(n).wait_recv())
    if add_up:
        out_ref[...] = (from_z[0].astype(f32) + from_z[1].astype(f32)) + (from_z[2].astype(f32) + from_z[3].astype(f32))
    else:
        for n in range(4):
            for g in range(3):
                out_ref[g, :, n * HD:(n + 1) * HD] = from_z[n, :, g * HD:(g + 1) * HD].astype(f32)
    for n in range(4):
        pair(n).wait_send()
        pl.when(z != n)(lambda: along(n).wait_send())


def deliver(parts, add_up, number):
    _, rows, width = parts.shape
    shape = (rows, width) if add_up else (3, rows, 4 * HD)
    return pl.pallas_call(
        functools.partial(deliver_kernel, add_up),
        in_specs=[VM], out_specs=VM, out_shape=jax.ShapeDtypeStruct(shape, f32),
        scratch_shapes=[pltpu.VMEM((4, rows, width), bf16)] * 3 + [
            pltpu.SemaphoreType.DMA((2, 4)), pltpu.SemaphoreType.DMA((2, 4)), pltpu.SemaphoreType.DMA],
        compiler_params=pltpu.CompilerParams(collective_id=number, has_side_effects=True, vmem_limit_bytes=48 * 2**20),
    )(parts)


def on_device(
    hidden_in,
    norm1_gain,
    w_query,
    w_key,
    w_value,
    w_out,
    query_gain,
    key_gain,
    norm2_gain,
    w_router,
    w_gate,
    w_up,
    w_down,
    routes,
    segments,
    cotangent,
):
    seq_len, width = hidden_in.shape
    local_width = w_query.shape[1]
    head_count = local_width // HEAD_DIM
    expert_devs = lax.axis_size("expert")
    local_experts = w_gate.shape[0]
    expert_total = w_router.shape[1]
    capacity = 2 * seq_len * TOP // expert_total
    slab_rows = local_experts * capacity
    my_index = lax.axis_index("expert")
    group = SEQ // seq_len
    rank = my_index % group
    f32 = jnp.float32
    bf16 = jnp.bfloat16

    def split_heads(values):
        return values.reshape(seq_len, head_count, HEAD_DIM)

    inputs = hidden_in.astype(f32)
    inverse_attn = inverse_rms(inputs)
    normed_attn = inputs * inverse_attn
    attn_input = (normed_attn * norm1_gain).astype(bf16)
    q_raw = split_heads(jnp.dot(attn_input, w_query, preferred_element_type=f32))
    k_raw = split_heads(jnp.dot(attn_input, w_key, preferred_element_type=f32))
    v_heads = split_heads(jnp.dot(attn_input, w_value, preferred_element_type=f32).astype(bf16))
    q_gains = query_gain.reshape(head_count, HEAD_DIM)
    k_gains = key_gain.reshape(head_count, HEAD_DIM)
    q_inverse = inverse_rms(q_raw)
    q_normed = q_raw * q_inverse
    k_inverse = inverse_rms(k_raw)
    k_normed = k_raw * k_inverse
    local_places = lax.iota(jnp.int32, seq_len)
    query_places = rank * seq_len + local_places
    cosine, sine_part = rope_tables(query_places.astype(f32), HEAD_DIM // 2)
    queries = rotate(q_normed * q_gains, cosine, sine_part, 1.0).astype(bf16)
    key_rot = rotate(k_normed * k_gains, cosine, sine_part, 1.0).astype(bf16)
    score_scale = HEAD_DIM ** (-0.5)
    keys_values = jnp.stack([key_rot, v_heads])
    pieces = [keys_values]
    for offset in range(1, group):
        keys_values = from_behind(keys_values, "expert", 1)
        pieces.append(keys_values)
    stacked = jnp.stack(pieces, 1).reshape(2, group * seq_len, head_count, HEAD_DIM)
    keys_all = stacked[0]
    values_all = stacked[1]
    query_segs = lax.dynamic_slice_in_dim(segments, my_index * seq_len, seq_len, 0)
    key_segs = jnp.concatenate(
        [
            lax.dynamic_slice_in_dim(
                segments, jnp.maximum(my_index - offset, 0) * seq_len, seq_len, 0
            )
            for offset in range(group)
        ],
        0,
    )
    offsets = lax.iota(jnp.int32, group)
    key_places = ((rank - offsets)[:, None] * seq_len + local_places[None, :]).reshape(-1)
    key_valid = jnp.repeat(rank - offsets >= 0, seq_len)
    allowed = (
        key_valid[None, :]
        & (query_places[:, None] >= key_places[None, :])
        & (query_segs[:, None] == key_segs[None, :])
    )

    def scores_of():
        raw_scores = (
            jnp.einsum("thd,shd->hts", queries, keys_all, preferred_element_type=f32) * score_scale
        )
        return jnp.where(allowed[None], raw_scores, MASKED)

    scores = scores_of()
    row_max = jnp.max(scores, -1, keepdims=True)
    raised = jnp.exp(scores - row_max)
    exp_total = jnp.sum(raised, -1, keepdims=True)
    log_total = row_max + jnp.log(exp_total)
    attn_probs = (raised / exp_total).astype(bf16)
    context = (
        jnp.einsum("hts,shd->thd", attn_probs, values_all, preferred_element_type=f32)
        .reshape(seq_len, local_width)
        .astype(bf16)
    )
    attn_part = jnp.dot(context, w_out, preferred_element_type=f32)
    middle = inputs + lax.psum(attn_part, "head")
    inverse_moe = inverse_rms(middle)
    normed_moe = middle * inverse_moe
    moe_input = (normed_moe * norm2_gain).astype(bf16)
    logits = jnp.dot(moe_input, w_router, preferred_element_type=f32)
    chosen = jnp.take_along_axis(logits, routes, 1)
    raised_gate = jnp.exp(chosen - jnp.max(chosen, -1, keepdims=True))
    gate_weights = raised_gate / jnp.sum(raised_gate, -1, keepdims=True)
    catalog = lax.iota(jnp.int32, expert_total)
    route_hot = (routes[:, :, None] == catalog).astype(jnp.int32)
    token_hot = jnp.sum(route_hot, 1, dtype=jnp.int32)
    earlier = jnp.cumsum(token_hot, 0, dtype=jnp.int32) - token_hot
    position = routes * capacity + jnp.take_along_axis(earlier, routes, 1)
    flat_pos = position.reshape(-1)
    owners = (
        jnp.full((expert_total * capacity,), seq_len, jnp.int32)
        .at[flat_pos]
        .set(jnp.repeat(lax.iota(jnp.int32, seq_len), TOP))
    )
    padded = jnp.concatenate([moe_input, jnp.zeros((1, width), bf16)], 0)
    outgoing = padded[owners].reshape(expert_devs, slab_rows, width)
    arrived = lax.all_to_all(outgoing, "expert", split_axis=0, concat_axis=0, tiled=True)
    rows_in = arrived.reshape(expert_devs, local_experts, capacity, width)
    gate_act = jnp.einsum("sjcd,jdf->sjcf", rows_in, w_gate, preferred_element_type=f32)
    up_act = jnp.einsum("sjcd,jdf->sjcf", rows_in, w_up, preferred_element_type=f32)
    hidden = (jax.nn.silu(gate_act) * up_act).astype(bf16)
    partial_out = jnp.einsum("sjcf,jfd->sjcd", hidden, w_down, preferred_element_type=f32).reshape(
        expert_devs, slab_rows, width
    )
    rows_out = (
        lax.psum_scatter(partial_out.astype(jnp.bfloat16), "head", scatter_dimension=2, tiled=True)
        .astype(jnp.float32)
        .astype(bf16)
    )
    leaving = lax.all_gather(rows_out, "head", axis=2, tiled=True)
    returned = lax.all_to_all(leaving, "expert", split_axis=0, concat_axis=0, tiled=True)
    picked = returned.reshape(expert_total * capacity, width)[position]
    moe_out = jnp.einsum("tk,tkd->td", gate_weights, picked, preferred_element_type=f32)
    output = (middle + moe_out).astype(bf16)
    grad_final = cotangent.astype(f32)
    grad_gates = jnp.einsum("td,tkd->tk", grad_final, picked, preferred_element_type=f32)
    grad_chosen = gate_weights * (
        grad_gates - jnp.sum(grad_gates * gate_weights, -1, keepdims=True)
    )
    grad_logits = jnp.einsum("tk,tke->te", grad_chosen, route_hot.astype(f32)).astype(bf16)
    grad_router = jnp.dot(moe_input.T, grad_logits, preferred_element_type=f32)
    grad_moe_input = jnp.dot(grad_logits, w_router.T, preferred_element_type=f32)
    grad_expert_out = (gate_weights[:, :, None] * grad_final[:, None, :]).astype(bf16)
    grad_slab = (
        jnp.zeros((expert_total * capacity, width), bf16)
        .at[flat_pos]
        .set(grad_expert_out.reshape(seq_len * TOP, width))
    )
    grad_slab = grad_slab.reshape(expert_devs, slab_rows, width)
    grad_arrived = lax.all_to_all(grad_slab, "expert", split_axis=0, concat_axis=0, tiled=True)
    grad_rows_out = grad_arrived.reshape(expert_devs, local_experts, capacity, width)
    grad_hidden = jnp.einsum("sjcd,jfd->sjcf", grad_rows_out, w_down, preferred_element_type=f32)
    grad_down = jnp.einsum("sjcf,sjcd->jfd", hidden, grad_rows_out, preferred_element_type=f32)
    sigmoid = jax.nn.sigmoid(gate_act)
    grad_up_act = (grad_hidden * gate_act * sigmoid).astype(bf16)
    grad_gate_act = (grad_hidden * up_act * sigmoid * (1.0 + gate_act * (1.0 - sigmoid))).astype(
        bf16
    )
    grad_gate = jnp.einsum("sjcd,sjcf->jdf", rows_in, grad_gate_act, preferred_element_type=f32)
    grad_up = jnp.einsum("sjcd,sjcf->jdf", rows_in, grad_up_act, preferred_element_type=f32)
    grad_rows_in = jnp.einsum("sjcf,jdf->sjcd", grad_gate_act, w_gate, preferred_element_type=f32)
    grad_rows_in = grad_rows_in + jnp.einsum(
        "sjcf,jdf->sjcd", grad_up_act, w_up, preferred_element_type=f32
    )
    grad_back = (
        lax.psum_scatter(
            grad_rows_in.reshape(expert_devs, slab_rows, width).astype(jnp.bfloat16),
            "head",
            scatter_dimension=2,
            tiled=True,
        )
        .astype(jnp.float32)
        .astype(bf16)
    )
    leaving_grad = lax.all_gather(grad_back, "head", axis=2, tiled=True)
    grad_home = lax.all_to_all(leaving_grad, "expert", split_axis=0, concat_axis=0, tiled=True)
    grad_moe_input = grad_moe_input + jnp.sum(
        grad_home.reshape(expert_total * capacity, width)[position], 1, dtype=f32
    )
    grad_norm2 = jnp.sum(grad_moe_input * normed_moe, 0)
    grad_middle = grad_final + norm_back(grad_moe_input * norm2_gain, normed_moe, inverse_moe)
    grad_attn = grad_middle.astype(bf16)
    grad_out_turned = jnp.dot(grad_attn.T, context, preferred_element_type=f32)
    grad_context = split_heads(jnp.dot(grad_attn, w_out.T, preferred_element_type=f32).astype(bf16))
    attn_full = jnp.exp(scores_of() - log_total)
    attn_low = attn_full.astype(bf16)
    grad_values_all = jnp.einsum("hts,thd->shd", attn_low, grad_context, preferred_element_type=f32)
    grad_probs = jnp.einsum("thd,shd->hts", grad_context, values_all, preferred_element_type=f32)
    grad_scores = (
        attn_full * (grad_probs - jnp.sum(grad_probs * attn_full, -1, keepdims=True))
    ).astype(bf16)
    grad_queries = (
        jnp.einsum("hts,shd->thd", grad_scores, keys_all, preferred_element_type=f32) * score_scale
    )
    grad_keys_all = (
        jnp.einsum("hts,thd->shd", grad_scores, queries, preferred_element_type=f32) * score_scale
    )
    kv_terms = jnp.stack([grad_keys_all, grad_values_all]).reshape(
        2, group, seq_len, head_count, HEAD_DIM
    )
    kv_total = kv_terms[:, 0]
    for offset in range(1, group):
        kv_total = kv_total + from_behind(
            kv_terms[:, offset].astype(jnp.bfloat16), "expert", -offset
        ).astype(jnp.float32)
    grad_keys = kv_total[0]
    grad_values = kv_total[1]
    grad_q_normed = rotate(grad_queries, cosine, sine_part, -1.0)
    grad_k_normed = rotate(grad_keys, cosine, sine_part, -1.0)
    grad_query_gain = jnp.sum(grad_q_normed * q_normed, 0).reshape(local_width)
    grad_key_gain = jnp.sum(grad_k_normed * k_normed, 0).reshape(local_width)
    grad_q_raw = (
        norm_back(grad_q_normed * q_gains, q_normed, q_inverse)
        .reshape(seq_len, local_width)
        .astype(bf16)
    )
    grad_k_raw = (
        norm_back(grad_k_normed * k_gains, k_normed, k_inverse)
        .reshape(seq_len, local_width)
        .astype(bf16)
    )
    grad_v_raw = grad_values.reshape(seq_len, local_width).astype(bf16)
    grad_query = jnp.dot(attn_input.T, grad_q_raw, preferred_element_type=f32)
    grad_key = jnp.dot(attn_input.T, grad_k_raw, preferred_element_type=f32)
    grad_value = jnp.dot(attn_input.T, grad_v_raw, preferred_element_type=f32)
    input_part = jnp.dot(grad_q_raw, w_query.T, preferred_element_type=f32)
    input_part = input_part + jnp.dot(grad_k_raw, w_key.T, preferred_element_type=f32)
    input_part = input_part + jnp.dot(grad_v_raw, w_value.T, preferred_element_type=f32)
    grad_attn_input = lax.psum(input_part.astype(jnp.bfloat16), "head").astype(jnp.float32)
    grad_norm1 = jnp.sum(grad_attn_input * normed_attn, 0)
    grad_input = grad_middle + norm_back(grad_attn_input * norm1_gain, normed_attn, inverse_attn)
    grad_query, grad_key, grad_value, grad_out_turned = (
        lax.psum_scatter(
            grad_query.astype(jnp.bfloat16), "expert", scatter_dimension=0, tiled=True
        ).astype(jnp.float32),
        lax.psum_scatter(
            grad_key.astype(jnp.bfloat16), "expert", scatter_dimension=0, tiled=True
        ).astype(jnp.float32),
        lax.psum_scatter(
            grad_value.astype(jnp.bfloat16), "expert", scatter_dimension=0, tiled=True
        ).astype(jnp.float32),
        lax.psum_scatter(
            grad_out_turned.astype(jnp.bfloat16), "expert", scatter_dimension=0, tiled=True
        ).astype(jnp.float32),
    )
    grad_router, grad_norm1, grad_norm2, grad_query_gain, grad_key_gain = (
        lax.psum(grad_router.astype(jnp.bfloat16), "expert").astype(jnp.float32),
        lax.psum(grad_norm1.astype(jnp.bfloat16), "expert").astype(jnp.float32),
        lax.psum(grad_norm2.astype(jnp.bfloat16), "expert").astype(jnp.float32),
        lax.psum(grad_query_gain.astype(jnp.bfloat16), "expert").astype(jnp.float32),
        lax.psum(grad_key_gain.astype(jnp.bfloat16), "expert").astype(jnp.float32),
    )
    return (
        output,
        grad_input,
        grad_norm1,
        grad_query,
        grad_key,
        grad_value,
        grad_out_turned.T,
        grad_query_gain,
        grad_key_gain,
        grad_norm2,
        grad_router,
        grad_gate,
        grad_up,
        grad_down,
    )


def dense_layer(
    hidden_in, norm1_gain, w_query, w_key, w_value, w_out, query_gain, key_gain, norm2_gain, w_router,
    w_gate, w_up, w_down, routes, segments, cotangent,
):
    rows, width = hidden_in.shape
    experts = w_router.shape[1]
    devices = lax.axis_size("expert")
    tokens = devices * rows
    local_experts = w_gate.shape[0]
    ff = w_gate.shape[2]
    my_index = lax.axis_index("expert")
    head = my_index // 2
    parity = jnp.full((1,), 1, jnp.int32) * (my_index % 2)

    def own_head(v):
        return lax.dynamic_slice_in_dim(v, head * HEAD_DIM, HEAD_DIM, v.ndim - 1)

    hidden_all = gather_all(hidden_in, 1).reshape(tokens, width)
    weights = jnp.concatenate([own_head(w_query), own_head(w_key), own_head(w_value)], 1)
    q_gain, k_gain = own_head(query_gain)[None], own_head(key_gain)[None]
    cosine, sine = rope_tables(lax.iota(jnp.int32, tokens).astype(f32), HEAD_DIM // 2)
    cosine, sine = cosine[:, 0], sine[:, 0]
    cosine = jnp.concatenate([cosine, cosine], 1)
    sine = jnp.concatenate([-sine, sine], 1)
    attn_all, queries, keys, values, q_raw, k_raw = project(
        hidden_all, norm1_gain[None], weights, q_gain, k_gain, cosine, sine
    )
    segc, segr = segments[:, None], segments[None]
    context = attend(queries, keys, values, segc, segr)
    attn_out, own_context = blend(context, [w_out], lambda a, w: dot(a, w[0][...]), 2)

    inputs = hidden_in.astype(f32)
    middle = inputs + attn_out.astype(f32)
    inverse_moe = inverse_rms(middle)
    normed_moe = middle * inverse_moe
    moe_input = (normed_moe * norm2_gain).astype(bf16)
    own_mask = jnp.sum((routes[:, :, None] == lax.iota(jnp.int32, experts)).astype(f32), 1)
    sent = jnp.concatenate([cotangent, jnp.pad(own_mask.astype(bf16), ((0, 0), (0, 128 - experts)))], 1)
    grads_all = gather_all(sent, 3).reshape(tokens, width + 128)
    everyone = gather_all(moe_input, 4).reshape(tokens, width)
    first = jnp.full((1,), local_experts, jnp.int32) * my_index
    weighted, grad_acts, parts = moe(first, everyone, grads_all, w_router, w_gate, w_up, w_down)
    grad_down = tn(weighted, grads_all, 512, 512, width).reshape(local_experts, ff, width)
    grad_gate, grad_up = expert_grads(everyone, grad_acts, local_experts)
    total = scatter_sum(parts.reshape(devices, rows, 2 * width + 128), 5)
    output = (middle + total[:, :width].astype(f32)).astype(bf16)
    grad_final = cotangent.astype(f32)
    tail = total[:, 2 * width :].astype(f32)
    grad_gates = tail[:, :experts] + tail[:, experts : 2 * experts]
    logits = jnp.where(
        own_mask > 0, jnp.dot(moe_input, w_router, preferred_element_type=f32), -jnp.inf
    )
    raised_gate = jnp.exp(logits - jnp.max(logits, -1, keepdims=True))
    gate_weights = raised_gate / jnp.sum(raised_gate, -1, keepdims=True)
    grad_logits = (
        gate_weights * (grad_gates - jnp.sum(grad_gates * gate_weights, -1, keepdims=True))
    ).astype(bf16)
    grad_router = jnp.dot(moe_input.T, grad_logits, preferred_element_type=f32)
    grad_moe_input = jnp.dot(grad_logits, w_router.T, preferred_element_type=f32)
    grad_moe_input = grad_moe_input + total[:, width : 2 * width].astype(f32)
    grad_norm2 = jnp.sum(grad_moe_input * normed_moe, 0)
    grad_middle = grad_final + norm_back(grad_moe_input * norm2_gain, normed_moe, inverse_moe)
    grad_router, grad_norm2 = lax.psum((grad_router, grad_norm2), "expert")

    grad_attn = grad_middle.astype(bf16)
    grad_context = jnp.dot(grad_attn, w_out.T, preferred_element_type=f32).astype(bf16)
    head_grad = hand_back(grad_context, 6)
    out_part = dot_tn(grad_attn, own_context).astype(bf16)
    grad_w_out = deliver(out_part.reshape(devices, rows, -1), True, 7)
    grad_q, own_kv, other_kv = attend_back(queries, keys, values, segc, segr, head_grad)
    raw_grads, gains = settle(grad_q, own_kv, other_kv, q_raw, k_raw, q_gain, k_gain, cosine, sine, 8)

    def back_through(a, w):
        span = 4 * HEAD_DIM
        return sum(dot_nt(a[:, g * span : (g + 1) * span], w[g][...]) for g in range(3))

    grad_attn_input, _ = blend(raw_grads, [w_query, w_key, w_value], back_through, 9)
    weight_part = grad_weight(parity, attn_all, raw_grads)
    grad_qkv = deliver(weight_part.reshape(devices, rows, -1), False, 10)
    grad_attn_input = grad_attn_input.astype(f32)
    inverse_attn = inverse_rms(inputs)
    normed_attn = inputs * inverse_attn
    grad_norm1 = jnp.sum(grad_attn_input * normed_attn, 0)
    grad_input = grad_middle + norm_back(grad_attn_input * norm1_gain, normed_attn, inverse_attn)
    wide = jnp.zeros((2, query_gain.shape[0]), f32)
    wide = lax.dynamic_update_slice_in_dim(wide, gains, head * HEAD_DIM, 1)
    grad_norm1, wide = lax.psum((grad_norm1, wide), "expert")
    return (
        output,
        grad_input,
        grad_norm1,
        grad_qkv[0],
        grad_qkv[1],
        grad_qkv[2],
        grad_w_out.T,
        wide[0],
        wide[1],
        grad_norm2,
        grad_router,
        grad_gate,
        grad_up,
        grad_down,
    )


def layer(*arrays):
    rows, experts = arrays[0].shape[0], arrays[9].shape[1]
    whole = 2 * rows * TOP // experts >= rows and rows * lax.axis_size("expert") == SEQ
    grid = (lax.axis_size("expert"), lax.axis_size("head")) == (8, 4)
    return dense_layer(*arrays) if whole and grid else on_device(*arrays)


def solution(mesh):
    return jax.shard_map(
        layer,
        mesh=mesh,
        in_specs=(
            P("expert", None),
            P(),
            P(None, "head"),
            P(None, "head"),
            P(None, "head"),
            P("head", None),
            P("head"),
            P("head"),
            P(),
            P(),
            P("expert", None, "head"),
            P("expert", None, "head"),
            P("expert", "head", None),
            P("expert", None),
            P(),
            P("expert", None),
        ),
        out_specs=(
            P("expert", None),
            P("expert", None),
            P(),
            P("expert", "head"),
            P("expert", "head"),
            P("expert", "head"),
            P("head", "expert"),
            P("head"),
            P("head"),
            P(),
            P(),
            P("expert", None, "head"),
            P("expert", None, "head"),
            P("expert", "head", None),
        ),
        check_vma=False,
    )
```

```python
import functools

import jax
import jax.numpy as jnp
from jax import lax
from jax.experimental import pallas as pl
from jax.experimental.pallas import tpu as pltpu
from jax.sharding import PartitionSpec as P

HEAD_DIM = 128
TOP = 8
SEQ = 2048
MESH = pl.DeviceIdType.MESH
bf16 = jnp.bfloat16
f32 = jnp.float32


EPSILON = 1e-05
ROPE_BASE = 10000.0
MASKED = -1000000000.0


def from_behind(shard, axis, by):
    size = lax.axis_size(axis)
    pairs = [(i, i + by) for i in range(size) if 0 <= i + by < size]
    return lax.ppermute(shard, axis, pairs)


def inverse_rms(values):
    return lax.rsqrt(jnp.mean(values * values, -1, keepdims=True) + EPSILON)


def norm_back(grad_normed, normed, inverse):
    return inverse * (grad_normed - normed * jnp.mean(grad_normed * normed, -1, keepdims=True))


def rope_tables(places, half_dim):
    inv_freq = ROPE_BASE ** (-lax.iota(jnp.int32, half_dim).astype(jnp.float32) / half_dim)
    angles = places[:, None] * inv_freq[None, :]
    return (jnp.cos(angles)[:, None, :], jnp.sin(angles)[:, None, :])


def rotate(values, cosine, sine_part, direction):
    half_dim = values.shape[-1] // 2
    first_half = values[..., :half_dim]
    second_half = values[..., half_dim:]
    turned = direction * sine_part
    return jnp.concatenate(
        [first_half * cosine - second_half * turned, second_half * cosine + first_half * turned], -1
    )


def place():
    block = lax.axis_index("expert")
    lane = lax.axis_index("head")
    return block // 2, block % 2, lane // 2, lane % 2


def device(z, y, x, core):
    return (z * 2 + y, x * 2 + core)


def greet(z, y, x, core):
    barrier = pltpu.get_barrier_semaphore()

    def signal(target):
        pl.semaphore_signal(barrier, inc=1, device_id=target, device_id_type=MESH)

    signal(device(z, 1 - y, x, core))
    signal(device(z, y, 1 - x, core))
    signal(device(z, y, x, 1 - core))

    @pl.when(z > 0)
    def _():
        signal(device(z - 1, y, x, core))

    @pl.when(z < 3)
    def _():
        signal(device(z + 1, y, x, core))

    pl.semaphore_wait(barrier, 3 + (z > 0).astype(jnp.int32) + (z < 3).astype(jnp.int32))


def gather_kernel(own, whole, local_sem, send, recv):
    z, y, x, core = place()
    rows = own.shape[0]
    eighth = rows // 8
    me = z * 2 + y
    slab = pl.ds(pl.multiple_of(core * 4 * eighth + x * eighth, eighth), 3 * eighth)
    mine = pl.ds(pl.multiple_of(core * 4 * eighth + x * 3 * eighth, eighth), eighth)
    theirs = pl.ds(pl.multiple_of(core * 4 * eighth + (1 - x) * 3 * eighth, eighth), eighth)
    UP, DOWN, Y, X, CORE, CORE_X = range(6)

    def copy(kind, block, part, target, from_own=False):
        source = own.at[part] if from_own else whole.at[block, part]
        return pltpu.make_async_remote_copy(
            src_ref=source, dst_ref=whole.at[block, part],
            send_sem=send.at[kind, block], recv_sem=recv.at[kind, block],
            device_id=target, device_id_type=MESH)

    up = lambda b, o=False: copy(UP, b, slab, device(z + 1, y, x, core), o)
    down = lambda b, o=False: copy(DOWN, b, slab, device(z - 1, y, x, core), o)
    over = lambda b, o=False: copy(Y, b, slab, device(z, 1 - y, x, core), o)
    side = lambda b: copy(X, b, mine, device(z, y, 1 - x, core))
    twin = lambda b: copy(CORE, b, slab, device(z, y, x, 1 - core))
    twin_x = lambda b: copy(CORE_X, b, theirs, device(z, y, x, 1 - core))

    greet(z, y, x, core)
    keep = pltpu.make_async_copy(own, whole.at[me], local_sem)
    keep.start()

    @pl.when(z < 3)
    def _():
        up(me, True).start()

    @pl.when(z > 0)
    def _():
        down(me, True).start()

    over(me, True).start()

    def spread(b):
        side(b).start()
        twin(b).start()

    def from_y(zb):
        b = zb * 2 + 1 - y
        over(b).wait_recv()
        spread(b)

    for d in range(1, 4):
        @pl.when(z >= d)
        def _():
            b = (z - d) * 2 + y
            up(b).wait_recv()

            @pl.when(z < 3)
            def _():
                up(b).start()
            over(b).start()
            spread(b)

        @pl.when(z + d <= 3)
        def _():
            b = (z + d) * 2 + y
            down(b).wait_recv()

            @pl.when(z > 0)
            def _():
                down(b).start()
            over(b).start()
            spread(b)

        if d == 1:
            from_y(z)
        else:
            @pl.when(z >= d - 1)
            def _():
                from_y(z - (d - 1))

            @pl.when(z + d - 1 <= 3)
            def _():
                from_y(z + d - 1)

    @pl.when(z >= 3)
    def _():
        from_y(z - 3)

    @pl.when(z <= 0)
    def _():
        from_y(z + 3)

    for d in range(0, 4):
        def through(zb):
            for yb in (y, 1 - y):
                b = zb * 2 + yb

                def move():
                    side_in = copy(X, b, theirs, device(z, y, 1 - x, core))
                    side_in.wait_recv()
                    twin_x(b).start()
                if d == 0 and yb is y:
                    continue
                move()
        if d == 0:
            through(z)
        else:
            @pl.when(z >= d)
            def _():
                through(z - d)

            @pl.when(z + d <= 3)
            def _():
                through(z + d)

    other = pl.ds(pl.multiple_of((1 - core) * 4 * eighth + x * eighth, eighth), 3 * eighth)
    other_x = pl.ds(pl.multiple_of((1 - core) * 4 * eighth + (1 - x) * 3 * eighth, eighth), eighth)
    for b in range(8):
        zb, yb = b // 2, b % 2

        @pl.when(me != b)
        def _():
            copy(CORE, b, other, device(z, y, x, 1 - core)).wait_recv()
            copy(CORE_X, b, other_x, device(z, y, x, 1 - core)).wait_recv()
            side(b).wait_send()
            twin(b).wait_send()
            twin_x(b).wait_send()

        @pl.when(yb == y)
        def _():
            over(b).wait_send()

        @pl.when((yb == y) & (zb <= z) & (z < 3))
        def _():
            up(b).wait_send()

        @pl.when((yb == y) & (zb >= z) & (z > 0))
        def _():
            down(b).wait_send()
    keep.wait()


def gather_all(own, number):
    rows, width = own.shape
    return pl.pallas_call(
        gather_kernel,
        out_shape=jax.ShapeDtypeStruct((8, rows, width), own.dtype),
        in_specs=[pl.BlockSpec(memory_space=pl.ANY)],
        out_specs=pl.BlockSpec(memory_space=pl.ANY),
        scratch_shapes=[pltpu.SemaphoreType.DMA, pltpu.SemaphoreType.DMA((6, 8)), pltpu.SemaphoreType.DMA((6, 8))],
        compiler_params=pltpu.CompilerParams(collective_id=number, has_side_effects=True),
    )(own)


def add_split(a, b):
    pair = a.astype(f32) + b.astype(f32)
    lanes = lax.broadcasted_iota(jnp.int32, pair.shape, 1)
    whole = jnp.where(lanes < 16, pair + pltpu.roll(pair, 112, 1), 0.0)
    high = whole.astype(bf16).astype(f32)
    return (high + pltpu.roll(whole - high, 16, 1)).astype(bf16)


def sum_of(a, b):
    width = a.shape[-1]
    main = width - width % 2048
    total = (a[:, :main].astype(f32) + b[:, :main].astype(f32)).astype(bf16)
    if main == width:
        return total
    return jnp.concatenate([total, add_split(a[:, main:], b[:, main:])], 1)


def add_rows(target, source, rows):
    step = 16

    @pl.loop(0, rows // step)
    def _(i):
        part = pl.ds(pl.multiple_of(i * step, step), step)
        target[part] = sum_of(target[part], source[part])


def scatter_kernel(parts, total, held, from_core, from_x, from_y, from_below, from_above, shared_in,
                   load_sem, send, recv, end_send, end_recv):
    z, y, x, core = place()
    half = parts.shape[1] // 2
    piece = half // 4
    me = z * 2 + y
    ahead = z // 2
    order = (3 - 3 * ahead, 2 - ahead, z + 1 - 2 * (z % 2), z)
    my_half = pl.ds(pl.multiple_of(core * half, half), half)
    other_half = pl.ds(pl.multiple_of((1 - core) * half, half), half)
    slab = pl.ds(pl.multiple_of(x * piece, piece), 3 * piece)
    mine = pl.ds(pl.multiple_of(x * 3 * piece, piece), piece)
    theirs = pl.ds(pl.multiple_of((1 - x) * 3 * piece, piece), piece)
    shared = pl.ds(piece, 2 * piece)
    CORE, X, Y, UP, DOWN = range(5)

    def remote(kind, number, source, target, where):
        return pltpu.make_async_remote_copy(
            src_ref=source, dst_ref=target, send_sem=send.at[kind, number],
            recv_sem=recv.at[kind, number], device_id=where, device_id_type=MESH)

    def load(b):
        return pltpu.make_async_copy(parts.at[b, my_half], held.at[b], load_sem.at[b])

    def to_core(b):
        return remote(CORE, b, parts.at[b, other_half], from_core.at[b], device(z, y, x, 1 - core))

    def to_x(b):
        return remote(X, b, held.at[b, theirs], from_x.at[b], device(z, y, 1 - x, core))

    def to_y(zb):
        return remote(Y, zb, held.at[zb * 2 + 1 - y, slab], from_y.at[zb], device(z, 1 - y, x, core))

    def to_above(zb):
        return remote(UP, zb, held.at[zb * 2 + y, slab], from_below.at[zb], device(z + 1, y, x, core))

    def to_below(zb):
        return remote(DOWN, zb, held.at[zb * 2 + y, slab], from_above.at[zb], device(z - 1, y, x, core))

    greet(z, y, x, core)
    for zb in order:
        for yb in (1 - y, y):
            load(zb * 2 + yb).start()
            to_core(zb * 2 + yb).start()

    def stage_core(zb, yb):
        b = zb * 2 + yb
        load(b).wait()
        to_core(b).wait_recv()
        add_rows(held.at[b], from_core.at[b], half)
        to_x(b).start()

    def stage_x(zb, yb):
        b = zb * 2 + yb
        to_x(b).wait_recv()
        add_rows(held.at[b, mine], from_x.at[b], piece)

    def stage_y(zb):
        stage_x(zb, 1 - y)
        to_y(zb).start()

    def climb(zb):
        @pl.when(z > 0)
        def _():
            to_above(zb).wait_recv()
            add_rows(held.at[zb * 2 + y, slab], from_below.at[zb], 3 * piece)
        to_above(zb).start()

    def descend(zb):
        @pl.when(z < 3)
        def _():
            to_below(zb).wait_recv()
            add_rows(held.at[zb * 2 + y, slab], from_above.at[zb], 3 * piece)
        to_below(zb).start()

    def stage_z(i):
        zb = order[i]
        to_y(zb).wait_recv()
        add_rows(held.at[zb * 2 + y, slab], from_y.at[zb], 3 * piece)
        rises = (ahead == 0) if i < 2 else (z % 2 == 0)

        @pl.when(rises)
        def _():
            climb(zb)

        @pl.when(jnp.logical_not(rises))
        def _():
            descend(zb)

    stage_core(order[0], 1 - y)
    stage_core(order[0], y)
    for i in range(4):
        if i < 3:
            stage_core(order[i + 1], 1 - y)
        stage_y(order[i])
        if i < 3:
            stage_core(order[i + 1], y)
        stage_x(order[i], y)
        if i > 0:
            stage_z(i - 1)

    own = held.at[me]
    to_y(z).wait_recv()
    add_rows(own.at[slab], from_y.at[z], 3 * piece)

    @pl.when(z > 0)
    def _():
        to_above(z).wait_recv()
        add_rows(own.at[slab], from_below.at[z], 3 * piece)

    @pl.when(z < 3)
    def _():
        to_below(z).wait_recv()
        add_rows(own.at[slab], from_above.at[z], 3 * piece)

    def at_end(number, source, target, where):
        return pltpu.make_async_remote_copy(
            src_ref=source, dst_ref=target, send_sem=end_send.at[number],
            recv_sem=end_recv.at[number], device_id=where, device_id_type=MESH)

    base = core * half
    out_mine = pl.ds(pl.multiple_of(base + x * 3 * piece, piece), piece)
    out_theirs = pl.ds(pl.multiple_of(base + (1 - x) * 3 * piece, piece), piece)
    sums = at_end(0, held.at[me, shared], shared_in, device(z, y, 1 - x, core))
    ready = at_end(1, held.at[me, mine], total.at[out_mine], device(z, y, 1 - x, core))
    sums.start()
    ready.start()
    total[out_mine] = held[me, mine]
    sums.wait_recv()
    out_shared = pl.ds(pl.multiple_of(base + piece, piece), 2 * piece)
    total[out_shared] = sum_of(held[me, shared], shared_in[...])
    at_end(1, held.at[me, mine], total.at[out_theirs], device(z, y, 1 - x, core)).wait_recv()
    finished = at_end(2, total.at[my_half], total.at[my_half], device(z, y, x, 1 - core))
    finished.start()
    at_end(2, total.at[my_half], total.at[other_half], device(z, y, x, 1 - core)).wait_recv()
    sums.wait_send()
    ready.wait_send()
    finished.wait_send()

    for b in range(8):
        zb, yb = b // 2, b % 2
        to_core(b).wait_send()
        to_x(b).wait_send()
        if yb == 0:
            to_y(zb).wait_send()

            @pl.when(zb > z)
            def _():
                to_above(zb).wait_send()

            @pl.when(zb < z)
            def _():
                to_below(zb).wait_send()


def scatter_sum(parts, number):
    _, rows, width = parts.shape
    half, piece = rows // 2, rows // 8
    return pl.pallas_call(
        scatter_kernel,
        out_shape=jax.ShapeDtypeStruct((rows, width), bf16),
        in_specs=[pl.BlockSpec(memory_space=pl.ANY)],
        out_specs=pl.BlockSpec(memory_space=pltpu.VMEM),
        scratch_shapes=[
            pltpu.VMEM((8, half, width), bf16),
            pltpu.VMEM((8, half, width), bf16),
            pltpu.VMEM((8, piece, width), bf16),
            pltpu.VMEM((4, 3 * piece, width), bf16),
            pltpu.VMEM((4, 3 * piece, width), bf16),
            pltpu.VMEM((4, 3 * piece, width), bf16),
            pltpu.VMEM((2 * piece, width), bf16),
            pltpu.SemaphoreType.DMA((8,)),
            pltpu.SemaphoreType.DMA((5, 8)),
            pltpu.SemaphoreType.DMA((5, 8)),
            pltpu.SemaphoreType.DMA((3,)),
            pltpu.SemaphoreType.DMA((3,)),
        ],
        compiler_params=pltpu.CompilerParams(collective_id=number, has_side_effects=True, vmem_limit_bytes=48 * 2**20),
    )(parts)
def dot(a,b): return jnp.dot(a,b,preferred_element_type=f32)
def dot_nt(a,b): return lax.dot_general(a,b,(((1,),(1,)),((),())),preferred_element_type=f32)
def dot_tn(a,b): return lax.dot_general(a,b,(((0,),(0,)),((),())),preferred_element_type=f32)

def moe_kernel(first, x_ref, g_ref, mask_ref, wr_ref, wg_ref, wu_ref, wd_ref, hg_ref, da_ref, parts_ref):
    x = x_ref[...]
    g = g_ref[...]
    logits = dot(x, wr_ref[...])
    mask = mask_ref[:, :wr_ref.shape[1]].astype(f32) > 0
    top = jnp.max(jnp.where(mask, logits, -jnp.inf), -1, keepdims=True)
    raised = jnp.where(mask, jnp.exp(jnp.where(mask, logits - top, 0.0)), 0.0)
    gates = raised / jnp.sum(raised, -1, keepdims=True)
    lanes = lax.broadcasted_iota(jnp.int32, gates.shape, 1)
    ff = wg_ref.shape[2]
    gx = None
    out = None
    gg = jnp.zeros(gates.shape, f32)
    for j in range(wg_ref.shape[0]):
        here = lanes == first[0] + j
        gate = jnp.sum(jnp.where(here, gates, 0.0), -1, keepdims=True)
        ga = dot(x, wg_ref[j])
        ua = dot(x, wu_ref[j])
        gw = dot_nt(g, wd_ref[j])
        s = 1.0 / (1.0 + jnp.exp(-ga))
        silu = ga * s
        h = (silu * ua).astype(bf16).astype(f32)
        gg = gg + jnp.where(here, jnp.sum(h * gw, -1, keepdims=True), 0.0)
        gh = gw * gate
        hg = (h * gate).astype(bf16)
        du = (gh * silu).astype(bf16)
        dg = (gh * ua * s * (1.0 + ga * (1.0 - s))).astype(bf16)
        hg_ref[:, j * ff:(j + 1) * ff] = hg
        da_ref[:, 2 * j * ff:(2 * j + 1) * ff] = dg
        da_ref[:, (2 * j + 1) * ff:(2 * j + 2) * ff] = du
        o = dot(hg, wd_ref[j])
        b = dot_nt(dg, wg_ref[j]) + dot_nt(du, wu_ref[j])
        out = o if out is None else out + o
        gx = b if gx is None else gx + b
    D = x.shape[1]
    parts_ref[:, :D] = out.astype(bf16)
    parts_ref[:, D:2 * D] = gx.astype(bf16)
    high = gg.astype(bf16)
    low = (gg - high.astype(f32)).astype(bf16)
    spare = jnp.zeros((gg.shape[0], 128 - 2 * gg.shape[1]), bf16)
    parts_ref[:, 2 * D:] = jnp.concatenate([high, low, spare], 1)

def moe(first, X, G, wr, wg, wu, wd, bt=512):
    T, D = X.shape
    E = wr.shape[1]
    J, _, F = wg.shape
    blk = lambda w: pl.BlockSpec((bt, w), lambda i, s: (i, 0))
    full = lambda *shp: pl.BlockSpec(shp, lambda i, s: (0,) * len(shp))
    return pl.pallas_call(moe_kernel,
        grid_spec=pltpu.PrefetchScalarGridSpec(num_scalar_prefetch=1, grid=(T // bt,),
        in_specs=[blk(D), blk(D), pl.BlockSpec((bt, 128), lambda i, s: (i, D // 128)), full(D, E), full(J, D, F), full(J, D, F), full(J, F, D)],
        out_specs=[blk(J * F), blk(2 * J * F), blk(2 * D + 128)]),
        out_shape=[jax.ShapeDtypeStruct((T, J * F), bf16), jax.ShapeDtypeStruct((T, 2 * J * F), bf16),
                   jax.ShapeDtypeStruct((T, 2 * D + 128), bf16)],
        compiler_params=pltpu.CompilerParams(vmem_limit_bytes=56 * 2**20),
    )(first, X, G, G, wr, wg, wu, wd)

def tn_kernel(a_ref, b_ref, o_ref):
    o_ref[...] = dot_tn(a_ref[...], b_ref[...])

def tn(a, b, bm, bn, N):
    T, M = a.shape
    return pl.pallas_call(tn_kernel, grid=(M // bm, N // bn),
        in_specs=[pl.BlockSpec((T, bm), lambda i, j: (0, i)), pl.BlockSpec((T, bn), lambda i, j: (0, j))],
        out_specs=pl.BlockSpec((bm, bn), lambda i, j: (i, j)),
        out_shape=jax.ShapeDtypeStruct((M, N), f32),
        compiler_params=pltpu.CompilerParams(vmem_limit_bytes=56 * 2**20))(a, b)


def expert_grads_kernel(a_ref, b_ref, gate_ref, up_ref):
    both = dot_tn(a_ref[...], b_ref[...])
    ff = gate_ref.shape[2]
    for j in range(gate_ref.shape[0]):
        gate_ref[j] = both[:, 2 * j * ff:(2 * j + 1) * ff]
        up_ref[j] = both[:, (2 * j + 1) * ff:(2 * j + 2) * ff]


def expert_grads(a, b, J, bm=512):
    T, D = a.shape
    F = b.shape[1] // (2 * J)
    spec = pl.BlockSpec((J, bm, F), lambda i: (0, i, 0))
    shape = jax.ShapeDtypeStruct((J, D, F), f32)
    return pl.pallas_call(expert_grads_kernel, grid=(D // bm,),
        in_specs=[pl.BlockSpec((T, bm), lambda i: (0, i)), pl.BlockSpec((T, 2 * J * F), lambda i: (0, 0))],
        out_specs=[spec, spec], out_shape=[shape, shape],
        compiler_params=pltpu.CompilerParams(vmem_limit_bytes=56 * 2**20))(a, b)


EPS = 1e-05
HD = 128
BLOCK = 256


def block_of(r, parity):
    return 2 * r + (parity if r % 2 == 0 else 1 - parity)


def norm_factor(v):
    return lax.rsqrt(jnp.mean(v * v, -1, keepdims=True) + EPS)


def project_kernel(x_ref, gain_ref, w_ref, qg_ref, kg_ref, cos_ref, sin_ref, a_ref, q_ref, k_ref, v_ref, qr_ref, kr_ref):
    x = x_ref[...].astype(f32)
    a = (x * norm_factor(x) * gain_ref[...]).astype(bf16)
    a_ref[...] = a
    raw = dot(a, w_ref[...])
    cosine, sine = cos_ref[...], sin_ref[...]

    def turned(part, gain):
        n = part * norm_factor(part) * gain
        return (n * cosine + pltpu.roll(n, HD // 2, 1) * sine).astype(bf16)

    q_raw, k_raw = raw[:, :HD], raw[:, HD:2 * HD]
    qr_ref[...] = q_raw
    kr_ref[...] = k_raw
    q_ref[...] = turned(q_raw, qg_ref[...])
    k_ref[...] = turned(k_raw, kg_ref[...])
    v_ref[...] = raw[:, 2 * HD:].astype(bf16)


def project(x, gain, w, qg, kg, cosine, sine, bt=256):
    T, D = x.shape
    blk = lambda n: pl.BlockSpec((bt, n), lambda i: (i, 0))
    full = lambda *s: pl.BlockSpec(s, lambda i: (0,) * len(s))
    sd = jax.ShapeDtypeStruct
    return pl.pallas_call(
        project_kernel, grid=(T // bt,),
        in_specs=[blk(D), full(1, D), full(D, 3 * HD), full(1, HD), full(1, HD), blk(HD), blk(HD)],
        out_specs=[blk(D)] + [blk(HD)] * 5,
        out_shape=[sd((T, D), bf16)] + [sd((T, HD), bf16)] * 3 + [sd((T, HD), f32)] * 2,
        compiler_params=pltpu.CompilerParams(vmem_limit_bytes=40 * 2**20),
    )(x, gain, w, qg, kg, cosine, sine)


def probabilities(r, start, q, k_ref, segc_ref, segr_ref):
    keys = (2 * r + 2) * BLOCK
    scores = dot_nt(q, k_ref[:keys]) * (HD ** -0.5)
    rows = start + lax.broadcasted_iota(jnp.int32, scores.shape, 0)
    columns = lax.broadcasted_iota(jnp.int32, scores.shape, 1)
    same = segc_ref[pl.ds(start, BLOCK)] == segr_ref[:, :keys]
    scores = jnp.where((rows >= columns) & same, scores, -1000000000.0)
    raised = jnp.exp(scores - jnp.max(scores, -1, keepdims=True))
    return raised / jnp.sum(raised, -1, keepdims=True)


def attend_kernel(q_ref, k_ref, v_ref, segc_ref, segr_ref, out_ref):
    parity = lax.axis_index("expert") % 2
    for r in range(4):
        start = pl.multiple_of(block_of(r, parity) * BLOCK, BLOCK)
        probs = probabilities(r, start, q_ref[pl.ds(start, BLOCK)], k_ref, segc_ref, segr_ref)
        out_ref[r] = dot(probs.astype(bf16), v_ref[:(2 * r + 2) * BLOCK]).astype(bf16)


VM = pl.BlockSpec(memory_space=pltpu.VMEM)


def attend(q, k, v, segc, segr):
    return pl.pallas_call(
        attend_kernel, in_specs=[VM] * 5, out_specs=VM,
        out_shape=jax.ShapeDtypeStruct((4, BLOCK, HD), bf16),
        compiler_params=pltpu.CompilerParams(vmem_limit_bytes=40 * 2**20),
    )(q, k, v, segc, segr)


def greet_owners(z, y, x, core, sources):
    barrier = pltpu.get_barrier_semaphore()
    for r in range(4):
        target = device(r, sources(r), x, core)

        def signal():
            pl.semaphore_signal(barrier, inc=1, device_id=target, device_id_type=MESH)
        pl.when((z != r) | (z % 2 == 1))(signal)
    return barrier


def blend_kernel(parts, groups, multiply, part_ref, *refs):
    weights = refs[:groups]
    total, gathered, out_half, in_half, kept, held, from_x, send, recv, pair_send, pair_recv, local = refs[groups:]
    z, y, x, core = place()
    targets = lambda r: (y if r % 2 == 0 else 1 - y)
    source_y = (y + z) % 2
    barrier = greet_owners(z, y, x, core, lambda r: source_y)
    for where in (device(z, y, 1 - x, core), device(z, y, x, 1 - core)):
        pl.semaphore_signal(barrier, inc=1, device_id=where, device_id_type=MESH)
    pl.semaphore_wait(barrier, 5 + z % 2)
    width = HD * 4

    def lanes(g, n):
        return pl.ds(pl.multiple_of(g * width + n * HD, HD), HD)

    def remote(r, g):
        return pltpu.make_async_remote_copy(
            src_ref=part_ref.at[r, :, pl.ds(g * HD, HD)], dst_ref=gathered.at[:, lanes(g, z)],
            send_sem=send.at[r, g], recv_sem=recv.at[z, g],
            device_id=device(r, targets(r), x, core), device_id_type=MESH)

    def arriving(n, g):
        return pltpu.make_async_remote_copy(
            src_ref=part_ref.at[n, :, pl.ds(g * HD, HD)], dst_ref=gathered.at[:, lanes(g, n)],
            send_sem=send.at[n, g], recv_sem=recv.at[n, g],
            device_id=device(n, source_y, x, core), device_id_type=MESH)

    def own(r, g):
        return pltpu.make_async_copy(
            part_ref.at[r, :, pl.ds(g * HD, HD)], gathered.at[:, lanes(g, r)], local.at[g])

    for r in range(4):
        here = (z == r) & (z % 2 == 0)

        @pl.when(here)
        def _():
            for g in range(groups):
                own(r, g).start()

        @pl.when(jnp.logical_not(here))
        def _():
            for g in range(groups):
                remote(r, g).start()
    for r in range(4):
        here = (z == r) & (z % 2 == 0)

        @pl.when(here)
        def _():
            for g in range(groups):
                own(r, g).wait()

        @pl.when(jnp.logical_not(here))
        def _():
            for g in range(groups):
                arriving(r, g).wait_recv()

    rows = total.shape[0]
    half = rows // 2
    chunk = half // 2
    my_half = core * half
    other_half = (1 - core) * half

    def pair(kind, c, source, target, where):
        return pltpu.make_async_remote_copy(
            src_ref=source, dst_ref=target, send_sem=pair_send.at[kind, c], recv_sem=pair_recv.at[kind, c],
            device_id=where, device_id_type=MESH)

    twin = device(z, y, x, 1 - core)
    across = device(z, y, 1 - x, core)
    piece = lambda c: pl.ds(c * chunk, chunk)
    first = [pair(0, c, out_half.at[piece(c)], in_half.at[piece(c)], twin) for c in range(2)]
    second = [pair(1, c, held.at[piece(c)], from_x.at[piece(c)], across) for c in range(2)]
    at = lambda base, c: pl.ds(pl.multiple_of(base + c * chunk, chunk), chunk)
    third = [pair(2, c, total.at[at(my_half, c)], total.at[at(my_half, c)], twin) for c in range(2)]
    for c in range(2):
        out_half[piece(c)] = multiply(gathered[at(other_half, c)], weights).astype(bf16)
        first[c].start()
    for c in range(2):
        kept[...] = multiply(gathered[at(my_half, c)], weights)
        first[c].wait_recv()
        held[piece(c)] = (kept[...] + in_half[piece(c)].astype(f32)).astype(bf16)
        second[c].start()
    for c in range(2):
        second[c].wait_recv()
        total[at(my_half, c)] = (held[piece(c)].astype(f32) + from_x[piece(c)].astype(f32)).astype(bf16)
        third[c].start()
    for c in range(2):
        pair(2, c, total.at[at(my_half, c)], total.at[at(other_half, c)], twin).wait_recv()
        first[c].wait_send()
        second[c].wait_send()
        third[c].wait_send()
    for r in range(4):
        here = (z == r) & (z % 2 == 0)

        @pl.when(jnp.logical_not(here))
        def _():
            for g in range(groups):
                remote(r, g).wait_send()


def blend(parts, weights, multiply, number):
    groups = parts.shape[2] // HD
    rows, width = BLOCK, 2048
    sd = jax.ShapeDtypeStruct
    half = rows // 2
    return pl.pallas_call(
        functools.partial(blend_kernel, 4, groups, multiply),
        in_specs=[VM] * (1 + groups), out_specs=[VM] * 2,
        out_shape=[sd((rows, width), bf16), sd((rows, 4 * groups * HD), bf16)],
        scratch_shapes=[
            pltpu.VMEM((half, width), bf16), pltpu.VMEM((half, width), bf16), pltpu.VMEM((half // 2, width), f32),
            pltpu.VMEM((half, width), bf16), pltpu.VMEM((half, width), bf16),
            pltpu.SemaphoreType.DMA((4, groups)), pltpu.SemaphoreType.DMA((4, groups)),
            pltpu.SemaphoreType.DMA((3, 2)), pltpu.SemaphoreType.DMA((3, 2)), pltpu.SemaphoreType.DMA((groups,)),
        ],
        compiler_params=pltpu.CompilerParams(collective_id=number, has_side_effects=True, vmem_limit_bytes=48 * 2**20),
    )(parts, *weights)


def masked_probs(b, q, k_ref, segc_ref, segr_ref):
    keys = (b + 1) * BLOCK
    scores = dot_nt(q, k_ref[:keys]) * (HD ** -0.5)
    rows = b * BLOCK + lax.broadcasted_iota(jnp.int32, scores.shape, 0)
    columns = lax.broadcasted_iota(jnp.int32, scores.shape, 1)
    same = segc_ref[b * BLOCK:keys] == segr_ref[:, :keys]
    scores = jnp.where((rows >= columns) & same, scores, -1000000000.0)
    raised = jnp.exp(scores - jnp.max(scores, -1, keepdims=True))
    return raised / jnp.sum(raised, -1, keepdims=True)


def far_first(z):
    ahead = z // 2
    return (3 - 3 * ahead, 2 - ahead, z + 1 - 2 * (z % 2), z)


def greet_peers(z, y, x, core, others):
    barrier = pltpu.get_barrier_semaphore()

    def signal(where):
        pl.semaphore_signal(barrier, inc=1, device_id=where, device_id_type=MESH)

    for n in range(4):
        pl.when(z != n)(lambda: signal(device(n, y, x, core)))
        pl.when(z != n)(lambda: signal(device(n, 1 - y, x, core)))
    signal(device(z, 1 - y, x, core))
    for where in others:
        signal(where)
    pl.semaphore_wait(barrier, 7 + len(others))


def heads_back_kernel(ga_ref, w_ref, ctx_ref, q_ref, k_ref, v_ref, segc_ref, segr_ref, qr_ref, kr_ref, qg_ref, kg_ref,
                      cos_ref, sin_ref, small_ref, raw_ref, gains_ref, wout_ref, small_out,
                      g_own, g_all, dk, dv, terms, from_y, held, from_z, small_y, small_sum, small_z,
                      send, recv, y_send, y_recv, z_send, z_recv, s_send, s_recv):
    z, y, x, core = place()
    me = z * 2 + y
    across, twin, corner = device(z, y, 1 - x, core), device(z, y, x, 1 - core), device(z, y, 1 - x, 1 - core)
    partner = device(z, 1 - y, x, core)
    greet_peers(z, y, x, core, (across, twin, corner))

    def remote(source, target, ssem, rsem, where):
        return pltpu.make_async_remote_copy(
            src_ref=source, dst_ref=target, send_sem=ssem, recv_sem=rsem, device_id=where, device_id_type=MESH)

    quarter = small_ref.shape[1] // 4

    def lanes(cx, cc):
        return pl.ds(pl.multiple_of((cx * 2 + cc) * quarter, quarter), quarter)

    own_lanes = lanes(x, core)
    small_pair = remote(small_ref.at[:, own_lanes], small_y, s_send.at[0], s_recv.at[0], partner)
    small_pair.start()

    g_context = dot_nt(ga_ref[...], w_ref[...]).astype(bf16)
    for n in range(4):
        g_own[n] = g_context[:, n * HD:(n + 1) * HD]

    def to_head(n, yt):
        return remote(g_own.at[n], g_all.at[me], send.at[n * 2 + yt], recv.at[me], device(n, yt, x, core))

    def from_block(b):
        return remote(g_own.at[b // 2], g_all.at[b], send.at[b], recv.at[b], device(b // 2, b % 2, x, core))

    for b in range(8):
        pl.when(me != b)(lambda: to_head(b // 2, b % 2).start())
    g_all[me] = g_own[z]

    for b in range(8):
        terms[b] = dot_tn(ga_ref[:, b * BLOCK:(b + 1) * BLOCK], ctx_ref[...]).astype(bf16)
    order = far_first(z)

    def term_pair(n):
        return remote(terms.at[n * 2 + 1 - y], from_y.at[n], y_send.at[n], y_recv.at[n], partner)

    def term_along(n):
        return remote(held.at[n], from_z.at[z], z_send.at[n], z_recv.at[z], device(n, y, x, core))

    def term_arriving(n):
        return remote(held.at[n], from_z.at[n], z_send.at[n], z_recv.at[n], device(n, y, x, core))

    for n in order:
        term_pair(n).start()

    def small_along(n):
        return remote(small_sum, small_z.at[z], s_send.at[1 + n], s_recv.at[1 + z], device(n, y, x, core))

    def small_arriving(n):
        return remote(small_sum, small_z.at[n], s_send.at[1 + n], s_recv.at[1 + n], device(n, y, x, core))

    def small_spread(i):
        where = (across, twin, corner)[i]
        return remote(small_out.at[:, own_lanes], small_out.at[:, own_lanes], s_send.at[5 + i], s_recv.at[5 + i], where)

    def small_spread_in(i):
        theirs = (lanes(1 - x, core), lanes(x, 1 - core), lanes(1 - x, 1 - core))[i]
        where = (across, twin, corner)[i]
        return remote(small_out.at[:, own_lanes], small_out.at[:, theirs], s_send.at[5 + i], s_recv.at[5 + i], where)

    for b in range(8):
        pl.when(me != b)(lambda: from_block(b).wait_recv())

    gain_sums = [jnp.zeros((1, HD), f32), jnp.zeros((1, HD), f32)]

    def back(turned, b, raw_in, gain, which):
        rows = slice(b * BLOCK, (b + 1) * BLOCK)
        g = turned * cos_ref[rows] - pltpu.roll(turned, HD // 2, 1) * sin_ref[rows]
        raw = raw_in[rows]
        factor = norm_factor(raw)
        n = raw * factor
        gain_sums[which] = gain_sums[which] + jnp.sum(g * n, 0, keepdims=True)
        g = g * gain[...]
        return (factor * (g - n * jnp.mean(g * n, -1, keepdims=True))).astype(bf16)

    for b in range(7, -1, -1):
        keys = (b + 1) * BLOCK
        q = q_ref[b * BLOCK:keys]
        g = g_all[b]
        probs = masked_probs(b, q, k_ref, segc_ref, segr_ref)
        gv = dot_tn(probs.astype(bf16), g)
        gp = dot_nt(g, v_ref[:keys])
        gs = (probs * (gp - jnp.sum(gp * probs, -1, keepdims=True))).astype(bf16)
        gk = dot_tn(gs, q)
        if b == 7:
            dv[...] = gv
            dk[...] = gk
        else:
            dv[:keys] += gv
            dk[:keys] += gk
        raw_ref[b, :, :HD] = back(dot(gs, k_ref[:keys]) * (HD ** -0.5), b, qr_ref, qg_ref, 0)
        if b == 5:
            small_pair.wait_recv()
            small_sum[...] = small_ref[:, own_lanes] + small_y[...]
            for n in range(4):
                pl.when(z != n)(lambda: small_along(n).start())
            small_z[z] = small_sum[...]
        if b in (4, 3, 2):
            n = order[4 - b]
            term_pair(n).wait_recv()
            held[n] = (terms[n * 2 + y].astype(f32) + from_y[n].astype(f32)).astype(bf16)
            term_along(n).start()
        if b == 1:
            for n in range(4):
                pl.when(z != n)(lambda: small_arriving(n).wait_recv())
            small_out[:, own_lanes] = (small_z[0] + small_z[1]) + (small_z[2] + small_z[3])
            for i in range(3):
                small_spread(i).start()
    term_pair(z).wait_recv()
    from_z[z] = (terms[me].astype(f32) + from_y[z].astype(f32)).astype(bf16)
    for b in range(8):
        rows = slice(b * BLOCK, (b + 1) * BLOCK)
        raw_ref[b, :, HD:2 * HD] = back(dk[rows] * (HD ** -0.5), b, kr_ref, kg_ref, 1)
        raw_ref[b, :, 2 * HD:] = dv[rows].astype(bf16)
    gains_ref[0:1] = gain_sums[0]
    gains_ref[1:2] = gain_sums[1]
    for n in range(4):
        pl.when(z != n)(lambda: term_arriving(n).wait_recv())
    wout_ref[...] = (from_z[0].astype(f32) + from_z[1].astype(f32)) + (from_z[2].astype(f32) + from_z[3].astype(f32))
    for i in range(3):
        small_spread_in(i).wait_recv()
        small_spread(i).wait_send()
    small_pair.wait_send()
    for b in range(8):
        pl.when(me != b)(lambda: to_head(b // 2, b % 2).wait_send())
    for n in range(4):
        term_pair(n).wait_send()
        pl.when(z != n)(lambda: term_along(n).wait_send())
        pl.when(z != n)(lambda: small_along(n).wait_send())


def heads_back(ga, w, ctx, q, k, v, segc, segr, qr, kr, qg, kg, cosine, sine, small, number):
    T, D = q.shape[0], ga.shape[1]
    S = small.shape[0]
    span = 4 * HD
    sd = jax.ShapeDtypeStruct
    dma = pltpu.SemaphoreType.DMA
    return pl.pallas_call(
        heads_back_kernel, in_specs=[VM] * 15, out_specs=[VM] * 4,
        out_shape=[sd((8, BLOCK, 3 * HD), bf16), sd((2, HD), f32), sd((BLOCK, span), f32), sd((S, D), f32)],
        scratch_shapes=[
            pltpu.VMEM((4, BLOCK, HD), bf16), pltpu.VMEM((8, BLOCK, HD), bf16),
            pltpu.VMEM((T, HD), f32), pltpu.VMEM((T, HD), f32),
            pltpu.VMEM((8, BLOCK, span), bf16), pltpu.VMEM((4, BLOCK, span), bf16),
            pltpu.VMEM((4, BLOCK, span), bf16), pltpu.VMEM((4, BLOCK, span), bf16),
            pltpu.VMEM((S, D // 4), f32), pltpu.VMEM((S, D // 4), f32), pltpu.VMEM((4, S, D // 4), f32),
            dma((8,)), dma((8,)), dma((4,)), dma((4,)), dma((4,)), dma((4,)), dma((8,)), dma((8,)),
        ],
        compiler_params=pltpu.CompilerParams(collective_id=number, has_side_effects=True, vmem_limit_bytes=56 * 2**20),
    )(ga, w, ctx, q, k, v, segc, segr, qr, kr, qg, kg, cosine, sine, small)


def finish_kernel(raw_ref, a_ref, wq_ref, wk_ref, wv_ref, gains_ref, hidden_ref, gain_ref, middle_ref,
                  grad_ref, weights_ref, norm_ref, gains_out,
                  columns, gathered, products, from_z, out_half, in_half, held, from_x, total, gains_in, norm_in,
                  load, send, recv, w_send, w_recv, pair_send, pair_recv, g_send, g_recv, n_send, n_recv):
    z, y, x, core = place()
    me = z * 2 + y
    across, twin = device(z, y, 1 - x, core), device(z, y, x, 1 - core)
    greet_peers(z, y, x, core, (across, twin))
    order = far_first(z)
    span = 4 * HD

    def remote(source, target, ssem, rsem, where):
        return pltpu.make_async_remote_copy(
            src_ref=source, dst_ref=target, send_sem=ssem, recv_sem=rsem, device_id=where, device_id_type=MESH)

    def lanes(g, n):
        return pl.ds(pl.multiple_of(g * span + n * HD, HD), HD)

    def rows_to(n, g):
        return remote(raw_ref.at[n * 2 + y, :, pl.ds(g * HD, HD)], gathered.at[:, lanes(g, z)],
                      send.at[n, g], recv.at[z, g], device(n, y, x, core))

    def rows_from(n, g):
        return remote(raw_ref.at[n * 2 + y, :, pl.ds(g * HD, HD)], gathered.at[:, lanes(g, n)],
                      send.at[n, g], recv.at[n, g], device(n, y, x, core))

    def column_load(n):
        block = pl.ds(pl.multiple_of((n * 2 + y) * BLOCK, BLOCK), BLOCK)
        return pltpu.make_async_copy(a_ref.at[:, block], columns.at[n], load.at[n])

    for n in order[:3]:
        for g in range(3):
            rows_to(n, g).start()
    for n in order:
        column_load(n).start()

    def gains_to(n):
        return remote(gains_ref, gains_in.at[z], g_send.at[n], g_recv.at[z], device(n, y, x, core))

    def gains_from(n):
        return remote(gains_ref, gains_in.at[n], g_send.at[n], g_recv.at[n], device(n, y, x, core))

    for n in range(4):
        pl.when(z != n)(lambda: gains_to(n).start())
    gains_in[z] = gains_ref[...]
    for g in range(3):
        gathered[:, lanes(g, z)] = raw_ref[me, :, g * HD:(g + 1) * HD]

    def products_to(n):
        return remote(products.at[n], from_z.at[z], w_send.at[n], w_recv.at[z], device(n, y, x, core))

    def products_from(n):
        return remote(products.at[n], from_z.at[n], w_send.at[n], w_recv.at[n], device(n, y, x, core))

    raw_all = raw_ref[...].reshape(8 * BLOCK, 3 * HD)
    for i, n in enumerate(order):
        column_load(n).wait()
        product = dot_tn(columns[n], raw_all).astype(bf16)
        if i < 3:
            products[n] = product
            products_to(n).start()
        else:
            from_z[z] = product

    for n in range(4):
        for g in range(3):
            pl.when(z != n)(lambda: rows_from(n, g).wait_recv())

    rows = total.shape[0]
    half = rows // 2
    chunk = half // 2
    my_half = core * half
    other_half = (1 - core) * half
    piece = lambda c: pl.ds(c * chunk, chunk)
    at = lambda base, c: pl.ds(pl.multiple_of(base + c * chunk, chunk), chunk)

    def pair(kind, c, source, target, where):
        return remote(source, target, pair_send.at[kind, c], pair_recv.at[kind, c], where)

    def multiply(part):
        return (dot_nt(part[:, :span], wq_ref[...]) + dot_nt(part[:, span:2 * span], wk_ref[...])
                + dot_nt(part[:, 2 * span:], wv_ref[...]))

    first = [pair(0, c, out_half.at[piece(c)], in_half.at[piece(c)], twin) for c in range(2)]
    second = [pair(1, c, held.at[piece(c)], from_x.at[piece(c)], across) for c in range(2)]
    third = [pair(2, c, total.at[at(my_half, c)], total.at[at(my_half, c)], twin) for c in range(2)]
    for c in range(2):
        out_half[piece(c)] = multiply(gathered[at(other_half, c)]).astype(bf16)
        first[c].start()
    for c in range(2):
        kept = multiply(gathered[at(my_half, c)])
        first[c].wait_recv()
        held[piece(c)] = (kept + in_half[piece(c)].astype(f32)).astype(bf16)
        second[c].start()
    for n in range(4):
        pl.when(z != n)(lambda: products_from(n).wait_recv())
    for n in range(4):
        for g in range(3):
            weights_ref[g, :, n * HD:(n + 1) * HD] = from_z[n, :, g * HD:(g + 1) * HD].astype(f32)
    for n in range(4):
        pl.when(z != n)(lambda: gains_from(n).wait_recv())
        gains_out[:, n * HD:(n + 1) * HD] = gains_in[n]
    for c in range(2):
        second[c].wait_recv()
        total[at(my_half, c)] = (held[piece(c)].astype(f32) + from_x[piece(c)].astype(f32)).astype(bf16)
        third[c].start()
    for c in range(2):
        pair(2, c, total.at[at(my_half, c)], total.at[at(other_half, c)], twin).wait_recv()

    norm_part = jnp.zeros((1, total.shape[1]), f32)
    step = 32

    def norm_rows(i, norm_part):
        part = pl.ds(pl.multiple_of(i * step, step), step)
        e = total[part].astype(f32)
        v = hidden_ref[part].astype(f32)
        factor = norm_factor(v)
        n = v * factor
        norm_part = norm_part + jnp.sum(e * n, 0, keepdims=True)
        e = e * gain_ref[...]
        grad_ref[part] = middle_ref[part] + factor * (e - n * jnp.mean(e * n, -1, keepdims=True))
        return norm_part

    norm_part = lax.fori_loop(0, rows // step, norm_rows, norm_part)
    norm_in[me] = jnp.broadcast_to(norm_part, (8, total.shape[1]))

    def norm_to(b):
        return remote(norm_in.at[me], norm_in.at[me], n_send.at[b], n_recv.at[me], device(b // 2, b % 2, x, core))

    def norm_from(b):
        return remote(norm_in.at[b], norm_in.at[b], n_send.at[b], n_recv.at[b], device(b // 2, b % 2, x, core))

    for b in range(8):
        pl.when(me != b)(lambda: norm_to(b).start())
    for b in range(8):
        pl.when(me != b)(lambda: norm_from(b).wait_recv())
    sums = [norm_in[b, 0:1] for b in range(8)]
    norm_ref[...] = ((sums[0] + sums[1]) + (sums[2] + sums[3])) + ((sums[4] + sums[5]) + (sums[6] + sums[7]))

    for c in range(2):
        first[c].wait_send()
        second[c].wait_send()
        third[c].wait_send()
    for b in range(8):
        pl.when(me != b)(lambda: norm_to(b).wait_send())
    for n in range(4):
        for g in range(3):
            pl.when(z != n)(lambda: rows_to(n, g).wait_send())
        pl.when(z != n)(lambda: products_to(n).wait_send())
        pl.when(z != n)(lambda: gains_to(n).wait_send())


def finish(raw, a, wq, wk, wv, gains, hidden, gain, middle, number):
    T, D = a.shape
    rows, half = BLOCK, BLOCK // 2
    span = 4 * HD
    sd = jax.ShapeDtypeStruct
    dma = pltpu.SemaphoreType.DMA
    vm = pltpu.VMEM
    return pl.pallas_call(
        finish_kernel, in_specs=[VM, pl.BlockSpec(memory_space=pl.ANY)] + [VM] * 7, out_specs=[VM] * 4,
        out_shape=[sd((rows, D), f32), sd((3, BLOCK, span), f32), sd((1, D), f32), sd((2, span), f32)],
        scratch_shapes=[
            vm((4, T, BLOCK), bf16), vm((rows, 3 * span), bf16), vm((4, BLOCK, 3 * HD), bf16), vm((4, BLOCK, 3 * HD), bf16),
            vm((half, D), bf16), vm((half, D), bf16), vm((half, D), bf16), vm((half, D), bf16), vm((rows, D), bf16),
            vm((4, 2, HD), f32), vm((8, 8, D), f32),
            dma((4,)), dma((4, 3)), dma((4, 3)), dma((4,)), dma((4,)), dma((3, 2)), dma((3, 2)),
            dma((4,)), dma((4,)), dma((8,)), dma((8,)),
        ],
        compiler_params=pltpu.CompilerParams(collective_id=number, has_side_effects=True, vmem_limit_bytes=56 * 2**20),
    )(raw, a, wq, wk, wv, gains, hidden, gain, middle)


def on_device(
    hidden_in,
    norm1_gain,
    w_query,
    w_key,
    w_value,
    w_out,
    query_gain,
    key_gain,
    norm2_gain,
    w_router,
    w_gate,
    w_up,
    w_down,
    routes,
    segments,
    cotangent,
):
    seq_len, width = hidden_in.shape
    local_width = w_query.shape[1]
    head_count = local_width // HEAD_DIM
    expert_devs = lax.axis_size("expert")
    local_experts = w_gate.shape[0]
    expert_total = w_router.shape[1]
    capacity = 2 * seq_len * TOP // expert_total
    slab_rows = local_experts * capacity
    my_index = lax.axis_index("expert")
    group = SEQ // seq_len
    rank = my_index % group
    f32 = jnp.float32
    bf16 = jnp.bfloat16

    def split_heads(values):
        return values.reshape(seq_len, head_count, HEAD_DIM)

    inputs = hidden_in.astype(f32)
    inverse_attn = inverse_rms(inputs)
    normed_attn = inputs * inverse_attn
    attn_input = (normed_attn * norm1_gain).astype(bf16)
    q_raw = split_heads(jnp.dot(attn_input, w_query, preferred_element_type=f32))
    k_raw = split_heads(jnp.dot(attn_input, w_key, preferred_element_type=f32))
    v_heads = split_heads(jnp.dot(attn_input, w_value, preferred_element_type=f32).astype(bf16))
    q_gains = query_gain.reshape(head_count, HEAD_DIM)
    k_gains = key_gain.reshape(head_count, HEAD_DIM)
    q_inverse = inverse_rms(q_raw)
    q_normed = q_raw * q_inverse
    k_inverse = inverse_rms(k_raw)
    k_normed = k_raw * k_inverse
    local_places = lax.iota(jnp.int32, seq_len)
    query_places = rank * seq_len + local_places
    cosine, sine_part = rope_tables(query_places.astype(f32), HEAD_DIM // 2)
    queries = rotate(q_normed * q_gains, cosine, sine_part, 1.0).astype(bf16)
    key_rot = rotate(k_normed * k_gains, cosine, sine_part, 1.0).astype(bf16)
    score_scale = HEAD_DIM ** (-0.5)
    keys_values = jnp.stack([key_rot, v_heads])
    pieces = [keys_values]
    for offset in range(1, group):
        keys_values = from_behind(keys_values, "expert", 1)
        pieces.append(keys_values)
    stacked = jnp.stack(pieces, 1).reshape(2, group * seq_len, head_count, HEAD_DIM)
    keys_all = stacked[0]
    values_all = stacked[1]
    query_segs = lax.dynamic_slice_in_dim(segments, my_index * seq_len, seq_len, 0)
    key_segs = jnp.concatenate(
        [
            lax.dynamic_slice_in_dim(
                segments, jnp.maximum(my_index - offset, 0) * seq_len, seq_len, 0
            )
            for offset in range(group)
        ],
        0,
    )
    offsets = lax.iota(jnp.int32, group)
    key_places = ((rank - offsets)[:, None] * seq_len + local_places[None, :]).reshape(-1)
    key_valid = jnp.repeat(rank - offsets >= 0, seq_len)
    allowed = (
        key_valid[None, :]
        & (query_places[:, None] >= key_places[None, :])
        & (query_segs[:, None] == key_segs[None, :])
    )

    def scores_of():
        raw_scores = (
            jnp.einsum("thd,shd->hts", queries, keys_all, preferred_element_type=f32) * score_scale
        )
        return jnp.where(allowed[None], raw_scores, MASKED)

    scores = scores_of()
    row_max = jnp.max(scores, -1, keepdims=True)
    raised = jnp.exp(scores - row_max)
    exp_total = jnp.sum(raised, -1, keepdims=True)
    log_total = row_max + jnp.log(exp_total)
    attn_probs = (raised / exp_total).astype(bf16)
    context = (
        jnp.einsum("hts,shd->thd", attn_probs, values_all, preferred_element_type=f32)
        .reshape(seq_len, local_width)
        .astype(bf16)
    )
    attn_part = jnp.dot(context, w_out, preferred_element_type=f32)
    middle = inputs + lax.psum(attn_part, "head")
    inverse_moe = inverse_rms(middle)
    normed_moe = middle * inverse_moe
    moe_input = (normed_moe * norm2_gain).astype(bf16)
    logits = jnp.dot(moe_input, w_router, preferred_element_type=f32)
    chosen = jnp.take_along_axis(logits, routes, 1)
    raised_gate = jnp.exp(chosen - jnp.max(chosen, -1, keepdims=True))
    gate_weights = raised_gate / jnp.sum(raised_gate, -1, keepdims=True)
    catalog = lax.iota(jnp.int32, expert_total)
    route_hot = (routes[:, :, None] == catalog).astype(jnp.int32)
    token_hot = jnp.sum(route_hot, 1, dtype=jnp.int32)
    earlier = jnp.cumsum(token_hot, 0, dtype=jnp.int32) - token_hot
    position = routes * capacity + jnp.take_along_axis(earlier, routes, 1)
    flat_pos = position.reshape(-1)
    owners = (
        jnp.full((expert_total * capacity,), seq_len, jnp.int32)
        .at[flat_pos]
        .set(jnp.repeat(lax.iota(jnp.int32, seq_len), TOP))
    )
    padded = jnp.concatenate([moe_input, jnp.zeros((1, width), bf16)], 0)
    outgoing = padded[owners].reshape(expert_devs, slab_rows, width)
    arrived = lax.all_to_all(outgoing, "expert", split_axis=0, concat_axis=0, tiled=True)
    rows_in = arrived.reshape(expert_devs, local_experts, capacity, width)
    gate_act = jnp.einsum("sjcd,jdf->sjcf", rows_in, w_gate, preferred_element_type=f32)
    up_act = jnp.einsum("sjcd,jdf->sjcf", rows_in, w_up, preferred_element_type=f32)
    hidden = (jax.nn.silu(gate_act) * up_act).astype(bf16)
    partial_out = jnp.einsum("sjcf,jfd->sjcd", hidden, w_down, preferred_element_type=f32).reshape(
        expert_devs, slab_rows, width
    )
    rows_out = (
        lax.psum_scatter(partial_out.astype(jnp.bfloat16), "head", scatter_dimension=2, tiled=True)
        .astype(jnp.float32)
        .astype(bf16)
    )
    leaving = lax.all_gather(rows_out, "head", axis=2, tiled=True)
    returned = lax.all_to_all(leaving, "expert", split_axis=0, concat_axis=0, tiled=True)
    picked = returned.reshape(expert_total * capacity, width)[position]
    moe_out = jnp.einsum("tk,tkd->td", gate_weights, picked, preferred_element_type=f32)
    output = (middle + moe_out).astype(bf16)
    grad_final = cotangent.astype(f32)
    grad_gates = jnp.einsum("td,tkd->tk", grad_final, picked, preferred_element_type=f32)
    grad_chosen = gate_weights * (
        grad_gates - jnp.sum(grad_gates * gate_weights, -1, keepdims=True)
    )
    grad_logits = jnp.einsum("tk,tke->te", grad_chosen, route_hot.astype(f32)).astype(bf16)
    grad_router = jnp.dot(moe_input.T, grad_logits, preferred_element_type=f32)
    grad_moe_input = jnp.dot(grad_logits, w_router.T, preferred_element_type=f32)
    grad_expert_out = (gate_weights[:, :, None] * grad_final[:, None, :]).astype(bf16)
    grad_slab = (
        jnp.zeros((expert_total * capacity, width), bf16)
        .at[flat_pos]
        .set(grad_expert_out.reshape(seq_len * TOP, width))
    )
    grad_slab = grad_slab.reshape(expert_devs, slab_rows, width)
    grad_arrived = lax.all_to_all(grad_slab, "expert", split_axis=0, concat_axis=0, tiled=True)
    grad_rows_out = grad_arrived.reshape(expert_devs, local_experts, capacity, width)
    grad_hidden = jnp.einsum("sjcd,jfd->sjcf", grad_rows_out, w_down, preferred_element_type=f32)
    grad_down = jnp.einsum("sjcf,sjcd->jfd", hidden, grad_rows_out, preferred_element_type=f32)
    sigmoid = jax.nn.sigmoid(gate_act)
    grad_up_act = (grad_hidden * gate_act * sigmoid).astype(bf16)
    grad_gate_act = (grad_hidden * up_act * sigmoid * (1.0 + gate_act * (1.0 - sigmoid))).astype(
        bf16
    )
    grad_gate = jnp.einsum("sjcd,sjcf->jdf", rows_in, grad_gate_act, preferred_element_type=f32)
    grad_up = jnp.einsum("sjcd,sjcf->jdf", rows_in, grad_up_act, preferred_element_type=f32)
    grad_rows_in = jnp.einsum("sjcf,jdf->sjcd", grad_gate_act, w_gate, preferred_element_type=f32)
    grad_rows_in = grad_rows_in + jnp.einsum(
        "sjcf,jdf->sjcd", grad_up_act, w_up, preferred_element_type=f32
    )
    grad_back = (
        lax.psum_scatter(
            grad_rows_in.reshape(expert_devs, slab_rows, width).astype(jnp.bfloat16),
            "head",
            scatter_dimension=2,
            tiled=True,
        )
        .astype(jnp.float32)
        .astype(bf16)
    )
    leaving_grad = lax.all_gather(grad_back, "head", axis=2, tiled=True)
    grad_home = lax.all_to_all(leaving_grad, "expert", split_axis=0, concat_axis=0, tiled=True)
    grad_moe_input = grad_moe_input + jnp.sum(
        grad_home.reshape(expert_total * capacity, width)[position], 1, dtype=f32
    )
    grad_norm2 = jnp.sum(grad_moe_input * normed_moe, 0)
    grad_middle = grad_final + norm_back(grad_moe_input * norm2_gain, normed_moe, inverse_moe)
    grad_attn = grad_middle.astype(bf16)
    grad_out_turned = jnp.dot(grad_attn.T, context, preferred_element_type=f32)
    grad_context = split_heads(jnp.dot(grad_attn, w_out.T, preferred_element_type=f32).astype(bf16))
    attn_full = jnp.exp(scores_of() - log_total)
    attn_low = attn_full.astype(bf16)
    grad_values_all = jnp.einsum("hts,thd->shd", attn_low, grad_context, preferred_element_type=f32)
    grad_probs = jnp.einsum("thd,shd->hts", grad_context, values_all, preferred_element_type=f32)
    grad_scores = (
        attn_full * (grad_probs - jnp.sum(grad_probs * attn_full, -1, keepdims=True))
    ).astype(bf16)
    grad_queries = (
        jnp.einsum("hts,shd->thd", grad_scores, keys_all, preferred_element_type=f32) * score_scale
    )
    grad_keys_all = (
        jnp.einsum("hts,thd->shd", grad_scores, queries, preferred_element_type=f32) * score_scale
    )
    kv_terms = jnp.stack([grad_keys_all, grad_values_all]).reshape(
        2, group, seq_len, head_count, HEAD_DIM
    )
    kv_total = kv_terms[:, 0]
    for offset in range(1, group):
        kv_total = kv_total + from_behind(
            kv_terms[:, offset].astype(jnp.bfloat16), "expert", -offset
        ).astype(jnp.float32)
    grad_keys = kv_total[0]
    grad_values = kv_total[1]
    grad_q_normed = rotate(grad_queries, cosine, sine_part, -1.0)
    grad_k_normed = rotate(grad_keys, cosine, sine_part, -1.0)
    grad_query_gain = jnp.sum(grad_q_normed * q_normed, 0).reshape(local_width)
    grad_key_gain = jnp.sum(grad_k_normed * k_normed, 0).reshape(local_width)
    grad_q_raw = (
        norm_back(grad_q_normed * q_gains, q_normed, q_inverse)
        .reshape(seq_len, local_width)
        .astype(bf16)
    )
    grad_k_raw = (
        norm_back(grad_k_normed * k_gains, k_normed, k_inverse)
        .reshape(seq_len, local_width)
        .astype(bf16)
    )
    grad_v_raw = grad_values.reshape(seq_len, local_width).astype(bf16)
    grad_query = jnp.dot(attn_input.T, grad_q_raw, preferred_element_type=f32)
    grad_key = jnp.dot(attn_input.T, grad_k_raw, preferred_element_type=f32)
    grad_value = jnp.dot(attn_input.T, grad_v_raw, preferred_element_type=f32)
    input_part = jnp.dot(grad_q_raw, w_query.T, preferred_element_type=f32)
    input_part = input_part + jnp.dot(grad_k_raw, w_key.T, preferred_element_type=f32)
    input_part = input_part + jnp.dot(grad_v_raw, w_value.T, preferred_element_type=f32)
    grad_attn_input = lax.psum(input_part.astype(jnp.bfloat16), "head").astype(jnp.float32)
    grad_norm1 = jnp.sum(grad_attn_input * normed_attn, 0)
    grad_input = grad_middle + norm_back(grad_attn_input * norm1_gain, normed_attn, inverse_attn)
    grad_query, grad_key, grad_value, grad_out_turned = (
        lax.psum_scatter(
            grad_query.astype(jnp.bfloat16), "expert", scatter_dimension=0, tiled=True
        ).astype(jnp.float32),
        lax.psum_scatter(
            grad_key.astype(jnp.bfloat16), "expert", scatter_dimension=0, tiled=True
        ).astype(jnp.float32),
        lax.psum_scatter(
            grad_value.astype(jnp.bfloat16), "expert", scatter_dimension=0, tiled=True
        ).astype(jnp.float32),
        lax.psum_scatter(
            grad_out_turned.astype(jnp.bfloat16), "expert", scatter_dimension=0, tiled=True
        ).astype(jnp.float32),
    )
    grad_router, grad_norm1, grad_norm2, grad_query_gain, grad_key_gain = (
        lax.psum(grad_router.astype(jnp.bfloat16), "expert").astype(jnp.float32),
        lax.psum(grad_norm1.astype(jnp.bfloat16), "expert").astype(jnp.float32),
        lax.psum(grad_norm2.astype(jnp.bfloat16), "expert").astype(jnp.float32),
        lax.psum(grad_query_gain.astype(jnp.bfloat16), "expert").astype(jnp.float32),
        lax.psum(grad_key_gain.astype(jnp.bfloat16), "expert").astype(jnp.float32),
    )
    return (
        output,
        grad_input,
        grad_norm1,
        grad_query,
        grad_key,
        grad_value,
        grad_out_turned.T,
        grad_query_gain,
        grad_key_gain,
        grad_norm2,
        grad_router,
        grad_gate,
        grad_up,
        grad_down,
    )


def dense_layer(
    hidden_in, norm1_gain, w_query, w_key, w_value, w_out, query_gain, key_gain, norm2_gain, w_router,
    w_gate, w_up, w_down, routes, segments, cotangent,
):
    rows, width = hidden_in.shape
    experts = w_router.shape[1]
    devices = lax.axis_size("expert")
    tokens = devices * rows
    local_experts = w_gate.shape[0]
    ff = w_gate.shape[2]
    my_index = lax.axis_index("expert")
    head = my_index // 2

    def own_head(v):
        return lax.dynamic_slice_in_dim(v, head * HEAD_DIM, HEAD_DIM, v.ndim - 1)

    hidden_all = gather_all(hidden_in, 1).reshape(tokens, width)
    weights = jnp.concatenate([own_head(w_query), own_head(w_key), own_head(w_value)], 1)
    q_gain, k_gain = own_head(query_gain)[None], own_head(key_gain)[None]
    cosine, sine = rope_tables(lax.iota(jnp.int32, tokens).astype(f32), HEAD_DIM // 2)
    cosine, sine = cosine[:, 0], sine[:, 0]
    cosine = jnp.concatenate([cosine, cosine], 1)
    sine = jnp.concatenate([-sine, sine], 1)
    attn_all, queries, keys, values, q_raw, k_raw = project(
        hidden_all, norm1_gain[None], weights, q_gain, k_gain, cosine, sine
    )
    segc, segr = segments[:, None], segments[None]
    context = attend(queries, keys, values, segc, segr)
    attn_out, own_context = blend(context, [w_out], lambda a, w: dot(a, w[0][...]), 2)

    inputs = hidden_in.astype(f32)
    middle = inputs + attn_out.astype(f32)
    inverse_moe = inverse_rms(middle)
    normed_moe = middle * inverse_moe
    moe_input = (normed_moe * norm2_gain).astype(bf16)
    own_mask = jnp.sum((routes[:, :, None] == lax.iota(jnp.int32, experts)).astype(f32), 1)
    sent = jnp.concatenate([cotangent, jnp.pad(own_mask.astype(bf16), ((0, 0), (0, 128 - experts)))], 1)
    grads_all = gather_all(sent, 3).reshape(tokens, width + 128)
    everyone = gather_all(moe_input, 4).reshape(tokens, width)
    first = jnp.full((1,), local_experts, jnp.int32) * my_index
    weighted, grad_acts, parts = moe(first, everyone, grads_all, w_router, w_gate, w_up, w_down)
    grad_down = tn(weighted, grads_all, 512, 512, width).reshape(local_experts, ff, width)
    grad_gate, grad_up = expert_grads(everyone, grad_acts, local_experts)
    total = scatter_sum(parts.reshape(devices, rows, 2 * width + 128), 5)
    output = (middle + total[:, :width].astype(f32)).astype(bf16)
    grad_final = cotangent.astype(f32)
    tail = total[:, 2 * width :].astype(f32)
    grad_gates = tail[:, :experts] + tail[:, experts : 2 * experts]
    logits = jnp.where(
        own_mask > 0, jnp.dot(moe_input, w_router, preferred_element_type=f32), -jnp.inf
    )
    raised_gate = jnp.exp(logits - jnp.max(logits, -1, keepdims=True))
    gate_weights = raised_gate / jnp.sum(raised_gate, -1, keepdims=True)
    grad_logits = (
        gate_weights * (grad_gates - jnp.sum(grad_gates * gate_weights, -1, keepdims=True))
    ).astype(bf16)
    grad_moe_input = jnp.dot(grad_logits, w_router.T, preferred_element_type=f32)
    grad_moe_input = grad_moe_input + total[:, width : 2 * width].astype(f32)
    grad_middle = grad_final + norm_back(grad_moe_input * norm2_gain, normed_moe, inverse_moe)
    small = jnp.concatenate(
        [
            lax.dot_general(grad_logits, moe_input, (((0,), (0,)), ((), ())), preferred_element_type=f32),
            jnp.sum(grad_moe_input * normed_moe, 0, keepdims=True),
            jnp.zeros((7, width), f32),
        ],
        0,
    )

    raw_grads, gains, grad_w_out, small = heads_back(
        grad_middle.astype(bf16), w_out, own_context, queries, keys, values, segc, segr,
        q_raw, k_raw, q_gain, k_gain, cosine, sine, small, 6,
    )
    grad_input, grad_qkv, grad_norm1, gains = finish(
        raw_grads, attn_all, w_query, w_key, w_value, gains, hidden_in, norm1_gain[None], grad_middle, 7
    )
    return (
        output,
        grad_input,
        grad_norm1[0],
        grad_qkv[0],
        grad_qkv[1],
        grad_qkv[2],
        grad_w_out.T,
        gains[0],
        gains[1],
        small[experts],
        small[:experts].T,
        grad_gate,
        grad_up,
        grad_down,
    )


def layer(*arrays):
    rows, experts = arrays[0].shape[0], arrays[9].shape[1]
    whole = 2 * rows * TOP // experts >= rows and rows * lax.axis_size("expert") == SEQ
    grid = (lax.axis_size("expert"), lax.axis_size("head")) == (8, 4)
    return dense_layer(*arrays) if whole and grid else on_device(*arrays)


def solution(mesh):
    return jax.shard_map(
        layer,
        mesh=mesh,
        in_specs=(
            P("expert", None),
            P(),
            P(None, "head"),
            P(None, "head"),
            P(None, "head"),
            P("head", None),
            P("head"),
            P("head"),
            P(),
            P(),
            P("expert", None, "head"),
            P("expert", None, "head"),
            P("expert", "head", None),
            P("expert", None),
            P(),
            P("expert", None),
        ),
        out_specs=(
            P("expert", None),
            P("expert", None),
            P(),
            P("expert", "head"),
            P("expert", "head"),
            P("expert", "head"),
            P("head", "expert"),
            P("head"),
            P("head"),
            P(),
            P(),
            P("expert", None, "head"),
            P("expert", None, "head"),
            P("expert", "head", None),
        ),
        check_vma=False,
    )
```

```python
import functools

import jax
import jax.numpy as jnp
from jax import lax
from jax.experimental import pallas as pl
from jax.experimental.pallas import tpu as pltpu
from jax.sharding import PartitionSpec as P

HEAD_DIM = 128
TOP = 8
SEQ = 2048
MESH = pl.DeviceIdType.MESH
bf16 = jnp.bfloat16
f32 = jnp.float32


EPSILON = 1e-05
ROPE_BASE = 10000.0
MASKED = -1000000000.0


def from_behind(shard, axis, by):
    size = lax.axis_size(axis)
    pairs = [(i, i + by) for i in range(size) if 0 <= i + by < size]
    return lax.ppermute(shard, axis, pairs)


def inverse_rms(values):
    return lax.rsqrt(jnp.mean(values * values, -1, keepdims=True) + EPSILON)


def norm_back(grad_normed, normed, inverse):
    return inverse * (grad_normed - normed * jnp.mean(grad_normed * normed, -1, keepdims=True))


def rope_tables(places, half_dim):
    inv_freq = ROPE_BASE ** (-lax.iota(jnp.int32, half_dim).astype(jnp.float32) / half_dim)
    angles = places[:, None] * inv_freq[None, :]
    return (jnp.cos(angles)[:, None, :], jnp.sin(angles)[:, None, :])


def rotate(values, cosine, sine_part, direction):
    half_dim = values.shape[-1] // 2
    first_half = values[..., :half_dim]
    second_half = values[..., half_dim:]
    turned = direction * sine_part
    return jnp.concatenate(
        [first_half * cosine - second_half * turned, second_half * cosine + first_half * turned], -1
    )


def place():
    block = lax.axis_index("expert")
    lane = lax.axis_index("head")
    return block // 2, block % 2, lane // 2, lane % 2


def device(z, y, x, core):
    return (z * 2 + y, x * 2 + core)


def greet(z, y, x, core):
    barrier = pltpu.get_barrier_semaphore()

    def signal(target):
        pl.semaphore_signal(barrier, inc=1, device_id=target, device_id_type=MESH)

    signal(device(z, 1 - y, x, core))
    signal(device(z, y, 1 - x, core))
    signal(device(z, y, x, 1 - core))

    @pl.when(z > 0)
    def _():
        signal(device(z - 1, y, x, core))

    @pl.when(z < 3)
    def _():
        signal(device(z + 1, y, x, core))

    pl.semaphore_wait(barrier, 3 + (z > 0).astype(jnp.int32) + (z < 3).astype(jnp.int32))


def add_split(a, b):
    pair = a.astype(f32) + b.astype(f32)
    lanes = lax.broadcasted_iota(jnp.int32, pair.shape, 1)
    whole = jnp.where(lanes < 16, pair + pltpu.roll(pair, 112, 1), 0.0)
    high = whole.astype(bf16).astype(f32)
    return (high + pltpu.roll(whole - high, 16, 1)).astype(bf16)


def dot(a,b): return jnp.dot(a,b,preferred_element_type=f32)
def dot_nt(a,b): return lax.dot_general(a,b,(((1,),(1,)),((),())),preferred_element_type=f32)
def dot_tn(a,b): return lax.dot_general(a,b,(((0,),(0,)),((),())),preferred_element_type=f32)


EPS = 1e-05
HD = 128
BLOCK = 256


def block_of(r, parity):
    return 2 * r + (parity if r % 2 == 0 else 1 - parity)


def norm_factor(v):
    return lax.rsqrt(jnp.mean(v * v, -1, keepdims=True) + EPS)


def probabilities(r, start, q, k_ref, segc_ref, segr_ref):
    keys = (2 * r + 2) * BLOCK
    scores = dot_nt(q, k_ref[:keys]) * (HD ** -0.5)
    rows = start + lax.broadcasted_iota(jnp.int32, scores.shape, 0)
    columns = lax.broadcasted_iota(jnp.int32, scores.shape, 1)
    same = segc_ref[pl.ds(start, BLOCK)] == segr_ref[:, :keys]
    scores = jnp.where((rows >= columns) & same, scores, -1000000000.0)
    raised = jnp.exp(scores - jnp.max(scores, -1, keepdims=True))
    return raised / jnp.sum(raised, -1, keepdims=True)


VM = pl.BlockSpec(memory_space=pltpu.VMEM)


def masked_probs(b, q, k_ref, segc_ref, segr_ref):
    keys = (b + 1) * BLOCK
    scores = dot_nt(q, k_ref[:keys]) * (HD ** -0.5)
    rows = b * BLOCK + lax.broadcasted_iota(jnp.int32, scores.shape, 0)
    columns = lax.broadcasted_iota(jnp.int32, scores.shape, 1)
    same = segc_ref[b * BLOCK:keys] == segr_ref[:, :keys]
    scores = jnp.where((rows >= columns) & same, scores, -1000000000.0)
    raised = jnp.exp(scores - jnp.max(scores, -1, keepdims=True))
    return raised / jnp.sum(raised, -1, keepdims=True)


def far_first(z):
    ahead = z // 2
    return (3 - 3 * ahead, 2 - ahead, z + 1 - 2 * (z % 2), z)


def greet_peers(z, y, x, core, others):
    barrier = pltpu.get_barrier_semaphore()

    def signal(where):
        pl.semaphore_signal(barrier, inc=1, device_id=where, device_id_type=MESH)

    for n in range(4):
        pl.when(z != n)(lambda: signal(device(n, y, x, core)))
        pl.when(z != n)(lambda: signal(device(n, 1 - y, x, core)))
    signal(device(z, 1 - y, x, core))
    for where in others:
        signal(where)
    pl.semaphore_wait(barrier, 7 + len(others))


def picked(i, values):
    if isinstance(i, int):
        return values[i]
    return sum((i == k).astype(jnp.int32) * v for k, v in enumerate(values))


class Gather:
    def __init__(self, own, whole, local_sem, send, recv, rows=BLOCK):
        self.own, self.whole, self.send, self.recv, self.rows = own, whole, send, recv, rows
        z, y, x, core = self.place = place()
        self.me = z * 2 + y
        half, eighth = rows // 2, rows // 8
        self.unit = eighth // 2
        self.keep = pltpu.make_async_copy(own, self.at(self.me, 0, rows), local_sem)

        def chunks(c):
            return ((c * half + x * 5 * self.unit, 3 * self.unit), (c * half + (3 - x) * self.unit, 3 * self.unit))

        def quarter(c, of):
            return (c * half + of * 3 * eighth, eighth)

        self.slab, self.twin_slab = chunks(core), chunks(1 - core)
        self.mine, self.theirs = quarter(core, x), quarter(core, 1 - x)
        self.twin_theirs = quarter(1 - core, 1 - x)

    def at(self, b, start, size):
        return self.whole.at[pl.ds(pl.multiple_of(b * self.rows + start, self.unit), size)]

    def copy(self, kind, c, b, part, where, own=False):
        if own:
            source = self.own.at[pl.ds(pl.multiple_of(part[0], self.unit), part[1])]
        else:
            source = self.at(b, *part)
        return pltpu.make_async_remote_copy(
            src_ref=source, dst_ref=self.at(b, *part), send_sem=self.send.at[kind, c, b], recv_sem=self.recv.at[kind, c, b],
            device_id=where, device_id_type=MESH)

    def up(self, b, c, own=False):
        z, y, x, core = self.place
        return self.copy(0, c, b, self.slab[c], device(z + 1, y, x, core), own)

    def down(self, b, c, own=False):
        z, y, x, core = self.place
        return self.copy(1, c, b, self.slab[c], device(z - 1, y, x, core), own)

    def over(self, b, c, own=False):
        z, y, x, core = self.place
        return self.copy(2, c, b, self.slab[c], device(z, 1 - y, x, core), own)

    def side(self, b, part):
        z, y, x, core = self.place
        return self.copy(3, 0, b, part, device(z, y, 1 - x, core))

    def twin(self, b, c, part):
        z, y, x, core = self.place
        return self.copy(4, c, b, part, device(z, y, x, 1 - core))

    def twin_x(self, b, part):
        z, y, x, core = self.place
        return self.copy(5, 0, b, part, device(z, y, x, 1 - core))

    def group(self, i):
        z = self.place[0]
        ahead = z // 2
        return picked(i, (z, z + 1 - 2 * (z % 2), 2 - ahead, 3 - 3 * ahead))

    def start(self):
        z, y, x, core = self.place
        for c in range(2):
            pl.when(z < 3)(lambda: self.up(self.me, c, True).start())
            pl.when(z > 0)(lambda: self.down(self.me, c, True).start())
            self.over(self.me, c, True).start()
        self.keep.start()

    def spread(self, b, c):
        if c == 0:
            self.side(b, self.mine).start()
        self.twin(b, c, self.slab[c]).start()

    def hop(self, i):
        z, y, x, core = self.place
        b = self.group(i) * 2 + y
        below = picked(i, (0, z % 2, z // 2, z // 2)) == 1
        for c in range(2):
            @pl.when(below)
            def _():
                self.up(b, c).wait_recv()
                pl.when(z < 3)(lambda: self.up(b, c).start())

            @pl.when(jnp.logical_not(below))
            def _():
                self.down(b, c).wait_recv()
                pl.when(z > 0)(lambda: self.down(b, c).start())

            self.over(b, c).start()
            self.spread(b, c)

    def hop_inside(self, i):
        z = self.place[0]
        pl.when((z > 0) & (z < 3))(lambda: self.hop(i))

    def hop_outside(self, i):
        z = self.place[0]
        pl.when(z % 3 == 0)(lambda: self.hop(i))

    def cross(self, i):
        b = self.group(i) * 2 + 1 - self.place[1]
        for c in range(2):
            self.over(b, c).wait_recv()
            self.spread(b, c)

    def blocks(self, i, act):
        y = self.place[1]
        n = self.group(i)
        act(n * 2 + 1 - y)
        if isinstance(i, int):
            if i > 0:
                act(n * 2 + y)
        else:
            pl.when(i > 0)(lambda: act(n * 2 + y))

    def flank(self, i):
        def act(b):
            self.side(b, self.theirs).wait_recv()
            self.twin_x(b, self.theirs).start()
        self.blocks(i, act)

    def complete(self, i):
        def act(b):
            for c in range(2):
                self.twin(b, c, self.twin_slab[c]).wait_recv()
            self.twin_x(b, self.twin_theirs).wait_recv()
        self.blocks(i, act)

    def drain(self):
        z, y, x, core = self.place
        for b in range(8):
            zb, yb = b // 2, b % 2

            @pl.when(self.me != b)
            def _():
                self.side(b, self.mine).wait_send()
                self.twin_x(b, self.theirs).wait_send()

            for c in range(2):
                pl.when(self.me != b)(lambda: self.twin(b, c, self.slab[c]).wait_send())
                pl.when(yb == y)(lambda: self.over(b, c).wait_send())
                pl.when((yb == y) & (zb <= z) & (z < 3))(lambda: self.up(b, c).wait_send())
                pl.when((yb == y) & (zb >= z) & (z > 0))(lambda: self.down(b, c).wait_send())

    def whole_run(self):
        self.start()
        self.hop(1)
        self.cross(0)
        self.hop_inside(2)
        self.flank(0)
        self.hop_outside(2)
        self.cross(1)
        self.hop_inside(3)
        self.flank(1)
        self.hop_outside(3)
        self.cross(2)
        self.cross(3)
        self.flank(2)
        self.flank(3)
        for i in range(4):
            self.complete(i)
        self.keep.wait()
        self.drain()


GATHER_SEMS = [pltpu.SemaphoreType.DMA, pltpu.SemaphoreType.DMA((6, 2, 8)), pltpu.SemaphoreType.DMA((6, 2, 8))]


ANY = pl.BlockSpec(memory_space=pl.ANY)


def project_all_kernel(own_ref, gain_ref, w_ref, qg_ref, kg_ref, cos_ref, sin_ref,
                       a_out, q_ref, k_ref, v_ref, qr_ref, kr_ref,
                       whole, a_buf, local_sem, send, recv, a_sem):
    greet(*place())
    gather = Gather(own_ref, whole, local_sem, send, recv)
    gather.start()
    gather.hop(1)
    gather.cross(0)
    gather.hop_inside(2)
    gather.flank(0)
    gather.keep.wait()
    span = 2 * BLOCK

    def rows_of(i):
        return pl.ds(pl.multiple_of(gather.group(i) * span, span), span)

    def stored(i, slot):
        return pltpu.make_async_copy(a_buf.at[slot], a_out.at[rows_of(i)], a_sem.at[slot])

    def step(i, _):
        gather.complete(i)
        pl.when(i == 0)(lambda: gather.hop_inside(3))
        rows = rows_of(i)
        slot = i % 2
        pl.when(i >= 2)(lambda: stored(i - 2, slot).wait())
        x = whole[rows].astype(f32)
        a = (x * norm_factor(x) * gain_ref[...]).astype(bf16)
        a_buf[slot] = a
        stored(i, slot).start()
        raw = dot(a, w_ref[...])
        cosine, sine = cos_ref[rows], sin_ref[rows]

        def turned(part, gain):
            n = part * norm_factor(part) * gain
            return (n * cosine + pltpu.roll(n, HD // 2, 1) * sine).astype(bf16)

        q_raw, k_raw = raw[:, :HD], raw[:, HD:2 * HD]
        qr_ref[rows] = q_raw
        kr_ref[rows] = k_raw
        q_ref[rows] = turned(q_raw, qg_ref[...])
        k_ref[rows] = turned(k_raw, kg_ref[...])
        v_ref[rows] = raw[:, 2 * HD:].astype(bf16)
        pl.when(i < 2)(lambda: gather.hop_outside(i + 2))
        pl.when(i < 3)(lambda: gather.cross(i + 1))
        pl.when(i < 3)(lambda: gather.flank(i + 1))
        return 0

    lax.fori_loop(0, 4, step, 0)
    stored(2, 0).wait()
    stored(3, 1).wait()
    gather.drain()


def project_all(own, gain, w, qg, kg, cosine, sine, number):
    rows, D = own.shape
    T = 8 * rows
    sd = jax.ShapeDtypeStruct
    return pl.pallas_call(
        project_all_kernel, in_specs=[ANY] + [VM] * 6, out_specs=[ANY] + [VM] * 5,
        out_shape=[sd((T, D), bf16)] + [sd((T, HD), bf16)] * 3 + [sd((T, HD), f32)] * 2,
        scratch_shapes=[pltpu.VMEM((T, D), bf16), pltpu.VMEM((2, 2 * rows, D), bf16)] + GATHER_SEMS + [pltpu.SemaphoreType.DMA((2,))],
        compiler_params=pltpu.CompilerParams(collective_id=number, has_side_effects=True, vmem_limit_bytes=56 * 2**20),
    )(own, gain, w, qg, kg, cosine, sine)


def attend_all_kernel(sent_ref, q_ref, k_ref, v_ref, segc_ref, segr_ref, w_ref, total, gathered, whole,
                      part, arrived, out_half, in_half, held, from_x, local_sem, g_send, g_recv,
                      send, recv, pair_send, pair_recv):
    z, y, x, core = place()
    across, twin = device(z, y, 1 - x, core), device(z, y, x, 1 - core)
    greet_peers(z, y, x, core, (across, twin))
    gather = Gather(sent_ref, whole, local_sem, g_send, g_recv)
    targets = lambda r: (y if r % 2 == 0 else 1 - y)
    source_y = (y + z) % 2

    def remote(source, target, ssem, rsem, where):
        return pltpu.make_async_remote_copy(
            src_ref=source, dst_ref=target, send_sem=ssem, recv_sem=rsem, device_id=where, device_id_type=MESH)

    def to_block(r):
        return remote(part.at[r], arrived.at[z], send.at[r], recv.at[z], device(r, targets(r), x, core))

    def from_head(n):
        return remote(part.at[n], arrived.at[n], send.at[n], recv.at[n], device(n, source_y, x, core))

    here = lambda r: (z == r) & (z % 2 == 0)
    gather.start()
    for r in range(3, -1, -1):
        start = pl.multiple_of(block_of(r, y) * BLOCK, BLOCK)
        probs = probabilities(r, start, q_ref[pl.ds(start, BLOCK)], k_ref, segc_ref, segr_ref)
        part[r] = dot(probs.astype(bf16), v_ref[:(2 * r + 2) * BLOCK]).astype(bf16)
        pl.when(jnp.logical_not(here(r)))(lambda: to_block(r).start())

    gather.hop(1)
    gather.cross(0)
    gather.hop_inside(2)

    @pl.when(z % 2 == 0)
    def _():
        arrived[z] = part[z]

    for n in range(4):
        pl.when(jnp.logical_not(here(n)))(lambda: from_head(n).wait_recv())
        gathered[:, n * HD:(n + 1) * HD] = arrived[n]

    rows = total.shape[0]
    half = rows // 2
    chunk = half // 2
    my_half = core * half
    other_half = (1 - core) * half
    piece = lambda c: pl.ds(c * chunk, chunk)
    at = lambda base, c: pl.ds(pl.multiple_of(base + c * chunk, chunk), chunk)

    def pair(kind, c, source, target, where):
        return remote(source, target, pair_send.at[kind, c], pair_recv.at[kind, c], where)

    first = [pair(0, c, out_half.at[piece(c)], in_half.at[piece(c)], twin) for c in range(2)]
    second = [pair(1, c, held.at[piece(c)], from_x.at[piece(c)], across) for c in range(2)]
    third = [pair(2, c, total.at[at(my_half, c)], total.at[at(my_half, c)], twin) for c in range(2)]
    for c in range(2):
        out_half[piece(c)] = dot(gathered[at(other_half, c)], w_ref[...]).astype(bf16)
        first[c].start()
    for c in range(2):
        kept = dot(gathered[at(my_half, c)], w_ref[...])
        first[c].wait_recv()
        held[piece(c)] = (kept + in_half[piece(c)].astype(f32)).astype(bf16)
        second[c].start()
    gather.flank(0)
    gather.hop_outside(2)
    gather.cross(1)
    gather.hop_inside(3)
    for c in range(2):
        second[c].wait_recv()
        total[at(my_half, c)] = (held[piece(c)].astype(f32) + from_x[piece(c)].astype(f32)).astype(bf16)
        third[c].start()
    gather.flank(1)
    gather.hop_outside(3)
    gather.cross(2)
    for c in range(2):
        pair(2, c, total.at[at(my_half, c)], total.at[at(other_half, c)], twin).wait_recv()
    gather.cross(3)
    gather.flank(2)
    gather.flank(3)
    for i in range(4):
        gather.complete(i)
    gather.keep.wait()
    gather.drain()
    for c in range(2):
        first[c].wait_send()
        second[c].wait_send()
        third[c].wait_send()
    for r in range(4):
        pl.when(jnp.logical_not(here(r)))(lambda: to_block(r).wait_send())


def attend_all(sent, q, k, v, segc, segr, w, number):
    rows, width = sent.shape
    D = w.shape[1]
    half = rows // 2
    sd = jax.ShapeDtypeStruct
    dma = pltpu.SemaphoreType.DMA
    return pl.pallas_call(
        attend_all_kernel, in_specs=[ANY] + [VM] * 6, out_specs=[VM, VM, ANY],
        out_shape=[sd((rows, D), bf16), sd((rows, 4 * HD), bf16), sd((8 * rows, width), bf16)],
        scratch_shapes=[pltpu.VMEM((4, BLOCK, HD), bf16)] * 2 + [pltpu.VMEM((half, D), bf16)] * 4 + GATHER_SEMS + [
            dma((4,)), dma((4,)), dma((3, 2)), dma((3, 2))],
        compiler_params=pltpu.CompilerParams(collective_id=number, has_side_effects=True, vmem_limit_bytes=56 * 2**20),
    )(sent, q, k, v, segc, segr, w)


def experts_kernel(own_ref, grads_ref, wr_ref, wg_in, wu_in, wd_in, x_out, weighted_out, acts_out, parts_out,
                   whole, wg, wu, wd, g_buf, mask_all, gw, w_buf, a_buf, p_buf,
                   local_sem, send, recv, weight_sem, g_sem, out_sem):
    z, y, x_place, core = place()
    first = (z * 2 + y) * wg_in.shape[0]
    D, ff = wg_in.shape[1], wg_in.shape[2]
    span = 2 * BLOCK
    weights = [pltpu.make_async_copy(source, target, weight_sem.at[k])
               for k, (source, target) in enumerate(((wd_in, wd), (wg_in, wg), (wu_in, wu)))]

    def grads_load(g):
        return pltpu.make_async_copy(grads_ref.at[pl.ds(g * span, span)], g_buf.at[g % 2], g_sem.at[g % 2])

    weights[0].start()
    grads_load(0).start()
    grads_load(1).start()
    weights[1].start()
    weights[2].start()
    greet(z, y, x_place, core)
    gather = Gather(own_ref, whole, local_sem, send, recv)
    gather.start()
    weights[0].wait()
    for g in range(4):
        grads_load(g).wait()
        rows = slice(g * span, (g + 1) * span)
        mask_all[rows] = g_buf[g % 2, :, D:]
        for j in range(2):
            gw[rows, j * ff:(j + 1) * ff] = dot_nt(g_buf[g % 2, :, :D], wd[j])
        if g < 2:
            grads_load(g + 2).start()
    gather.hop(1)
    gather.cross(0)
    gather.hop_inside(2)
    gather.flank(0)
    gather.keep.wait()
    weights[1].wait()
    weights[2].wait()

    def rows_of(i):
        return pl.ds(pl.multiple_of(gather.group(i) * span, span), span)

    def stores(i, slot):
        rows = rows_of(i)
        return [
            pltpu.make_async_copy(w_buf.at[slot], weighted_out.at[rows], out_sem.at[slot, 0]),
            pltpu.make_async_copy(a_buf.at[slot], acts_out.at[rows], out_sem.at[slot, 1]),
            pltpu.make_async_copy(p_buf.at[slot], parts_out.at[rows], out_sem.at[slot, 2]),
        ]

    def x_store(i, slot):
        return pltpu.make_async_copy(whole.at[rows_of(i)], x_out.at[rows_of(i)], out_sem.at[slot, 3])

    def step(i, _):
        gather.complete(i)
        slot = i % 2

        @pl.when(i >= 2)
        def _():
            for copy in stores(i - 2, slot):
                copy.wait()
            x_store(i - 2, slot).wait()

        x_store(i, slot).start()
        rows = rows_of(i)
        x = whole[rows]
        logits = dot(x, wr_ref[...])
        count = logits.shape[1]
        mask = mask_all[rows, :count].astype(f32) > 0
        top = jnp.max(jnp.where(mask, logits, -jnp.inf), -1, keepdims=True)
        raised = jnp.where(mask, jnp.exp(jnp.where(mask, logits - top, 0.0)), 0.0)
        gates = raised / jnp.sum(raised, -1, keepdims=True)
        lane = lax.broadcasted_iota(jnp.int32, gates.shape, 1)
        gg = jnp.zeros(gates.shape, f32)
        for j in range(2):
            here = lane == first + j
            gate = jnp.sum(jnp.where(here, gates, 0.0), -1, keepdims=True)
            ga = dot(x, wg[j])
            ua = dot(x, wu[j])
            gw_j = gw[rows, j * ff:(j + 1) * ff]
            s = 1.0 / (1.0 + jnp.exp(-ga))
            silu = ga * s
            h = (silu * ua).astype(bf16).astype(f32)
            gg = gg + jnp.where(here, jnp.sum(h * gw_j, -1, keepdims=True), 0.0)
            gh = gw_j * gate
            w_buf[slot, :, j * ff:(j + 1) * ff] = (h * gate).astype(bf16)
            a_buf[slot, :, 2 * j * ff:(2 * j + 1) * ff] = (gh * ua * s * (1.0 + ga * (1.0 - s))).astype(bf16)
            a_buf[slot, :, (2 * j + 1) * ff:(2 * j + 2) * ff] = (gh * silu).astype(bf16)
            if j == 0:
                pl.when(i == 0)(lambda: gather.hop_inside(3))
        pl.when(i < 2)(lambda: gather.hop_outside(i + 2))
        pl.when(i < 3)(lambda: gather.cross(i + 1))
        p_buf[slot, :, :D] = dot(w_buf[slot], wd[...].reshape(2 * ff, D)).astype(bf16)
        gx = dot_nt(a_buf[slot, :, :ff], wg[0])
        for k, weight in ((1, wu[0]), (2, wg[1]), (3, wu[1])):
            gx = gx + dot_nt(a_buf[slot, :, k * ff:(k + 1) * ff], weight)
        p_buf[slot, :, D:2 * D] = gx.astype(bf16)
        high = gg.astype(bf16)
        low = (gg - high.astype(f32)).astype(bf16)
        spare = jnp.zeros((span, 128 - 2 * count), bf16)
        p_buf[slot, :, 2 * D:] = jnp.concatenate([high, low, spare], 1)
        for copy in stores(i, slot):
            copy.start()
        pl.when(i < 3)(lambda: gather.flank(i + 1))
        return 0

    lax.fori_loop(0, 4, step, 0)
    for i in (2, 3):
        for copy in stores(i, i % 2):
            copy.wait()
        x_store(i, i % 2).wait()
    gather.drain()


def experts_all(own, grads, wr, wg, wu, wd, number):
    rows, D = own.shape
    T = 8 * rows
    J, _, F = wg.shape
    span = 2 * rows
    sd = jax.ShapeDtypeStruct
    dma = pltpu.SemaphoreType.DMA
    vm = pltpu.VMEM
    return pl.pallas_call(
        experts_kernel, in_specs=[ANY, ANY, VM, ANY, ANY, ANY], out_specs=[ANY] * 4,
        out_shape=[sd((T, D), bf16), sd((T, J * F), bf16), sd((T, 2 * J * F), bf16), sd((T, 2 * D + 128), bf16)],
        scratch_shapes=[
            vm((T, D), bf16), vm((J, D, F), bf16), vm((J, D, F), bf16), vm((J, F, D), bf16),
            vm((2, span, D + 128), bf16), vm((T, 128), bf16), vm((T, J * F), f32),
            vm((2, span, J * F), bf16), vm((2, span, 2 * J * F), bf16), vm((2, span, 2 * D + 128), bf16),
        ] + GATHER_SEMS + [dma((3,)), dma((2,)), dma((2, 4))],
        compiler_params=pltpu.CompilerParams(collective_id=number, has_side_effects=True, vmem_limit_bytes=60 * 2**20),
    )(own, grads, wr, wg, wu, wd)


def sum_rows(target, source, cols, rows):
    step = 16
    main = cols.size - cols.size % 2048

    @pl.loop(0, rows // step)
    def _(i):
        part = pl.ds(pl.multiple_of(i * step, step), step)
        wide = pl.ds(cols.start, main)
        target[part, wide] = (target[part, wide].astype(f32) + source[part, wide].astype(f32)).astype(bf16)
        if main < cols.size:
            tail = pl.ds(cols.start + main, cols.size - main)
            target[part, tail] = add_split(target[part, tail], source[part, tail])


def sums_kernel(parts, x_ref, acts_ref, grads_ref, weighted_ref, total, gate_out, up_out, down_out,
                held, from_core, from_x, from_y, from_below, from_above, shared_in,
                acts, weighted, x_buf, g_buf, gu_buf, down_buf,
                load_sem, send, recv, end_send, end_recv, fixed_sem, x_sem, g_sem, gu_sem, down_sem):
    z, y, x, core = place()
    D = x_ref.shape[1]
    half = parts.shape[1] // 2
    piece = half // 4
    me = z * 2 + y
    order = far_first(z)
    my_half = pl.ds(pl.multiple_of(core * half, half), half)
    other_half = pl.ds(pl.multiple_of((1 - core) * half, half), half)
    slab = pl.ds(pl.multiple_of(x * piece, piece), 3 * piece)
    mine = pl.ds(pl.multiple_of(x * 3 * piece, piece), piece)
    theirs = pl.ds(pl.multiple_of((1 - x) * 3 * piece, piece), piece)
    shared = pl.ds(piece, 2 * piece)
    spans = (pl.ds(0, D), pl.ds(D, parts.shape[2] - D))
    CORE, X, Y, UP, DOWN = range(5)
    everything = pl.ds(0, half)

    def remote(kind, h, number, source, target, where):
        return pltpu.make_async_remote_copy(
            src_ref=source, dst_ref=target, send_sem=send.at[kind, h, number],
            recv_sem=recv.at[kind, h, number], device_id=where, device_id_type=MESH)

    def load(b, h):
        return pltpu.make_async_copy(parts.at[b, my_half, spans[h]], held.at[b, everything, spans[h]], load_sem.at[h, b])

    def to_core(b, h):
        return remote(CORE, h, b, parts.at[b, other_half, spans[h]], from_core.at[b, everything, spans[h]], device(z, y, x, 1 - core))

    def to_x(b, h):
        return remote(X, h, b, held.at[b, theirs, spans[h]], from_x.at[b, pl.ds(0, piece), spans[h]], device(z, y, 1 - x, core))

    def to_y(zb, h):
        return remote(Y, h, zb, held.at[zb * 2 + 1 - y, slab, spans[h]], from_y.at[zb, pl.ds(0, 3 * piece), spans[h]], device(z, 1 - y, x, core))

    def to_above(zb, h):
        return remote(UP, h, zb, held.at[zb * 2 + y, slab, spans[h]], from_below.at[zb, pl.ds(0, 3 * piece), spans[h]], device(z + 1, y, x, core))

    def to_below(zb, h):
        return remote(DOWN, h, zb, held.at[zb * 2 + y, slab, spans[h]], from_above.at[zb, pl.ds(0, 3 * piece), spans[h]], device(z - 1, y, x, core))

    fixed = [pltpu.make_async_copy(acts_ref, acts, fixed_sem.at[0]), pltpu.make_async_copy(weighted_ref, weighted, fixed_sem.at[1])]
    ff = weighted.shape[1] // 2
    x_pieces, g_pieces = D // BLOCK, D // 512

    def x_load(k):
        return pltpu.make_async_copy(x_ref.at[:, pl.ds(k * BLOCK, BLOCK)], x_buf.at[k % 2], x_sem.at[k % 2])

    def g_load(k):
        return pltpu.make_async_copy(grads_ref.at[:, pl.ds(k * 512, 512)], g_buf.at[k % 2], g_sem.at[k % 2])

    def gu_store(k):
        rows = pl.ds(k * BLOCK, BLOCK)
        return [pltpu.make_async_copy(gu_buf.at[k % 2, u, j], (gate_out, up_out)[u].at[j, rows], gu_sem.at[k % 2, u, j])
                for u in range(2) for j in range(2)]

    def down_store(k):
        return [pltpu.make_async_copy(down_buf.at[k % 2, j], down_out.at[j, :, pl.ds(k * 512, 512)], down_sem.at[k % 2, j])
                for j in range(2)]

    def x_piece(k):
        if k == 0:
            fixed[0].wait()
        x_load(k).wait()
        if k >= 2:
            for copy in gu_store(k - 2):
                copy.wait()
        both = dot_tn(x_buf[k % 2], acts[...])
        for j in range(2):
            for u in range(2):
                gu_buf[k % 2, u, j] = both[:, (2 * j + u) * ff:(2 * j + u + 1) * ff]
        for copy in gu_store(k):
            copy.start()
        if k + 2 < x_pieces:
            x_load(k + 2).start()

    def g_piece(k):
        if k == 0:
            fixed[1].wait()
        g_load(k).wait()
        if k >= 2:
            for copy in down_store(k - 2):
                copy.wait()
        both = dot_tn(weighted[...], g_buf[k % 2])
        for j in range(2):
            down_buf[k % 2, j] = both[j * ff:(j + 1) * ff]
        for copy in down_store(k):
            copy.start()
        if k + 2 < g_pieces:
            g_load(k + 2).start()

    fillers = [functools.partial(x_piece, k) for k in range(x_pieces)]
    for k in range(g_pieces):
        fillers.insert(3 * k + 2, functools.partial(g_piece, k))

    greet(z, y, x, core)
    items = [(zb, h) for zb in order for h in (1, 0)]
    for k, (zb, h) in enumerate(items):
        for yb in (1 - y, y):
            load(zb * 2 + yb, h).start()
            to_core(zb * 2 + yb, h).start()
        if k == 1:
            for copy in fixed:
                copy.start()
            for j in range(2):
                x_load(j).start()
                g_load(j).start()

    def stage_core(zb, h, yb):
        b = zb * 2 + yb
        load(b, h).wait()
        to_core(b, h).wait_recv()
        sum_rows(held.at[b], from_core.at[b], spans[h], half)
        to_x(b, h).start()

    def stage_x(zb, h, yb):
        b = zb * 2 + yb
        to_x(b, h).wait_recv()
        sum_rows(held.at[b, mine], from_x.at[b], spans[h], piece)

    def stage_y(zb, h):
        stage_x(zb, h, 1 - y)
        to_y(zb, h).start()

    def climb(zb, h):
        @pl.when(z > 0)
        def _():
            to_above(zb, h).wait_recv()
            sum_rows(held.at[zb * 2 + y, slab], from_below.at[zb], spans[h], 3 * piece)
        to_above(zb, h).start()

    def descend(zb, h):
        @pl.when(z < 3)
        def _():
            to_below(zb, h).wait_recv()
            sum_rows(held.at[zb * 2 + y, slab], from_above.at[zb], spans[h], 3 * piece)
        to_below(zb, h).start()

    def stage_z(k):
        zb, h = items[k]
        to_y(zb, h).wait_recv()
        sum_rows(held.at[zb * 2 + y, slab], from_y.at[zb], spans[h], 3 * piece)
        rises = (z // 2 == 0) if k < 4 else (z % 2 == 0)
        pl.when(rises)(lambda: climb(zb, h))
        pl.when(jnp.logical_not(rises))(lambda: descend(zb, h))

    base = core * half
    out_mine = pl.ds(pl.multiple_of(base + x * 3 * piece, piece), piece)
    out_theirs = pl.ds(pl.multiple_of(base + (1 - x) * 3 * piece, piece), piece)
    out_shared = pl.ds(pl.multiple_of(base + piece, piece), 2 * piece)

    def at_end(number, h, source, target, where):
        return pltpu.make_async_remote_copy(
            src_ref=source, dst_ref=target, send_sem=end_send.at[h, number],
            recv_sem=end_recv.at[h, number], device_id=where, device_id_type=MESH)

    across, twin = device(z, y, 1 - x, core), device(z, y, x, 1 - core)
    end_sums = lambda h: at_end(0, h, held.at[me, shared, spans[h]], shared_in.at[pl.ds(0, 2 * piece), spans[h]], across)
    end_ready = lambda h, rows: at_end(1, h, held.at[me, mine, spans[h]], total.at[rows, spans[h]], across)
    end_twin = lambda h, rows: at_end(2, h, total.at[my_half, spans[h]], total.at[rows, spans[h]], twin)

    def own_sum(h):
        own = held.at[me]
        to_y(z, h).wait_recv()
        sum_rows(own.at[slab], from_y.at[z], spans[h], 3 * piece)

        @pl.when(z > 0)
        def _():
            to_above(z, h).wait_recv()
            sum_rows(own.at[slab], from_below.at[z], spans[h], 3 * piece)

        @pl.when(z < 3)
        def _():
            to_below(z, h).wait_recv()
            sum_rows(own.at[slab], from_above.at[z], spans[h], 3 * piece)
        end_sums(h).start()
        end_ready(h, out_mine).start()
        total[out_mine, spans[h]] = held[me, mine, spans[h]]

    def own_end(h):
        end_sums(h).wait_recv()
        sum_rows(held.at[me, shared], shared_in, spans[h], 2 * piece)
        total[out_shared, spans[h]] = held[me, shared, spans[h]]
        end_ready(h, out_theirs).wait_recv()
        end_twin(h, my_half).start()

    zb, h = items[0]
    stage_core(zb, h, 1 - y)
    stage_core(zb, h, y)
    for k, (zb, h) in enumerate(items):
        if k < 7:
            stage_core(*items[k + 1], 1 - y)
        stage_y(zb, h)
        if k < 7:
            stage_core(*items[k + 1], y)
        stage_x(zb, h, y)
        if 0 < k < 7:
            stage_z(k - 1)
        if k < 7:
            for fill in fillers[2 * k:2 * k + 2]:
                fill()
    for fill in fillers[14:]:
        fill()
    own_sum(1)
    own_sum(0)
    end_sums(1).wait_send()
    own_end(1)
    end_sums(0).wait_send()
    own_end(0)
    for h in (1, 0):
        end_twin(h, other_half).wait_recv()
        end_ready(h, out_mine).wait_send()
        end_twin(h, my_half).wait_send()
        for b in range(8):
            zb, yb = b // 2, b % 2
            to_core(b, h).wait_send()
            to_x(b, h).wait_send()
            if yb == 0:
                to_y(zb, h).wait_send()
                pl.when(zb > z)(lambda: to_above(zb, h).wait_send())
                pl.when(zb < z)(lambda: to_below(zb, h).wait_send())
    for k in (x_pieces - 2, x_pieces - 1):
        for copy in gu_store(k):
            copy.wait()
    for k in (g_pieces - 2, g_pieces - 1):
        for copy in down_store(k):
            copy.wait()


def sums_all(parts, x, acts, grads, weighted, number):
    _, rows, width = parts.shape
    T, D = x.shape
    ff = weighted.shape[1] // 2
    half, piece = rows // 2, rows // 8
    sd = jax.ShapeDtypeStruct
    dma = pltpu.SemaphoreType.DMA
    vm = pltpu.VMEM
    return pl.pallas_call(
        sums_kernel, in_specs=[ANY] * 5, out_specs=[VM, ANY, ANY, ANY],
        out_shape=[sd((rows, width), bf16), sd((2, D, ff), f32), sd((2, D, ff), f32), sd((2, ff, D), f32)],
        scratch_shapes=[
            vm((8, half, width), bf16), vm((8, half, width), bf16), vm((8, piece, width), bf16),
            vm((4, 3 * piece, width), bf16), vm((4, 3 * piece, width), bf16), vm((4, 3 * piece, width), bf16),
            vm((2 * piece, width), bf16),
            vm(acts.shape, bf16), vm(weighted.shape, bf16), vm((2, T, BLOCK), bf16), vm((2, T, 512), bf16),
            vm((2, 2, 2, BLOCK, ff), f32), vm((2, 2, ff, 512), f32),
            dma((2, 8)), dma((5, 2, 8)), dma((5, 2, 8)), dma((2, 3)), dma((2, 3)),
            dma((2,)), dma((2,)), dma((2,)), dma((2, 2, 2)), dma((2, 2)),
        ],
        compiler_params=pltpu.CompilerParams(collective_id=number, has_side_effects=True, vmem_limit_bytes=62 * 2**20),
    )(parts, x, acts, grads, weighted)


def backward_kernel(ga_ref, segc_ref, segr_ref, qg_ref, kg_ref, gains_small, gain_ref,
                    w_in, ctx_ref, q_in, k_in, v_in, qr_in, kr_in, cos_in, sin_in, wq_in, wk_in, wv_in, a_in, hidden_in, middle_in,
                    grad_ref, weights_ref, norm_ref, gains_out, wout_ref, small_out,
                    w_ref, q_ref, k_ref, v_ref, qr_ref, kr_ref, cos_ref, sin_ref, wq_ref, wk_ref, wv_ref, columns, hidden_ref, middle_ref,
                    raw_ref, g_own, g_all, dk, dv, terms, from_y, held_terms, from_below, from_above,
                    small_y, small_sum, small_z, raw_in, gathered, products, from_z, out_half, in_half, held, from_x, total, gains_own, gains_in, norm_in,
                    load, g_send, g_recv, f_send, f_recv, t_send, t_recv, s_send, s_recv, send, recv, w_send, w_recv,
                    pair_send, pair_recv, e_send, e_recv, n_send, n_recv):
    small_ref = gains_small
    z, y, x, core = place()
    me = z * 2 + y
    order = far_first(z)
    span = 4 * HD
    across, twin, corner = device(z, y, 1 - x, core), device(z, y, x, 1 - core), device(z, y, 1 - x, 1 - core)
    partner = device(z, 1 - y, x, core)

    loads = [pltpu.make_async_copy(source, target, load.at[k]) for k, (source, target) in enumerate((
        (w_in, w_ref), (q_in, q_ref), (k_in, k_ref), (v_in, v_ref), (qr_in, qr_ref), (kr_in, kr_ref), (cos_in, cos_ref),
        (sin_in, sin_ref), (wq_in, wq_ref), (wk_in, wk_ref), (wv_in, wv_ref), (hidden_in, hidden_ref), (middle_in, middle_ref)))]

    def column_load(n):
        block = pl.ds(pl.multiple_of((n * 2 + y) * BLOCK, BLOCK), BLOCK)
        return pltpu.make_async_copy(a_in.at[:, block], columns.at[n], load.at[13 + n])

    for copy in loads:
        copy.start()
    for n in range(4):
        column_load(n).start()
    greet_peers(z, y, x, core, (across, twin, corner))

    def remote(source, target, ssem, rsem, where):
        return pltpu.make_async_remote_copy(
            src_ref=source, dst_ref=target, send_sem=ssem, recv_sem=rsem, device_id=where, device_id_type=MESH)

    def when_away(n, act):
        pl.when(z != n)(act)

    loads[0].wait()
    g_context = dot_nt(ga_ref[...], w_ref[...]).astype(bf16)
    for n in range(4):
        g_own[n] = g_context[:, n * HD:(n + 1) * HD]

    def g_to(n):
        return remote(g_own.at[n], g_all.at[me], g_send.at[n], g_recv.at[z], device(n, y, x, core))

    def g_from(n):
        return remote(g_own.at[n], g_all.at[n * 2 + y], g_send.at[n], g_recv.at[n], device(n, y, x, core))

    def g_over(n):
        return remote(g_all.at[n * 2 + y], g_all.at[n * 2 + y], f_send.at[n], f_recv.at[n], partner)

    def g_over_in(n):
        return remote(g_all.at[n * 2 + 1 - y], g_all.at[n * 2 + 1 - y], f_send.at[n], f_recv.at[n], partner)

    for n in range(4):
        when_away(n, lambda: g_to(n).start())
    g_all[me] = g_own[z]
    g_over(z).start()

    quarter = small_ref.shape[1] // 4

    def lanes(cx, cc):
        return pl.ds(pl.multiple_of((cx * 2 + cc) * quarter, quarter), quarter)

    own_lanes = lanes(x, core)
    small_pair = remote(small_ref.at[:, own_lanes], small_y, s_send.at[0], s_recv.at[0], partner)
    small_pair.start()

    def small_along(n):
        return remote(small_sum, small_z.at[z], s_send.at[1 + n], s_recv.at[1 + z], device(n, y, x, core))

    def small_arriving(n):
        return remote(small_sum, small_z.at[n], s_send.at[1 + n], s_recv.at[1 + n], device(n, y, x, core))

    fans = (across, twin, corner)
    fan_lanes = (lanes(1 - x, core), lanes(x, 1 - core), lanes(1 - x, 1 - core))

    def small_spread(i):
        return remote(small_out.at[:, own_lanes], small_out.at[:, own_lanes], s_send.at[5 + i], s_recv.at[5 + i], fans[i])

    def small_spread_in(i):
        return remote(small_out.at[:, own_lanes], small_out.at[:, fan_lanes[i]], s_send.at[5 + i], s_recv.at[5 + i], fans[i])

    for b in range(8):
        terms[b] = dot_tn(ga_ref[:, b * BLOCK:(b + 1) * BLOCK], ctx_ref[...]).astype(bf16)

    def term_pair(n):
        return remote(terms.at[n * 2 + 1 - y], from_y.at[n], t_send.at[0, n], t_recv.at[0, n], partner)

    def term_up(n):
        return remote(held_terms.at[n], from_below.at[n], t_send.at[1, n], t_recv.at[1, n], device(z + 1, y, x, core))

    def term_down(n):
        return remote(held_terms.at[n], from_above.at[n], t_send.at[2, n], t_recv.at[2, n], device(z - 1, y, x, core))

    def paired(n):
        return terms[n * 2 + y].astype(f32) + from_y[n].astype(f32)

    def term_stage(k):
        n = order[k]
        term_pair(n).wait_recv()
        held_terms[n] = paired(n).astype(bf16)
        rises = (z // 2 == 0) if k < 2 else (z % 2 == 0)

        @pl.when(rises)
        def _():
            @pl.when(z > 0)
            def _():
                term_up(n).wait_recv()
                held_terms[n] = (paired(n) + from_below[n].astype(f32)).astype(bf16)
            term_up(n).start()

        @pl.when(jnp.logical_not(rises))
        def _():
            @pl.when(z < 3)
            def _():
                term_down(n).wait_recv()
                held_terms[n] = (paired(n) + from_above[n].astype(f32)).astype(bf16)
            term_down(n).start()

    for n in range(4):
        when_away(n, lambda: g_from(n).wait_recv())
        when_away(n, lambda: g_over(n).start())
    for n in order:
        term_pair(n).start()

    def rows_to(n):
        return remote(raw_ref.at[n * 2 + y], raw_in.at[z], send.at[n], recv.at[z], device(n, y, x, core))

    def rows_from(n):
        return remote(raw_ref.at[n * 2 + y], raw_in.at[n], send.at[n], recv.at[n], device(n, y, x, core))

    gain_sums = [jnp.zeros((1, HD), f32), jnp.zeros((1, HD), f32)]

    def back(turned, b, raw_in, gain, which):
        rows = slice(b * BLOCK, (b + 1) * BLOCK)
        g = turned * cos_ref[rows] - pltpu.roll(turned, HD // 2, 1) * sin_ref[rows]
        raw = raw_in[rows]
        factor = norm_factor(raw)
        n = raw * factor
        gain_sums[which] = gain_sums[which] + jnp.sum(g * n, 0, keepdims=True)
        g = g * gain[...]
        return (factor * (g - n * jnp.mean(g * n, -1, keepdims=True))).astype(bf16)

    for copy in loads[1:8]:
        copy.wait()
    for b in range(7, -1, -1):
        keys = (b + 1) * BLOCK
        rows = slice(b * BLOCK, keys)
        pl.when(y != b % 2)(lambda: g_over_in(b // 2).wait_recv())
        q = q_ref[rows]
        g = g_all[b]
        probs = masked_probs(b, q, k_ref, segc_ref, segr_ref)
        gv = dot_tn(probs.astype(bf16), g)
        gp = dot_nt(g, v_ref[:keys])
        gs = (probs * (gp - jnp.sum(gp * probs, -1, keepdims=True))).astype(bf16)
        gk = dot_tn(gs, q)
        if b == 7:
            dv[...] = gv
            dk[...] = gk
        else:
            dv[:keys] += gv
            dk[:keys] += gk
        raw_ref[b, :, :HD] = back(dot(gs, k_ref[:keys]) * (HD ** -0.5), b, qr_ref, qg_ref, 0)
        raw_ref[b, :, HD:2 * HD] = back(dk[rows] * (HD ** -0.5), b, kr_ref, kg_ref, 1)
        raw_ref[b, :, 2 * HD:] = dv[rows].astype(bf16)

        @pl.when(y == b % 2)
        def _():
            when_away(b // 2, lambda: rows_to(b // 2).start())

        if b == 5:
            small_pair.wait_recv()
            small_sum[...] = small_ref[:, own_lanes] + small_y[...]
            for n in range(4):
                when_away(n, lambda: small_along(n).start())
            small_z[z] = small_sum[...]
        if b == 1:
            for n in range(4):
                when_away(n, lambda: small_arriving(n).wait_recv())
            small_out[:, own_lanes] = (small_z[0] + small_z[1]) + (small_z[2] + small_z[3])
            for i in range(3):
                small_spread(i).start()

    gains_own[0:1] = gain_sums[0]
    gains_own[1:2] = gain_sums[1]

    def gains_to(n):
        return remote(gains_own, gains_in.at[z], e_send.at[n], e_recv.at[z], device(n, y, x, core))

    def gains_from(n):
        return remote(gains_own, gains_in.at[n], e_send.at[n], e_recv.at[n], device(n, y, x, core))

    for n in range(4):
        when_away(n, lambda: gains_to(n).start())
    gains_in[z] = gains_own[...]
    raw_in[z] = raw_ref[me]

    def products_to(n):
        return remote(products.at[n], from_z.at[z], w_send.at[n], w_recv.at[z], device(n, y, x, core))

    def products_from(n):
        return remote(products.at[n], from_z.at[n], w_send.at[n], w_recv.at[n], device(n, y, x, core))

    raw_all = raw_ref[...].reshape(8 * BLOCK, 3 * HD)
    for i, n in enumerate(order):
        column_load(n).wait()
        product = dot_tn(columns[n], raw_all).astype(bf16)
        if i < 3:
            products[n] = product
            products_to(n).start()
        else:
            from_z[z] = product

    for copy in loads[8:]:
        copy.wait()
    term_stage(0)
    for n in range(4):
        when_away(n, lambda: rows_from(n).wait_recv())
        for g in range(3):
            gathered[:, g * span + n * HD:g * span + (n + 1) * HD] = raw_in[n, :, g * HD:(g + 1) * HD]

    rows = total.shape[0]
    half = rows // 2
    chunk = half // 2
    my_half = core * half
    other_half = (1 - core) * half
    piece = lambda c: pl.ds(c * chunk, chunk)
    at = lambda base, c: pl.ds(pl.multiple_of(base + c * chunk, chunk), chunk)

    def pair(kind, c, source, target, where):
        return remote(source, target, pair_send.at[kind, c], pair_recv.at[kind, c], where)

    def multiply(part):
        return (dot_nt(part[:, :span], wq_ref[...]) + dot_nt(part[:, span:2 * span], wk_ref[...])
                + dot_nt(part[:, 2 * span:], wv_ref[...]))

    first = [pair(0, c, out_half.at[piece(c)], in_half.at[piece(c)], twin) for c in range(2)]
    second = [pair(1, c, held.at[piece(c)], from_x.at[piece(c)], across) for c in range(2)]
    third = [pair(2, c, total.at[at(my_half, c)], total.at[at(my_half, c)], twin) for c in range(2)]
    for c in range(2):
        out_half[piece(c)] = multiply(gathered[at(other_half, c)]).astype(bf16)
        first[c].start()
    for c in range(2):
        kept = multiply(gathered[at(my_half, c)])
        first[c].wait_recv()
        held[piece(c)] = (kept + in_half[piece(c)].astype(f32)).astype(bf16)
        second[c].start()

    term_stage(1)
    term_stage(2)
    term_pair(z).wait_recv()
    wout_ref[...] = paired(z)

    @pl.when(z > 0)
    def _():
        term_up(z).wait_recv()
        wout_ref[...] += from_below[z].astype(f32)

    @pl.when(z < 3)
    def _():
        term_down(z).wait_recv()
        wout_ref[...] += from_above[z].astype(f32)

    for n in range(4):
        when_away(n, lambda: gains_from(n).wait_recv())
        gains_out[:, n * HD:(n + 1) * HD] = gains_in[n]
    for c in range(2):
        second[c].wait_recv()
        total[at(my_half, c)] = (held[piece(c)].astype(f32) + from_x[piece(c)].astype(f32)).astype(bf16)
        third[c].start()

    step = 32

    def norm_rows(base):
        def body(i, norm_part):
            part = pl.ds(pl.multiple_of(base + i * step, step), step)
            e = total[part].astype(f32)
            v = hidden_ref[part].astype(f32)
            factor = norm_factor(v)
            n = v * factor
            norm_part = norm_part + jnp.sum(e * n, 0, keepdims=True)
            e = e * gain_ref[...]
            grad_ref[part] = middle_ref[part] + factor * (e - n * jnp.mean(e * n, -1, keepdims=True))
            return norm_part
        return body

    nothing = jnp.zeros((1, total.shape[1]), f32)
    mine_part = lax.fori_loop(0, half // step, norm_rows(my_half), nothing)
    for c in range(2):
        pair(2, c, total.at[at(my_half, c)], total.at[at(other_half, c)], twin).wait_recv()
    other_part = lax.fori_loop(0, half // step, norm_rows(other_half), nothing)
    norm_part = mine_part + other_part
    for t in range(norm_in.shape[1]):
        norm_in[me, t:t + 1] = norm_part[:, t * 128:(t + 1) * 128]

    def norm_to(b):
        return remote(norm_in.at[me], norm_in.at[me], n_send.at[b], n_recv.at[me], device(b // 2, b % 2, x, core))

    def norm_from(b):
        return remote(norm_in.at[b], norm_in.at[b], n_send.at[b], n_recv.at[b], device(b // 2, b % 2, x, core))

    for b in range(8):
        pl.when(me != b)(lambda: norm_to(b).start())
    for n in range(4):
        when_away(n, lambda: products_from(n).wait_recv())
    for n in range(4):
        for g in range(3):
            weights_ref[g, :, n * HD:(n + 1) * HD] = from_z[n, :, g * HD:(g + 1) * HD].astype(f32)
    for b in range(8):
        pl.when(me != b)(lambda: norm_from(b).wait_recv())
    sums = [norm_in[b] for b in range(8)]
    norm_sum = ((sums[0] + sums[1]) + (sums[2] + sums[3])) + ((sums[4] + sums[5]) + (sums[6] + sums[7]))
    for t in range(norm_in.shape[1]):
        norm_ref[:, t * 128:(t + 1) * 128] = norm_sum[t:t + 1]

    for i in range(3):
        small_spread_in(i).wait_recv()
        small_spread(i).wait_send()
    small_pair.wait_send()
    for c in range(2):
        first[c].wait_send()
        second[c].wait_send()
        third[c].wait_send()
    for b in range(8):
        pl.when(me != b)(lambda: norm_to(b).wait_send())
    for n in range(4):
        when_away(n, lambda: g_to(n).wait_send())
        g_over(n).wait_send()
        term_pair(n).wait_send()
        pl.when(n > z)(lambda: term_up(n).wait_send())
        pl.when(n < z)(lambda: term_down(n).wait_send())
        when_away(n, lambda: small_along(n).wait_send())
        when_away(n, lambda: rows_to(n).wait_send())
        when_away(n, lambda: products_to(n).wait_send())
        when_away(n, lambda: gains_to(n).wait_send())


def backward_all(ga, segc, segr, qg, kg, small, gain, w, ctx, q, k, v, qr, kr, cosine, sine, wq, wk, wv, a, hidden, middle, number):
    T, D = a.shape
    rows, half = BLOCK, BLOCK // 2
    span = 4 * HD
    S = small.shape[0]
    sd = jax.ShapeDtypeStruct
    dma = pltpu.SemaphoreType.DMA
    vm = pltpu.VMEM
    like = lambda m: vm(m.shape, m.dtype)
    return pl.pallas_call(
        backward_kernel, in_specs=[VM] * 7 + [ANY, VM] + [ANY] * 13, out_specs=[VM] * 6,
        out_shape=[sd((rows, D), f32), sd((3, BLOCK, span), f32), sd((1, D), f32), sd((2, span), f32),
                   sd((BLOCK, span), f32), sd((S, D), f32)],
        scratch_shapes=[like(m) for m in (w, q, k, v, qr, kr, cosine, sine, wq, wk, wv)] + [
            vm((4, T, BLOCK), bf16), like(hidden), like(middle),
            vm((8, BLOCK, 3 * HD), bf16), vm((4, BLOCK, HD), bf16), vm((8, BLOCK, HD), bf16), vm((T, HD), f32), vm((T, HD), f32),
            vm((8, BLOCK, span), bf16)] + [vm((4, BLOCK, span), bf16)] * 4 + [
            vm((S, D // 4), f32), vm((S, D // 4), f32), vm((4, S, D // 4), f32),
            vm((4, BLOCK, 3 * HD), bf16), vm((rows, 3 * span), bf16), vm((4, BLOCK, 3 * HD), bf16), vm((4, BLOCK, 3 * HD), bf16)] + [vm((half, D), bf16)] * 4 + [
            vm((rows, D), bf16), vm((2, HD), f32), vm((4, 2, HD), f32), vm((8, D // 128, 128), f32),
            dma((17,)), dma((4,)), dma((4,)), dma((4,)), dma((4,)), dma((3, 4)), dma((3, 4)), dma((8,)), dma((8,)),
            dma((4,)), dma((4,)), dma((4,)), dma((4,)), dma((3, 2)), dma((3, 2)), dma((4,)), dma((4,)), dma((8,)), dma((8,)),
        ],
        compiler_params=pltpu.CompilerParams(collective_id=number, has_side_effects=True, vmem_limit_bytes=60 * 2**20),
    )(ga, segc, segr, qg, kg, small, gain, w, ctx, q, k, v, qr, kr, cosine, sine, wq, wk, wv, a, hidden, middle)


def on_device(
    hidden_in,
    norm1_gain,
    w_query,
    w_key,
    w_value,
    w_out,
    query_gain,
    key_gain,
    norm2_gain,
    w_router,
    w_gate,
    w_up,
    w_down,
    routes,
    segments,
    cotangent,
):
    seq_len, width = hidden_in.shape
    local_width = w_query.shape[1]
    head_count = local_width // HEAD_DIM
    expert_devs = lax.axis_size("expert")
    local_experts = w_gate.shape[0]
    expert_total = w_router.shape[1]
    capacity = 2 * seq_len * TOP // expert_total
    slab_rows = local_experts * capacity
    my_index = lax.axis_index("expert")
    group = SEQ // seq_len
    rank = my_index % group
    f32 = jnp.float32
    bf16 = jnp.bfloat16

    def split_heads(values):
        return values.reshape(seq_len, head_count, HEAD_DIM)

    inputs = hidden_in.astype(f32)
    inverse_attn = inverse_rms(inputs)
    normed_attn = inputs * inverse_attn
    attn_input = (normed_attn * norm1_gain).astype(bf16)
    q_raw = split_heads(jnp.dot(attn_input, w_query, preferred_element_type=f32))
    k_raw = split_heads(jnp.dot(attn_input, w_key, preferred_element_type=f32))
    v_heads = split_heads(jnp.dot(attn_input, w_value, preferred_element_type=f32).astype(bf16))
    q_gains = query_gain.reshape(head_count, HEAD_DIM)
    k_gains = key_gain.reshape(head_count, HEAD_DIM)
    q_inverse = inverse_rms(q_raw)
    q_normed = q_raw * q_inverse
    k_inverse = inverse_rms(k_raw)
    k_normed = k_raw * k_inverse
    local_places = lax.iota(jnp.int32, seq_len)
    query_places = rank * seq_len + local_places
    cosine, sine_part = rope_tables(query_places.astype(f32), HEAD_DIM // 2)
    queries = rotate(q_normed * q_gains, cosine, sine_part, 1.0).astype(bf16)
    key_rot = rotate(k_normed * k_gains, cosine, sine_part, 1.0).astype(bf16)
    score_scale = HEAD_DIM ** (-0.5)
    keys_values = jnp.stack([key_rot, v_heads])
    pieces = [keys_values]
    for offset in range(1, group):
        keys_values = from_behind(keys_values, "expert", 1)
        pieces.append(keys_values)
    stacked = jnp.stack(pieces, 1).reshape(2, group * seq_len, head_count, HEAD_DIM)
    keys_all = stacked[0]
    values_all = stacked[1]
    query_segs = lax.dynamic_slice_in_dim(segments, my_index * seq_len, seq_len, 0)
    key_segs = jnp.concatenate(
        [
            lax.dynamic_slice_in_dim(
                segments, jnp.maximum(my_index - offset, 0) * seq_len, seq_len, 0
            )
            for offset in range(group)
        ],
        0,
    )
    offsets = lax.iota(jnp.int32, group)
    key_places = ((rank - offsets)[:, None] * seq_len + local_places[None, :]).reshape(-1)
    key_valid = jnp.repeat(rank - offsets >= 0, seq_len)
    allowed = (
        key_valid[None, :]
        & (query_places[:, None] >= key_places[None, :])
        & (query_segs[:, None] == key_segs[None, :])
    )

    def scores_of():
        raw_scores = (
            jnp.einsum("thd,shd->hts", queries, keys_all, preferred_element_type=f32) * score_scale
        )
        return jnp.where(allowed[None], raw_scores, MASKED)

    scores = scores_of()
    row_max = jnp.max(scores, -1, keepdims=True)
    raised = jnp.exp(scores - row_max)
    exp_total = jnp.sum(raised, -1, keepdims=True)
    log_total = row_max + jnp.log(exp_total)
    attn_probs = (raised / exp_total).astype(bf16)
    context = (
        jnp.einsum("hts,shd->thd", attn_probs, values_all, preferred_element_type=f32)
        .reshape(seq_len, local_width)
        .astype(bf16)
    )
    attn_part = jnp.dot(context, w_out, preferred_element_type=f32)
    middle = inputs + lax.psum(attn_part, "head")
    inverse_moe = inverse_rms(middle)
    normed_moe = middle * inverse_moe
    moe_input = (normed_moe * norm2_gain).astype(bf16)
    logits = jnp.dot(moe_input, w_router, preferred_element_type=f32)
    chosen = jnp.take_along_axis(logits, routes, 1)
    raised_gate = jnp.exp(chosen - jnp.max(chosen, -1, keepdims=True))
    gate_weights = raised_gate / jnp.sum(raised_gate, -1, keepdims=True)
    catalog = lax.iota(jnp.int32, expert_total)
    route_hot = (routes[:, :, None] == catalog).astype(jnp.int32)
    token_hot = jnp.sum(route_hot, 1, dtype=jnp.int32)
    earlier = jnp.cumsum(token_hot, 0, dtype=jnp.int32) - token_hot
    position = routes * capacity + jnp.take_along_axis(earlier, routes, 1)
    flat_pos = position.reshape(-1)
    owners = (
        jnp.full((expert_total * capacity,), seq_len, jnp.int32)
        .at[flat_pos]
        .set(jnp.repeat(lax.iota(jnp.int32, seq_len), TOP))
    )
    padded = jnp.concatenate([moe_input, jnp.zeros((1, width), bf16)], 0)
    outgoing = padded[owners].reshape(expert_devs, slab_rows, width)
    arrived = lax.all_to_all(outgoing, "expert", split_axis=0, concat_axis=0, tiled=True)
    rows_in = arrived.reshape(expert_devs, local_experts, capacity, width)
    gate_act = jnp.einsum("sjcd,jdf->sjcf", rows_in, w_gate, preferred_element_type=f32)
    up_act = jnp.einsum("sjcd,jdf->sjcf", rows_in, w_up, preferred_element_type=f32)
    hidden = (jax.nn.silu(gate_act) * up_act).astype(bf16)
    partial_out = jnp.einsum("sjcf,jfd->sjcd", hidden, w_down, preferred_element_type=f32).reshape(
        expert_devs, slab_rows, width
    )
    rows_out = (
        lax.psum_scatter(partial_out.astype(jnp.bfloat16), "head", scatter_dimension=2, tiled=True)
        .astype(jnp.float32)
        .astype(bf16)
    )
    leaving = lax.all_gather(rows_out, "head", axis=2, tiled=True)
    returned = lax.all_to_all(leaving, "expert", split_axis=0, concat_axis=0, tiled=True)
    picked = returned.reshape(expert_total * capacity, width)[position]
    moe_out = jnp.einsum("tk,tkd->td", gate_weights, picked, preferred_element_type=f32)
    output = (middle + moe_out).astype(bf16)
    grad_final = cotangent.astype(f32)
    grad_gates = jnp.einsum("td,tkd->tk", grad_final, picked, preferred_element_type=f32)
    grad_chosen = gate_weights * (
        grad_gates - jnp.sum(grad_gates * gate_weights, -1, keepdims=True)
    )
    grad_logits = jnp.einsum("tk,tke->te", grad_chosen, route_hot.astype(f32)).astype(bf16)
    grad_router = jnp.dot(moe_input.T, grad_logits, preferred_element_type=f32)
    grad_moe_input = jnp.dot(grad_logits, w_router.T, preferred_element_type=f32)
    grad_expert_out = (gate_weights[:, :, None] * grad_final[:, None, :]).astype(bf16)
    grad_slab = (
        jnp.zeros((expert_total * capacity, width), bf16)
        .at[flat_pos]
        .set(grad_expert_out.reshape(seq_len * TOP, width))
    )
    grad_slab = grad_slab.reshape(expert_devs, slab_rows, width)
    grad_arrived = lax.all_to_all(grad_slab, "expert", split_axis=0, concat_axis=0, tiled=True)
    grad_rows_out = grad_arrived.reshape(expert_devs, local_experts, capacity, width)
    grad_hidden = jnp.einsum("sjcd,jfd->sjcf", grad_rows_out, w_down, preferred_element_type=f32)
    grad_down = jnp.einsum("sjcf,sjcd->jfd", hidden, grad_rows_out, preferred_element_type=f32)
    sigmoid = jax.nn.sigmoid(gate_act)
    grad_up_act = (grad_hidden * gate_act * sigmoid).astype(bf16)
    grad_gate_act = (grad_hidden * up_act * sigmoid * (1.0 + gate_act * (1.0 - sigmoid))).astype(
        bf16
    )
    grad_gate = jnp.einsum("sjcd,sjcf->jdf", rows_in, grad_gate_act, preferred_element_type=f32)
    grad_up = jnp.einsum("sjcd,sjcf->jdf", rows_in, grad_up_act, preferred_element_type=f32)
    grad_rows_in = jnp.einsum("sjcf,jdf->sjcd", grad_gate_act, w_gate, preferred_element_type=f32)
    grad_rows_in = grad_rows_in + jnp.einsum(
        "sjcf,jdf->sjcd", grad_up_act, w_up, preferred_element_type=f32
    )
    grad_back = (
        lax.psum_scatter(
            grad_rows_in.reshape(expert_devs, slab_rows, width).astype(jnp.bfloat16),
            "head",
            scatter_dimension=2,
            tiled=True,
        )
        .astype(jnp.float32)
        .astype(bf16)
    )
    leaving_grad = lax.all_gather(grad_back, "head", axis=2, tiled=True)
    grad_home = lax.all_to_all(leaving_grad, "expert", split_axis=0, concat_axis=0, tiled=True)
    grad_moe_input = grad_moe_input + jnp.sum(
        grad_home.reshape(expert_total * capacity, width)[position], 1, dtype=f32
    )
    grad_norm2 = jnp.sum(grad_moe_input * normed_moe, 0)
    grad_middle = grad_final + norm_back(grad_moe_input * norm2_gain, normed_moe, inverse_moe)
    grad_attn = grad_middle.astype(bf16)
    grad_out_turned = jnp.dot(grad_attn.T, context, preferred_element_type=f32)
    grad_context = split_heads(jnp.dot(grad_attn, w_out.T, preferred_element_type=f32).astype(bf16))
    attn_full = jnp.exp(scores_of() - log_total)
    attn_low = attn_full.astype(bf16)
    grad_values_all = jnp.einsum("hts,thd->shd", attn_low, grad_context, preferred_element_type=f32)
    grad_probs = jnp.einsum("thd,shd->hts", grad_context, values_all, preferred_element_type=f32)
    grad_scores = (
        attn_full * (grad_probs - jnp.sum(grad_probs * attn_full, -1, keepdims=True))
    ).astype(bf16)
    grad_queries = (
        jnp.einsum("hts,shd->thd", grad_scores, keys_all, preferred_element_type=f32) * score_scale
    )
    grad_keys_all = (
        jnp.einsum("hts,thd->shd", grad_scores, queries, preferred_element_type=f32) * score_scale
    )
    kv_terms = jnp.stack([grad_keys_all, grad_values_all]).reshape(
        2, group, seq_len, head_count, HEAD_DIM
    )
    kv_total = kv_terms[:, 0]
    for offset in range(1, group):
        kv_total = kv_total + from_behind(
            kv_terms[:, offset].astype(jnp.bfloat16), "expert", -offset
        ).astype(jnp.float32)
    grad_keys = kv_total[0]
    grad_values = kv_total[1]
    grad_q_normed = rotate(grad_queries, cosine, sine_part, -1.0)
    grad_k_normed = rotate(grad_keys, cosine, sine_part, -1.0)
    grad_query_gain = jnp.sum(grad_q_normed * q_normed, 0).reshape(local_width)
    grad_key_gain = jnp.sum(grad_k_normed * k_normed, 0).reshape(local_width)
    grad_q_raw = (
        norm_back(grad_q_normed * q_gains, q_normed, q_inverse)
        .reshape(seq_len, local_width)
        .astype(bf16)
    )
    grad_k_raw = (
        norm_back(grad_k_normed * k_gains, k_normed, k_inverse)
        .reshape(seq_len, local_width)
        .astype(bf16)
    )
    grad_v_raw = grad_values.reshape(seq_len, local_width).astype(bf16)
    grad_query = jnp.dot(attn_input.T, grad_q_raw, preferred_element_type=f32)
    grad_key = jnp.dot(attn_input.T, grad_k_raw, preferred_element_type=f32)
    grad_value = jnp.dot(attn_input.T, grad_v_raw, preferred_element_type=f32)
    input_part = jnp.dot(grad_q_raw, w_query.T, preferred_element_type=f32)
    input_part = input_part + jnp.dot(grad_k_raw, w_key.T, preferred_element_type=f32)
    input_part = input_part + jnp.dot(grad_v_raw, w_value.T, preferred_element_type=f32)
    grad_attn_input = lax.psum(input_part.astype(jnp.bfloat16), "head").astype(jnp.float32)
    grad_norm1 = jnp.sum(grad_attn_input * normed_attn, 0)
    grad_input = grad_middle + norm_back(grad_attn_input * norm1_gain, normed_attn, inverse_attn)
    grad_query, grad_key, grad_value, grad_out_turned = (
        lax.psum_scatter(
            grad_query.astype(jnp.bfloat16), "expert", scatter_dimension=0, tiled=True
        ).astype(jnp.float32),
        lax.psum_scatter(
            grad_key.astype(jnp.bfloat16), "expert", scatter_dimension=0, tiled=True
        ).astype(jnp.float32),
        lax.psum_scatter(
            grad_value.astype(jnp.bfloat16), "expert", scatter_dimension=0, tiled=True
        ).astype(jnp.float32),
        lax.psum_scatter(
            grad_out_turned.astype(jnp.bfloat16), "expert", scatter_dimension=0, tiled=True
        ).astype(jnp.float32),
    )
    grad_router, grad_norm1, grad_norm2, grad_query_gain, grad_key_gain = (
        lax.psum(grad_router.astype(jnp.bfloat16), "expert").astype(jnp.float32),
        lax.psum(grad_norm1.astype(jnp.bfloat16), "expert").astype(jnp.float32),
        lax.psum(grad_norm2.astype(jnp.bfloat16), "expert").astype(jnp.float32),
        lax.psum(grad_query_gain.astype(jnp.bfloat16), "expert").astype(jnp.float32),
        lax.psum(grad_key_gain.astype(jnp.bfloat16), "expert").astype(jnp.float32),
    )
    return (
        output,
        grad_input,
        grad_norm1,
        grad_query,
        grad_key,
        grad_value,
        grad_out_turned.T,
        grad_query_gain,
        grad_key_gain,
        grad_norm2,
        grad_router,
        grad_gate,
        grad_up,
        grad_down,
    )


def full_tables(tokens):
    half_dim = HEAD_DIM // 2
    fine_cos, fine_sin = rope_tables(lax.iota(jnp.int32, 64).astype(f32), half_dim)
    coarse = (64 * lax.iota(jnp.int32, tokens // 64)).astype(f32)
    coarse_cos, coarse_sin = rope_tables(coarse, half_dim)
    fine_cos, fine_sin = fine_cos.reshape(1, 64, half_dim), fine_sin.reshape(1, 64, half_dim)
    cosine = (coarse_cos * fine_cos - coarse_sin * fine_sin).reshape(tokens, half_dim)
    sine = (coarse_sin * fine_cos + coarse_cos * fine_sin).reshape(tokens, half_dim)
    return jnp.concatenate([cosine, cosine], 1), jnp.concatenate([-sine, sine], 1)


def dense_layer(
    hidden_in, norm1_gain, w_query, w_key, w_value, w_out, query_gain, key_gain, norm2_gain, w_router,
    w_gate, w_up, w_down, routes, segments, cotangent,
):
    rows, width = hidden_in.shape
    experts = w_router.shape[1]
    devices = lax.axis_size("expert")
    tokens = devices * rows
    my_index = lax.axis_index("expert")
    head = my_index // 2

    def own_head(v):
        return lax.dynamic_slice_in_dim(v, head * HEAD_DIM, HEAD_DIM, v.ndim - 1)

    weights = jnp.concatenate([own_head(w_query), own_head(w_key), own_head(w_value)], 1)
    q_gain, k_gain = own_head(query_gain)[None], own_head(key_gain)[None]
    cosine, sine = full_tables(tokens)
    attn_all, queries, keys, values, q_raw, k_raw = project_all(
        hidden_in, norm1_gain[None], weights, q_gain, k_gain, cosine, sine, 1
    )
    segc, segr = segments[:, None], segments[None]
    own_mask = jnp.sum((routes[:, :, None] == lax.iota(jnp.int32, experts)).astype(f32), 1)
    sent = jnp.concatenate([cotangent, jnp.pad(own_mask.astype(bf16), ((0, 0), (0, 128 - experts)))], 1)
    attn_out, own_context, grads_all = attend_all(
        sent, queries, keys, values, segc, segr, w_out, 2
    )

    inputs = hidden_in.astype(f32)
    middle = inputs + attn_out.astype(f32)
    inverse_moe = inverse_rms(middle)
    normed_moe = middle * inverse_moe
    moe_input = (normed_moe * norm2_gain).astype(bf16)
    everyone, weighted, grad_acts, parts = experts_all(
        moe_input, grads_all, w_router, w_gate, w_up, w_down, 3
    )
    total, grad_gate, grad_up, grad_down = sums_all(
        parts.reshape(devices, rows, 2 * width + 128), everyone, grad_acts, grads_all, weighted, 4
    )
    output = (middle + total[:, :width].astype(f32)).astype(bf16)
    grad_final = cotangent.astype(f32)
    tail = total[:, 2 * width :].astype(f32)
    grad_gates = tail[:, :experts] + tail[:, experts : 2 * experts]
    logits = jnp.where(
        own_mask > 0, jnp.dot(moe_input, w_router, preferred_element_type=f32), -jnp.inf
    )
    raised_gate = jnp.exp(logits - jnp.max(logits, -1, keepdims=True))
    gate_weights = raised_gate / jnp.sum(raised_gate, -1, keepdims=True)
    grad_logits = (
        gate_weights * (grad_gates - jnp.sum(grad_gates * gate_weights, -1, keepdims=True))
    ).astype(bf16)
    grad_moe_input = jnp.dot(grad_logits, w_router.T, preferred_element_type=f32)
    grad_moe_input = grad_moe_input + total[:, width : 2 * width].astype(f32)
    grad_middle = grad_final + norm_back(grad_moe_input * norm2_gain, normed_moe, inverse_moe)
    small = jnp.concatenate(
        [
            lax.dot_general(grad_logits, moe_input, (((0,), (0,)), ((), ())), preferred_element_type=f32),
            jnp.sum(grad_moe_input * normed_moe, 0, keepdims=True),
            jnp.zeros((7, width), f32),
        ],
        0,
    )

    grad_input, grad_qkv, grad_norm1, gains, grad_w_out, small = backward_all(
        grad_middle.astype(bf16), segc, segr, q_gain, k_gain, small, norm1_gain[None], w_out, own_context,
        queries, keys, values, q_raw, k_raw, cosine, sine, w_query, w_key, w_value, attn_all, hidden_in, grad_middle, 5,
    )
    return (
        output,
        grad_input,
        grad_norm1[0],
        grad_qkv[0],
        grad_qkv[1],
        grad_qkv[2],
        grad_w_out.T,
        gains[0],
        gains[1],
        small[experts],
        small[:experts].T,
        grad_gate,
        grad_up,
        grad_down,
    )


def layer(*arrays):
    rows, experts = arrays[0].shape[0], arrays[9].shape[1]
    whole = 2 * rows * TOP // experts >= rows and rows * lax.axis_size("expert") == SEQ
    grid = (lax.axis_size("expert"), lax.axis_size("head")) == (8, 4)
    return dense_layer(*arrays) if whole and grid else on_device(*arrays)


def solution(mesh):
    return jax.shard_map(
        layer,
        mesh=mesh,
        in_specs=(
            P("expert", None),
            P(),
            P(None, "head"),
            P(None, "head"),
            P(None, "head"),
            P("head", None),
            P("head"),
            P("head"),
            P(),
            P(),
            P("expert", None, "head"),
            P("expert", None, "head"),
            P("expert", "head", None),
            P("expert", None),
            P(),
            P("expert", None),
        ),
        out_specs=(
            P("expert", None),
            P("expert", None),
            P(),
            P("expert", "head"),
            P("expert", "head"),
            P("expert", "head"),
            P("head", "expert"),
            P("head"),
            P("head"),
            P(),
            P(),
            P("expert", None, "head"),
            P("expert", None, "head"),
            P("expert", "head", None),
        ),
        check_vma=False,
    )
```

```python
import functools

import jax
import jax.numpy as jnp
from jax import lax
from jax.experimental import pallas as pl
from jax.experimental.pallas import tpu as pltpu
from jax.sharding import PartitionSpec as P

HEAD_DIM = 128
TOP = 8
SEQ = 2048
MESH = pl.DeviceIdType.MESH
bf16 = jnp.bfloat16
f32 = jnp.float32


EPSILON = 1e-05
ROPE_BASE = 10000.0
MASKED = -1000000000.0


def from_behind(shard, axis, by):
    size = lax.axis_size(axis)
    pairs = [(i, i + by) for i in range(size) if 0 <= i + by < size]
    return lax.ppermute(shard, axis, pairs)


def inverse_rms(values):
    return lax.rsqrt(jnp.mean(values * values, -1, keepdims=True) + EPSILON)


def norm_back(grad_normed, normed, inverse):
    return inverse * (grad_normed - normed * jnp.mean(grad_normed * normed, -1, keepdims=True))


def rope_tables(places, half_dim):
    inv_freq = ROPE_BASE ** (-lax.iota(jnp.int32, half_dim).astype(jnp.float32) / half_dim)
    angles = places[:, None] * inv_freq[None, :]
    return (jnp.cos(angles)[:, None, :], jnp.sin(angles)[:, None, :])


def rotate(values, cosine, sine_part, direction):
    half_dim = values.shape[-1] // 2
    first_half = values[..., :half_dim]
    second_half = values[..., half_dim:]
    turned = direction * sine_part
    return jnp.concatenate(
        [first_half * cosine - second_half * turned, second_half * cosine + first_half * turned], -1
    )


def place():
    block = lax.axis_index("expert")
    lane = lax.axis_index("head")
    return block // 2, block % 2, lane // 2, lane % 2


def device(z, y, x, core):
    return (z * 2 + y, x * 2 + core)


def greet(z, y, x, core):
    barrier = pltpu.get_barrier_semaphore()

    def signal(target):
        pl.semaphore_signal(barrier, inc=1, device_id=target, device_id_type=MESH)

    signal(device(z, 1 - y, x, core))
    signal(device(z, y, 1 - x, core))
    signal(device(z, y, x, 1 - core))

    @pl.when(z > 0)
    def _():
        signal(device(z - 1, y, x, core))

    @pl.when(z < 3)
    def _():
        signal(device(z + 1, y, x, core))

    pl.semaphore_wait(barrier, 3 + (z > 0).astype(jnp.int32) + (z < 3).astype(jnp.int32))


def add_split(a, b):
    pair = a.astype(f32) + b.astype(f32)
    lanes = lax.broadcasted_iota(jnp.int32, pair.shape, 1)
    whole = jnp.where(lanes < 16, pair + pltpu.roll(pair, 112, 1), 0.0)
    high = whole.astype(bf16).astype(f32)
    return (high + pltpu.roll(whole - high, 16, 1)).astype(bf16)


def dot(a,b): return jnp.dot(a,b,preferred_element_type=f32)
def dot_nt(a,b): return lax.dot_general(a,b,(((1,),(1,)),((),())),preferred_element_type=f32)
def dot_tn(a,b): return lax.dot_general(a,b,(((0,),(0,)),((),())),preferred_element_type=f32)


EPS = 1e-05
HD = 128
BLOCK = 256


def block_of(r, parity):
    return 2 * r + (parity if r % 2 == 0 else 1 - parity)


def norm_factor(v):
    return lax.rsqrt(jnp.mean(v * v, -1, keepdims=True) + EPS)


def probabilities(r, start, q, k_ref, segc_ref, segr_ref):
    keys = (2 * r + 2) * BLOCK
    scores = dot_nt(q, k_ref[:keys]) * (HD ** -0.5)
    rows = start + lax.broadcasted_iota(jnp.int32, scores.shape, 0)
    columns = lax.broadcasted_iota(jnp.int32, scores.shape, 1)
    same = segc_ref[pl.ds(start, BLOCK)] == segr_ref[:, :keys]
    scores = jnp.where((rows >= columns) & same, scores, -1000000000.0)
    raised = jnp.exp(scores - jnp.max(scores, -1, keepdims=True))
    return raised / jnp.sum(raised, -1, keepdims=True)


VM = pl.BlockSpec(memory_space=pltpu.VMEM)


def masked_probs(b, q, k_ref, segc_ref, segr_ref):
    keys = (b + 1) * BLOCK
    scores = dot_nt(q, k_ref[:keys]) * (HD ** -0.5)
    rows = b * BLOCK + lax.broadcasted_iota(jnp.int32, scores.shape, 0)
    columns = lax.broadcasted_iota(jnp.int32, scores.shape, 1)
    same = segc_ref[b * BLOCK:keys] == segr_ref[:, :keys]
    scores = jnp.where((rows >= columns) & same, scores, -1000000000.0)
    raised = jnp.exp(scores - jnp.max(scores, -1, keepdims=True))
    return raised / jnp.sum(raised, -1, keepdims=True)


def far_first(z):
    ahead = z // 2
    return (3 - 3 * ahead, 2 - ahead, z + 1 - 2 * (z % 2), z)


def greet_peers(z, y, x, core, others):
    barrier = pltpu.get_barrier_semaphore()

    def signal(where):
        pl.semaphore_signal(barrier, inc=1, device_id=where, device_id_type=MESH)

    for n in range(4):
        pl.when(z != n)(lambda: signal(device(n, y, x, core)))
        pl.when(z != n)(lambda: signal(device(n, 1 - y, x, core)))
    signal(device(z, 1 - y, x, core))
    for where in others:
        signal(where)
    pl.semaphore_wait(barrier, 7 + len(others))


def picked(i, values):
    if isinstance(i, int):
        return values[i]
    return sum((i == k).astype(jnp.int32) * v for k, v in enumerate(values))


class Gather:
    def __init__(self, own, whole, local_sem, send, recv, rows=BLOCK):
        self.own, self.whole, self.send, self.recv, self.rows = own, whole, send, recv, rows
        z, y, x, core = self.place = place()
        self.me = z * 2 + y
        half, eighth = rows // 2, rows // 8
        self.unit = eighth // 2
        self.keep = pltpu.make_async_copy(own, self.at(self.me, 0, rows), local_sem)

        def chunks(c):
            return ((c * half + x * 5 * self.unit, 3 * self.unit), (c * half + (3 - x) * self.unit, 3 * self.unit))

        def quarter(c, of):
            return (c * half + of * 3 * eighth, eighth)

        self.slab, self.twin_slab = chunks(core), chunks(1 - core)
        self.mine, self.theirs = quarter(core, x), quarter(core, 1 - x)
        self.twin_theirs = quarter(1 - core, 1 - x)

    def at(self, b, start, size):
        return self.whole.at[pl.ds(pl.multiple_of(b * self.rows + start, self.unit), size)]

    def copy(self, first, c, index, b, part, where, own=False):
        if own:
            source = self.own.at[pl.ds(pl.multiple_of(part[0], self.unit), part[1])]
        else:
            source = self.at(b, *part)
        return pltpu.make_async_remote_copy(
            src_ref=source, dst_ref=self.at(b, *part), send_sem=self.send.at[first + index], recv_sem=self.recv.at[first + index],
            device_id=where, device_id_type=MESH)

    def up(self, b, c, own=False):
        z, y, x, core = self.place
        return self.copy(0, c, c * 4 + b // 2, b, self.slab[c], device(z + 1, y, x, core), own)

    def down(self, b, c, own=False):
        z, y, x, core = self.place
        return self.copy(8, c, c * 4 + b // 2, b, self.slab[c], device(z - 1, y, x, core), own)

    def over(self, b, c, own=False):
        z, y, x, core = self.place
        return self.copy(16, c, c * 4 + b // 2, b, self.slab[c], device(z, 1 - y, x, core), own)

    def side(self, b, part):
        z, y, x, core = self.place
        return self.copy(24, 0, b, b, part, device(z, y, 1 - x, core))

    def twin(self, b, c, part):
        z, y, x, core = self.place
        return self.copy(32, c, c * 8 + b, b, part, device(z, y, x, 1 - core))

    def twin_x(self, b, part):
        z, y, x, core = self.place
        return self.copy(48, 0, b, b, part, device(z, y, x, 1 - core))

    def group(self, i):
        z = self.place[0]
        ahead = z // 2
        return picked(i, (z, z + 1 - 2 * (z % 2), 2 - ahead, 3 - 3 * ahead))

    def start_chunk(self, c):
        z, y, x, core = self.place
        pl.when(z < 3)(lambda: self.up(self.me, c, True).start())
        pl.when(z > 0)(lambda: self.down(self.me, c, True).start())
        self.over(self.me, c, True).start()

    def start(self):
        self.start_chunk(0)
        self.start_chunk(1)
        self.keep.start()

    def spread(self, b, c):
        if c == 0:
            self.side(b, self.mine).start()
        self.twin(b, c, self.slab[c]).start()

    def hop(self, i):
        z, y, x, core = self.place
        b = self.group(i) * 2 + y
        below = picked(i, (0, z % 2, z // 2, z // 2)) == 1
        for c in range(2):
            @pl.when(below)
            def _():
                self.up(b, c).wait_recv()
                pl.when(z < 3)(lambda: self.up(b, c).start())

            @pl.when(jnp.logical_not(below))
            def _():
                self.down(b, c).wait_recv()
                pl.when(z > 0)(lambda: self.down(b, c).start())

            self.over(b, c).start()
            self.spread(b, c)

    def hop_inside(self, i):
        z = self.place[0]
        pl.when((z > 0) & (z < 3))(lambda: self.hop(i))

    def hop_outside(self, i):
        z = self.place[0]
        pl.when(z % 3 == 0)(lambda: self.hop(i))

    def cross(self, i):
        b = self.group(i) * 2 + 1 - self.place[1]
        for c in range(2):
            self.over(b, c).wait_recv()
            self.spread(b, c)

    def blocks(self, i, act):
        y = self.place[1]
        n = self.group(i)
        act(n * 2 + 1 - y)
        if isinstance(i, int):
            if i > 0:
                act(n * 2 + y)
        else:
            pl.when(i > 0)(lambda: act(n * 2 + y))

    def flank(self, i):
        def act(b):
            self.side(b, self.theirs).wait_recv()
            self.twin_x(b, self.theirs).start()
        self.blocks(i, act)

    def complete(self, i):
        def act(b):
            for c in range(2):
                self.twin(b, c, self.twin_slab[c]).wait_recv()
            self.twin_x(b, self.twin_theirs).wait_recv()
        self.blocks(i, act)

    def drain(self):
        z, y, x, core = self.place
        for b in range(8):
            zb, yb = b // 2, b % 2

            @pl.when(self.me != b)
            def _():
                self.side(b, self.mine).wait_send()
                self.twin_x(b, self.theirs).wait_send()

            for c in range(2):
                pl.when(self.me != b)(lambda: self.twin(b, c, self.slab[c]).wait_send())
                pl.when(yb == y)(lambda: self.over(b, c).wait_send())
                pl.when((yb == y) & (zb <= z) & (z < 3))(lambda: self.up(b, c).wait_send())
                pl.when((yb == y) & (zb >= z) & (z > 0))(lambda: self.down(b, c).wait_send())

    def whole_run(self):
        self.start()
        self.hop(1)
        self.cross(0)
        self.hop_inside(2)
        self.flank(0)
        self.hop_outside(2)
        self.cross(1)
        self.hop_inside(3)
        self.flank(1)
        self.hop_outside(3)
        self.cross(2)
        self.cross(3)
        self.flank(2)
        self.flank(3)
        for i in range(4):
            self.complete(i)
        self.keep.wait()
        self.drain()


GATHER_SEMS = [pltpu.SemaphoreType.DMA, pltpu.SemaphoreType.DMA((56,)), pltpu.SemaphoreType.DMA((56,))]


ANY = pl.BlockSpec(memory_space=pl.ANY)


def sum_rows(target, source, cols, rows):
    step = 16
    main = cols.size - cols.size % 2048

    @pl.loop(0, rows // step)
    def _(i):
        part = pl.ds(pl.multiple_of(i * step, step), step)
        wide = pl.ds(cols.start, main)
        target[part, wide] = (target[part, wide].astype(f32) + source[part, wide].astype(f32)).astype(bf16)
        if main < cols.size:
            tail = pl.ds(cols.start + main, cols.size - main)
            target[part, tail] = add_split(target[part, tail], source[part, tail])


def sums_kernel(parts, x_ref, acts_ref, grads_ref, weighted_ref, total, gate_out, up_out, down_out,
                held, from_core, from_x, from_y, from_below, from_above, shared_in,
                acts, weighted, x_buf, g_buf, gu_buf, down_buf,
                load_sem, send, recv, end_send, end_recv, fixed_sem, x_sem, g_sem, gu_sem, down_sem):
    z, y, x, core = place()
    D = x_ref.shape[1]
    half = parts.shape[1] // 2
    piece = half // 4
    me = z * 2 + y
    order = far_first(z)
    my_half = pl.ds(pl.multiple_of(core * half, half), half)
    other_half = pl.ds(pl.multiple_of((1 - core) * half, half), half)
    slab = pl.ds(pl.multiple_of(x * piece, piece), 3 * piece)
    mine = pl.ds(pl.multiple_of(x * 3 * piece, piece), piece)
    theirs = pl.ds(pl.multiple_of((1 - x) * 3 * piece, piece), piece)
    shared = pl.ds(piece, 2 * piece)
    spans = (pl.ds(0, D), pl.ds(D, parts.shape[2] - D))
    CORE, X, Y, UP, DOWN = range(5)
    everything = pl.ds(0, half)

    def remote(kind, h, number, source, target, where):
        return pltpu.make_async_remote_copy(
            src_ref=source, dst_ref=target, send_sem=send.at[kind, h, number],
            recv_sem=recv.at[kind, h, number], device_id=where, device_id_type=MESH)

    def load(b, h):
        return pltpu.make_async_copy(parts.at[b, my_half, spans[h]], held.at[b, everything, spans[h]], load_sem.at[h, b])

    def to_core(b, h):
        return remote(CORE, h, b, parts.at[b, other_half, spans[h]], from_core.at[b, everything, spans[h]], device(z, y, x, 1 - core))

    def to_x(b, h):
        return remote(X, h, b, held.at[b, theirs, spans[h]], from_x.at[b, pl.ds(0, piece), spans[h]], device(z, y, 1 - x, core))

    def to_y(zb, h):
        return remote(Y, h, zb, held.at[zb * 2 + 1 - y, slab, spans[h]], from_y.at[zb, pl.ds(0, 3 * piece), spans[h]], device(z, 1 - y, x, core))

    def to_above(zb, h):
        return remote(UP, h, zb, held.at[zb * 2 + y, slab, spans[h]], from_below.at[zb, pl.ds(0, 3 * piece), spans[h]], device(z + 1, y, x, core))

    def to_below(zb, h):
        return remote(DOWN, h, zb, held.at[zb * 2 + y, slab, spans[h]], from_above.at[zb, pl.ds(0, 3 * piece), spans[h]], device(z - 1, y, x, core))

    fixed = [pltpu.make_async_copy(acts_ref, acts, fixed_sem.at[0]), pltpu.make_async_copy(weighted_ref, weighted, fixed_sem.at[1])]
    ff = weighted.shape[1] // 2
    x_pieces, g_pieces = D // BLOCK, D // 512

    def x_load(k):
        return pltpu.make_async_copy(x_ref.at[:, pl.ds(k * BLOCK, BLOCK)], x_buf.at[k % 2], x_sem.at[k % 2])

    def g_load(k):
        return pltpu.make_async_copy(grads_ref.at[:, pl.ds(k * 512, 512)], g_buf.at[k % 2], g_sem.at[k % 2])

    def gu_store(k):
        rows = pl.ds(k * BLOCK, BLOCK)
        return [pltpu.make_async_copy(gu_buf.at[k % 2, u, j], (gate_out, up_out)[u].at[j, rows], gu_sem.at[k % 2, u, j])
                for u in range(2) for j in range(2)]

    def down_store(k):
        return [pltpu.make_async_copy(down_buf.at[k % 2, j], down_out.at[j, :, pl.ds(k * 512, 512)], down_sem.at[k % 2, j])
                for j in range(2)]

    def x_piece(k):
        if k == 0:
            fixed[0].wait()
        x_load(k).wait()
        if k >= 2:
            for copy in gu_store(k - 2):
                copy.wait()
        both = dot_tn(x_buf[k % 2], acts[...])
        for j in range(2):
            for u in range(2):
                gu_buf[k % 2, u, j] = both[:, (2 * j + u) * ff:(2 * j + u + 1) * ff]
        for copy in gu_store(k):
            copy.start()
        if k + 2 < x_pieces:
            x_load(k + 2).start()

    def g_piece(k):
        if k == 0:
            fixed[1].wait()
        g_load(k).wait()
        if k >= 2:
            for copy in down_store(k - 2):
                copy.wait()
        both = dot_tn(weighted[...], g_buf[k % 2])
        for j in range(2):
            down_buf[k % 2, j] = both[j * ff:(j + 1) * ff]
        for copy in down_store(k):
            copy.start()
        if k + 2 < g_pieces:
            g_load(k + 2).start()

    fillers = [functools.partial(x_piece, k) for k in range(x_pieces)]
    for k in range(g_pieces):
        fillers.insert(3 * k + 2, functools.partial(g_piece, k))

    greet(z, y, x, core)
    items = [(zb, h) for zb in order for h in (1, 0)]
    for k, (zb, h) in enumerate(items):
        for yb in (1 - y, y):
            load(zb * 2 + yb, h).start()
            to_core(zb * 2 + yb, h).start()
        if k == 1:
            for copy in fixed:
                copy.start()
            for j in range(2):
                x_load(j).start()
                g_load(j).start()

    def stage_core(zb, h, yb):
        b = zb * 2 + yb
        load(b, h).wait()
        to_core(b, h).wait_recv()
        sum_rows(held.at[b], from_core.at[b], spans[h], half)
        to_x(b, h).start()

    def stage_x(zb, h, yb):
        b = zb * 2 + yb
        to_x(b, h).wait_recv()
        sum_rows(held.at[b, mine], from_x.at[b], spans[h], piece)

    def stage_y(zb, h):
        stage_x(zb, h, 1 - y)
        to_y(zb, h).start()

    def climb(zb, h):
        @pl.when(z > 0)
        def _():
            to_above(zb, h).wait_recv()
            sum_rows(held.at[zb * 2 + y, slab], from_below.at[zb], spans[h], 3 * piece)
        to_above(zb, h).start()

    def descend(zb, h):
        @pl.when(z < 3)
        def _():
            to_below(zb, h).wait_recv()
            sum_rows(held.at[zb * 2 + y, slab], from_above.at[zb], spans[h], 3 * piece)
        to_below(zb, h).start()

    def stage_z(k):
        zb, h = items[k]
        to_y(zb, h).wait_recv()
        sum_rows(held.at[zb * 2 + y, slab], from_y.at[zb], spans[h], 3 * piece)
        rises = (z // 2 == 0) if k < 4 else (z % 2 == 0)
        pl.when(rises)(lambda: climb(zb, h))
        pl.when(jnp.logical_not(rises))(lambda: descend(zb, h))

    base = core * half
    out_mine = pl.ds(pl.multiple_of(base + x * 3 * piece, piece), piece)
    out_theirs = pl.ds(pl.multiple_of(base + (1 - x) * 3 * piece, piece), piece)
    out_shared = pl.ds(pl.multiple_of(base + piece, piece), 2 * piece)

    def at_end(number, h, source, target, where):
        return pltpu.make_async_remote_copy(
            src_ref=source, dst_ref=target, send_sem=end_send.at[h, number],
            recv_sem=end_recv.at[h, number], device_id=where, device_id_type=MESH)

    across, twin = device(z, y, 1 - x, core), device(z, y, x, 1 - core)
    end_sums = lambda h: at_end(0, h, held.at[me, shared, spans[h]], shared_in.at[pl.ds(0, 2 * piece), spans[h]], across)
    end_ready = lambda h, rows: at_end(1, h, held.at[me, mine, spans[h]], total.at[rows, spans[h]], across)
    end_twin = lambda h, rows: at_end(2, h, total.at[my_half, spans[h]], total.at[rows, spans[h]], twin)

    def own_sum(h):
        own = held.at[me]
        to_y(z, h).wait_recv()
        sum_rows(own.at[slab], from_y.at[z], spans[h], 3 * piece)

        @pl.when(z > 0)
        def _():
            to_above(z, h).wait_recv()
            sum_rows(own.at[slab], from_below.at[z], spans[h], 3 * piece)

        @pl.when(z < 3)
        def _():
            to_below(z, h).wait_recv()
            sum_rows(own.at[slab], from_above.at[z], spans[h], 3 * piece)
        end_sums(h).start()
        end_ready(h, out_mine).start()
        total[out_mine, spans[h]] = held[me, mine, spans[h]]

    def own_end(h):
        end_sums(h).wait_recv()
        sum_rows(held.at[me, shared], shared_in, spans[h], 2 * piece)
        total[out_shared, spans[h]] = held[me, shared, spans[h]]
        end_ready(h, out_theirs).wait_recv()
        end_twin(h, my_half).start()

    zb, h = items[0]
    stage_core(zb, h, 1 - y)
    stage_core(zb, h, y)
    for k, (zb, h) in enumerate(items):
        if k < 7:
            stage_core(*items[k + 1], 1 - y)
        stage_y(zb, h)
        if k < 7:
            stage_core(*items[k + 1], y)
        stage_x(zb, h, y)
        if 0 < k < 7:
            stage_z(k - 1)
        if k < 7:
            for fill in fillers[2 * k:2 * k + 2]:
                fill()
    for fill in fillers[14:]:
        fill()
    own_sum(1)
    own_sum(0)
    end_sums(1).wait_send()
    own_end(1)
    end_sums(0).wait_send()
    own_end(0)
    for h in (1, 0):
        end_twin(h, other_half).wait_recv()
        end_ready(h, out_mine).wait_send()
        end_twin(h, my_half).wait_send()
        for b in range(8):
            zb, yb = b // 2, b % 2
            to_core(b, h).wait_send()
            to_x(b, h).wait_send()
            if yb == 0:
                to_y(zb, h).wait_send()
                pl.when(zb > z)(lambda: to_above(zb, h).wait_send())
                pl.when(zb < z)(lambda: to_below(zb, h).wait_send())
    for k in (x_pieces - 2, x_pieces - 1):
        for copy in gu_store(k):
            copy.wait()
    for k in (g_pieces - 2, g_pieces - 1):
        for copy in down_store(k):
            copy.wait()


def sums_all(parts, x, acts, grads, weighted, number):
    _, rows, width = parts.shape
    T, D = x.shape
    ff = weighted.shape[1] // 2
    half, piece = rows // 2, rows // 8
    sd = jax.ShapeDtypeStruct
    dma = pltpu.SemaphoreType.DMA
    vm = pltpu.VMEM
    return pl.pallas_call(
        sums_kernel, in_specs=[ANY] * 5, out_specs=[VM, ANY, ANY, ANY],
        out_shape=[sd((rows, width), bf16), sd((2, D, ff), f32), sd((2, D, ff), f32), sd((2, ff, D), f32)],
        scratch_shapes=[
            vm((8, half, width), bf16), vm((8, half, width), bf16), vm((8, piece, width), bf16),
            vm((4, 3 * piece, width), bf16), vm((4, 3 * piece, width), bf16), vm((4, 3 * piece, width), bf16),
            vm((2 * piece, width), bf16),
            vm(acts.shape, bf16), vm(weighted.shape, bf16), vm((2, T, BLOCK), bf16), vm((2, T, 512), bf16),
            vm((2, 2, 2, BLOCK, ff), f32), vm((2, 2, ff, 512), f32),
            dma((2, 8)), dma((5, 2, 8)), dma((5, 2, 8)), dma((2, 3)), dma((2, 3)),
            dma((2,)), dma((2,)), dma((2,)), dma((2, 2, 2)), dma((2, 2)),
        ],
        compiler_params=pltpu.CompilerParams(collective_id=number, has_side_effects=True, vmem_limit_bytes=62 * 2**20),
    )(parts, x, acts, grads, weighted)


def forward_kernel(hidden, sent_ref, gain1_ref, gain2_ref, qg_ref, kg_ref, segc_ref, segr_ref, wr_ref,
                   wq_in, wk_in, wv_in, cos_in, sin_in, wout_in, wg_in, wu_in, wd_in,
                   gathered, middle_out, moe_out, x_all, a_out, q_out, k_out, v_out, qr_out, kr_out, grads_all,
                   m_out, weighted_out, acts_out, parts_out,
                   w_qkv, cos_ref, sin_ref, w_out, wg, wu, wd, q_ref, k_ref, v_ref, qr_ref, kr_ref,
                   part, arrived, out_half, in_half, held, from_x, total, middle_ref, moe, whole, mask_all, w_buf, a_buf, p_buf,
                   x_keep, x_send, x_recv, c_keep, c_send, c_recv, m_keep, m_send, m_recv,
                   load, stream, out_sem, kept_sem, send, recv, pair_send, pair_recv):
    z, y, x, core = place()
    across, twin = device(z, y, 1 - x, core), device(z, y, x, 1 - core)
    first_expert = (z * 2 + y) * wg_in.shape[0]
    D, ff = wg_in.shape[1], wg_in.shape[2]
    span = 2 * BLOCK
    head = pl.ds(pl.multiple_of(z * HD, HD), HD)
    loads = [pltpu.make_async_copy(source, target, load.at[k]) for k, (source, target) in enumerate((
        (wq_in.at[:, head], w_qkv.at[:, pl.ds(0, HD)]), (wk_in.at[:, head], w_qkv.at[:, pl.ds(HD, HD)]),
        (wv_in.at[:, head], w_qkv.at[:, pl.ds(2 * HD, HD)]), (cos_in, cos_ref), (sin_in, sin_ref),
        (wout_in, w_out), (wd_in, wd), (wg_in, wg), (wu_in, wu)))]
    for copy in loads:
        copy.start()
    greet_peers(z, y, x, core, (across, twin))
    gather = Gather(hidden, x_all, x_keep, x_send, x_recv)
    cot = Gather(sent_ref, grads_all, c_keep, c_send, c_recv)
    experts = Gather(moe, whole, m_keep, m_send, m_recv)

    def remote(source, target, ssem, rsem, where):
        return pltpu.make_async_remote_copy(
            src_ref=source, dst_ref=target, send_sem=ssem, recv_sem=rsem, device_id=where, device_id_type=MESH)

    gather.start()
    gather.hop(1)
    gather.cross(0)
    gather.hop_inside(2)
    gather.flank(0)
    gather.keep.wait()
    for copy in loads[:5]:
        copy.wait()

    def rows_of(i):
        return pl.ds(pl.multiple_of(gather.group(i) * span, span), span)

    x_part, a_part = p_buf.at[:, pl.ds(0, D)], p_buf.at[:, pl.ds(D, D)]

    def a_store(i):
        return pltpu.make_async_copy(a_part, a_out.at[rows_of(i)], stream.at[1])

    def project(i):
        gather.complete(i)
        rows = rows_of(i)
        fetch = pltpu.make_async_copy(x_all.at[rows], x_part, stream.at[0])
        fetch.start()
        if i > 0:
            a_store(i - 1).wait()
        fetch.wait()
        v = p_buf[:, :D].astype(f32)
        a = (v * norm_factor(v) * gain1_ref[...]).astype(bf16)
        p_buf[:, D:2 * D] = a
        a_store(i).start()
        raw = dot(a, w_qkv[...])
        cosine, sine = cos_ref[rows], sin_ref[rows]

        def turned(part, gain):
            n = part * norm_factor(part) * gain
            return (n * cosine + pltpu.roll(n, HD // 2, 1) * sine).astype(bf16)

        q_raw, k_raw = raw[:, :HD], raw[:, HD:2 * HD]
        qr_ref[rows] = q_raw
        kr_ref[rows] = k_raw
        q_ref[rows] = turned(q_raw, qg_ref[:, head])
        k_ref[rows] = turned(k_raw, kg_ref[:, head])
        v_ref[rows] = raw[:, 2 * HD:].astype(bf16)

    for i in range(4):
        if i < 2:
            gather.hop_outside(i + 2)
        if i < 3:
            gather.cross(i + 1)
        if i == 0:
            gather.hop_inside(3)
        if i == 1:
            cot.start()
        project(i)
        if i < 3:
            gather.flank(i + 1)
    a_store(3).wait()
    keeps = [pltpu.make_async_copy(source, target, kept_sem.at[k]) for k, (source, target) in enumerate((
        (q_ref, q_out), (k_ref, k_out), (v_ref, v_out), (qr_ref, qr_out), (kr_ref, kr_out),
        (middle_ref, middle_out), (moe, moe_out)))]
    for copy in keeps[:5]:
        copy.start()
    cot.hop(1)
    cot.cross(0)
    cot.hop_inside(2)

    targets = lambda r: (y if r % 2 == 0 else 1 - y)
    source_y = (y + z) % 2

    def to_block(r):
        return remote(part.at[r], arrived.at[z], send.at[r], recv.at[z], device(r, targets(r), x, core))

    def from_head(n):
        return remote(part.at[n], arrived.at[n], send.at[n], recv.at[n], device(n, source_y, x, core))

    here = lambda r: (z == r) & (z % 2 == 0)
    for r in range(3, -1, -1):
        start = pl.multiple_of(block_of(r, y) * BLOCK, BLOCK)
        probs = probabilities(r, start, q_ref[pl.ds(start, BLOCK)], k_ref, segc_ref, segr_ref)
        part[r] = dot(probs.astype(bf16), v_ref[:(2 * r + 2) * BLOCK]).astype(bf16)
        pl.when(jnp.logical_not(here(r)))(lambda: to_block(r).start())
    cot.flank(0)

    @pl.when(z % 2 == 0)
    def _():
        arrived[z] = part[z]

    loads[5].wait()
    for n in range(4):
        pl.when(jnp.logical_not(here(n)))(lambda: from_head(n).wait_recv())
        gathered[:, n * HD:(n + 1) * HD] = arrived[n]
    cot.hop_outside(2)
    cot.cross(1)
    cot.hop_inside(3)

    half = BLOCK // 2
    chunk = half // 2
    my_half = core * half
    other_half = (1 - core) * half
    piece = lambda c: pl.ds(pl.multiple_of(c * chunk, chunk), chunk)
    at = lambda base, c: pl.ds(pl.multiple_of(base + c * chunk, chunk), chunk)

    def pair(kind, c, source, target, where):
        return remote(source, target, pair_send.at[kind, c], pair_recv.at[kind, c], where)

    first = lambda c: pair(0, c, out_half.at[piece(c)], in_half.at[piece(c)], twin)
    second = lambda c: pair(1, c, held.at[piece(c)], from_x.at[piece(c)], across)
    third = lambda c: pair(2, c, total.at[at(my_half, c)], total.at[at(my_half, c)], twin)
    for c in (1 - x, x):
        out_half[piece(c)] = dot(gathered[at(other_half, c)], w_out[...]).astype(bf16)
        first(c).start()
    for c in (1 - x, x):
        kept = dot(gathered[at(my_half, c)], w_out[...])
        first(c).wait_recv()
        held[piece(c)] = (kept + in_half[piece(c)].astype(f32)).astype(bf16)
        second(c).start()
    cot.flank(1)
    step = 32

    def norm_rows(base, count):
        def body(i, _):
            rows = pl.ds(pl.multiple_of(base + i * step, step), step)
            v = hidden[rows].astype(f32) + total[rows].astype(f32)
            middle_ref[rows] = v
            moe[rows] = (v * norm_factor(v) * gain2_ref[...]).astype(bf16)
            return 0
        lax.fori_loop(0, count // step, body, 0)

    for k, c in enumerate((x, 1 - x)):
        second(c).wait_recv()
        total[at(my_half, c)] = (held[piece(c)].astype(f32) + from_x[piece(c)].astype(f32)).astype(bf16)
        third(c).start()
        norm_rows(my_half + c * chunk, chunk)
        experts.start_chunk(k)
        if k == 0:
            cot.hop_outside(3)
            cot.cross(2)
    for c in (x, 1 - x):
        pair(2, c, total.at[at(my_half, c)], total.at[at(other_half, c)], twin).wait_recv()
    norm_rows(other_half, half)
    experts.keep.start()
    for copy in keeps[5:]:
        copy.start()
    cot.flank(2)
    experts.hop(1)
    experts.cross(0)
    cot.cross(3)
    experts.hop_inside(2)
    experts.flank(0)
    cot.flank(3)
    experts.keep.wait()
    cot.keep.wait()
    for copy in loads[6:]:
        copy.wait()

    def grads_load(i):
        rows = rows_of(i)
        return [pltpu.make_async_copy(grads_all.at[rows, pl.ds(0, D)], p_buf.at[:, pl.ds(0, D)], stream.at[1]),
                pltpu.make_async_copy(grads_all.at[rows, pl.ds(D, 128)], mask_all, stream.at[2])]

    def stores(i):
        rows = rows_of(i)
        return [
            pltpu.make_async_copy(w_buf.at[i % 2], weighted_out.at[rows], out_sem.at[i % 2, 0]),
            pltpu.make_async_copy(a_buf.at[i % 2], acts_out.at[rows], out_sem.at[i % 2, 1]),
            pltpu.make_async_copy(whole.at[rows], m_out.at[rows], out_sem.at[i % 2, 2]),
        ]

    def parts_store(i):
        return pltpu.make_async_copy(p_buf, parts_out.at[rows_of(i)], stream.at[0])

    def run_experts(i):
        cot.complete(i)
        if i > 0:
            parts_store(i - 1).wait()
        fetches = grads_load(i)
        for copy in fetches:
            copy.start()
        experts.complete(i)
        slot = i % 2
        if i >= 2:
            for copy in stores(i - 2):
                copy.wait()

        rows = rows_of(i)
        v = whole[rows]
        logits = dot(v, wr_ref[...])
        count = logits.shape[1]
        for copy in fetches:
            copy.wait()
        mask = mask_all[:, :count].astype(f32) > 0
        top = jnp.max(jnp.where(mask, logits, -jnp.inf), -1, keepdims=True)
        raised = jnp.where(mask, jnp.exp(jnp.where(mask, logits - top, 0.0)), 0.0)
        gates = raised / jnp.sum(raised, -1, keepdims=True)
        lane = lax.broadcasted_iota(jnp.int32, gates.shape, 1)
        gg = jnp.zeros(gates.shape, f32)
        for j in range(2):
            mine = lane == first_expert + j
            gate = jnp.sum(jnp.where(mine, gates, 0.0), -1, keepdims=True)
            ga = dot(v, wg[j])
            ua = dot(v, wu[j])
            gw_j = dot_nt(p_buf[:, :D], wd[j])
            s = 1.0 / (1.0 + jnp.exp(-ga))
            silu = ga * s
            h = (silu * ua).astype(bf16).astype(f32)
            gg = gg + jnp.where(mine, jnp.sum(h * gw_j, -1, keepdims=True), 0.0)
            gh = gw_j * gate
            w_buf[slot, :, j * ff:(j + 1) * ff] = (h * gate).astype(bf16)
            a_buf[slot, :, 2 * j * ff:(2 * j + 1) * ff] = (gh * ua * s * (1.0 + ga * (1.0 - s))).astype(bf16)
            a_buf[slot, :, (2 * j + 1) * ff:(2 * j + 2) * ff] = (gh * silu).astype(bf16)
        for copy in stores(i):
            copy.start()
        if i < 3:
            experts.flank(i + 1)
        p_buf[:, :D] = dot(w_buf[slot], wd[...].reshape(2 * ff, D)).astype(bf16)
        gx = dot_nt(a_buf[slot, :, :ff], wg[0])
        for k, weight in ((1, wu[0]), (2, wg[1]), (3, wu[1])):
            gx = gx + dot_nt(a_buf[slot, :, k * ff:(k + 1) * ff], weight)
        p_buf[:, D:2 * D] = gx.astype(bf16)
        high = gg.astype(bf16)
        low = (gg - high.astype(f32)).astype(bf16)
        spare = jnp.zeros((span, 128 - 2 * count), bf16)
        p_buf[:, 2 * D:] = jnp.concatenate([high, low, spare], 1)
        parts_store(i).start()

    for i in range(4):
        if i < 2:
            experts.hop_outside(i + 2)
        if i < 3:
            experts.cross(i + 1)
        if i == 0:
            experts.hop_inside(3)
        run_experts(i)
    parts_store(3).wait()
    for i in (2, 3):
        for copy in stores(i):
            copy.wait()
    for copy in keeps:
        copy.wait()
    gather.drain()
    cot.drain()
    experts.drain()
    for c in range(2):
        first(c).wait_send()
        second(c).wait_send()
        third(c).wait_send()
    for r in range(4):
        pl.when(jnp.logical_not(here(r)))(lambda: to_block(r).wait_send())


def forward_all(hidden, sent, gain1, gain2, qg, kg, segc, segr, wr, wq, wk, wv, cosine, sine, wout, wg, wu, wd, number):
    rows, D = hidden.shape
    T = 8 * rows
    J, _, F = wg.shape
    half, span = rows // 2, 2 * rows
    sd = jax.ShapeDtypeStruct
    dma = pltpu.SemaphoreType.DMA
    vm = pltpu.VMEM
    like = lambda m: vm(m.shape, m.dtype)
    heads = [((T, HD), bf16)] * 3 + [((T, HD), f32)] * 2
    return pl.pallas_call(
        forward_kernel, in_specs=[VM] * 9 + [ANY] * 9, out_specs=[VM] + [ANY] * 14,
        out_shape=[sd((rows, 4 * HD), bf16), sd((rows, D), f32), sd((rows, D), bf16), sd((T, D), bf16), sd((T, D), bf16)]
        + [sd(*m) for m in heads] + [sd((T, D + 128), bf16), sd((T, D), bf16), sd((T, J * F), bf16), sd((T, 2 * J * F), bf16),
                                     sd((T, 2 * D + 128), bf16)],
        scratch_shapes=[vm((D, 3 * HD), bf16)] + [like(m) for m in (cosine, sine, wout, wg, wu, wd)]
        + [vm(*m) for m in heads] + [vm((4, BLOCK, HD), bf16)] * 2 + [vm((half, D), bf16)] * 4 + [vm((rows, D), bf16), vm((rows, D), f32), vm((rows, D), bf16)] + [
            vm((T, D), bf16), vm((span, 128), bf16), vm((2, span, J * F), bf16), vm((2, span, 2 * J * F), bf16),
            vm((span, 2 * D + 128), bf16)] + GATHER_SEMS * 3 + [
            dma((9,)), dma((3,)), dma((2, 3)), dma((7,)), dma((4,)), dma((4,)), dma((3, 2)), dma((3, 2))],
        compiler_params=pltpu.CompilerParams(collective_id=number, has_side_effects=True, vmem_limit_bytes=62 * 2**20),
    )(hidden, sent, gain1, gain2, qg, kg, segc, segr, wr, wq, wk, wv, cosine, sine, wout, wg, wu, wd)


def backward_kernel(ga_ref, segc_ref, segr_ref, qg_ref, kg_ref, gains_small, gain_ref,
                    w_in, ctx_ref, q_in, k_in, v_in, qr_in, kr_in, cos_in, sin_in, wq_in, wk_in, wv_in, a_in, hidden_in, middle_in,
                    grad_ref, weights_q, weights_k, weights_v, norm_ref, gains_out, wout_ref, small_out,
                    w_ref, q_ref, k_ref, v_ref, qr_ref, kr_ref, cos_ref, sin_ref, wq_ref, wk_ref, wv_ref, columns, hidden_ref, middle_ref,
                    raw_ref, g_own, g_all, dk, dv, terms, from_y, held_terms, from_below, from_above,
                    small_y, small_sum, small_z, raw_in, gathered, products, from_z, out_half, in_half, held, from_x, total, gains_own, gains_in, norm_in,
                    load, g_send, g_recv, f_send, f_recv, t_send, t_recv, s_send, s_recv, send, recv, w_send, w_recv,
                    pair_send, pair_recv, e_send, e_recv, n_send, n_recv):
    small_ref = gains_small
    z, y, x, core = place()
    me = z * 2 + y
    order = far_first(z)
    span = 4 * HD
    across, twin, corner = device(z, y, 1 - x, core), device(z, y, x, 1 - core), device(z, y, 1 - x, 1 - core)
    partner = device(z, 1 - y, x, core)

    loads = [pltpu.make_async_copy(source, target, load.at[k]) for k, (source, target) in enumerate((
        (w_in, w_ref), (q_in, q_ref), (k_in, k_ref), (v_in, v_ref), (qr_in, qr_ref), (kr_in, kr_ref), (cos_in, cos_ref),
        (sin_in, sin_ref), (wq_in, wq_ref), (wk_in, wk_ref), (wv_in, wv_ref), (hidden_in, hidden_ref), (middle_in, middle_ref)))]

    def column_load(n):
        block = pl.ds(pl.multiple_of((n * 2 + y) * BLOCK, BLOCK), BLOCK)
        return pltpu.make_async_copy(a_in.at[:, block], columns.at[n], load.at[13 + n])

    for copy in loads:
        copy.start()
    for n in range(4):
        column_load(n).start()
    greet_peers(z, y, x, core, (across, twin, corner))

    def remote(source, target, ssem, rsem, where):
        return pltpu.make_async_remote_copy(
            src_ref=source, dst_ref=target, send_sem=ssem, recv_sem=rsem, device_id=where, device_id_type=MESH)

    def when_away(n, act):
        pl.when(z != n)(act)

    loads[0].wait()
    g_context = dot_nt(ga_ref[...], w_ref[...]).astype(bf16)
    for n in range(4):
        g_own[n] = g_context[:, n * HD:(n + 1) * HD]

    def g_to(n):
        return remote(g_own.at[n], g_all.at[me], g_send.at[n], g_recv.at[z], device(n, y, x, core))

    def g_from(n):
        return remote(g_own.at[n], g_all.at[n * 2 + y], g_send.at[n], g_recv.at[n], device(n, y, x, core))

    def g_over(n):
        return remote(g_all.at[n * 2 + y], g_all.at[n * 2 + y], f_send.at[n], f_recv.at[n], partner)

    def g_over_in(n):
        return remote(g_all.at[n * 2 + 1 - y], g_all.at[n * 2 + 1 - y], f_send.at[n], f_recv.at[n], partner)

    for n in range(4):
        when_away(n, lambda: g_to(n).start())
    g_all[me] = g_own[z]
    g_over(z).start()

    quarter = small_ref.shape[1] // 4

    def lanes(cx, cc):
        return pl.ds(pl.multiple_of((cx * 2 + cc) * quarter, quarter), quarter)

    own_lanes = lanes(x, core)
    small_pair = remote(small_ref.at[:, own_lanes], small_y, s_send.at[0], s_recv.at[0], partner)
    small_pair.start()

    def small_along(n):
        return remote(small_sum, small_z.at[z], s_send.at[1 + n], s_recv.at[1 + z], device(n, y, x, core))

    def small_arriving(n):
        return remote(small_sum, small_z.at[n], s_send.at[1 + n], s_recv.at[1 + n], device(n, y, x, core))

    fans = (across, twin, corner)
    fan_lanes = (lanes(1 - x, core), lanes(x, 1 - core), lanes(1 - x, 1 - core))

    def small_spread(i):
        return remote(small_out.at[:, own_lanes], small_out.at[:, own_lanes], s_send.at[5 + i], s_recv.at[5 + i], fans[i])

    def small_spread_in(i):
        return remote(small_out.at[:, own_lanes], small_out.at[:, fan_lanes[i]], s_send.at[5 + i], s_recv.at[5 + i], fans[i])

    for b in range(8):
        terms[b] = dot_tn(ctx_ref[...], ga_ref[:, b * BLOCK:(b + 1) * BLOCK]).astype(bf16)

    def term_pair(n):
        return remote(terms.at[n * 2 + 1 - y], from_y.at[n], t_send.at[0, n], t_recv.at[0, n], partner)

    def term_up(n):
        return remote(held_terms.at[n], from_below.at[n], t_send.at[1, n], t_recv.at[1, n], device(z + 1, y, x, core))

    def term_down(n):
        return remote(held_terms.at[n], from_above.at[n], t_send.at[2, n], t_recv.at[2, n], device(z - 1, y, x, core))

    def paired(n):
        return terms[n * 2 + y].astype(f32) + from_y[n].astype(f32)

    def term_stage(k):
        n = order[k]
        term_pair(n).wait_recv()
        held_terms[n] = paired(n).astype(bf16)
        rises = (z // 2 == 0) if k < 2 else (z % 2 == 0)

        @pl.when(rises)
        def _():
            @pl.when(z > 0)
            def _():
                term_up(n).wait_recv()
                held_terms[n] = (paired(n) + from_below[n].astype(f32)).astype(bf16)
            term_up(n).start()

        @pl.when(jnp.logical_not(rises))
        def _():
            @pl.when(z < 3)
            def _():
                term_down(n).wait_recv()
                held_terms[n] = (paired(n) + from_above[n].astype(f32)).astype(bf16)
            term_down(n).start()

    for n in range(4):
        when_away(n, lambda: g_from(n).wait_recv())
        when_away(n, lambda: g_over(n).start())
    for n in order:
        term_pair(n).start()

    def rows_to(n):
        return remote(raw_ref.at[n * 2 + y], raw_in.at[z], send.at[n], recv.at[z], device(n, y, x, core))

    def rows_from(n):
        return remote(raw_ref.at[n * 2 + y], raw_in.at[n], send.at[n], recv.at[n], device(n, y, x, core))

    gain_sums = [jnp.zeros((1, HD), f32), jnp.zeros((1, HD), f32)]

    def back(turned, b, raw_in, gain, which):
        rows = slice(b * BLOCK, (b + 1) * BLOCK)
        g = turned * cos_ref[rows] - pltpu.roll(turned, HD // 2, 1) * sin_ref[rows]
        raw = raw_in[rows]
        factor = norm_factor(raw)
        n = raw * factor
        gain_sums[which] = gain_sums[which] + jnp.sum(g * n, 0, keepdims=True)
        g = g * gain[:, pl.ds(pl.multiple_of(z * HD, HD), HD)]
        return (factor * (g - n * jnp.mean(g * n, -1, keepdims=True))).astype(bf16)

    for copy in loads[1:8]:
        copy.wait()
    for b in range(7, -1, -1):
        keys = (b + 1) * BLOCK
        rows = slice(b * BLOCK, keys)
        pl.when(y != b % 2)(lambda: g_over_in(b // 2).wait_recv())
        q = q_ref[rows]
        g = g_all[b]
        probs = masked_probs(b, q, k_ref, segc_ref, segr_ref)
        gv = dot_tn(probs.astype(bf16), g)
        gp = dot_nt(g, v_ref[:keys])
        gs = (probs * (gp - jnp.sum(gp * probs, -1, keepdims=True))).astype(bf16)
        gk = dot_tn(gs, q)
        if b == 7:
            dv[...] = gv
            dk[...] = gk
        else:
            dv[:keys] += gv
            dk[:keys] += gk
        raw_ref[b, :, :HD] = back(dot(gs, k_ref[:keys]) * (HD ** -0.5), b, qr_ref, qg_ref, 0)
        raw_ref[b, :, HD:2 * HD] = back(dk[rows] * (HD ** -0.5), b, kr_ref, kg_ref, 1)
        raw_ref[b, :, 2 * HD:] = dv[rows].astype(bf16)

        @pl.when(y == b % 2)
        def _():
            when_away(b // 2, lambda: rows_to(b // 2).start())

    small_pair.wait_recv()
    small_sum[...] = small_ref[:, own_lanes] + small_y[...]
    for n in range(4):
        when_away(n, lambda: small_along(n).start())
    small_z[z] = small_sum[...]
    gains_own[0:1] = gain_sums[0]
    gains_own[1:2] = gain_sums[1]

    def gains_to(n):
        return remote(gains_own, gains_in.at[z], e_send.at[n], e_recv.at[z], device(n, y, x, core))

    def gains_from(n):
        return remote(gains_own, gains_in.at[n], e_send.at[n], e_recv.at[n], device(n, y, x, core))

    for n in range(4):
        when_away(n, lambda: gains_to(n).start())
    gains_in[z] = gains_own[...]
    raw_in[z] = raw_ref[me]

    def products_to(n):
        return remote(products.at[n], from_z.at[z], w_send.at[n], w_recv.at[z], device(n, y, x, core))

    def products_from(n):
        return remote(products.at[n], from_z.at[n], w_send.at[n], w_recv.at[n], device(n, y, x, core))

    raw_all = raw_ref[...].reshape(8 * BLOCK, 3 * HD)
    for i, n in enumerate(order):
        column_load(n).wait()
        product = dot_tn(columns[n], raw_all).astype(bf16)
        if i < 3:
            products[n] = product
            products_to(n).start()
        else:
            from_z[z] = product
        if i % 2 == 0:
            term_stage(i // 2)

    for copy in loads[8:]:
        copy.wait()
    for n in range(4):
        when_away(n, lambda: rows_from(n).wait_recv())
        for g in range(3):
            gathered[:, g * span + n * HD:g * span + (n + 1) * HD] = raw_in[n, :, g * HD:(g + 1) * HD]

    rows = total.shape[0]
    half = rows // 2
    chunk = half // 2
    my_half = core * half
    other_half = (1 - core) * half
    piece = lambda c: pl.ds(c * chunk, chunk)
    at = lambda base, c: pl.ds(pl.multiple_of(base + c * chunk, chunk), chunk)

    def pair(kind, c, source, target, where):
        return remote(source, target, pair_send.at[kind, c], pair_recv.at[kind, c], where)

    def multiply(part):
        return (dot_nt(part[:, :span], wq_ref[...]) + dot_nt(part[:, span:2 * span], wk_ref[...])
                + dot_nt(part[:, 2 * span:], wv_ref[...]))

    first = [pair(0, c, out_half.at[piece(c)], in_half.at[piece(c)], twin) for c in range(2)]
    second = [pair(1, c, held.at[piece(c)], from_x.at[piece(c)], across) for c in range(2)]
    third = [pair(2, c, total.at[at(my_half, c)], total.at[at(my_half, c)], twin) for c in range(2)]
    for c in range(2):
        out_half[piece(c)] = multiply(gathered[at(other_half, c)]).astype(bf16)
        first[c].start()
    for c in range(2):
        kept = multiply(gathered[at(my_half, c)])
        first[c].wait_recv()
        held[piece(c)] = (kept + in_half[piece(c)].astype(f32)).astype(bf16)
        second[c].start()

    term_stage(2)
    term_pair(z).wait_recv()
    wout_ref[...] = paired(z)

    @pl.when(z > 0)
    def _():
        term_up(z).wait_recv()
        wout_ref[...] += from_below[z].astype(f32)

    @pl.when(z < 3)
    def _():
        term_down(z).wait_recv()
        wout_ref[...] += from_above[z].astype(f32)

    for n in range(4):
        when_away(n, lambda: small_arriving(n).wait_recv())
    small_out[:, own_lanes] = (small_z[0] + small_z[1]) + (small_z[2] + small_z[3])
    for i in range(3):
        small_spread(i).start()
    for n in range(4):
        when_away(n, lambda: gains_from(n).wait_recv())
        gains_out[:, n * HD:(n + 1) * HD] = gains_in[n]
    for c in range(2):
        second[c].wait_recv()
        total[at(my_half, c)] = (held[piece(c)].astype(f32) + from_x[piece(c)].astype(f32)).astype(bf16)
        third[c].start()

    step = 32

    def norm_rows(base):
        def body(i, norm_part):
            part = pl.ds(pl.multiple_of(base + i * step, step), step)
            e = total[part].astype(f32)
            v = hidden_ref[part].astype(f32)
            factor = norm_factor(v)
            n = v * factor
            norm_part = norm_part + jnp.sum(e * n, 0, keepdims=True)
            e = e * gain_ref[...]
            grad_ref[part] = middle_ref[part] + factor * (e - n * jnp.mean(e * n, -1, keepdims=True))
            return norm_part
        return body

    nothing = jnp.zeros((1, total.shape[1]), f32)
    mine_part = lax.fori_loop(0, half // step, norm_rows(my_half), nothing)
    for c in range(2):
        pair(2, c, total.at[at(my_half, c)], total.at[at(other_half, c)], twin).wait_recv()
    other_part = lax.fori_loop(0, half // step, norm_rows(other_half), nothing)
    norm_part = mine_part + other_part
    for t in range(norm_in.shape[1]):
        norm_in[me, t:t + 1] = norm_part[:, t * 128:(t + 1) * 128]

    def norm_to(b):
        return remote(norm_in.at[me], norm_in.at[me], n_send.at[b], n_recv.at[me], device(b // 2, b % 2, x, core))

    def norm_from(b):
        return remote(norm_in.at[b], norm_in.at[b], n_send.at[b], n_recv.at[b], device(b // 2, b % 2, x, core))

    for b in range(8):
        pl.when(me != b)(lambda: norm_to(b).start())
    for n in range(4):
        when_away(n, lambda: products_from(n).wait_recv())
    for n in range(4):
        for g in range(3):
            (weights_q, weights_k, weights_v)[g][:, n * HD:(n + 1) * HD] = from_z[n, :, g * HD:(g + 1) * HD].astype(f32)
    for b in range(8):
        pl.when(me != b)(lambda: norm_from(b).wait_recv())
    sums = [norm_in[b] for b in range(8)]
    norm_sum = ((sums[0] + sums[1]) + (sums[2] + sums[3])) + ((sums[4] + sums[5]) + (sums[6] + sums[7]))
    for t in range(norm_in.shape[1]):
        norm_ref[:, t * 128:(t + 1) * 128] = norm_sum[t:t + 1]

    for i in range(3):
        small_spread_in(i).wait_recv()
        small_spread(i).wait_send()
    small_pair.wait_send()
    for c in range(2):
        first[c].wait_send()
        second[c].wait_send()
        third[c].wait_send()
    for b in range(8):
        pl.when(me != b)(lambda: norm_to(b).wait_send())
    for n in range(4):
        when_away(n, lambda: g_to(n).wait_send())
        g_over(n).wait_send()
        term_pair(n).wait_send()
        pl.when(n > z)(lambda: term_up(n).wait_send())
        pl.when(n < z)(lambda: term_down(n).wait_send())
        when_away(n, lambda: small_along(n).wait_send())
        when_away(n, lambda: rows_to(n).wait_send())
        when_away(n, lambda: products_to(n).wait_send())
        when_away(n, lambda: gains_to(n).wait_send())


def backward_all(ga, segc, segr, qg, kg, small, gain, w, ctx, q, k, v, qr, kr, cosine, sine, wq, wk, wv, a, hidden, middle, number):
    T, D = a.shape
    rows, half = BLOCK, BLOCK // 2
    span = 4 * HD
    S = small.shape[0]
    sd = jax.ShapeDtypeStruct
    dma = pltpu.SemaphoreType.DMA
    vm = pltpu.VMEM
    like = lambda m: vm(m.shape, m.dtype)
    return pl.pallas_call(
        backward_kernel, in_specs=[VM] * 7 + [ANY, VM] + [ANY] * 13, out_specs=[VM] * 8,
        out_shape=[sd((rows, D), f32), sd((BLOCK, span), f32), sd((BLOCK, span), f32), sd((BLOCK, span), f32), sd((1, D), f32), sd((2, span), f32),
                   sd((span, BLOCK), f32), sd((S, D), f32)],
        scratch_shapes=[like(m) for m in (w, q, k, v, qr, kr, cosine, sine, wq, wk, wv)] + [
            vm((4, T, BLOCK), bf16), like(hidden), like(middle),
            vm((8, BLOCK, 3 * HD), bf16), vm((4, BLOCK, HD), bf16), vm((8, BLOCK, HD), bf16), vm((T, HD), f32), vm((T, HD), f32),
            vm((8, span, BLOCK), bf16)] + [vm((4, span, BLOCK), bf16)] * 4 + [
            vm((S, D // 4), f32), vm((S, D // 4), f32), vm((4, S, D // 4), f32),
            vm((4, BLOCK, 3 * HD), bf16), vm((rows, 3 * span), bf16), vm((4, BLOCK, 3 * HD), bf16), vm((4, BLOCK, 3 * HD), bf16)] + [vm((half, D), bf16)] * 4 + [
            vm((rows, D), bf16), vm((2, HD), f32), vm((4, 2, HD), f32), vm((8, D // 128, 128), f32),
            dma((17,)), dma((4,)), dma((4,)), dma((4,)), dma((4,)), dma((3, 4)), dma((3, 4)), dma((8,)), dma((8,)),
            dma((4,)), dma((4,)), dma((4,)), dma((4,)), dma((3, 2)), dma((3, 2)), dma((4,)), dma((4,)), dma((8,)), dma((8,)),
        ],
        compiler_params=pltpu.CompilerParams(collective_id=number, has_side_effects=True, vmem_limit_bytes=60 * 2**20),
    )(ga, segc, segr, qg, kg, small, gain, w, ctx, q, k, v, qr, kr, cosine, sine, wq, wk, wv, a, hidden, middle)


def on_device(
    hidden_in,
    norm1_gain,
    w_query,
    w_key,
    w_value,
    w_out,
    query_gain,
    key_gain,
    norm2_gain,
    w_router,
    w_gate,
    w_up,
    w_down,
    routes,
    segments,
    cotangent,
):
    seq_len, width = hidden_in.shape
    local_width = w_query.shape[1]
    head_count = local_width // HEAD_DIM
    expert_devs = lax.axis_size("expert")
    local_experts = w_gate.shape[0]
    expert_total = w_router.shape[1]
    capacity = 2 * seq_len * TOP // expert_total
    slab_rows = local_experts * capacity
    my_index = lax.axis_index("expert")
    group = SEQ // seq_len
    rank = my_index % group
    f32 = jnp.float32
    bf16 = jnp.bfloat16

    def split_heads(values):
        return values.reshape(seq_len, head_count, HEAD_DIM)

    inputs = hidden_in.astype(f32)
    inverse_attn = inverse_rms(inputs)
    normed_attn = inputs * inverse_attn
    attn_input = (normed_attn * norm1_gain).astype(bf16)
    q_raw = split_heads(jnp.dot(attn_input, w_query, preferred_element_type=f32))
    k_raw = split_heads(jnp.dot(attn_input, w_key, preferred_element_type=f32))
    v_heads = split_heads(jnp.dot(attn_input, w_value, preferred_element_type=f32).astype(bf16))
    q_gains = query_gain.reshape(head_count, HEAD_DIM)
    k_gains = key_gain.reshape(head_count, HEAD_DIM)
    q_inverse = inverse_rms(q_raw)
    q_normed = q_raw * q_inverse
    k_inverse = inverse_rms(k_raw)
    k_normed = k_raw * k_inverse
    local_places = lax.iota(jnp.int32, seq_len)
    query_places = rank * seq_len + local_places
    cosine, sine_part = rope_tables(query_places.astype(f32), HEAD_DIM // 2)
    queries = rotate(q_normed * q_gains, cosine, sine_part, 1.0).astype(bf16)
    key_rot = rotate(k_normed * k_gains, cosine, sine_part, 1.0).astype(bf16)
    score_scale = HEAD_DIM ** (-0.5)
    keys_values = jnp.stack([key_rot, v_heads])
    pieces = [keys_values]
    for offset in range(1, group):
        keys_values = from_behind(keys_values, "expert", 1)
        pieces.append(keys_values)
    stacked = jnp.stack(pieces, 1).reshape(2, group * seq_len, head_count, HEAD_DIM)
    keys_all = stacked[0]
    values_all = stacked[1]
    query_segs = lax.dynamic_slice_in_dim(segments, my_index * seq_len, seq_len, 0)
    key_segs = jnp.concatenate(
        [
            lax.dynamic_slice_in_dim(
                segments, jnp.maximum(my_index - offset, 0) * seq_len, seq_len, 0
            )
            for offset in range(group)
        ],
        0,
    )
    offsets = lax.iota(jnp.int32, group)
    key_places = ((rank - offsets)[:, None] * seq_len + local_places[None, :]).reshape(-1)
    key_valid = jnp.repeat(rank - offsets >= 0, seq_len)
    allowed = (
        key_valid[None, :]
        & (query_places[:, None] >= key_places[None, :])
        & (query_segs[:, None] == key_segs[None, :])
    )

    def scores_of():
        raw_scores = (
            jnp.einsum("thd,shd->hts", queries, keys_all, preferred_element_type=f32) * score_scale
        )
        return jnp.where(allowed[None], raw_scores, MASKED)

    scores = scores_of()
    row_max = jnp.max(scores, -1, keepdims=True)
    raised = jnp.exp(scores - row_max)
    exp_total = jnp.sum(raised, -1, keepdims=True)
    log_total = row_max + jnp.log(exp_total)
    attn_probs = (raised / exp_total).astype(bf16)
    context = (
        jnp.einsum("hts,shd->thd", attn_probs, values_all, preferred_element_type=f32)
        .reshape(seq_len, local_width)
        .astype(bf16)
    )
    attn_part = jnp.dot(context, w_out, preferred_element_type=f32)
    middle = inputs + lax.psum(attn_part, "head")
    inverse_moe = inverse_rms(middle)
    normed_moe = middle * inverse_moe
    moe_input = (normed_moe * norm2_gain).astype(bf16)
    logits = jnp.dot(moe_input, w_router, preferred_element_type=f32)
    chosen = jnp.take_along_axis(logits, routes, 1)
    raised_gate = jnp.exp(chosen - jnp.max(chosen, -1, keepdims=True))
    gate_weights = raised_gate / jnp.sum(raised_gate, -1, keepdims=True)
    catalog = lax.iota(jnp.int32, expert_total)
    route_hot = (routes[:, :, None] == catalog).astype(jnp.int32)
    token_hot = jnp.sum(route_hot, 1, dtype=jnp.int32)
    earlier = jnp.cumsum(token_hot, 0, dtype=jnp.int32) - token_hot
    position = routes * capacity + jnp.take_along_axis(earlier, routes, 1)
    flat_pos = position.reshape(-1)
    owners = (
        jnp.full((expert_total * capacity,), seq_len, jnp.int32)
        .at[flat_pos]
        .set(jnp.repeat(lax.iota(jnp.int32, seq_len), TOP))
    )
    padded = jnp.concatenate([moe_input, jnp.zeros((1, width), bf16)], 0)
    outgoing = padded[owners].reshape(expert_devs, slab_rows, width)
    arrived = lax.all_to_all(outgoing, "expert", split_axis=0, concat_axis=0, tiled=True)
    rows_in = arrived.reshape(expert_devs, local_experts, capacity, width)
    gate_act = jnp.einsum("sjcd,jdf->sjcf", rows_in, w_gate, preferred_element_type=f32)
    up_act = jnp.einsum("sjcd,jdf->sjcf", rows_in, w_up, preferred_element_type=f32)
    hidden = (jax.nn.silu(gate_act) * up_act).astype(bf16)
    partial_out = jnp.einsum("sjcf,jfd->sjcd", hidden, w_down, preferred_element_type=f32).reshape(
        expert_devs, slab_rows, width
    )
    rows_out = (
        lax.psum_scatter(partial_out.astype(jnp.bfloat16), "head", scatter_dimension=2, tiled=True)
        .astype(jnp.float32)
        .astype(bf16)
    )
    leaving = lax.all_gather(rows_out, "head", axis=2, tiled=True)
    returned = lax.all_to_all(leaving, "expert", split_axis=0, concat_axis=0, tiled=True)
    picked = returned.reshape(expert_total * capacity, width)[position]
    moe_out = jnp.einsum("tk,tkd->td", gate_weights, picked, preferred_element_type=f32)
    output = (middle + moe_out).astype(bf16)
    grad_final = cotangent.astype(f32)
    grad_gates = jnp.einsum("td,tkd->tk", grad_final, picked, preferred_element_type=f32)
    grad_chosen = gate_weights * (
        grad_gates - jnp.sum(grad_gates * gate_weights, -1, keepdims=True)
    )
    grad_logits = jnp.einsum("tk,tke->te", grad_chosen, route_hot.astype(f32)).astype(bf16)
    grad_router = jnp.dot(moe_input.T, grad_logits, preferred_element_type=f32)
    grad_moe_input = jnp.dot(grad_logits, w_router.T, preferred_element_type=f32)
    grad_expert_out = (gate_weights[:, :, None] * grad_final[:, None, :]).astype(bf16)
    grad_slab = (
        jnp.zeros((expert_total * capacity, width), bf16)
        .at[flat_pos]
        .set(grad_expert_out.reshape(seq_len * TOP, width))
    )
    grad_slab = grad_slab.reshape(expert_devs, slab_rows, width)
    grad_arrived = lax.all_to_all(grad_slab, "expert", split_axis=0, concat_axis=0, tiled=True)
    grad_rows_out = grad_arrived.reshape(expert_devs, local_experts, capacity, width)
    grad_hidden = jnp.einsum("sjcd,jfd->sjcf", grad_rows_out, w_down, preferred_element_type=f32)
    grad_down = jnp.einsum("sjcf,sjcd->jfd", hidden, grad_rows_out, preferred_element_type=f32)
    sigmoid = jax.nn.sigmoid(gate_act)
    grad_up_act = (grad_hidden * gate_act * sigmoid).astype(bf16)
    grad_gate_act = (grad_hidden * up_act * sigmoid * (1.0 + gate_act * (1.0 - sigmoid))).astype(
        bf16
    )
    grad_gate = jnp.einsum("sjcd,sjcf->jdf", rows_in, grad_gate_act, preferred_element_type=f32)
    grad_up = jnp.einsum("sjcd,sjcf->jdf", rows_in, grad_up_act, preferred_element_type=f32)
    grad_rows_in = jnp.einsum("sjcf,jdf->sjcd", grad_gate_act, w_gate, preferred_element_type=f32)
    grad_rows_in = grad_rows_in + jnp.einsum(
        "sjcf,jdf->sjcd", grad_up_act, w_up, preferred_element_type=f32
    )
    grad_back = (
        lax.psum_scatter(
            grad_rows_in.reshape(expert_devs, slab_rows, width).astype(jnp.bfloat16),
            "head",
            scatter_dimension=2,
            tiled=True,
        )
        .astype(jnp.float32)
        .astype(bf16)
    )
    leaving_grad = lax.all_gather(grad_back, "head", axis=2, tiled=True)
    grad_home = lax.all_to_all(leaving_grad, "expert", split_axis=0, concat_axis=0, tiled=True)
    grad_moe_input = grad_moe_input + jnp.sum(
        grad_home.reshape(expert_total * capacity, width)[position], 1, dtype=f32
    )
    grad_norm2 = jnp.sum(grad_moe_input * normed_moe, 0)
    grad_middle = grad_final + norm_back(grad_moe_input * norm2_gain, normed_moe, inverse_moe)
    grad_attn = grad_middle.astype(bf16)
    grad_out_turned = jnp.dot(grad_attn.T, context, preferred_element_type=f32)
    grad_context = split_heads(jnp.dot(grad_attn, w_out.T, preferred_element_type=f32).astype(bf16))
    attn_full = jnp.exp(scores_of() - log_total)
    attn_low = attn_full.astype(bf16)
    grad_values_all = jnp.einsum("hts,thd->shd", attn_low, grad_context, preferred_element_type=f32)
    grad_probs = jnp.einsum("thd,shd->hts", grad_context, values_all, preferred_element_type=f32)
    grad_scores = (
        attn_full * (grad_probs - jnp.sum(grad_probs * attn_full, -1, keepdims=True))
    ).astype(bf16)
    grad_queries = (
        jnp.einsum("hts,shd->thd", grad_scores, keys_all, preferred_element_type=f32) * score_scale
    )
    grad_keys_all = (
        jnp.einsum("hts,thd->shd", grad_scores, queries, preferred_element_type=f32) * score_scale
    )
    kv_terms = jnp.stack([grad_keys_all, grad_values_all]).reshape(
        2, group, seq_len, head_count, HEAD_DIM
    )
    kv_total = kv_terms[:, 0]
    for offset in range(1, group):
        kv_total = kv_total + from_behind(
            kv_terms[:, offset].astype(jnp.bfloat16), "expert", -offset
        ).astype(jnp.float32)
    grad_keys = kv_total[0]
    grad_values = kv_total[1]
    grad_q_normed = rotate(grad_queries, cosine, sine_part, -1.0)
    grad_k_normed = rotate(grad_keys, cosine, sine_part, -1.0)
    grad_query_gain = jnp.sum(grad_q_normed * q_normed, 0).reshape(local_width)
    grad_key_gain = jnp.sum(grad_k_normed * k_normed, 0).reshape(local_width)
    grad_q_raw = (
        norm_back(grad_q_normed * q_gains, q_normed, q_inverse)
        .reshape(seq_len, local_width)
        .astype(bf16)
    )
    grad_k_raw = (
        norm_back(grad_k_normed * k_gains, k_normed, k_inverse)
        .reshape(seq_len, local_width)
        .astype(bf16)
    )
    grad_v_raw = grad_values.reshape(seq_len, local_width).astype(bf16)
    grad_query = jnp.dot(attn_input.T, grad_q_raw, preferred_element_type=f32)
    grad_key = jnp.dot(attn_input.T, grad_k_raw, preferred_element_type=f32)
    grad_value = jnp.dot(attn_input.T, grad_v_raw, preferred_element_type=f32)
    input_part = jnp.dot(grad_q_raw, w_query.T, preferred_element_type=f32)
    input_part = input_part + jnp.dot(grad_k_raw, w_key.T, preferred_element_type=f32)
    input_part = input_part + jnp.dot(grad_v_raw, w_value.T, preferred_element_type=f32)
    grad_attn_input = lax.psum(input_part.astype(jnp.bfloat16), "head").astype(jnp.float32)
    grad_norm1 = jnp.sum(grad_attn_input * normed_attn, 0)
    grad_input = grad_middle + norm_back(grad_attn_input * norm1_gain, normed_attn, inverse_attn)
    grad_query, grad_key, grad_value, grad_out_turned = (
        lax.psum_scatter(
            grad_query.astype(jnp.bfloat16), "expert", scatter_dimension=0, tiled=True
        ).astype(jnp.float32),
        lax.psum_scatter(
            grad_key.astype(jnp.bfloat16), "expert", scatter_dimension=0, tiled=True
        ).astype(jnp.float32),
        lax.psum_scatter(
            grad_value.astype(jnp.bfloat16), "expert", scatter_dimension=0, tiled=True
        ).astype(jnp.float32),
        lax.psum_scatter(
            grad_out_turned.astype(jnp.bfloat16), "expert", scatter_dimension=0, tiled=True
        ).astype(jnp.float32),
    )
    grad_router, grad_norm1, grad_norm2, grad_query_gain, grad_key_gain = (
        lax.psum(grad_router.astype(jnp.bfloat16), "expert").astype(jnp.float32),
        lax.psum(grad_norm1.astype(jnp.bfloat16), "expert").astype(jnp.float32),
        lax.psum(grad_norm2.astype(jnp.bfloat16), "expert").astype(jnp.float32),
        lax.psum(grad_query_gain.astype(jnp.bfloat16), "expert").astype(jnp.float32),
        lax.psum(grad_key_gain.astype(jnp.bfloat16), "expert").astype(jnp.float32),
    )
    return (
        output,
        grad_input,
        grad_norm1,
        grad_query,
        grad_key,
        grad_value,
        grad_out_turned.T,
        grad_query_gain,
        grad_key_gain,
        grad_norm2,
        grad_router,
        grad_gate,
        grad_up,
        grad_down,
    )


def full_tables(tokens):
    half_dim = HEAD_DIM // 2
    fine_cos, fine_sin = rope_tables(lax.iota(jnp.int32, 64).astype(f32), half_dim)
    coarse = (64 * lax.iota(jnp.int32, tokens // 64)).astype(f32)
    coarse_cos, coarse_sin = rope_tables(coarse, half_dim)
    fine_cos, fine_sin = fine_cos.reshape(1, 64, half_dim), fine_sin.reshape(1, 64, half_dim)
    cosine = (coarse_cos * fine_cos - coarse_sin * fine_sin).reshape(tokens, half_dim)
    sine = (coarse_sin * fine_cos + coarse_cos * fine_sin).reshape(tokens, half_dim)
    return jnp.concatenate([cosine, cosine], 1), jnp.concatenate([-sine, sine], 1)


def dense_layer(
    hidden_in, norm1_gain, w_query, w_key, w_value, w_out, query_gain, key_gain, norm2_gain, w_router,
    w_gate, w_up, w_down, routes, segments, cotangent,
):
    rows, width = hidden_in.shape
    experts = w_router.shape[1]
    devices = lax.axis_size("expert")
    tokens = devices * rows

    cosine, sine = full_tables(tokens)
    segc, segr = segments[:, None], segments[None]
    own_mask = jnp.sum((routes[:, :, None] == lax.iota(jnp.int32, experts)).astype(f32), 1)
    sent = jnp.concatenate([cotangent, jnp.pad(own_mask.astype(bf16), ((0, 0), (0, 128 - experts)))], 1)
    own_context, middle, moe_input, _, attn_all, queries, keys, values, q_raw, k_raw, grads_all, everyone, weighted, grad_acts, parts = (
        forward_all(
            hidden_in, sent, norm1_gain[None], norm2_gain[None], query_gain[None], key_gain[None], segc, segr, w_router,
            w_query, w_key, w_value, cosine, sine, w_out, w_gate, w_up, w_down, 1,
        )
    )
    inverse_moe = inverse_rms(middle)
    normed_moe = middle * inverse_moe
    total, grad_gate, grad_up, grad_down = sums_all(
        parts.reshape(devices, rows, 2 * width + 128), everyone, grad_acts, grads_all, weighted, 2
    )
    output = (middle + total[:, :width].astype(f32)).astype(bf16)
    grad_final = cotangent.astype(f32)
    tail = total[:, 2 * width :].astype(f32)
    grad_gates = tail[:, :experts] + tail[:, experts : 2 * experts]
    logits = jnp.where(
        own_mask > 0, jnp.dot(moe_input, w_router, preferred_element_type=f32), -jnp.inf
    )
    raised_gate = jnp.exp(logits - jnp.max(logits, -1, keepdims=True))
    gate_weights = raised_gate / jnp.sum(raised_gate, -1, keepdims=True)
    grad_logits = (
        gate_weights * (grad_gates - jnp.sum(grad_gates * gate_weights, -1, keepdims=True))
    ).astype(bf16)
    grad_moe_input = jnp.dot(grad_logits, w_router.T, preferred_element_type=f32)
    grad_moe_input = grad_moe_input + total[:, width : 2 * width].astype(f32)
    grad_middle = grad_final + norm_back(grad_moe_input * norm2_gain, normed_moe, inverse_moe)
    small = jnp.concatenate(
        [
            lax.dot_general(grad_logits, moe_input, (((0,), (0,)), ((), ())), preferred_element_type=f32),
            jnp.sum(grad_moe_input * normed_moe, 0, keepdims=True),
            jnp.zeros((7, width), f32),
        ],
        0,
    )

    grad_input, grad_query, grad_key, grad_value, grad_norm1, gains, grad_w_out, small = backward_all(
        grad_middle.astype(bf16), segc, segr, query_gain[None], key_gain[None], small, norm1_gain[None], w_out, own_context,
        queries, keys, values, q_raw, k_raw, cosine, sine, w_query, w_key, w_value, attn_all, hidden_in, grad_middle, 3,
    )
    return (
        output,
        grad_input,
        grad_norm1[0],
        grad_query,
        grad_key,
        grad_value,
        grad_w_out,
        gains[0],
        gains[1],
        small[experts],
        small[:experts].T,
        grad_gate,
        grad_up,
        grad_down,
    )


def layer(*arrays):
    rows, experts = arrays[0].shape[0], arrays[9].shape[1]
    whole = 2 * rows * TOP // experts >= rows and rows * lax.axis_size("expert") == SEQ
    grid = (lax.axis_size("expert"), lax.axis_size("head")) == (8, 4)
    return dense_layer(*arrays) if whole and grid else on_device(*arrays)


def solution(mesh):
    return jax.shard_map(
        layer,
        mesh=mesh,
        in_specs=(
            P("expert", None),
            P(),
            P(None, "head"),
            P(None, "head"),
            P(None, "head"),
            P("head", None),
            P("head"),
            P("head"),
            P(),
            P(),
            P("expert", None, "head"),
            P("expert", None, "head"),
            P("expert", "head", None),
            P("expert", None),
            P(),
            P("expert", None),
        ),
        out_specs=(
            P("expert", None),
            P("expert", None),
            P(),
            P("expert", "head"),
            P("expert", "head"),
            P("expert", "head"),
            P("head", "expert"),
            P("head"),
            P("head"),
            P(),
            P(),
            P("expert", None, "head"),
            P("expert", None, "head"),
            P("expert", "head", None),
        ),
        check_vma=False,
    )
```

```python
import functools

import jax
import jax.numpy as jnp
from jax import lax
from jax.experimental import pallas as pl
from jax.experimental.pallas import tpu as pltpu
from jax.sharding import PartitionSpec as P

HEAD_DIM = 128
TOP = 8
SEQ = 2048
MESH = pl.DeviceIdType.MESH
bf16 = jnp.bfloat16
f32 = jnp.float32


EPSILON = 1e-05
ROPE_BASE = 10000.0
MASKED = -1000000000.0


def from_behind(shard, axis, by):
    size = lax.axis_size(axis)
    pairs = [(i, i + by) for i in range(size) if 0 <= i + by < size]
    return lax.ppermute(shard, axis, pairs)


def inverse_rms(values):
    return lax.rsqrt(jnp.mean(values * values, -1, keepdims=True) + EPSILON)


def norm_back(grad_normed, normed, inverse):
    return inverse * (grad_normed - normed * jnp.mean(grad_normed * normed, -1, keepdims=True))


def rope_tables(places, half_dim):
    inv_freq = ROPE_BASE ** (-lax.iota(jnp.int32, half_dim).astype(jnp.float32) / half_dim)
    angles = places[:, None] * inv_freq[None, :]
    return (jnp.cos(angles)[:, None, :], jnp.sin(angles)[:, None, :])


def rotate(values, cosine, sine_part, direction):
    half_dim = values.shape[-1] // 2
    first_half = values[..., :half_dim]
    second_half = values[..., half_dim:]
    turned = direction * sine_part
    return jnp.concatenate(
        [first_half * cosine - second_half * turned, second_half * cosine + first_half * turned], -1
    )


def place():
    block = lax.axis_index("expert")
    lane = lax.axis_index("head")
    return block // 2, block % 2, lane // 2, lane % 2


def device(z, y, x, core):
    return (z * 2 + y, x * 2 + core)


def greet(z, y, x, core):
    barrier = pltpu.get_barrier_semaphore()

    def signal(target):
        pl.semaphore_signal(barrier, inc=1, device_id=target, device_id_type=MESH)

    signal(device(z, 1 - y, x, core))
    signal(device(z, y, 1 - x, core))
    signal(device(z, y, x, 1 - core))

    @pl.when(z > 0)
    def _():
        signal(device(z - 1, y, x, core))

    @pl.when(z < 3)
    def _():
        signal(device(z + 1, y, x, core))

    pl.semaphore_wait(barrier, 3 + (z > 0).astype(jnp.int32) + (z < 3).astype(jnp.int32))


def add_split(a, b):
    pair = a.astype(f32) + b.astype(f32)
    lanes = lax.broadcasted_iota(jnp.int32, pair.shape, 1)
    whole = jnp.where(lanes < 16, pair + pltpu.roll(pair, 112, 1), 0.0)
    high = whole.astype(bf16).astype(f32)
    return (high + pltpu.roll(whole - high, 16, 1)).astype(bf16)


def dot(a,b): return jnp.dot(a,b,preferred_element_type=f32)
def dot_nt(a,b): return lax.dot_general(a,b,(((1,),(1,)),((),())),preferred_element_type=f32)
def dot_tn(a,b): return lax.dot_general(a,b,(((0,),(0,)),((),())),preferred_element_type=f32)


EPS = 1e-05
HD = 128
BLOCK = 256


def block_of(r, parity):
    return 2 * r + (parity if r % 2 == 0 else 1 - parity)


def norm_factor(v):
    return lax.rsqrt(jnp.mean(v * v, -1, keepdims=True) + EPS)


def probabilities(r, start, q, k_ref, segc_ref, segr_ref):
    keys = (2 * r + 2) * BLOCK
    scores = dot_nt(q, k_ref[:keys]) * (HD ** -0.5)
    rows = start + lax.broadcasted_iota(jnp.int32, scores.shape, 0)
    columns = lax.broadcasted_iota(jnp.int32, scores.shape, 1)
    same = segc_ref[pl.ds(start, BLOCK)] == segr_ref[:, :keys]
    scores = jnp.where((rows >= columns) & same, scores, -1000000000.0)
    raised = jnp.exp(scores - jnp.max(scores, -1, keepdims=True))
    return raised / jnp.sum(raised, -1, keepdims=True)


VM = pl.BlockSpec(memory_space=pltpu.VMEM)


def masked_probs(b, q, k_ref, segc_ref, segr_ref):
    keys = (b + 1) * BLOCK
    scores = dot_nt(q, k_ref[:keys]) * (HD ** -0.5)
    rows = b * BLOCK + lax.broadcasted_iota(jnp.int32, scores.shape, 0)
    columns = lax.broadcasted_iota(jnp.int32, scores.shape, 1)
    same = segc_ref[b * BLOCK:keys] == segr_ref[:, :keys]
    scores = jnp.where((rows >= columns) & same, scores, -1000000000.0)
    raised = jnp.exp(scores - jnp.max(scores, -1, keepdims=True))
    return raised / jnp.sum(raised, -1, keepdims=True)


def far_first(z):
    ahead = z // 2
    return (3 - 3 * ahead, 2 - ahead, z + 1 - 2 * (z % 2), z)


def greet_peers(z, y, x, core, others):
    barrier = pltpu.get_barrier_semaphore()

    def signal(where):
        pl.semaphore_signal(barrier, inc=1, device_id=where, device_id_type=MESH)

    for n in range(4):
        pl.when(z != n)(lambda: signal(device(n, y, x, core)))
        pl.when(z != n)(lambda: signal(device(n, 1 - y, x, core)))
    signal(device(z, 1 - y, x, core))
    for where in others:
        signal(where)
    pl.semaphore_wait(barrier, 7 + len(others))


def picked(i, values):
    if isinstance(i, int):
        return values[i]
    return sum((i == k).astype(jnp.int32) * v for k, v in enumerate(values))


class Gather:
    def __init__(self, own, whole, local_sem, send, recv, lone=2, rows=BLOCK):
        self.own, self.whole, self.send, self.recv, self.rows = own, whole, send, recv, rows
        z, y, x, core = self.place = place()
        self.me = z * 2 + y
        half, eighth = rows // 2, rows // 8
        self.unit = eighth // 2
        lone, lead = lone * self.unit, 3 * self.unit
        self.keep = pltpu.make_async_copy(own, self.at(self.me, 0, rows), local_sem)

        def chunks(c):
            return ((c * half + x * (half - lead), lead), (c * half + (1 - x) * lead + x * lone, half - lead - lone))

        def edge(c, of):
            return (c * half + of * (half - lone), lone)

        self.slab, self.twin_slab = chunks(core), chunks(1 - core)
        self.mine, self.theirs = edge(core, x), edge(core, 1 - x)
        self.twin_theirs = edge(1 - core, 1 - x)

    def at(self, b, start, size):
        return self.whole.at[pl.ds(pl.multiple_of(b * self.rows + start, self.unit), size)]

    def copy(self, first, c, index, b, part, where, own=False):
        if own:
            source = self.own.at[pl.ds(pl.multiple_of(part[0], self.unit), part[1])]
        else:
            source = self.at(b, *part)
        return pltpu.make_async_remote_copy(
            src_ref=source, dst_ref=self.at(b, *part), send_sem=self.send.at[first + index], recv_sem=self.recv.at[first + index],
            device_id=where, device_id_type=MESH)

    def up(self, b, c, own=False):
        z, y, x, core = self.place
        return self.copy(0, c, c * 4 + b // 2, b, self.slab[c], device(z + 1, y, x, core), own)

    def down(self, b, c, own=False):
        z, y, x, core = self.place
        return self.copy(8, c, c * 4 + b // 2, b, self.slab[c], device(z - 1, y, x, core), own)

    def over(self, b, c, own=False):
        z, y, x, core = self.place
        return self.copy(16, c, c * 4 + b // 2, b, self.slab[c], device(z, 1 - y, x, core), own)

    def side(self, b, part):
        z, y, x, core = self.place
        return self.copy(24, 0, b, b, part, device(z, y, 1 - x, core))

    def twin(self, b, c, part):
        z, y, x, core = self.place
        return self.copy(32, c, c * 8 + b, b, part, device(z, y, x, 1 - core))

    def twin_x(self, b, part):
        z, y, x, core = self.place
        return self.copy(48, 0, b, b, part, device(z, y, x, 1 - core))

    def group(self, i):
        z = self.place[0]
        ahead = z // 2
        return picked(i, (z, z + 1 - 2 * (z % 2), 2 - ahead, 3 - 3 * ahead))

    def start_chunk(self, c):
        z, y, x, core = self.place
        pl.when(z < 3)(lambda: self.up(self.me, c, True).start())
        pl.when(z > 0)(lambda: self.down(self.me, c, True).start())
        self.over(self.me, c, True).start()

    def start(self):
        self.start_chunk(0)
        self.start_chunk(1)
        self.keep.start()

    def spread(self, b, c):
        if c == 0:
            self.side(b, self.mine).start()
        self.twin(b, c, self.slab[c]).start()

    def hop(self, i):
        z, y, x, core = self.place
        b = self.group(i) * 2 + y
        below = picked(i, (0, z % 2, z // 2, z // 2)) == 1
        for c in range(2):
            @pl.when(below)
            def _():
                self.up(b, c).wait_recv()
                pl.when(z < 3)(lambda: self.up(b, c).start())

            @pl.when(jnp.logical_not(below))
            def _():
                self.down(b, c).wait_recv()
                pl.when(z > 0)(lambda: self.down(b, c).start())

            self.over(b, c).start()
            self.spread(b, c)

    def hop_inside(self, i):
        z = self.place[0]
        pl.when((z > 0) & (z < 3))(lambda: self.hop(i))

    def hop_outside(self, i):
        z = self.place[0]
        pl.when(z % 3 == 0)(lambda: self.hop(i))

    def cross(self, i):
        b = self.group(i) * 2 + 1 - self.place[1]
        for c in range(2):
            self.over(b, c).wait_recv()
            self.spread(b, c)

    def blocks(self, i, act):
        y = self.place[1]
        n = self.group(i)
        act(n * 2 + 1 - y)
        if isinstance(i, int):
            if i > 0:
                act(n * 2 + y)
        else:
            pl.when(i > 0)(lambda: act(n * 2 + y))

    def flank(self, i):
        def act(b):
            self.side(b, self.theirs).wait_recv()
            self.twin_x(b, self.theirs).start()
        self.blocks(i, act)

    def complete(self, i):
        def act(b):
            for c in range(2):
                self.twin(b, c, self.twin_slab[c]).wait_recv()
            self.twin_x(b, self.twin_theirs).wait_recv()
        self.blocks(i, act)

    def drain(self):
        z, y, x, core = self.place
        for b in range(8):
            zb, yb = b // 2, b % 2

            @pl.when(self.me != b)
            def _():
                self.side(b, self.mine).wait_send()
                self.twin_x(b, self.theirs).wait_send()

            for c in range(2):
                pl.when(self.me != b)(lambda: self.twin(b, c, self.slab[c]).wait_send())
                pl.when(yb == y)(lambda: self.over(b, c).wait_send())
                pl.when((yb == y) & (zb <= z) & (z < 3))(lambda: self.up(b, c).wait_send())
                pl.when((yb == y) & (zb >= z) & (z > 0))(lambda: self.down(b, c).wait_send())

    def whole_run(self):
        self.start()
        self.hop(1)
        self.cross(0)
        self.hop_inside(2)
        self.flank(0)
        self.hop_outside(2)
        self.cross(1)
        self.hop_inside(3)
        self.flank(1)
        self.hop_outside(3)
        self.cross(2)
        self.cross(3)
        self.flank(2)
        self.flank(3)
        for i in range(4):
            self.complete(i)
        self.keep.wait()
        self.drain()


GATHER_SEMS = [pltpu.SemaphoreType.DMA, pltpu.SemaphoreType.DMA((56,)), pltpu.SemaphoreType.DMA((56,))]


ANY = pl.BlockSpec(memory_space=pl.ANY)


def sum_rows(target, source, rows):
    step = 32
    width = target.shape[-1]
    main = width - width % 1024

    @pl.loop(0, rows // step)
    def _(i):
        part = pl.ds(pl.multiple_of(i * step, step), step)
        wide = pl.ds(0, main)
        target[part, wide] = (target[part, wide].astype(f32) + source[part, wide].astype(f32)).astype(bf16)
        if main < width:
            tail = pl.ds(main, width - main)
            target[part, tail] = add_split(target[part, tail], source[part, tail])


class Scatter:
    def __init__(self, parts, start, total, buffers, sems):
        self.parts, self.total = parts, total
        self.cols = pl.ds(start, total.shape[1])
        self.held, self.from_core, self.from_x, self.from_y, self.from_below, self.from_above, self.shared_in = buffers
        self.load_sem, self.sems, self.recv_sems, self.end_send, self.end_recv = sems
        z, y, x, core = self.place = place()
        self.me = z * 2 + y
        self.order = far_first(z)
        self.half = half = parts.shape[1] // 2
        self.piece = piece = half // 4
        ds = lambda start, size: pl.ds(pl.multiple_of(start, piece), size)
        self.my_half, self.other_half = ds(core * half, half), ds((1 - core) * half, half)
        self.slab, self.mine, self.theirs = ds(x * piece, 3 * piece), ds(x * 3 * piece, piece), ds((1 - x) * 3 * piece, piece)
        self.shared = pl.ds(piece, 2 * piece)
        base = core * half
        self.out_mine, self.out_theirs = ds(base + x * 3 * piece, piece), ds(base + (1 - x) * 3 * piece, piece)
        self.out_shared = ds(base + piece, 2 * piece)
        self.across, self.twin = device(z, y, 1 - x, core), device(z, y, x, 1 - core)

    def remote(self, number, source, target, where):
        return pltpu.make_async_remote_copy(
            src_ref=source, dst_ref=target, send_sem=self.sems.at[number], recv_sem=self.recv_sems.at[number],
            device_id=where, device_id_type=MESH)

    def load(self, b):
        return pltpu.make_async_copy(self.parts.at[b, self.my_half, self.cols], self.held.at[b], self.load_sem.at[b])

    def to_core(self, b):
        return self.remote(b, self.parts.at[b, self.other_half, self.cols], self.from_core.at[b], self.twin)

    def to_x(self, b):
        return self.remote(8 + b, self.held.at[b, self.theirs], self.from_x.at[b], self.across)

    def to_y(self, zb):
        z, y, x, core = self.place
        return self.remote(16 + zb, self.held.at[zb * 2 + 1 - y, self.slab], self.from_y.at[zb], device(z, 1 - y, x, core))

    def to_above(self, zb):
        z, y, x, core = self.place
        return self.remote(20 + zb, self.held.at[zb * 2 + y, self.slab], self.from_below.at[zb], device(z + 1, y, x, core))

    def to_below(self, zb):
        z, y, x, core = self.place
        return self.remote(24 + zb, self.held.at[zb * 2 + y, self.slab], self.from_above.at[zb], device(z - 1, y, x, core))

    def begin(self, k):
        y = self.place[1]
        for yb in (1 - y, y):
            self.load(self.order[k] * 2 + yb).start()
            self.to_core(self.order[k] * 2 + yb).start()

    def stage_core(self, k, other):
        y = self.place[1]
        b = self.order[k] * 2 + (1 - y if other else y)
        self.load(b).wait()
        self.to_core(b).wait_recv()
        sum_rows(self.held.at[b], self.from_core.at[b], self.half)
        self.to_x(b).start()

    def stage_x(self, k, other=False):
        y = self.place[1]
        b = self.order[k] * 2 + (1 - y if other else y)
        self.to_x(b).wait_recv()
        sum_rows(self.held.at[b, self.mine], self.from_x.at[b], self.piece)

    def stage_y(self, k):
        self.stage_x(k, True)
        self.to_y(self.order[k]).start()

    def add_slab(self, zb, source):
        sum_rows(self.held.at[zb * 2 + self.place[1], self.slab], source.at[zb], 3 * self.piece)

    def stage_z(self, k):
        z = self.place[0]
        zb = self.order[k]
        self.to_y(zb).wait_recv()
        self.add_slab(zb, self.from_y)
        rises = (z // 2 == 0) if k < 2 else (z % 2 == 0)

        @pl.when(rises)
        def _():
            @pl.when(z > 0)
            def _():
                self.to_above(zb).wait_recv()
                self.add_slab(zb, self.from_below)
            self.to_above(zb).start()

        @pl.when(jnp.logical_not(rises))
        def _():
            @pl.when(z < 3)
            def _():
                self.to_below(zb).wait_recv()
                self.add_slab(zb, self.from_above)
            self.to_below(zb).start()

    def at_end(self, number, source, target, where):
        return pltpu.make_async_remote_copy(
            src_ref=source, dst_ref=target, send_sem=self.end_send.at[number], recv_sem=self.end_recv.at[number],
            device_id=where, device_id_type=MESH)

    def end_sums(self):
        return self.at_end(0, self.held.at[self.me, self.shared], self.shared_in, self.across)

    def end_ready(self, rows):
        return self.at_end(1, self.held.at[self.me, self.mine], self.total.at[rows], self.across)

    def end_twin(self, rows):
        return self.at_end(2, self.total.at[self.my_half], self.total.at[rows], self.twin)

    def own_sum(self):
        z = self.place[0]
        self.to_y(z).wait_recv()
        self.add_slab(z, self.from_y)

        @pl.when(z > 0)
        def _():
            self.to_above(z).wait_recv()
            self.add_slab(z, self.from_below)

        @pl.when(z < 3)
        def _():
            self.to_below(z).wait_recv()
            self.add_slab(z, self.from_above)
        self.end_sums().start()
        self.end_ready(self.out_mine).start()
        self.total[self.out_mine] = self.held[self.me, self.mine]

    def own_end(self):
        self.end_sums().wait()
        sum_rows(self.held.at[self.me, self.shared], self.shared_in, 2 * self.piece)
        self.total[self.out_shared] = self.held[self.me, self.shared]
        self.end_ready(self.out_theirs).wait_recv()
        self.end_twin(self.my_half).start()

    def finish(self):
        z = self.place[0]
        self.end_twin(self.other_half).wait_recv()
        self.end_ready(self.out_mine).wait_send()
        self.end_twin(self.my_half).wait_send()
        for b in range(8):
            self.to_core(b).wait_send()
            self.to_x(b).wait_send()
        for zb in range(4):
            self.to_y(zb).wait_send()
            pl.when(zb > z)(lambda: self.to_above(zb).wait_send())
            pl.when(zb < z)(lambda: self.to_below(zb).wait_send())


def scatter_buffers(rows, width):
    half, piece = rows // 2, rows // 8
    vm = pltpu.VMEM
    return [vm((8, half, width), bf16), vm((8, half, width), bf16), vm((8, piece, width), bf16)] + [
        vm((4, 3 * piece, width), bf16)] * 3 + [vm((2 * piece, width), bf16)]


SCATTER_SEMS = [pltpu.SemaphoreType.DMA((n,)) for n in (8, 28, 28, 3, 3)]


def sums_kernel(parts, x_ref, acts_ref, grads_ref, weighted_ref, total_a, total_b, gate_out, up_out, down_out, *rest):
    buffers_a, buffers_b, rest = rest[:7], rest[7:14], rest[14:]
    acts, weighted, x_buf, g_buf, gu_buf, down_buf = rest[:6]
    sems_a, sems_b, rest = rest[6:11], rest[11:16], rest[16:]
    fixed_sem, x_sem, g_sem, gu_sem, down_sem = rest
    z, y, x, core = place()
    D = x_ref.shape[1]
    sums = (Scatter(parts, D + total_a.shape[1], total_b, buffers_b, sems_b), Scatter(parts, D, total_a, buffers_a, sems_a))

    fixed = [pltpu.make_async_copy(acts_ref, acts, fixed_sem.at[0]), pltpu.make_async_copy(weighted_ref, weighted, fixed_sem.at[1])]
    ff = weighted.shape[1] // 2
    x_pieces, g_pieces = D // BLOCK, D // 512

    def x_load(k):
        return pltpu.make_async_copy(x_ref.at[:, pl.ds(k * BLOCK, BLOCK)], x_buf.at[k % 2], x_sem.at[k % 2])

    def g_load(k):
        return pltpu.make_async_copy(grads_ref.at[:, pl.ds(k * 512, 512)], g_buf.at[k % 2], g_sem.at[k % 2])

    def gu_store(k):
        rows = pl.ds(k * BLOCK, BLOCK)
        return [pltpu.make_async_copy(gu_buf.at[k % 2, u, j], (gate_out, up_out)[u].at[j, rows], gu_sem.at[k % 2, u, j])
                for u in range(2) for j in range(2)]

    def down_store(k):
        return [pltpu.make_async_copy(down_buf.at[k % 2, j], down_out.at[j, :, pl.ds(k * 512, 512)], down_sem.at[k % 2, j])
                for j in range(2)]

    def x_piece(k):
        if k == 0:
            fixed[0].wait()
        x_load(k).wait()
        if k >= 2:
            for copy in gu_store(k - 2):
                copy.wait()
        both = dot_tn(x_buf[k % 2], acts[...])
        for j in range(2):
            for u in range(2):
                gu_buf[k % 2, u, j] = both[:, (2 * j + u) * ff:(2 * j + u + 1) * ff]
        for copy in gu_store(k):
            copy.start()
        if k + 2 < x_pieces:
            x_load(k + 2).start()

    def g_piece(k):
        if k == 0:
            fixed[1].wait()
        g_load(k).wait()
        if k >= 2:
            for copy in down_store(k - 2):
                copy.wait()
        both = dot_tn(weighted[...], g_buf[k % 2])
        for j in range(2):
            down_buf[k % 2, j] = both[j * ff:(j + 1) * ff]
        for copy in down_store(k):
            copy.start()
        if k + 2 < g_pieces:
            g_load(k + 2).start()

    fillers = [functools.partial(x_piece, k) for k in range(x_pieces)]
    for k in range(g_pieces):
        fillers.insert(3 * k + 2, functools.partial(g_piece, k))

    greet(z, y, x, core)
    for k in range(4):
        for s in sums:
            s.begin(k)
        if k == 0:
            for copy in fixed:
                copy.start()
            for j in range(2):
                x_load(j).start()
                g_load(j).start()
    items = [(k, s) for k in range(4) for s in sums]
    for other in (True, False):
        sums[0].stage_core(0, other)
    for i, (k, s) in enumerate(items):
        if i < 7:
            items[i + 1][1].stage_core(items[i + 1][0], True)
        s.stage_y(k)
        if i < 7:
            items[i + 1][1].stage_core(items[i + 1][0], False)
        s.stage_x(k)
        if 0 < i < 7:
            items[i - 1][1].stage_z(items[i - 1][0])
        if i < 7:
            for fill in fillers[2 * i:2 * i + 2]:
                fill()
    for fill in fillers[14:]:
        fill()
    for s in sums:
        s.own_sum()
    for s in sums:
        s.own_end()
    for s in sums:
        s.finish()
    for k in (x_pieces - 2, x_pieces - 1):
        for copy in gu_store(k):
            copy.wait()
    for k in (g_pieces - 2, g_pieces - 1):
        for copy in down_store(k):
            copy.wait()


def sums_all(parts, x, acts, grads, weighted, number):
    _, rows, width = parts.shape
    T, D = x.shape
    ff = weighted.shape[1] // 2
    widths = (D // 2, D // 2 + 128)
    sd = jax.ShapeDtypeStruct
    dma = pltpu.SemaphoreType.DMA
    vm = pltpu.VMEM
    return pl.pallas_call(
        sums_kernel, in_specs=[ANY] * 5, out_specs=[VM, VM, ANY, ANY, ANY],
        out_shape=[sd((rows, w), bf16) for w in widths] + [sd((2, D, ff), f32), sd((2, D, ff), f32), sd((2, ff, D), f32)],
        scratch_shapes=scatter_buffers(rows, widths[0]) + scatter_buffers(rows, widths[1]) + [
            vm(acts.shape, bf16), vm(weighted.shape, bf16), vm((2, T, BLOCK), bf16), vm((2, T, 512), bf16),
            vm((2, 2, 2, BLOCK, ff), f32), vm((2, 2, ff, 512), f32)] + SCATTER_SEMS * 2 + [
            dma((2,)), dma((2,)), dma((2,)), dma((2, 2, 2)), dma((2, 2))],
        compiler_params=pltpu.CompilerParams(collective_id=number, has_side_effects=True, vmem_limit_bytes=62 * 2**20),
    )(parts, x, acts, grads, weighted)


def forward_kernel(hidden, sent_ref, gain1_ref, gain2_ref, qg_ref, kg_ref, segc_ref, segr_ref, wr_ref,
                   wq_in, wk_in, wv_in, cos_in, sin_in, wout_in, wg_in, wu_in, wd_in,
                   gathered, middle_out, moe_out, x_all, a_out, q_out, k_out, v_out, qr_out, kr_out, grads_all,
                   m_out, weighted_out, acts_out, parts_out,
                   w_qkv, cos_ref, sin_ref, w_out, wg, wu, wd, q_ref, k_ref, v_ref, qr_ref, kr_ref,
                   part, arrived, out_half, in_half, held, from_x, total, middle_ref, moe, whole, mask_all, w_buf, a_buf, p_buf,
                   x_keep, x_send, x_recv, c_keep, c_send, c_recv, m_keep, m_send, m_recv,
                   load, stream, out_sem, kept_sem, send, recv, pair_send, pair_recv):
    z, y, x, core = place()
    across, twin = device(z, y, 1 - x, core), device(z, y, x, 1 - core)
    first_expert = (z * 2 + y) * wg_in.shape[0]
    D, ff = wg_in.shape[1], wg_in.shape[2]
    span = 2 * BLOCK
    head = pl.ds(pl.multiple_of(z * HD, HD), HD)
    loads = [pltpu.make_async_copy(source, target, load.at[k]) for k, (source, target) in enumerate((
        (wq_in.at[:, head], w_qkv.at[:, pl.ds(0, HD)]), (wk_in.at[:, head], w_qkv.at[:, pl.ds(HD, HD)]),
        (wv_in.at[:, head], w_qkv.at[:, pl.ds(2 * HD, HD)]), (cos_in, cos_ref), (sin_in, sin_ref),
        (wout_in, w_out), (wd_in, wd), (wg_in, wg), (wu_in, wu)))]
    for copy in loads:
        copy.start()
    greet_peers(z, y, x, core, (across, twin))
    gather = Gather(hidden, x_all, x_keep, x_send, x_recv, 3)
    cot = Gather(sent_ref, grads_all, c_keep, c_send, c_recv)
    experts = Gather(moe, whole, m_keep, m_send, m_recv)

    def remote(source, target, ssem, rsem, where):
        return pltpu.make_async_remote_copy(
            src_ref=source, dst_ref=target, send_sem=ssem, recv_sem=rsem, device_id=where, device_id_type=MESH)

    gather.start()
    gather.hop(1)
    gather.cross(0)
    gather.hop_inside(2)
    gather.flank(0)
    gather.keep.wait()
    for copy in loads[:5]:
        copy.wait()

    def rows_of(i):
        return pl.ds(pl.multiple_of(gather.group(i) * span, span), span)

    x_part, a_part = p_buf.at[:, pl.ds(0, D)], p_buf.at[:, pl.ds(D, D)]

    def a_store(i):
        return pltpu.make_async_copy(a_part, a_out.at[rows_of(i)], stream.at[1])

    def project(i):
        gather.complete(i)
        rows = rows_of(i)
        fetch = pltpu.make_async_copy(x_all.at[rows], x_part, stream.at[0])
        fetch.start()
        if i > 0:
            a_store(i - 1).wait()
        fetch.wait()
        v = p_buf[:, :D].astype(f32)
        a = (v * norm_factor(v) * gain1_ref[...]).astype(bf16)
        p_buf[:, D:2 * D] = a
        a_store(i).start()
        raw = dot(a, w_qkv[...])
        cosine, sine = cos_ref[rows], sin_ref[rows]

        def turned(part, gain):
            n = part * norm_factor(part) * gain
            return (n * cosine + pltpu.roll(n, HD // 2, 1) * sine).astype(bf16)

        q_raw, k_raw = raw[:, :HD], raw[:, HD:2 * HD]
        qr_ref[rows] = q_raw
        kr_ref[rows] = k_raw
        q_ref[rows] = turned(q_raw, qg_ref[:, head])
        k_ref[rows] = turned(k_raw, kg_ref[:, head])
        v_ref[rows] = raw[:, 2 * HD:].astype(bf16)

    for i in range(4):
        if i < 2:
            gather.hop_outside(i + 2)
        if i < 3:
            gather.cross(i + 1)
        if i == 0:
            gather.hop_inside(3)
        if i == 1:
            cot.start()
        project(i)
        if i < 3:
            gather.flank(i + 1)
    a_store(3).wait()
    keeps = [pltpu.make_async_copy(source, target, kept_sem.at[k]) for k, (source, target) in enumerate((
        (q_ref, q_out), (k_ref, k_out), (v_ref, v_out), (qr_ref, qr_out), (kr_ref, kr_out),
        (middle_ref, middle_out), (moe, moe_out)))]
    for copy in keeps[:5]:
        copy.start()
    cot.hop(1)
    cot.cross(0)
    cot.hop_inside(2)

    targets = lambda r: (y if r % 2 == 0 else 1 - y)
    source_y = (y + z) % 2

    def to_block(r):
        return remote(part.at[r], arrived.at[z], send.at[r], recv.at[z], device(r, targets(r), x, core))

    def from_head(n):
        return remote(part.at[n], arrived.at[n], send.at[n], recv.at[n], device(n, source_y, x, core))

    here = lambda r: (z == r) & (z % 2 == 0)
    for r in range(3, -1, -1):
        start = pl.multiple_of(block_of(r, y) * BLOCK, BLOCK)
        probs = probabilities(r, start, q_ref[pl.ds(start, BLOCK)], k_ref, segc_ref, segr_ref)
        part[r] = dot(probs.astype(bf16), v_ref[:(2 * r + 2) * BLOCK]).astype(bf16)
        pl.when(jnp.logical_not(here(r)))(lambda: to_block(r).start())
    cot.flank(0)

    @pl.when(z % 2 == 0)
    def _():
        arrived[z] = part[z]

    loads[5].wait()
    for n in range(4):
        pl.when(jnp.logical_not(here(n)))(lambda: from_head(n).wait_recv())
        gathered[:, n * HD:(n + 1) * HD] = arrived[n]
    cot.hop_outside(2)
    cot.cross(1)
    cot.hop_inside(3)

    half = BLOCK // 2
    chunk = half // 2
    my_half = core * half
    other_half = (1 - core) * half
    piece = lambda c: pl.ds(pl.multiple_of(c * chunk, chunk), chunk)
    at = lambda base, c: pl.ds(pl.multiple_of(base + c * chunk, chunk), chunk)

    def pair(kind, c, source, target, where):
        return remote(source, target, pair_send.at[kind, c], pair_recv.at[kind, c], where)

    first = lambda c: pair(0, c, out_half.at[piece(c)], in_half.at[piece(c)], twin)
    second = lambda c: pair(1, c, held.at[piece(c)], from_x.at[piece(c)], across)
    third = lambda c: pair(2, c, total.at[at(my_half, c)], total.at[at(my_half, c)], twin)
    for c in (1 - x, x):
        out_half[piece(c)] = dot(gathered[at(other_half, c)], w_out[...]).astype(bf16)
        first(c).start()
    for c in (1 - x, x):
        kept = dot(gathered[at(my_half, c)], w_out[...])
        first(c).wait_recv()
        held[piece(c)] = (kept + in_half[piece(c)].astype(f32)).astype(bf16)
        second(c).start()
    cot.flank(1)
    step = 32

    def norm_rows(base, count):
        def body(i, _):
            rows = pl.ds(pl.multiple_of(base + i * step, step), step)
            v = hidden[rows].astype(f32) + total[rows].astype(f32)
            middle_ref[rows] = v
            moe[rows] = (v * norm_factor(v) * gain2_ref[...]).astype(bf16)
            return 0
        lax.fori_loop(0, count // step, body, 0)

    for k, c in enumerate((x, 1 - x)):
        second(c).wait_recv()
        total[at(my_half, c)] = (held[piece(c)].astype(f32) + from_x[piece(c)].astype(f32)).astype(bf16)
        third(c).start()
        norm_rows(my_half + c * chunk, chunk)
        experts.start_chunk(k)
        if k == 0:
            cot.hop_outside(3)
            cot.cross(2)
    for c in (x, 1 - x):
        pair(2, c, total.at[at(my_half, c)], total.at[at(other_half, c)], twin).wait_recv()
    norm_rows(other_half, half)
    experts.keep.start()
    for copy in keeps[5:]:
        copy.start()
    cot.flank(2)
    experts.hop(1)
    experts.cross(0)
    cot.cross(3)
    experts.hop_inside(2)
    experts.flank(0)
    cot.flank(3)
    experts.keep.wait()
    cot.keep.wait()
    for copy in loads[6:]:
        copy.wait()

    def grads_load(i):
        rows = rows_of(i)
        return [pltpu.make_async_copy(grads_all.at[rows, pl.ds(0, D)], p_buf.at[:, pl.ds(0, D)], stream.at[1]),
                pltpu.make_async_copy(grads_all.at[rows, pl.ds(D, 128)], mask_all, stream.at[2])]

    def stores(i):
        rows = rows_of(i)
        return [
            pltpu.make_async_copy(w_buf.at[i % 2], weighted_out.at[rows], out_sem.at[i % 2, 0]),
            pltpu.make_async_copy(a_buf.at[i % 2], acts_out.at[rows], out_sem.at[i % 2, 1]),
            pltpu.make_async_copy(whole.at[rows], m_out.at[rows], out_sem.at[i % 2, 2]),
        ]

    def parts_store(i):
        return pltpu.make_async_copy(p_buf, parts_out.at[rows_of(i)], stream.at[0])

    def run_experts(i):
        cot.complete(i)
        if i > 0:
            parts_store(i - 1).wait()
        fetches = grads_load(i)
        for copy in fetches:
            copy.start()
        experts.complete(i)
        slot = i % 2
        if i >= 2:
            for copy in stores(i - 2):
                copy.wait()

        rows = rows_of(i)
        v = whole[rows]
        logits = dot(v, wr_ref[...])
        count = logits.shape[1]
        for copy in fetches:
            copy.wait()
        mask = mask_all[:, :count].astype(f32) > 0
        top = jnp.max(jnp.where(mask, logits, -jnp.inf), -1, keepdims=True)
        raised = jnp.where(mask, jnp.exp(jnp.where(mask, logits - top, 0.0)), 0.0)
        gates = raised / jnp.sum(raised, -1, keepdims=True)
        lane = lax.broadcasted_iota(jnp.int32, gates.shape, 1)
        gg = jnp.zeros(gates.shape, f32)
        for j in range(2):
            mine = lane == first_expert + j
            gate = jnp.sum(jnp.where(mine, gates, 0.0), -1, keepdims=True)
            ga = dot(v, wg[j])
            ua = dot(v, wu[j])
            gw_j = dot_nt(p_buf[:, :D], wd[j])
            s = 1.0 / (1.0 + jnp.exp(-ga))
            silu = ga * s
            h = (silu * ua).astype(bf16).astype(f32)
            gg = gg + jnp.where(mine, jnp.sum(h * gw_j, -1, keepdims=True), 0.0)
            gh = gw_j * gate
            w_buf[slot, :, j * ff:(j + 1) * ff] = (h * gate).astype(bf16)
            a_buf[slot, :, 2 * j * ff:(2 * j + 1) * ff] = (gh * ua * s * (1.0 + ga * (1.0 - s))).astype(bf16)
            a_buf[slot, :, (2 * j + 1) * ff:(2 * j + 2) * ff] = (gh * silu).astype(bf16)
        for copy in stores(i):
            copy.start()
        if i < 3:
            experts.flank(i + 1)
        p_buf[:, :D] = dot(w_buf[slot], wd[...].reshape(2 * ff, D)).astype(bf16)
        gx = dot_nt(a_buf[slot, :, :ff], wg[0])
        for k, weight in ((1, wu[0]), (2, wg[1]), (3, wu[1])):
            gx = gx + dot_nt(a_buf[slot, :, k * ff:(k + 1) * ff], weight)
        p_buf[:, D:2 * D] = gx.astype(bf16)
        high = gg.astype(bf16)
        low = (gg - high.astype(f32)).astype(bf16)
        spare = jnp.zeros((span, 128 - 2 * count), bf16)
        p_buf[:, 2 * D:] = jnp.concatenate([high, low, spare], 1)
        parts_store(i).start()

    for i in range(4):
        if i < 2:
            experts.hop_outside(i + 2)
        if i < 3:
            experts.cross(i + 1)
        if i == 0:
            experts.hop_inside(3)
        run_experts(i)
    parts_store(3).wait()
    for i in (2, 3):
        for copy in stores(i):
            copy.wait()
    for copy in keeps:
        copy.wait()
    gather.drain()
    cot.drain()
    experts.drain()
    for c in range(2):
        first(c).wait_send()
        second(c).wait_send()
        third(c).wait_send()
    for r in range(4):
        pl.when(jnp.logical_not(here(r)))(lambda: to_block(r).wait_send())


def forward_all(hidden, sent, gain1, gain2, qg, kg, segc, segr, wr, wq, wk, wv, cosine, sine, wout, wg, wu, wd, number):
    rows, D = hidden.shape
    T = 8 * rows
    J, _, F = wg.shape
    half, span = rows // 2, 2 * rows
    sd = jax.ShapeDtypeStruct
    dma = pltpu.SemaphoreType.DMA
    vm = pltpu.VMEM
    like = lambda m: vm(m.shape, m.dtype)
    heads = [((T, HD), bf16)] * 3 + [((T, HD), f32)] * 2
    return pl.pallas_call(
        forward_kernel, in_specs=[VM] * 9 + [ANY] * 9, out_specs=[VM] + [ANY] * 14,
        out_shape=[sd((rows, 4 * HD), bf16), sd((rows, D), f32), sd((rows, D), bf16), sd((T, D), bf16), sd((T, D), bf16)]
        + [sd(*m) for m in heads] + [sd((T, D + 128), bf16), sd((T, D), bf16), sd((T, J * F), bf16), sd((T, 2 * J * F), bf16),
                                     sd((T, 2 * D + 128), bf16)],
        scratch_shapes=[vm((D, 3 * HD), bf16)] + [like(m) for m in (cosine, sine, wout, wg, wu, wd)]
        + [vm(*m) for m in heads] + [vm((4, BLOCK, HD), bf16)] * 2 + [vm((half, D), bf16)] * 4 + [vm((rows, D), bf16), vm((rows, D), f32), vm((rows, D), bf16)] + [
            vm((T, D), bf16), vm((span, 128), bf16), vm((2, span, J * F), bf16), vm((2, span, 2 * J * F), bf16),
            vm((span, 2 * D + 128), bf16)] + GATHER_SEMS * 3 + [
            dma((9,)), dma((3,)), dma((2, 3)), dma((7,)), dma((4,)), dma((4,)), dma((3, 2)), dma((3, 2))],
        compiler_params=pltpu.CompilerParams(collective_id=number, has_side_effects=True, vmem_limit_bytes=62 * 2**20),
    )(hidden, sent, gain1, gain2, qg, kg, segc, segr, wr, wq, wk, wv, cosine, sine, wout, wg, wu, wd)


def backward_kernel(ga_ref, segc_ref, segr_ref, qg_ref, kg_ref, gains_small, gain_ref,
                    w_in, ctx_ref, q_in, k_in, v_in, qr_in, kr_in, cos_in, sin_in, wq_in, wk_in, wv_in, a_in, hidden_in, middle_in, parts,
                    grad_ref, weights_q, weights_k, weights_v, norm_ref, gains_out, wout_ref, small_out, sum_ref,
                    w_ref, q_ref, k_ref, v_ref, qr_ref, kr_ref, cos_ref, sin_ref, wq_ref, wk_ref, wv_ref, columns, hidden_ref, middle_ref,
                    raw_ref, g_own, g_all, dk, dv, terms, from_y, held_terms, from_below, from_above,
                    small_y, small_sum, small_z, raw_in, gathered, products, from_z, out_half, in_half, held, from_x, total, gains_own, gains_in, norm_in,
                    load, g_send, g_recv, f_send, f_recv, t_send, t_recv, s_send, s_recv, send, recv, w_send, w_recv,
                    pair_send, pair_recv, e_send, e_recv, n_send, n_recv, *scatter):
    small_ref = gains_small
    z, y, x, core = place()
    me = z * 2 + y
    order = far_first(z)
    span = 4 * HD
    across, twin, corner = device(z, y, 1 - x, core), device(z, y, x, 1 - core), device(z, y, 1 - x, 1 - core)
    partner = device(z, 1 - y, x, core)

    loads = [pltpu.make_async_copy(source, target, load.at[k]) for k, (source, target) in enumerate((
        (w_in, w_ref), (q_in, q_ref), (k_in, k_ref), (v_in, v_ref), (qr_in, qr_ref), (kr_in, kr_ref), (cos_in, cos_ref),
        (sin_in, sin_ref), (wq_in, wq_ref), (wk_in, wk_ref), (wv_in, wv_ref), (hidden_in, hidden_ref), (middle_in, middle_ref)))]

    def column_load(n):
        block = pl.ds(pl.multiple_of((order[n] * 2 + y) * BLOCK, BLOCK), BLOCK)
        return pltpu.make_async_copy(a_in.at[:, block], columns.at[n % 2], load.at[13 + n % 2])

    for copy in loads:
        copy.start()
    greet_peers(z, y, x, core, (across, twin, corner))
    sums = Scatter(parts, 0, sum_ref, scatter[:7], scatter[7:])
    for k in range(4):
        sums.begin(k)
    column_load(0).start()
    column_load(1).start()

    def remote(source, target, ssem, rsem, where):
        return pltpu.make_async_remote_copy(
            src_ref=source, dst_ref=target, send_sem=ssem, recv_sem=rsem, device_id=where, device_id_type=MESH)

    def when_away(n, act):
        pl.when(z != n)(act)

    loads[0].wait()
    g_context = dot_nt(ga_ref[...], w_ref[...]).astype(bf16)
    for n in range(4):
        g_own[n] = g_context[:, n * HD:(n + 1) * HD]

    def g_to(n):
        return remote(g_own.at[n], g_all.at[me], g_send.at[n], g_recv.at[z], device(n, y, x, core))

    def g_from(n):
        return remote(g_own.at[n], g_all.at[n * 2 + y], g_send.at[n], g_recv.at[n], device(n, y, x, core))

    def g_over(n):
        return remote(g_all.at[n * 2 + y], g_all.at[n * 2 + y], f_send.at[n], f_recv.at[n], partner)

    def g_over_in(n):
        return remote(g_all.at[n * 2 + 1 - y], g_all.at[n * 2 + 1 - y], f_send.at[n], f_recv.at[n], partner)

    for n in range(4):
        when_away(n, lambda: g_to(n).start())
    g_all[me] = g_own[z]
    g_over(z).start()

    quarter = small_ref.shape[1] // 4

    def lanes(cx, cc):
        return pl.ds(pl.multiple_of((cx * 2 + cc) * quarter, quarter), quarter)

    own_lanes = lanes(x, core)
    small_pair = remote(small_ref.at[:, own_lanes], small_y, s_send.at[0], s_recv.at[0], partner)
    small_pair.start()

    def small_along(n):
        return remote(small_sum, small_z.at[z], s_send.at[1 + n], s_recv.at[1 + z], device(n, y, x, core))

    def small_arriving(n):
        return remote(small_sum, small_z.at[n], s_send.at[1 + n], s_recv.at[1 + n], device(n, y, x, core))

    fans = (across, twin, corner)
    fan_lanes = (lanes(1 - x, core), lanes(x, 1 - core), lanes(1 - x, 1 - core))

    def small_spread(i):
        return remote(small_out.at[:, own_lanes], small_out.at[:, own_lanes], s_send.at[5 + i], s_recv.at[5 + i], fans[i])

    def small_spread_in(i):
        return remote(small_out.at[:, own_lanes], small_out.at[:, fan_lanes[i]], s_send.at[5 + i], s_recv.at[5 + i], fans[i])

    for b in range(8):
        terms[b] = dot_tn(ctx_ref[...], ga_ref[:, b * BLOCK:(b + 1) * BLOCK]).astype(bf16)

    def term_pair(n):
        return remote(terms.at[n * 2 + 1 - y], from_y.at[n], t_send.at[0, n], t_recv.at[0, n], partner)

    def term_up(n):
        return remote(held_terms.at[n], from_below.at[n], t_send.at[1, n], t_recv.at[1, n], device(z + 1, y, x, core))

    def term_down(n):
        return remote(held_terms.at[n], from_above.at[n], t_send.at[2, n], t_recv.at[2, n], device(z - 1, y, x, core))

    def paired(n):
        return terms[n * 2 + y].astype(f32) + from_y[n].astype(f32)

    def term_stage(k):
        n = order[k]
        term_pair(n).wait_recv()
        held_terms[n] = paired(n).astype(bf16)
        rises = (z // 2 == 0) if k < 2 else (z % 2 == 0)

        @pl.when(rises)
        def _():
            @pl.when(z > 0)
            def _():
                term_up(n).wait_recv()
                held_terms[n] = (paired(n) + from_below[n].astype(f32)).astype(bf16)
            term_up(n).start()

        @pl.when(jnp.logical_not(rises))
        def _():
            @pl.when(z < 3)
            def _():
                term_down(n).wait_recv()
                held_terms[n] = (paired(n) + from_above[n].astype(f32)).astype(bf16)
            term_down(n).start()

    for k in range(3):
        sums.stage_core(k, True)
        sums.stage_core(k, False)
    for n in range(4):
        when_away(n, lambda: g_from(n).wait_recv())
        when_away(n, lambda: g_over(n).start())
    for n in order:
        term_pair(n).start()

    def rows_to(n):
        return remote(raw_ref.at[n * 2 + y], raw_in.at[z], send.at[n], recv.at[z], device(n, y, x, core))

    def rows_from(n):
        return remote(raw_ref.at[n * 2 + y], raw_in.at[n], send.at[n], recv.at[n], device(n, y, x, core))

    gain_sums = [jnp.zeros((1, HD), f32), jnp.zeros((1, HD), f32)]

    def back(turned, b, raw_in, gain, which):
        rows = slice(b * BLOCK, (b + 1) * BLOCK)
        g = turned * cos_ref[rows] - pltpu.roll(turned, HD // 2, 1) * sin_ref[rows]
        raw = raw_in[rows]
        factor = norm_factor(raw)
        n = raw * factor
        gain_sums[which] = gain_sums[which] + jnp.sum(g * n, 0, keepdims=True)
        g = g * gain[:, pl.ds(pl.multiple_of(z * HD, HD), HD)]
        return (factor * (g - n * jnp.mean(g * n, -1, keepdims=True))).astype(bf16)

    for copy in loads[1:8]:
        copy.wait()
    for b in range(7, -1, -1):
        keys = (b + 1) * BLOCK
        rows = slice(b * BLOCK, keys)
        pl.when(y != b % 2)(lambda: g_over_in(b // 2).wait_recv())
        q = q_ref[rows]
        g = g_all[b]
        probs = masked_probs(b, q, k_ref, segc_ref, segr_ref)
        gv = dot_tn(probs.astype(bf16), g)
        gp = dot_nt(g, v_ref[:keys])
        gs = (probs * (gp - jnp.sum(gp * probs, -1, keepdims=True))).astype(bf16)
        gk = dot_tn(gs, q)
        if b == 7:
            dv[...] = gv
            dk[...] = gk
        else:
            dv[:keys] += gv
            dk[:keys] += gk
        raw_ref[b, :, :HD] = back(dot(gs, k_ref[:keys]) * (HD ** -0.5), b, qr_ref, qg_ref, 0)
        raw_ref[b, :, HD:2 * HD] = back(dk[rows] * (HD ** -0.5), b, kr_ref, kg_ref, 1)
        raw_ref[b, :, 2 * HD:] = dv[rows].astype(bf16)

        @pl.when(y == b % 2)
        def _():
            when_away(b // 2, lambda: rows_to(b // 2).start())

    for k in range(3):
        sums.stage_y(k)
        sums.stage_x(k)

    small_pair.wait_recv()
    small_sum[...] = small_ref[:, own_lanes] + small_y[...]
    for n in range(4):
        when_away(n, lambda: small_along(n).start())
    small_z[z] = small_sum[...]
    gains_own[0:1] = gain_sums[0]
    gains_own[1:2] = gain_sums[1]

    def gains_to(n):
        return remote(gains_own, gains_in.at[z], e_send.at[n], e_recv.at[z], device(n, y, x, core))

    def gains_from(n):
        return remote(gains_own, gains_in.at[n], e_send.at[n], e_recv.at[n], device(n, y, x, core))

    for n in range(4):
        when_away(n, lambda: gains_to(n).start())
    gains_in[z] = gains_own[...]
    raw_in[z] = raw_ref[me]

    def products_to(n):
        return remote(products.at[n], from_z.at[z], w_send.at[n], w_recv.at[z], device(n, y, x, core))

    def products_from(n):
        return remote(products.at[n], from_z.at[n], w_send.at[n], w_recv.at[n], device(n, y, x, core))

    raw_all = raw_ref[...].reshape(8 * BLOCK, 3 * HD)
    for i, n in enumerate(order):
        column_load(i).wait()
        product = dot_tn(columns[i % 2], raw_all).astype(bf16)
        if i < 2:
            column_load(i + 2).start()
        if i < 3:
            products[n] = product
            products_to(n).start()
        else:
            from_z[z] = product

    for copy in loads[8:]:
        copy.wait()
    for n in range(4):
        when_away(n, lambda: rows_from(n).wait_recv())
        for g in range(3):
            gathered[:, g * span + n * HD:g * span + (n + 1) * HD] = raw_in[n, :, g * HD:(g + 1) * HD]

    rows = total.shape[0]
    half = rows // 2
    chunk = half // 2
    my_half = core * half
    other_half = (1 - core) * half
    piece = lambda c: pl.ds(c * chunk, chunk)
    at = lambda base, c: pl.ds(pl.multiple_of(base + c * chunk, chunk), chunk)

    def pair(kind, c, source, target, where):
        return remote(source, target, pair_send.at[kind, c], pair_recv.at[kind, c], where)

    def multiply(part):
        return (dot_nt(part[:, :span], wq_ref[...]) + dot_nt(part[:, span:2 * span], wk_ref[...])
                + dot_nt(part[:, 2 * span:], wv_ref[...]))

    first = [pair(0, c, out_half.at[piece(c)], in_half.at[piece(c)], twin) for c in range(2)]
    second = [pair(1, c, held.at[piece(c)], from_x.at[piece(c)], across) for c in range(2)]
    third = [pair(2, c, total.at[at(my_half, c)], total.at[at(my_half, c)], twin) for c in range(2)]
    for c in range(2):
        out_half[piece(c)] = multiply(gathered[at(other_half, c)]).astype(bf16)
        first[c].start()
    for c in range(2):
        kept = multiply(gathered[at(my_half, c)])
        first[c].wait_recv()
        held[piece(c)] = (kept + in_half[piece(c)].astype(f32)).astype(bf16)
        second[c].start()

    term_stage(0)
    sums.stage_core(3, True)
    sums.stage_core(3, False)
    sums.stage_z(0)
    term_stage(1)
    for c in range(2):
        second[c].wait_recv()
        total[at(my_half, c)] = (held[piece(c)].astype(f32) + from_x[piece(c)].astype(f32)).astype(bf16)
        third[c].start()

    step = 32

    def norm_rows(base):
        def body(i, norm_part):
            part = pl.ds(pl.multiple_of(base + i * step, step), step)
            e = total[part].astype(f32)
            v = hidden_ref[part].astype(f32)
            factor = norm_factor(v)
            n = v * factor
            norm_part = norm_part + jnp.sum(e * n, 0, keepdims=True)
            e = e * gain_ref[...]
            grad_ref[part] = middle_ref[part] + factor * (e - n * jnp.mean(e * n, -1, keepdims=True))
            return norm_part
        return body

    nothing = jnp.zeros((1, total.shape[1]), f32)
    mine_part = lax.fori_loop(0, half // step, norm_rows(my_half), nothing)
    for c in range(2):
        pair(2, c, total.at[at(my_half, c)], total.at[at(other_half, c)], twin).wait_recv()
    other_part = lax.fori_loop(0, half // step, norm_rows(other_half), nothing)
    norm_part = mine_part + other_part
    for t in range(norm_in.shape[1]):
        norm_in[me, t:t + 1] = norm_part[:, t * 128:(t + 1) * 128]

    def norm_to(b):
        return remote(norm_in.at[me], norm_in.at[me], n_send.at[b], n_recv.at[me], device(b // 2, b % 2, x, core))

    def norm_from(b):
        return remote(norm_in.at[b], norm_in.at[b], n_send.at[b], n_recv.at[b], device(b // 2, b % 2, x, core))

    for b in range(8):
        pl.when(me != b)(lambda: norm_to(b).start())
    sums.stage_y(3)
    sums.stage_x(3)
    sums.stage_z(1)
    term_stage(2)
    sums.stage_z(2)
    term_pair(z).wait_recv()
    wout_ref[...] = paired(z)

    @pl.when(z > 0)
    def _():
        term_up(z).wait_recv()
        wout_ref[...] += from_below[z].astype(f32)

    @pl.when(z < 3)
    def _():
        term_down(z).wait_recv()
        wout_ref[...] += from_above[z].astype(f32)

    for n in range(4):
        when_away(n, lambda: small_arriving(n).wait_recv())
    small_out[:, own_lanes] = (small_z[0] + small_z[1]) + (small_z[2] + small_z[3])
    for i in range(3):
        small_spread(i).start()
    for n in range(4):
        when_away(n, lambda: gains_from(n).wait_recv())
        gains_out[:, n * HD:(n + 1) * HD] = gains_in[n]
    sums.own_sum()
    for n in range(4):
        when_away(n, lambda: products_from(n).wait_recv())
    for n in range(4):
        for g in range(3):
            (weights_q, weights_k, weights_v)[g][:, n * HD:(n + 1) * HD] = from_z[n, :, g * HD:(g + 1) * HD].astype(f32)
    sums.own_end()
    for b in range(8):
        pl.when(me != b)(lambda: norm_from(b).wait_recv())
    norms = [norm_in[b] for b in range(8)]
    norm_sum = ((norms[0] + norms[1]) + (norms[2] + norms[3])) + ((norms[4] + norms[5]) + (norms[6] + norms[7]))
    for t in range(norm_in.shape[1]):
        norm_ref[:, t * 128:(t + 1) * 128] = norm_sum[t:t + 1]

    sums.finish()
    for i in range(3):
        small_spread_in(i).wait_recv()
        small_spread(i).wait_send()
    small_pair.wait_send()
    for c in range(2):
        first[c].wait_send()
        second[c].wait_send()
        third[c].wait_send()
    for b in range(8):
        pl.when(me != b)(lambda: norm_to(b).wait_send())
    for n in range(4):
        when_away(n, lambda: g_to(n).wait_send())
        g_over(n).wait_send()
        term_pair(n).wait_send()
        pl.when(n > z)(lambda: term_up(n).wait_send())
        pl.when(n < z)(lambda: term_down(n).wait_send())
        when_away(n, lambda: small_along(n).wait_send())
        when_away(n, lambda: rows_to(n).wait_send())
        when_away(n, lambda: products_to(n).wait_send())
        when_away(n, lambda: gains_to(n).wait_send())


def backward_all(ga, segc, segr, qg, kg, small, gain, w, ctx, q, k, v, qr, kr, cosine, sine, wq, wk, wv, a, hidden, middle, parts, number):
    T, D = a.shape
    rows, half = BLOCK, BLOCK // 2
    span = 4 * HD
    S = small.shape[0]
    sd = jax.ShapeDtypeStruct
    dma = pltpu.SemaphoreType.DMA
    vm = pltpu.VMEM
    like = lambda m: vm(m.shape, m.dtype)
    return pl.pallas_call(
        backward_kernel, in_specs=[VM] * 7 + [ANY, VM] + [ANY] * 14, out_specs=[VM] * 9,
        out_shape=[sd((rows, D), f32), sd((BLOCK, span), f32), sd((BLOCK, span), f32), sd((BLOCK, span), f32), sd((1, D), f32), sd((2, span), f32),
                   sd((span, BLOCK), f32), sd((S, D), f32), sd((rows, D), bf16)],
        scratch_shapes=[like(m) for m in (w, q, k, v, qr, kr, cosine, sine, wq, wk, wv)] + [
            vm((2, T, BLOCK), bf16), like(hidden), like(middle),
            vm((8, BLOCK, 3 * HD), bf16), vm((4, BLOCK, HD), bf16), vm((8, BLOCK, HD), bf16), vm((T, HD), f32), vm((T, HD), f32),
            vm((8, span, BLOCK), bf16)] + [vm((4, span, BLOCK), bf16)] * 4 + [
            vm((S, D // 4), f32), vm((S, D // 4), f32), vm((4, S, D // 4), f32),
            vm((4, BLOCK, 3 * HD), bf16), vm((rows, 3 * span), bf16), vm((4, BLOCK, 3 * HD), bf16), vm((4, BLOCK, 3 * HD), bf16)] + [vm((half, D), bf16)] * 4 + [
            vm((rows, D), bf16), vm((2, HD), f32), vm((4, 2, HD), f32), vm((8, D // 128, 128), f32),
            dma((15,)), dma((4,)), dma((4,)), dma((4,)), dma((4,)), dma((3, 4)), dma((3, 4)), dma((8,)), dma((8,)),
            dma((4,)), dma((4,)), dma((4,)), dma((4,)), dma((3, 2)), dma((3, 2)), dma((4,)), dma((4,)), dma((8,)), dma((8,)),
        ] + scatter_buffers(rows, D) + SCATTER_SEMS,
        compiler_params=pltpu.CompilerParams(collective_id=number, has_side_effects=True, vmem_limit_bytes=63 * 2**20),
    )(ga, segc, segr, qg, kg, small, gain, w, ctx, q, k, v, qr, kr, cosine, sine, wq, wk, wv, a, hidden, middle, parts)


def on_device(
    hidden_in,
    norm1_gain,
    w_query,
    w_key,
    w_value,
    w_out,
    query_gain,
    key_gain,
    norm2_gain,
    w_router,
    w_gate,
    w_up,
    w_down,
    routes,
    segments,
    cotangent,
):
    seq_len, width = hidden_in.shape
    local_width = w_query.shape[1]
    head_count = local_width // HEAD_DIM
    expert_devs = lax.axis_size("expert")
    local_experts = w_gate.shape[0]
    expert_total = w_router.shape[1]
    capacity = 2 * seq_len * TOP // expert_total
    slab_rows = local_experts * capacity
    my_index = lax.axis_index("expert")
    group = SEQ // seq_len
    rank = my_index % group
    f32 = jnp.float32
    bf16 = jnp.bfloat16

    def split_heads(values):
        return values.reshape(seq_len, head_count, HEAD_DIM)

    inputs = hidden_in.astype(f32)
    inverse_attn = inverse_rms(inputs)
    normed_attn = inputs * inverse_attn
    attn_input = (normed_attn * norm1_gain).astype(bf16)
    q_raw = split_heads(jnp.dot(attn_input, w_query, preferred_element_type=f32))
    k_raw = split_heads(jnp.dot(attn_input, w_key, preferred_element_type=f32))
    v_heads = split_heads(jnp.dot(attn_input, w_value, preferred_element_type=f32).astype(bf16))
    q_gains = query_gain.reshape(head_count, HEAD_DIM)
    k_gains = key_gain.reshape(head_count, HEAD_DIM)
    q_inverse = inverse_rms(q_raw)
    q_normed = q_raw * q_inverse
    k_inverse = inverse_rms(k_raw)
    k_normed = k_raw * k_inverse
    local_places = lax.iota(jnp.int32, seq_len)
    query_places = rank * seq_len + local_places
    cosine, sine_part = rope_tables(query_places.astype(f32), HEAD_DIM // 2)
    queries = rotate(q_normed * q_gains, cosine, sine_part, 1.0).astype(bf16)
    key_rot = rotate(k_normed * k_gains, cosine, sine_part, 1.0).astype(bf16)
    score_scale = HEAD_DIM ** (-0.5)
    keys_values = jnp.stack([key_rot, v_heads])
    pieces = [keys_values]
    for offset in range(1, group):
        keys_values = from_behind(keys_values, "expert", 1)
        pieces.append(keys_values)
    stacked = jnp.stack(pieces, 1).reshape(2, group * seq_len, head_count, HEAD_DIM)
    keys_all = stacked[0]
    values_all = stacked[1]
    query_segs = lax.dynamic_slice_in_dim(segments, my_index * seq_len, seq_len, 0)
    key_segs = jnp.concatenate(
        [
            lax.dynamic_slice_in_dim(
                segments, jnp.maximum(my_index - offset, 0) * seq_len, seq_len, 0
            )
            for offset in range(group)
        ],
        0,
    )
    offsets = lax.iota(jnp.int32, group)
    key_places = ((rank - offsets)[:, None] * seq_len + local_places[None, :]).reshape(-1)
    key_valid = jnp.repeat(rank - offsets >= 0, seq_len)
    allowed = (
        key_valid[None, :]
        & (query_places[:, None] >= key_places[None, :])
        & (query_segs[:, None] == key_segs[None, :])
    )

    def scores_of():
        raw_scores = (
            jnp.einsum("thd,shd->hts", queries, keys_all, preferred_element_type=f32) * score_scale
        )
        return jnp.where(allowed[None], raw_scores, MASKED)

    scores = scores_of()
    row_max = jnp.max(scores, -1, keepdims=True)
    raised = jnp.exp(scores - row_max)
    exp_total = jnp.sum(raised, -1, keepdims=True)
    log_total = row_max + jnp.log(exp_total)
    attn_probs = (raised / exp_total).astype(bf16)
    context = (
        jnp.einsum("hts,shd->thd", attn_probs, values_all, preferred_element_type=f32)
        .reshape(seq_len, local_width)
        .astype(bf16)
    )
    attn_part = jnp.dot(context, w_out, preferred_element_type=f32)
    middle = inputs + lax.psum(attn_part, "head")
    inverse_moe = inverse_rms(middle)
    normed_moe = middle * inverse_moe
    moe_input = (normed_moe * norm2_gain).astype(bf16)
    logits = jnp.dot(moe_input, w_router, preferred_element_type=f32)
    chosen = jnp.take_along_axis(logits, routes, 1)
    raised_gate = jnp.exp(chosen - jnp.max(chosen, -1, keepdims=True))
    gate_weights = raised_gate / jnp.sum(raised_gate, -1, keepdims=True)
    catalog = lax.iota(jnp.int32, expert_total)
    route_hot = (routes[:, :, None] == catalog).astype(jnp.int32)
    token_hot = jnp.sum(route_hot, 1, dtype=jnp.int32)
    earlier = jnp.cumsum(token_hot, 0, dtype=jnp.int32) - token_hot
    position = routes * capacity + jnp.take_along_axis(earlier, routes, 1)
    flat_pos = position.reshape(-1)
    owners = (
        jnp.full((expert_total * capacity,), seq_len, jnp.int32)
        .at[flat_pos]
        .set(jnp.repeat(lax.iota(jnp.int32, seq_len), TOP))
    )
    padded = jnp.concatenate([moe_input, jnp.zeros((1, width), bf16)], 0)
    outgoing = padded[owners].reshape(expert_devs, slab_rows, width)
    arrived = lax.all_to_all(outgoing, "expert", split_axis=0, concat_axis=0, tiled=True)
    rows_in = arrived.reshape(expert_devs, local_experts, capacity, width)
    gate_act = jnp.einsum("sjcd,jdf->sjcf", rows_in, w_gate, preferred_element_type=f32)
    up_act = jnp.einsum("sjcd,jdf->sjcf", rows_in, w_up, preferred_element_type=f32)
    hidden = (jax.nn.silu(gate_act) * up_act).astype(bf16)
    partial_out = jnp.einsum("sjcf,jfd->sjcd", hidden, w_down, preferred_element_type=f32).reshape(
        expert_devs, slab_rows, width
    )
    rows_out = (
        lax.psum_scatter(partial_out.astype(jnp.bfloat16), "head", scatter_dimension=2, tiled=True)
        .astype(jnp.float32)
        .astype(bf16)
    )
    leaving = lax.all_gather(rows_out, "head", axis=2, tiled=True)
    returned = lax.all_to_all(leaving, "expert", split_axis=0, concat_axis=0, tiled=True)
    picked = returned.reshape(expert_total * capacity, width)[position]
    moe_out = jnp.einsum("tk,tkd->td", gate_weights, picked, preferred_element_type=f32)
    output = (middle + moe_out).astype(bf16)
    grad_final = cotangent.astype(f32)
    grad_gates = jnp.einsum("td,tkd->tk", grad_final, picked, preferred_element_type=f32)
    grad_chosen = gate_weights * (
        grad_gates - jnp.sum(grad_gates * gate_weights, -1, keepdims=True)
    )
    grad_logits = jnp.einsum("tk,tke->te", grad_chosen, route_hot.astype(f32)).astype(bf16)
    grad_router = jnp.dot(moe_input.T, grad_logits, preferred_element_type=f32)
    grad_moe_input = jnp.dot(grad_logits, w_router.T, preferred_element_type=f32)
    grad_expert_out = (gate_weights[:, :, None] * grad_final[:, None, :]).astype(bf16)
    grad_slab = (
        jnp.zeros((expert_total * capacity, width), bf16)
        .at[flat_pos]
        .set(grad_expert_out.reshape(seq_len * TOP, width))
    )
    grad_slab = grad_slab.reshape(expert_devs, slab_rows, width)
    grad_arrived = lax.all_to_all(grad_slab, "expert", split_axis=0, concat_axis=0, tiled=True)
    grad_rows_out = grad_arrived.reshape(expert_devs, local_experts, capacity, width)
    grad_hidden = jnp.einsum("sjcd,jfd->sjcf", grad_rows_out, w_down, preferred_element_type=f32)
    grad_down = jnp.einsum("sjcf,sjcd->jfd", hidden, grad_rows_out, preferred_element_type=f32)
    sigmoid = jax.nn.sigmoid(gate_act)
    grad_up_act = (grad_hidden * gate_act * sigmoid).astype(bf16)
    grad_gate_act = (grad_hidden * up_act * sigmoid * (1.0 + gate_act * (1.0 - sigmoid))).astype(
        bf16
    )
    grad_gate = jnp.einsum("sjcd,sjcf->jdf", rows_in, grad_gate_act, preferred_element_type=f32)
    grad_up = jnp.einsum("sjcd,sjcf->jdf", rows_in, grad_up_act, preferred_element_type=f32)
    grad_rows_in = jnp.einsum("sjcf,jdf->sjcd", grad_gate_act, w_gate, preferred_element_type=f32)
    grad_rows_in = grad_rows_in + jnp.einsum(
        "sjcf,jdf->sjcd", grad_up_act, w_up, preferred_element_type=f32
    )
    grad_back = (
        lax.psum_scatter(
            grad_rows_in.reshape(expert_devs, slab_rows, width).astype(jnp.bfloat16),
            "head",
            scatter_dimension=2,
            tiled=True,
        )
        .astype(jnp.float32)
        .astype(bf16)
    )
    leaving_grad = lax.all_gather(grad_back, "head", axis=2, tiled=True)
    grad_home = lax.all_to_all(leaving_grad, "expert", split_axis=0, concat_axis=0, tiled=True)
    grad_moe_input = grad_moe_input + jnp.sum(
        grad_home.reshape(expert_total * capacity, width)[position], 1, dtype=f32
    )
    grad_norm2 = jnp.sum(grad_moe_input * normed_moe, 0)
    grad_middle = grad_final + norm_back(grad_moe_input * norm2_gain, normed_moe, inverse_moe)
    grad_attn = grad_middle.astype(bf16)
    grad_out_turned = jnp.dot(grad_attn.T, context, preferred_element_type=f32)
    grad_context = split_heads(jnp.dot(grad_attn, w_out.T, preferred_element_type=f32).astype(bf16))
    attn_full = jnp.exp(scores_of() - log_total)
    attn_low = attn_full.astype(bf16)
    grad_values_all = jnp.einsum("hts,thd->shd", attn_low, grad_context, preferred_element_type=f32)
    grad_probs = jnp.einsum("thd,shd->hts", grad_context, values_all, preferred_element_type=f32)
    grad_scores = (
        attn_full * (grad_probs - jnp.sum(grad_probs * attn_full, -1, keepdims=True))
    ).astype(bf16)
    grad_queries = (
        jnp.einsum("hts,shd->thd", grad_scores, keys_all, preferred_element_type=f32) * score_scale
    )
    grad_keys_all = (
        jnp.einsum("hts,thd->shd", grad_scores, queries, preferred_element_type=f32) * score_scale
    )
    kv_terms = jnp.stack([grad_keys_all, grad_values_all]).reshape(
        2, group, seq_len, head_count, HEAD_DIM
    )
    kv_total = kv_terms[:, 0]
    for offset in range(1, group):
        kv_total = kv_total + from_behind(
            kv_terms[:, offset].astype(jnp.bfloat16), "expert", -offset
        ).astype(jnp.float32)
    grad_keys = kv_total[0]
    grad_values = kv_total[1]
    grad_q_normed = rotate(grad_queries, cosine, sine_part, -1.0)
    grad_k_normed = rotate(grad_keys, cosine, sine_part, -1.0)
    grad_query_gain = jnp.sum(grad_q_normed * q_normed, 0).reshape(local_width)
    grad_key_gain = jnp.sum(grad_k_normed * k_normed, 0).reshape(local_width)
    grad_q_raw = (
        norm_back(grad_q_normed * q_gains, q_normed, q_inverse)
        .reshape(seq_len, local_width)
        .astype(bf16)
    )
    grad_k_raw = (
        norm_back(grad_k_normed * k_gains, k_normed, k_inverse)
        .reshape(seq_len, local_width)
        .astype(bf16)
    )
    grad_v_raw = grad_values.reshape(seq_len, local_width).astype(bf16)
    grad_query = jnp.dot(attn_input.T, grad_q_raw, preferred_element_type=f32)
    grad_key = jnp.dot(attn_input.T, grad_k_raw, preferred_element_type=f32)
    grad_value = jnp.dot(attn_input.T, grad_v_raw, preferred_element_type=f32)
    input_part = jnp.dot(grad_q_raw, w_query.T, preferred_element_type=f32)
    input_part = input_part + jnp.dot(grad_k_raw, w_key.T, preferred_element_type=f32)
    input_part = input_part + jnp.dot(grad_v_raw, w_value.T, preferred_element_type=f32)
    grad_attn_input = lax.psum(input_part.astype(jnp.bfloat16), "head").astype(jnp.float32)
    grad_norm1 = jnp.sum(grad_attn_input * normed_attn, 0)
    grad_input = grad_middle + norm_back(grad_attn_input * norm1_gain, normed_attn, inverse_attn)
    grad_query, grad_key, grad_value, grad_out_turned = (
        lax.psum_scatter(
            grad_query.astype(jnp.bfloat16), "expert", scatter_dimension=0, tiled=True
        ).astype(jnp.float32),
        lax.psum_scatter(
            grad_key.astype(jnp.bfloat16), "expert", scatter_dimension=0, tiled=True
        ).astype(jnp.float32),
        lax.psum_scatter(
            grad_value.astype(jnp.bfloat16), "expert", scatter_dimension=0, tiled=True
        ).astype(jnp.float32),
        lax.psum_scatter(
            grad_out_turned.astype(jnp.bfloat16), "expert", scatter_dimension=0, tiled=True
        ).astype(jnp.float32),
    )
    grad_router, grad_norm1, grad_norm2, grad_query_gain, grad_key_gain = (
        lax.psum(grad_router.astype(jnp.bfloat16), "expert").astype(jnp.float32),
        lax.psum(grad_norm1.astype(jnp.bfloat16), "expert").astype(jnp.float32),
        lax.psum(grad_norm2.astype(jnp.bfloat16), "expert").astype(jnp.float32),
        lax.psum(grad_query_gain.astype(jnp.bfloat16), "expert").astype(jnp.float32),
        lax.psum(grad_key_gain.astype(jnp.bfloat16), "expert").astype(jnp.float32),
    )
    return (
        output,
        grad_input,
        grad_norm1,
        grad_query,
        grad_key,
        grad_value,
        grad_out_turned.T,
        grad_query_gain,
        grad_key_gain,
        grad_norm2,
        grad_router,
        grad_gate,
        grad_up,
        grad_down,
    )


def full_tables(tokens):
    half_dim = HEAD_DIM // 2
    fine_cos, fine_sin = rope_tables(lax.iota(jnp.int32, 64).astype(f32), half_dim)
    coarse = (64 * lax.iota(jnp.int32, tokens // 64)).astype(f32)
    coarse_cos, coarse_sin = rope_tables(coarse, half_dim)
    fine_cos, fine_sin = fine_cos.reshape(1, 64, half_dim), fine_sin.reshape(1, 64, half_dim)
    cosine = (coarse_cos * fine_cos - coarse_sin * fine_sin).reshape(tokens, half_dim)
    sine = (coarse_sin * fine_cos + coarse_cos * fine_sin).reshape(tokens, half_dim)
    return jnp.concatenate([cosine, cosine], 1), jnp.concatenate([-sine, sine], 1)


def dense_layer(
    hidden_in, norm1_gain, w_query, w_key, w_value, w_out, query_gain, key_gain, norm2_gain, w_router,
    w_gate, w_up, w_down, routes, segments, cotangent,
):
    rows, width = hidden_in.shape
    experts = w_router.shape[1]
    devices = lax.axis_size("expert")
    tokens = devices * rows

    cosine, sine = full_tables(tokens)
    segc, segr = segments[:, None], segments[None]
    own_mask = jnp.sum((routes[:, :, None] == lax.iota(jnp.int32, experts)).astype(f32), 1)
    sent = jnp.concatenate([cotangent, jnp.pad(own_mask.astype(bf16), ((0, 0), (0, 128 - experts)))], 1)
    own_context, middle, moe_input, _, attn_all, queries, keys, values, q_raw, k_raw, grads_all, everyone, weighted, grad_acts, parts = (
        forward_all(
            hidden_in, sent, norm1_gain[None], norm2_gain[None], query_gain[None], key_gain[None], segc, segr, w_router,
            w_query, w_key, w_value, cosine, sine, w_out, w_gate, w_up, w_down, 1,
        )
    )
    inverse_moe = inverse_rms(middle)
    normed_moe = middle * inverse_moe
    parts = parts.reshape(devices, rows, 2 * width + 128)
    total_a, total_b, grad_gate, grad_up, grad_down = sums_all(parts, everyone, grad_acts, grads_all, weighted, 2)
    total = jnp.concatenate([total_a, total_b], 1)
    grad_final = cotangent.astype(f32)
    tail = total[:, width:].astype(f32)
    grad_gates = tail[:, :experts] + tail[:, experts : 2 * experts]
    logits = jnp.where(
        own_mask > 0, jnp.dot(moe_input, w_router, preferred_element_type=f32), -jnp.inf
    )
    raised_gate = jnp.exp(logits - jnp.max(logits, -1, keepdims=True))
    gate_weights = raised_gate / jnp.sum(raised_gate, -1, keepdims=True)
    grad_logits = (
        gate_weights * (grad_gates - jnp.sum(grad_gates * gate_weights, -1, keepdims=True))
    ).astype(bf16)
    grad_moe_input = jnp.dot(grad_logits, w_router.T, preferred_element_type=f32)
    grad_moe_input = grad_moe_input + total[:, :width].astype(f32)
    grad_middle = grad_final + norm_back(grad_moe_input * norm2_gain, normed_moe, inverse_moe)
    small = jnp.concatenate(
        [
            lax.dot_general(grad_logits, moe_input, (((0,), (0,)), ((), ())), preferred_element_type=f32),
            jnp.sum(grad_moe_input * normed_moe, 0, keepdims=True),
            jnp.zeros((7, width), f32),
        ],
        0,
    )

    grad_input, grad_query, grad_key, grad_value, grad_norm1, gains, grad_w_out, small, moe_out = backward_all(
        grad_middle.astype(bf16), segc, segr, query_gain[None], key_gain[None], small, norm1_gain[None], w_out, own_context,
        queries, keys, values, q_raw, k_raw, cosine, sine, w_query, w_key, w_value, attn_all, hidden_in, grad_middle, parts, 3,
    )
    output = (middle + moe_out.astype(f32)).astype(bf16)
    return (
        output,
        grad_input,
        grad_norm1[0],
        grad_query,
        grad_key,
        grad_value,
        grad_w_out,
        gains[0],
        gains[1],
        small[experts],
        small[:experts].T,
        grad_gate,
        grad_up,
        grad_down,
    )


def layer(*arrays):
    rows, experts = arrays[0].shape[0], arrays[9].shape[1]
    whole = 2 * rows * TOP // experts >= rows and rows * lax.axis_size("expert") == SEQ
    grid = (lax.axis_size("expert"), lax.axis_size("head")) == (8, 4)
    return dense_layer(*arrays) if whole and grid else on_device(*arrays)


def solution(mesh):
    return jax.shard_map(
        layer,
        mesh=mesh,
        in_specs=(
            P("expert", None),
            P(),
            P(None, "head"),
            P(None, "head"),
            P(None, "head"),
            P("head", None),
            P("head"),
            P("head"),
            P(),
            P(),
            P("expert", None, "head"),
            P("expert", None, "head"),
            P("expert", "head", None),
            P("expert", None),
            P(),
            P("expert", None),
        ),
        out_specs=(
            P("expert", None),
            P("expert", None),
            P(),
            P("expert", "head"),
            P("expert", "head"),
            P("expert", "head"),
            P("head", "expert"),
            P("head"),
            P("head"),
            P(),
            P(),
            P("expert", None, "head"),
            P("expert", None, "head"),
            P("expert", "head", None),
        ),
        check_vma=False,
    )
```

```python
import functools

import jax
import jax.numpy as jnp
from jax import lax
from jax.experimental import pallas as pl
from jax.experimental.pallas import tpu as pltpu
from jax.sharding import PartitionSpec as P

HEAD_DIM = 128
TOP = 8
SEQ = 2048
MESH = pl.DeviceIdType.MESH
bf16 = jnp.bfloat16
f32 = jnp.float32


EPSILON = 1e-05
ROPE_BASE = 10000.0
MASKED = -1000000000.0


def from_behind(shard, axis, by):
    size = lax.axis_size(axis)
    pairs = [(i, i + by) for i in range(size) if 0 <= i + by < size]
    return lax.ppermute(shard, axis, pairs)


def inverse_rms(values):
    return lax.rsqrt(jnp.mean(values * values, -1, keepdims=True) + EPSILON)


def norm_back(grad_normed, normed, inverse):
    return inverse * (grad_normed - normed * jnp.mean(grad_normed * normed, -1, keepdims=True))


def rope_tables(places, half_dim):
    inv_freq = ROPE_BASE ** (-lax.iota(jnp.int32, half_dim).astype(jnp.float32) / half_dim)
    angles = places[:, None] * inv_freq[None, :]
    return (jnp.cos(angles)[:, None, :], jnp.sin(angles)[:, None, :])


def rotate(values, cosine, sine_part, direction):
    half_dim = values.shape[-1] // 2
    first_half = values[..., :half_dim]
    second_half = values[..., half_dim:]
    turned = direction * sine_part
    return jnp.concatenate(
        [first_half * cosine - second_half * turned, second_half * cosine + first_half * turned], -1
    )


def place():
    block = lax.axis_index("expert")
    lane = lax.axis_index("head")
    return block // 2, block % 2, lane // 2, lane % 2


def device(z, y, x, core):
    return (z * 2 + y, x * 2 + core)


def greet(z, y, x, core):
    barrier = pltpu.get_barrier_semaphore()

    def signal(target):
        pl.semaphore_signal(barrier, inc=1, device_id=target, device_id_type=MESH)

    signal(device(z, 1 - y, x, core))
    signal(device(z, y, 1 - x, core))
    signal(device(z, y, x, 1 - core))

    @pl.when(z > 0)
    def _():
        signal(device(z - 1, y, x, core))

    @pl.when(z < 3)
    def _():
        signal(device(z + 1, y, x, core))

    pl.semaphore_wait(barrier, 3 + (z > 0).astype(jnp.int32) + (z < 3).astype(jnp.int32))


def add_split(a, b):
    pair = a.astype(f32) + b.astype(f32)
    lanes = lax.broadcasted_iota(jnp.int32, pair.shape, 1)
    whole = jnp.where(lanes < 16, pair + pltpu.roll(pair, 112, 1), 0.0)
    high = whole.astype(bf16).astype(f32)
    return (high + pltpu.roll(whole - high, 16, 1)).astype(bf16)


def dot(a,b): return jnp.dot(a,b,preferred_element_type=f32)
def dot_nt(a,b): return lax.dot_general(a,b,(((1,),(1,)),((),())),preferred_element_type=f32)
def dot_tn(a,b): return lax.dot_general(a,b,(((0,),(0,)),((),())),preferred_element_type=f32)


EPS = 1e-05
HD = 128
BLOCK = 256


def block_of(r, parity):
    return 2 * r + (parity if r % 2 == 0 else 1 - parity)


def norm_factor(v):
    return lax.rsqrt(jnp.mean(v * v, -1, keepdims=True) + EPS)


def probabilities(r, start, q, k_ref, segc_ref, segr_ref):
    keys = (2 * r + 2) * BLOCK
    scores = dot_nt(q, k_ref[:keys]) * (HD ** -0.5)
    rows = start + lax.broadcasted_iota(jnp.int32, scores.shape, 0)
    columns = lax.broadcasted_iota(jnp.int32, scores.shape, 1)
    same = segc_ref[pl.ds(start, BLOCK)] == segr_ref[:, :keys]
    scores = jnp.where((rows >= columns) & same, scores, -1000000000.0)
    raised = jnp.exp(scores - jnp.max(scores, -1, keepdims=True))
    return raised / jnp.sum(raised, -1, keepdims=True)


VM = pl.BlockSpec(memory_space=pltpu.VMEM)


def masked_probs(b, q, k_ref, segc_ref, segr_ref):
    keys = (b + 1) * BLOCK
    scores = dot_nt(q, k_ref[:keys]) * (HD ** -0.5)
    rows = b * BLOCK + lax.broadcasted_iota(jnp.int32, scores.shape, 0)
    columns = lax.broadcasted_iota(jnp.int32, scores.shape, 1)
    same = segc_ref[b * BLOCK:keys] == segr_ref[:, :keys]
    scores = jnp.where((rows >= columns) & same, scores, -1000000000.0)
    raised = jnp.exp(scores - jnp.max(scores, -1, keepdims=True))
    return raised / jnp.sum(raised, -1, keepdims=True)


def far_first(z):
    ahead = z // 2
    return (3 - 3 * ahead, 2 - ahead, z + 1 - 2 * (z % 2), z)


def greet_peers(z, y, x, core, others):
    barrier = pltpu.get_barrier_semaphore()

    def signal(where):
        pl.semaphore_signal(barrier, inc=1, device_id=where, device_id_type=MESH)

    for n in range(4):
        pl.when(z != n)(lambda: signal(device(n, y, x, core)))
        pl.when(z != n)(lambda: signal(device(n, 1 - y, x, core)))
    signal(device(z, 1 - y, x, core))
    for where in others:
        signal(where)
    pl.semaphore_wait(barrier, 7 + len(others))


def picked(i, values):
    if isinstance(i, int):
        return values[i]
    return sum((i == k).astype(jnp.int32) * v for k, v in enumerate(values))


class Gather:
    def __init__(self, own, whole, local_sem, send, recv, lone=2, rows=BLOCK):
        self.own, self.whole, self.send, self.recv, self.rows = own, whole, send, recv, rows
        z, y, x, core = self.place = place()
        self.me = z * 2 + y
        half, eighth = rows // 2, rows // 8
        self.unit = eighth // 2
        lone, lead = lone * self.unit, 3 * self.unit
        self.keep = pltpu.make_async_copy(own, self.at(self.me, 0, rows), local_sem)

        def chunks(c):
            return ((c * half + x * (half - lead), lead), (c * half + (1 - x) * lead + x * lone, half - lead - lone))

        def edge(c, of):
            return (c * half + of * (half - lone), lone)

        self.slab, self.twin_slab = chunks(core), chunks(1 - core)
        self.mine, self.theirs = edge(core, x), edge(core, 1 - x)
        self.twin_theirs = edge(1 - core, 1 - x)

    def at(self, b, start, size):
        return self.whole.at[pl.ds(pl.multiple_of(b * self.rows + start, self.unit), size)]

    def copy(self, first, c, index, b, part, where, own=False):
        if own:
            source = self.own.at[pl.ds(pl.multiple_of(part[0], self.unit), part[1])]
        else:
            source = self.at(b, *part)
        return pltpu.make_async_remote_copy(
            src_ref=source, dst_ref=self.at(b, *part), send_sem=self.send.at[first + index], recv_sem=self.recv.at[first + index],
            device_id=where, device_id_type=MESH)

    def up(self, b, c, own=False):
        z, y, x, core = self.place
        return self.copy(0, c, c * 4 + b // 2, b, self.slab[c], device(z + 1, y, x, core), own)

    def down(self, b, c, own=False):
        z, y, x, core = self.place
        return self.copy(8, c, c * 4 + b // 2, b, self.slab[c], device(z - 1, y, x, core), own)

    def over(self, b, c, own=False):
        z, y, x, core = self.place
        return self.copy(16, c, c * 4 + b // 2, b, self.slab[c], device(z, 1 - y, x, core), own)

    def side(self, b, part):
        z, y, x, core = self.place
        return self.copy(24, 0, b, b, part, device(z, y, 1 - x, core))

    def twin(self, b, c, part):
        z, y, x, core = self.place
        return self.copy(32, c, c * 8 + b, b, part, device(z, y, x, 1 - core))

    def twin_x(self, b, part):
        z, y, x, core = self.place
        return self.copy(48, 0, b, b, part, device(z, y, x, 1 - core))

    def group(self, i):
        z = self.place[0]
        ahead = z // 2
        return picked(i, (z, z + 1 - 2 * (z % 2), 2 - ahead, 3 - 3 * ahead))

    def start_chunk(self, c):
        z, y, x, core = self.place
        pl.when(z < 3)(lambda: self.up(self.me, c, True).start())
        pl.when(z > 0)(lambda: self.down(self.me, c, True).start())
        self.over(self.me, c, True).start()

    def start(self):
        self.start_chunk(0)
        self.start_chunk(1)
        self.keep.start()

    def spread(self, b, c):
        if c == 0:
            self.side(b, self.mine).start()
        self.twin(b, c, self.slab[c]).start()

    def hop(self, i):
        z, y, x, core = self.place
        b = self.group(i) * 2 + y
        below = picked(i, (0, z % 2, z // 2, z // 2)) == 1
        for c in range(2):
            @pl.when(below)
            def _():
                self.up(b, c).wait_recv()
                pl.when(z < 3)(lambda: self.up(b, c).start())

            @pl.when(jnp.logical_not(below))
            def _():
                self.down(b, c).wait_recv()
                pl.when(z > 0)(lambda: self.down(b, c).start())

            self.over(b, c).start()
            self.spread(b, c)

    def hop_inside(self, i):
        z = self.place[0]
        pl.when((z > 0) & (z < 3))(lambda: self.hop(i))

    def hop_outside(self, i):
        z = self.place[0]
        pl.when(z % 3 == 0)(lambda: self.hop(i))

    def cross(self, i):
        b = self.group(i) * 2 + 1 - self.place[1]
        for c in range(2):
            self.over(b, c).wait_recv()
            self.spread(b, c)

    def blocks(self, i, act):
        y = self.place[1]
        n = self.group(i)
        act(n * 2 + 1 - y)
        if isinstance(i, int):
            if i > 0:
                act(n * 2 + y)
        else:
            pl.when(i > 0)(lambda: act(n * 2 + y))

    def flank(self, i):
        def act(b):
            self.side(b, self.theirs).wait_recv()
            self.twin_x(b, self.theirs).start()
        self.blocks(i, act)

    def complete(self, i):
        def act(b):
            for c in range(2):
                self.twin(b, c, self.twin_slab[c]).wait_recv()
            self.twin_x(b, self.twin_theirs).wait_recv()
        self.blocks(i, act)

    def drain(self):
        z, y, x, core = self.place
        for b in range(8):
            zb, yb = b // 2, b % 2

            @pl.when(self.me != b)
            def _():
                self.side(b, self.mine).wait_send()
                self.twin_x(b, self.theirs).wait_send()

            for c in range(2):
                pl.when(self.me != b)(lambda: self.twin(b, c, self.slab[c]).wait_send())
                pl.when(yb == y)(lambda: self.over(b, c).wait_send())
                pl.when((yb == y) & (zb <= z) & (z < 3))(lambda: self.up(b, c).wait_send())
                pl.when((yb == y) & (zb >= z) & (z > 0))(lambda: self.down(b, c).wait_send())

    def whole_run(self):
        self.start()
        self.hop(1)
        self.cross(0)
        self.hop_inside(2)
        self.flank(0)
        self.hop_outside(2)
        self.cross(1)
        self.hop_inside(3)
        self.flank(1)
        self.hop_outside(3)
        self.cross(2)
        self.cross(3)
        self.flank(2)
        self.flank(3)
        for i in range(4):
            self.complete(i)
        self.keep.wait()
        self.drain()


GATHER_SEMS = [pltpu.SemaphoreType.DMA, pltpu.SemaphoreType.DMA((56,)), pltpu.SemaphoreType.DMA((56,))]


ANY = pl.BlockSpec(memory_space=pl.ANY)


def sum_rows(target, source, rows):
    step = 32
    width = target.shape[-1]
    main = width - width % 1024

    @pl.loop(0, rows // step)
    def _(i):
        part = pl.ds(pl.multiple_of(i * step, step), step)
        wide = pl.ds(0, main)
        target[part, wide] = (target[part, wide].astype(f32) + source[part, wide].astype(f32)).astype(bf16)
        if main < width:
            tail = pl.ds(main, width - main)
            target[part, tail] = add_split(target[part, tail], source[part, tail])


class Scatter:
    def __init__(self, parts, start, total, buffers, sems):
        self.parts, self.total = parts, total
        self.cols = pl.ds(start, total.shape[1])
        self.held, self.from_core, self.from_x, self.from_y, self.from_below, self.from_above, self.shared_in = buffers
        self.load_sem, self.sems, self.recv_sems, self.end_send, self.end_recv = sems
        z, y, x, core = self.place = place()
        self.me = z * 2 + y
        self.order = far_first(z)
        self.half = half = parts.shape[1] // 2
        self.piece = piece = half // 4
        ds = lambda start, size: pl.ds(pl.multiple_of(start, piece), size)
        self.my_half, self.other_half = ds(core * half, half), ds((1 - core) * half, half)
        self.slab, self.mine, self.theirs = ds(x * piece, 3 * piece), ds(x * 3 * piece, piece), ds((1 - x) * 3 * piece, piece)
        self.shared = pl.ds(piece, 2 * piece)
        base = core * half
        self.out_mine, self.out_theirs = ds(base + x * 3 * piece, piece), ds(base + (1 - x) * 3 * piece, piece)
        self.out_shared = ds(base + piece, 2 * piece)
        self.across, self.twin = device(z, y, 1 - x, core), device(z, y, x, 1 - core)

    def remote(self, number, source, target, where):
        return pltpu.make_async_remote_copy(
            src_ref=source, dst_ref=target, send_sem=self.sems.at[number], recv_sem=self.recv_sems.at[number],
            device_id=where, device_id_type=MESH)

    def load(self, b):
        return pltpu.make_async_copy(self.parts.at[b, self.my_half, self.cols], self.held.at[b], self.load_sem.at[b])

    def to_core(self, b):
        return self.remote(b, self.parts.at[b, self.other_half, self.cols], self.from_core.at[b], self.twin)

    def to_x(self, b):
        return self.remote(8 + b, self.held.at[b, self.theirs], self.from_x.at[b], self.across)

    def to_y(self, zb):
        z, y, x, core = self.place
        return self.remote(16 + zb, self.held.at[zb * 2 + 1 - y, self.slab], self.from_y.at[zb], device(z, 1 - y, x, core))

    def to_above(self, zb):
        z, y, x, core = self.place
        return self.remote(20 + zb, self.held.at[zb * 2 + y, self.slab], self.from_below.at[zb], device(z + 1, y, x, core))

    def to_below(self, zb):
        z, y, x, core = self.place
        return self.remote(24 + zb, self.held.at[zb * 2 + y, self.slab], self.from_above.at[zb], device(z - 1, y, x, core))

    def begin(self, k):
        y = self.place[1]
        for yb in (1 - y, y):
            self.load(self.order[k] * 2 + yb).start()
            self.to_core(self.order[k] * 2 + yb).start()

    def stage_core(self, k, other):
        y = self.place[1]
        b = self.order[k] * 2 + (1 - y if other else y)
        self.load(b).wait()
        self.to_core(b).wait_recv()
        sum_rows(self.held.at[b], self.from_core.at[b], self.half)
        self.to_x(b).start()

    def stage_x(self, k, other=False):
        y = self.place[1]
        b = self.order[k] * 2 + (1 - y if other else y)
        self.to_x(b).wait_recv()
        sum_rows(self.held.at[b, self.mine], self.from_x.at[b], self.piece)

    def stage_y(self, k):
        self.stage_x(k, True)
        self.to_y(self.order[k]).start()

    def add_slab(self, zb, source):
        sum_rows(self.held.at[zb * 2 + self.place[1], self.slab], source.at[zb], 3 * self.piece)

    def stage_z(self, k):
        z = self.place[0]
        zb = self.order[k]
        self.to_y(zb).wait_recv()
        self.add_slab(zb, self.from_y)
        rises = (z // 2 == 0) if k < 2 else (z % 2 == 0)

        @pl.when(rises)
        def _():
            @pl.when(z > 0)
            def _():
                self.to_above(zb).wait_recv()
                self.add_slab(zb, self.from_below)
            self.to_above(zb).start()

        @pl.when(jnp.logical_not(rises))
        def _():
            @pl.when(z < 3)
            def _():
                self.to_below(zb).wait_recv()
                self.add_slab(zb, self.from_above)
            self.to_below(zb).start()

    def at_end(self, number, source, target, where):
        return pltpu.make_async_remote_copy(
            src_ref=source, dst_ref=target, send_sem=self.end_send.at[number], recv_sem=self.end_recv.at[number],
            device_id=where, device_id_type=MESH)

    def end_sums(self):
        return self.at_end(0, self.held.at[self.me, self.shared], self.shared_in, self.across)

    def end_ready(self, rows):
        return self.at_end(1, self.held.at[self.me, self.mine], self.total.at[rows], self.across)

    def end_twin(self, rows):
        return self.at_end(2, self.total.at[self.my_half], self.total.at[rows], self.twin)

    def own_sum(self):
        z = self.place[0]
        self.to_y(z).wait_recv()
        self.add_slab(z, self.from_y)

        @pl.when(z > 0)
        def _():
            self.to_above(z).wait_recv()
            self.add_slab(z, self.from_below)

        @pl.when(z < 3)
        def _():
            self.to_below(z).wait_recv()
            self.add_slab(z, self.from_above)
        self.end_sums().start()
        self.end_ready(self.out_mine).start()
        self.total[self.out_mine] = self.held[self.me, self.mine]

    def own_end(self):
        self.end_sums().wait()
        sum_rows(self.held.at[self.me, self.shared], self.shared_in, 2 * self.piece)
        self.total[self.out_shared] = self.held[self.me, self.shared]
        self.end_ready(self.out_theirs).wait_recv()
        self.end_twin(self.my_half).start()

    def finish(self):
        z = self.place[0]
        self.end_twin(self.other_half).wait_recv()
        self.end_ready(self.out_mine).wait_send()
        self.end_twin(self.my_half).wait_send()
        for b in range(8):
            self.to_core(b).wait_send()
            self.to_x(b).wait_send()
        for zb in range(4):
            self.to_y(zb).wait_send()
            pl.when(zb > z)(lambda: self.to_above(zb).wait_send())
            pl.when(zb < z)(lambda: self.to_below(zb).wait_send())


def scatter_buffers(rows, width):
    half, piece = rows // 2, rows // 8
    vm = pltpu.VMEM
    return [vm((8, half, width), bf16), vm((8, half, width), bf16), vm((8, piece, width), bf16)] + [
        vm((4, 3 * piece, width), bf16)] * 3 + [vm((2 * piece, width), bf16)]


SCATTER_SEMS = [pltpu.SemaphoreType.DMA((n,)) for n in (8, 28, 28, 3, 3)]


def sums_kernel(parts, x_ref, acts_ref, grads_ref, weighted_ref, total_a, total_b, gate_out, up_out, down_out, *rest):
    buffers_a, buffers_b, rest = rest[:7], rest[7:14], rest[14:]
    acts, weighted, x_buf, g_buf, gu_buf, down_buf = rest[:6]
    sems_a, sems_b, rest = rest[6:11], rest[11:16], rest[16:]
    fixed_sem, x_sem, g_sem, gu_sem, down_sem = rest
    z, y, x, core = place()
    D = x_ref.shape[1]
    sums = (Scatter(parts, D + total_a.shape[1], total_b, buffers_b, sems_b), Scatter(parts, D, total_a, buffers_a, sems_a))

    fixed = [pltpu.make_async_copy(acts_ref, acts, fixed_sem.at[0]), pltpu.make_async_copy(weighted_ref, weighted, fixed_sem.at[1])]
    ff = weighted.shape[1] // 2
    x_pieces, g_pieces = D // BLOCK, D // 512

    def x_load(k):
        return pltpu.make_async_copy(x_ref.at[:, pl.ds(k * BLOCK, BLOCK)], x_buf.at[k % 2], x_sem.at[k % 2])

    def g_load(k):
        return pltpu.make_async_copy(grads_ref.at[:, pl.ds(k * 512, 512)], g_buf.at[k % 2], g_sem.at[k % 2])

    def gu_store(k):
        rows = pl.ds(k * BLOCK, BLOCK)
        return [pltpu.make_async_copy(gu_buf.at[k % 2, u, j], (gate_out, up_out)[u].at[j, rows], gu_sem.at[k % 2, u, j])
                for u in range(2) for j in range(2)]

    def down_store(k):
        return [pltpu.make_async_copy(down_buf.at[k % 2, j], down_out.at[j, :, pl.ds(k * 512, 512)], down_sem.at[k % 2, j])
                for j in range(2)]

    def x_piece(k):
        if k == 0:
            fixed[0].wait()
        x_load(k).wait()
        if k >= 2:
            for copy in gu_store(k - 2):
                copy.wait()
        both = dot_tn(x_buf[k % 2], acts[...])
        for j in range(2):
            for u in range(2):
                gu_buf[k % 2, u, j] = both[:, (2 * j + u) * ff:(2 * j + u + 1) * ff]
        for copy in gu_store(k):
            copy.start()
        if k + 2 < x_pieces:
            x_load(k + 2).start()

    def g_piece(k):
        if k == 0:
            fixed[1].wait()
        g_load(k).wait()
        if k >= 2:
            for copy in down_store(k - 2):
                copy.wait()
        both = dot_tn(weighted[...], g_buf[k % 2])
        for j in range(2):
            down_buf[k % 2, j] = both[j * ff:(j + 1) * ff]
        for copy in down_store(k):
            copy.start()
        if k + 2 < g_pieces:
            g_load(k + 2).start()

    fillers = [functools.partial(x_piece, k) for k in range(x_pieces)]
    for k in range(g_pieces):
        fillers.insert(3 * k + 2, functools.partial(g_piece, k))

    greet(z, y, x, core)
    for k in range(4):
        for s in sums:
            s.begin(k)
        if k == 0:
            for copy in fixed:
                copy.start()
            for j in range(2):
                x_load(j).start()
                g_load(j).start()
    items = [(k, s) for k in range(4) for s in sums]
    for other in (True, False):
        sums[0].stage_core(0, other)
    for i, (k, s) in enumerate(items):
        if i < 7:
            items[i + 1][1].stage_core(items[i + 1][0], True)
        s.stage_y(k)
        if i < 7:
            items[i + 1][1].stage_core(items[i + 1][0], False)
        s.stage_x(k)
        if 0 < i < 7:
            items[i - 1][1].stage_z(items[i - 1][0])
        if i < 7:
            for fill in fillers[2 * i:2 * i + 2]:
                fill()
    for fill in fillers[14:]:
        fill()
    for s in sums:
        s.own_sum()
    for s in sums:
        s.own_end()
    for s in sums:
        s.finish()
    for k in (x_pieces - 2, x_pieces - 1):
        for copy in gu_store(k):
            copy.wait()
    for k in (g_pieces - 2, g_pieces - 1):
        for copy in down_store(k):
            copy.wait()


def sums_all(parts, x, acts, grads, weighted, number):
    _, rows, width = parts.shape
    T, D = x.shape
    ff = weighted.shape[1] // 2
    widths = (D // 2, D // 2 + 128)
    sd = jax.ShapeDtypeStruct
    dma = pltpu.SemaphoreType.DMA
    vm = pltpu.VMEM
    return pl.pallas_call(
        sums_kernel, in_specs=[ANY] * 5, out_specs=[VM, VM, ANY, ANY, ANY],
        out_shape=[sd((rows, w), bf16) for w in widths] + [sd((2, D, ff), f32), sd((2, D, ff), f32), sd((2, ff, D), f32)],
        scratch_shapes=scatter_buffers(rows, widths[0]) + scatter_buffers(rows, widths[1]) + [
            vm(acts.shape, bf16), vm(weighted.shape, bf16), vm((2, T, BLOCK), bf16), vm((2, T, 512), bf16),
            vm((2, 2, 2, BLOCK, ff), f32), vm((2, 2, ff, 512), f32)] + SCATTER_SEMS * 2 + [
            dma((2,)), dma((2,)), dma((2,)), dma((2, 2, 2)), dma((2, 2))],
        compiler_params=pltpu.CompilerParams(collective_id=number, has_side_effects=True, vmem_limit_bytes=62 * 2**20),
    )(parts, x, acts, grads, weighted)


def forward_kernel(hidden, sent_ref, gain1_ref, gain2_ref, qg_ref, kg_ref, segc_ref, segr_ref, wr_ref,
                   wq_in, wk_in, wv_in, cos_in, sin_in, wout_in, wg_in, wu_in, wd_in,
                   gathered, middle_out, moe_out, x_all, a_out, q_out, k_out, v_out, qr_out, kr_out, grads_all,
                   m_out, weighted_out, acts_out, parts_out,
                   w_qkv, cos_ref, sin_ref, w_out, wg, wu, wd, q_ref, k_ref, v_ref, qr_ref, kr_ref,
                   part, arrived, out_half, in_half, held, from_x, total, middle_ref, moe, whole, mask_all, w_buf, a_buf, p_buf,
                   x_keep, x_send, x_recv, c_keep, c_send, c_recv, m_keep, m_send, m_recv,
                   load, stream, out_sem, kept_sem, send, recv, pair_send, pair_recv):
    z, y, x, core = place()
    across, twin = device(z, y, 1 - x, core), device(z, y, x, 1 - core)
    first_expert = (z * 2 + y) * wg_in.shape[0]
    D, ff = wg_in.shape[1], wg_in.shape[2]
    span = 2 * BLOCK
    head = pl.ds(pl.multiple_of(z * HD, HD), HD)
    loads = [pltpu.make_async_copy(source, target, load.at[k]) for k, (source, target) in enumerate((
        (wq_in.at[:, head], w_qkv.at[:, pl.ds(0, HD)]), (wk_in.at[:, head], w_qkv.at[:, pl.ds(HD, HD)]),
        (wv_in.at[:, head], w_qkv.at[:, pl.ds(2 * HD, HD)]), (cos_in, cos_ref), (sin_in, sin_ref),
        (wout_in, w_out), (wd_in, wd), (wg_in, wg), (wu_in, wu)))]
    for copy in loads:
        copy.start()
    greet_peers(z, y, x, core, (across, twin))
    gather = Gather(hidden, x_all, x_keep, x_send, x_recv, 3)
    cot = Gather(sent_ref, grads_all, c_keep, c_send, c_recv)
    experts = Gather(moe, whole, m_keep, m_send, m_recv)

    def remote(source, target, ssem, rsem, where):
        return pltpu.make_async_remote_copy(
            src_ref=source, dst_ref=target, send_sem=ssem, recv_sem=rsem, device_id=where, device_id_type=MESH)

    gather.start()
    gather.hop(1)
    gather.cross(0)
    gather.hop_inside(2)
    gather.flank(0)
    gather.keep.wait()
    for copy in loads[:5]:
        copy.wait()

    def rows_of(i):
        return pl.ds(pl.multiple_of(gather.group(i) * span, span), span)

    x_part, a_part = p_buf.at[:, pl.ds(0, D)], p_buf.at[:, pl.ds(D, D)]

    def a_store(i):
        return pltpu.make_async_copy(a_part, a_out.at[rows_of(i)], stream.at[1])

    def project(i):
        gather.complete(i)
        rows = rows_of(i)
        fetch = pltpu.make_async_copy(x_all.at[rows], x_part, stream.at[0])
        fetch.start()
        if i > 0:
            a_store(i - 1).wait()
        fetch.wait()
        v = p_buf[:, :D].astype(f32)
        a = (v * norm_factor(v) * gain1_ref[...]).astype(bf16)
        p_buf[:, D:2 * D] = a
        a_store(i).start()
        raw = dot(a, w_qkv[...])
        cosine, sine = cos_ref[rows], sin_ref[rows]

        def turned(part, gain):
            n = part * norm_factor(part) * gain
            return (n * cosine + pltpu.roll(n, HD // 2, 1) * sine).astype(bf16)

        q_raw, k_raw = raw[:, :HD], raw[:, HD:2 * HD]
        qr_ref[rows] = q_raw
        kr_ref[rows] = k_raw
        q_ref[rows] = turned(q_raw, qg_ref[:, head])
        k_ref[rows] = turned(k_raw, kg_ref[:, head])
        v_ref[rows] = raw[:, 2 * HD:].astype(bf16)

    for i in range(4):
        if i < 2:
            gather.hop_outside(i + 2)
        if i < 3:
            gather.cross(i + 1)
        if i == 0:
            gather.hop_inside(3)
        if i == 1:
            cot.start()
        project(i)
        if i < 3:
            gather.flank(i + 1)
    a_store(3).wait()
    keeps = [pltpu.make_async_copy(source, target, kept_sem.at[k]) for k, (source, target) in enumerate((
        (q_ref, q_out), (k_ref, k_out), (v_ref, v_out), (qr_ref, qr_out), (kr_ref, kr_out),
        (middle_ref, middle_out), (moe, moe_out)))]
    for copy in keeps[:5]:
        copy.start()
    targets = lambda r: (y if r % 2 == 0 else 1 - y)
    source_y = (y + z) % 2

    def to_block(r):
        return remote(part.at[r], arrived.at[z], send.at[r], recv.at[z], device(r, targets(r), x, core))

    def from_head(n):
        return remote(part.at[n], arrived.at[n], send.at[n], recv.at[n], device(n, source_y, x, core))

    here = lambda r: (z == r) & (z % 2 == 0)
    for r in range(3, -1, -1):
        start = pl.multiple_of(block_of(r, y) * BLOCK, BLOCK)
        probs = probabilities(r, start, q_ref[pl.ds(start, BLOCK)], k_ref, segc_ref, segr_ref)
        part[r] = dot(probs.astype(bf16), v_ref[:(2 * r + 2) * BLOCK]).astype(bf16)
        pl.when(jnp.logical_not(here(r)))(lambda: to_block(r).start())
    cot.hop(1)
    cot.cross(0)
    cot.hop_inside(2)
    cot.flank(0)

    @pl.when(z % 2 == 0)
    def _():
        arrived[z] = part[z]

    loads[5].wait()
    for n in range(4):
        pl.when(jnp.logical_not(here(n)))(lambda: from_head(n).wait_recv())
        gathered[:, n * HD:(n + 1) * HD] = arrived[n]
    cot.hop_outside(2)
    cot.cross(1)
    cot.hop_inside(3)

    half = BLOCK // 2
    chunk = half // 2
    my_half = core * half
    other_half = (1 - core) * half
    piece = lambda c: pl.ds(pl.multiple_of(c * chunk, chunk), chunk)
    at = lambda base, c: pl.ds(pl.multiple_of(base + c * chunk, chunk), chunk)

    def pair(kind, c, source, target, where):
        return remote(source, target, pair_send.at[kind, c], pair_recv.at[kind, c], where)

    first = lambda c: pair(0, c, out_half.at[piece(c)], in_half.at[piece(c)], twin)
    second = lambda c: pair(1, c, held.at[piece(c)], from_x.at[piece(c)], across)
    third = lambda c: pair(2, c, total.at[at(my_half, c)], total.at[at(my_half, c)], twin)
    for c in (1 - x, x):
        out_half[piece(c)] = dot(gathered[at(other_half, c)], w_out[...]).astype(bf16)
        first(c).start()
    for c in (1 - x, x):
        kept = dot(gathered[at(my_half, c)], w_out[...])
        first(c).wait_recv()
        held[piece(c)] = (kept + in_half[piece(c)].astype(f32)).astype(bf16)
        second(c).start()
    cot.flank(1)
    step = 32

    def norm_rows(base, count):
        def body(i, _):
            rows = pl.ds(pl.multiple_of(base + i * step, step), step)
            v = hidden[rows].astype(f32) + total[rows].astype(f32)
            middle_ref[rows] = v
            moe[rows] = (v * norm_factor(v) * gain2_ref[...]).astype(bf16)
            return 0
        lax.fori_loop(0, count // step, body, 0)

    for k, c in enumerate((x, 1 - x)):
        second(c).wait_recv()
        total[at(my_half, c)] = (held[piece(c)].astype(f32) + from_x[piece(c)].astype(f32)).astype(bf16)
        third(c).start()
        norm_rows(my_half + c * chunk, chunk)
        experts.start_chunk(k)
        if k == 0:
            cot.hop_outside(3)
            cot.cross(2)
    for c in (x, 1 - x):
        pair(2, c, total.at[at(my_half, c)], total.at[at(other_half, c)], twin).wait_recv()
    norm_rows(other_half, half)
    experts.keep.start()
    for copy in keeps[5:]:
        copy.start()
    cot.flank(2)
    experts.hop(1)
    experts.cross(0)
    cot.cross(3)
    experts.hop_inside(2)
    experts.flank(0)
    cot.flank(3)
    experts.keep.wait()
    cot.keep.wait()
    for copy in loads[6:]:
        copy.wait()

    def grads_load(i):
        rows = rows_of(i)
        return [pltpu.make_async_copy(grads_all.at[rows, pl.ds(0, D)], p_buf.at[:, pl.ds(0, D)], stream.at[1]),
                pltpu.make_async_copy(grads_all.at[rows, pl.ds(D, 128)], mask_all, stream.at[2])]

    def stores(i):
        rows = rows_of(i)
        return [
            pltpu.make_async_copy(w_buf.at[i % 2], weighted_out.at[rows], out_sem.at[i % 2, 0]),
            pltpu.make_async_copy(a_buf.at[i % 2], acts_out.at[rows], out_sem.at[i % 2, 1]),
            pltpu.make_async_copy(whole.at[rows], m_out.at[rows], out_sem.at[i % 2, 2]),
        ]

    def parts_store(i):
        return pltpu.make_async_copy(p_buf, parts_out.at[rows_of(i)], stream.at[0])

    def run_experts(i):
        cot.complete(i)
        if i > 0:
            parts_store(i - 1).wait()
        fetches = grads_load(i)
        for copy in fetches:
            copy.start()
        slot = i % 2
        if i >= 2:
            for copy in stores(i - 2):
                copy.wait()
        for copy in fetches:
            copy.wait()
        gw = [dot_nt(p_buf[:, :D], wd[j]) for j in range(2)]
        experts.complete(i)

        rows = rows_of(i)
        v = whole[rows]
        logits = dot_nt(v, wr_ref[...])
        count = logits.shape[1]
        mask = mask_all[:, :count].astype(f32) > 0
        top = jnp.max(jnp.where(mask, logits, -jnp.inf), -1, keepdims=True)
        raised = jnp.where(mask, jnp.exp(jnp.where(mask, logits - top, 0.0)), 0.0)
        gates = raised / jnp.sum(raised, -1, keepdims=True)
        lane = lax.broadcasted_iota(jnp.int32, gates.shape, 1)
        gg = jnp.zeros(gates.shape, f32)
        for j in range(2):
            mine = lane == first_expert + j
            gate = jnp.sum(jnp.where(mine, gates, 0.0), -1, keepdims=True)
            ga = dot(v, wg[j])
            ua = dot(v, wu[j])
            gw_j = gw[j]
            s = 1.0 / (1.0 + jnp.exp(-ga))
            silu = ga * s
            h = (silu * ua).astype(bf16).astype(f32)
            gg = gg + jnp.where(mine, jnp.sum(h * gw_j, -1, keepdims=True), 0.0)
            gh = gw_j * gate
            w_buf[slot, :, j * ff:(j + 1) * ff] = (h * gate).astype(bf16)
            a_buf[slot, :, 2 * j * ff:(2 * j + 1) * ff] = (gh * ua * s * (1.0 + ga * (1.0 - s))).astype(bf16)
            a_buf[slot, :, (2 * j + 1) * ff:(2 * j + 2) * ff] = (gh * silu).astype(bf16)
        for copy in stores(i):
            copy.start()
        if i < 3:
            experts.flank(i + 1)
        p_buf[:, :D] = dot(w_buf[slot], wd[...].reshape(2 * ff, D)).astype(bf16)
        gx = dot_nt(a_buf[slot, :, :ff], wg[0])
        for k, weight in ((1, wu[0]), (2, wg[1]), (3, wu[1])):
            gx = gx + dot_nt(a_buf[slot, :, k * ff:(k + 1) * ff], weight)
        p_buf[:, D:2 * D] = gx.astype(bf16)
        high = gg.astype(bf16)
        low = (gg - high.astype(f32)).astype(bf16)
        spare = jnp.zeros((span, 128 - 2 * count), bf16)
        p_buf[:, 2 * D:] = jnp.concatenate([high, low, spare], 1)
        parts_store(i).start()

    for i in range(4):
        if i < 2:
            experts.hop_outside(i + 2)
        if i < 3:
            experts.cross(i + 1)
        if i == 0:
            experts.hop_inside(3)
        run_experts(i)
    parts_store(3).wait()
    for i in (2, 3):
        for copy in stores(i):
            copy.wait()
    for copy in keeps:
        copy.wait()
    gather.drain()
    cot.drain()
    experts.drain()
    for c in range(2):
        first(c).wait_send()
        second(c).wait_send()
        third(c).wait_send()
    for r in range(4):
        pl.when(jnp.logical_not(here(r)))(lambda: to_block(r).wait_send())


def forward_all(hidden, sent, gain1, gain2, qg, kg, segc, segr, wr, wq, wk, wv, cosine, sine, wout, wg, wu, wd, number):
    rows, D = hidden.shape
    T = 8 * rows
    J, _, F = wg.shape
    half, span = rows // 2, 2 * rows
    sd = jax.ShapeDtypeStruct
    dma = pltpu.SemaphoreType.DMA
    vm = pltpu.VMEM
    like = lambda m: vm(m.shape, m.dtype)
    heads = [((T, HD), bf16)] * 3 + [((T, HD), f32)] * 2
    return pl.pallas_call(
        forward_kernel, in_specs=[VM] * 9 + [ANY] * 9, out_specs=[VM] + [ANY] * 14,
        out_shape=[sd((rows, 4 * HD), bf16), sd((rows, D), f32), sd((rows, D), bf16), sd((T, D), bf16), sd((T, D), bf16)]
        + [sd(*m) for m in heads] + [sd((T, D + 128), bf16), sd((T, D), bf16), sd((T, J * F), bf16), sd((T, 2 * J * F), bf16),
                                     sd((T, 2 * D + 128), bf16)],
        scratch_shapes=[vm((D, 3 * HD), bf16)] + [like(m) for m in (cosine, sine, wout, wg, wu, wd)]
        + [vm(*m) for m in heads] + [vm((4, BLOCK, HD), bf16)] * 2 + [vm((half, D), bf16)] * 4 + [vm((rows, D), bf16), vm((rows, D), f32), vm((rows, D), bf16)] + [
            vm((T, D), bf16), vm((span, 128), bf16), vm((2, span, J * F), bf16), vm((2, span, 2 * J * F), bf16),
            vm((span, 2 * D + 128), bf16)] + GATHER_SEMS * 3 + [
            dma((9,)), dma((3,)), dma((2, 3)), dma((7,)), dma((4,)), dma((4,)), dma((3, 2)), dma((3, 2))],
        compiler_params=pltpu.CompilerParams(collective_id=number, has_side_effects=True, vmem_limit_bytes=62 * 2**20),
    )(hidden, sent, gain1, gain2, qg, kg, segc, segr, wr, wq, wk, wv, cosine, sine, wout, wg, wu, wd)


def backward_kernel(ga_ref, segc_ref, segr_ref, qg_ref, kg_ref, gains_small, gain_ref,
                    w_in, ctx_ref, q_in, k_in, v_in, qr_in, kr_in, cos_in, sin_in, wq_in, wk_in, wv_in, a_in, hidden_in, middle_in, parts,
                    grad_ref, weights_q, weights_k, weights_v, norm_ref, gains_out, wout_ref, small_out, sum_ref,
                    w_ref, q_ref, k_ref, v_ref, qr_ref, kr_ref, cos_ref, sin_ref, wq_ref, wk_ref, wv_ref, columns, hidden_ref, middle_ref,
                    raw_ref, g_own, g_all, dk, dv, terms, from_y, held_terms, from_below, from_above,
                    small_y, small_sum, small_z, raw_in, gathered, products, from_z, out_half, in_half, held, from_x, total, gains_own, gains_in, norm_in,
                    load, g_send, g_recv, f_send, f_recv, t_send, t_recv, s_send, s_recv, send, recv, w_send, w_recv,
                    pair_send, pair_recv, e_send, e_recv, n_send, n_recv, *scatter):
    small_ref = gains_small
    z, y, x, core = place()
    me = z * 2 + y
    order = far_first(z)
    span = 4 * HD
    across, twin, corner = device(z, y, 1 - x, core), device(z, y, x, 1 - core), device(z, y, 1 - x, 1 - core)
    partner = device(z, 1 - y, x, core)

    loads = [pltpu.make_async_copy(source, target, load.at[k]) for k, (source, target) in enumerate((
        (w_in, w_ref), (q_in, q_ref), (k_in, k_ref), (v_in, v_ref), (qr_in, qr_ref), (kr_in, kr_ref), (cos_in, cos_ref),
        (sin_in, sin_ref), (wq_in, wq_ref), (wk_in, wk_ref), (wv_in, wv_ref), (hidden_in, hidden_ref), (middle_in, middle_ref)))]

    def column_load(n):
        block = pl.ds(pl.multiple_of((order[n] * 2 + y) * BLOCK, BLOCK), BLOCK)
        return pltpu.make_async_copy(a_in.at[:, block], columns.at[n % 2], load.at[13 + n % 2])

    for copy in loads:
        copy.start()
    greet_peers(z, y, x, core, (across, twin, corner))
    sums = Scatter(parts, 0, sum_ref, scatter[:7], scatter[7:])
    for k in range(4):
        sums.begin(k)
    column_load(0).start()
    column_load(1).start()

    def remote(source, target, ssem, rsem, where):
        return pltpu.make_async_remote_copy(
            src_ref=source, dst_ref=target, send_sem=ssem, recv_sem=rsem, device_id=where, device_id_type=MESH)

    def when_away(n, act):
        pl.when(z != n)(act)

    loads[0].wait()
    g_context = dot_nt(ga_ref[...], w_ref[...]).astype(bf16)
    for n in range(4):
        g_own[n] = g_context[:, n * HD:(n + 1) * HD]

    def g_to(n):
        return remote(g_own.at[n], g_all.at[me], g_send.at[n], g_recv.at[z], device(n, y, x, core))

    def g_from(n):
        return remote(g_own.at[n], g_all.at[n * 2 + y], g_send.at[n], g_recv.at[n], device(n, y, x, core))

    def g_over(n):
        return remote(g_all.at[n * 2 + y], g_all.at[n * 2 + y], f_send.at[n], f_recv.at[n], partner)

    def g_over_in(n):
        return remote(g_all.at[n * 2 + 1 - y], g_all.at[n * 2 + 1 - y], f_send.at[n], f_recv.at[n], partner)

    for n in range(4):
        when_away(n, lambda: g_to(n).start())
    g_all[me] = g_own[z]
    g_over(z).start()

    quarter = small_ref.shape[1] // 4

    def lanes(cx, cc):
        return pl.ds(pl.multiple_of((cx * 2 + cc) * quarter, quarter), quarter)

    own_lanes = lanes(x, core)
    small_pair = remote(small_ref.at[:, own_lanes], small_y, s_send.at[0], s_recv.at[0], partner)
    small_pair.start()

    def small_along(n):
        return remote(small_sum, small_z.at[z], s_send.at[1 + n], s_recv.at[1 + z], device(n, y, x, core))

    def small_arriving(n):
        return remote(small_sum, small_z.at[n], s_send.at[1 + n], s_recv.at[1 + n], device(n, y, x, core))

    fans = (across, twin, corner)
    fan_lanes = (lanes(1 - x, core), lanes(x, 1 - core), lanes(1 - x, 1 - core))

    def small_spread(i):
        return remote(small_out.at[:, own_lanes], small_out.at[:, own_lanes], s_send.at[5 + i], s_recv.at[5 + i], fans[i])

    def small_spread_in(i):
        return remote(small_out.at[:, own_lanes], small_out.at[:, fan_lanes[i]], s_send.at[5 + i], s_recv.at[5 + i], fans[i])

    for b in range(8):
        terms[b] = dot_tn(ctx_ref[...], ga_ref[:, b * BLOCK:(b + 1) * BLOCK]).astype(bf16)

    def term_pair(n):
        return remote(terms.at[n * 2 + 1 - y], from_y.at[n], t_send.at[0, n], t_recv.at[0, n], partner)

    def term_up(n):
        return remote(held_terms.at[n], from_below.at[n], t_send.at[1, n], t_recv.at[1, n], device(z + 1, y, x, core))

    def term_down(n):
        return remote(held_terms.at[n], from_above.at[n], t_send.at[2, n], t_recv.at[2, n], device(z - 1, y, x, core))

    def paired(n):
        return terms[n * 2 + y].astype(f32) + from_y[n].astype(f32)

    def term_stage(k):
        n = order[k]
        term_pair(n).wait_recv()
        held_terms[n] = paired(n).astype(bf16)
        rises = (z // 2 == 0) if k < 2 else (z % 2 == 0)

        @pl.when(rises)
        def _():
            @pl.when(z > 0)
            def _():
                term_up(n).wait_recv()
                held_terms[n] = (paired(n) + from_below[n].astype(f32)).astype(bf16)
            term_up(n).start()

        @pl.when(jnp.logical_not(rises))
        def _():
            @pl.when(z < 3)
            def _():
                term_down(n).wait_recv()
                held_terms[n] = (paired(n) + from_above[n].astype(f32)).astype(bf16)
            term_down(n).start()

    for k in range(3):
        sums.stage_core(k, True)
        sums.stage_core(k, False)
    for n in range(4):
        when_away(n, lambda: g_from(n).wait_recv())
        when_away(n, lambda: g_over(n).start())
    for n in order:
        term_pair(n).start()

    def rows_to(n):
        return remote(raw_ref.at[n * 2 + y], raw_in.at[z], send.at[n], recv.at[z], device(n, y, x, core))

    def rows_from(n):
        return remote(raw_ref.at[n * 2 + y], raw_in.at[n], send.at[n], recv.at[n], device(n, y, x, core))

    gain_sums = [jnp.zeros((1, HD), f32), jnp.zeros((1, HD), f32)]

    def back(turned, b, raw_in, gain, which):
        rows = slice(b * BLOCK, (b + 1) * BLOCK)
        g = turned * cos_ref[rows] - pltpu.roll(turned, HD // 2, 1) * sin_ref[rows]
        raw = raw_in[rows]
        factor = norm_factor(raw)
        n = raw * factor
        gain_sums[which] = gain_sums[which] + jnp.sum(g * n, 0, keepdims=True)
        g = g * gain[:, pl.ds(pl.multiple_of(z * HD, HD), HD)]
        return (factor * (g - n * jnp.mean(g * n, -1, keepdims=True))).astype(bf16)

    for copy in loads[1:8]:
        copy.wait()
    for b in range(7, -1, -1):
        keys = (b + 1) * BLOCK
        rows = slice(b * BLOCK, keys)
        pl.when(y != b % 2)(lambda: g_over_in(b // 2).wait_recv())
        q = q_ref[rows]
        g = g_all[b]
        probs = masked_probs(b, q, k_ref, segc_ref, segr_ref)
        gv = dot_tn(probs.astype(bf16), g)
        gp = dot_nt(g, v_ref[:keys])
        gs = (probs * (gp - jnp.sum(gp * probs, -1, keepdims=True))).astype(bf16)
        gk = dot_tn(gs, q)
        if b == 7:
            dv[...] = gv
            dk[...] = gk
        else:
            dv[:keys] += gv
            dk[:keys] += gk
        raw_ref[b, :, :HD] = back(dot(gs, k_ref[:keys]) * (HD ** -0.5), b, qr_ref, qg_ref, 0)
        raw_ref[b, :, HD:2 * HD] = back(dk[rows] * (HD ** -0.5), b, kr_ref, kg_ref, 1)
        raw_ref[b, :, 2 * HD:] = dv[rows].astype(bf16)

        @pl.when(y == b % 2)
        def _():
            when_away(b // 2, lambda: rows_to(b // 2).start())

    for k in range(3):
        sums.stage_y(k)
        sums.stage_x(k)

    small_pair.wait_recv()
    small_sum[...] = small_ref[:, own_lanes] + small_y[...]
    for n in range(4):
        when_away(n, lambda: small_along(n).start())
    small_z[z] = small_sum[...]
    gains_own[0:1] = gain_sums[0]
    gains_own[1:2] = gain_sums[1]

    def gains_to(n):
        return remote(gains_own, gains_in.at[z], e_send.at[n], e_recv.at[z], device(n, y, x, core))

    def gains_from(n):
        return remote(gains_own, gains_in.at[n], e_send.at[n], e_recv.at[n], device(n, y, x, core))

    for n in range(4):
        when_away(n, lambda: gains_to(n).start())
    gains_in[z] = gains_own[...]
    raw_in[z] = raw_ref[me]

    def products_to(n):
        return remote(products.at[n], from_z.at[z], w_send.at[n], w_recv.at[z], device(n, y, x, core))

    def products_from(n):
        return remote(products.at[n], from_z.at[n], w_send.at[n], w_recv.at[n], device(n, y, x, core))

    raw_all = raw_ref[...].reshape(8 * BLOCK, 3 * HD)
    for i, n in enumerate(order):
        column_load(i).wait()
        product = dot_tn(columns[i % 2], raw_all).astype(bf16)
        if i < 2:
            column_load(i + 2).start()
        if i < 3:
            products[n] = product
            products_to(n).start()
        else:
            from_z[z] = product

    for copy in loads[8:]:
        copy.wait()
    for n in range(4):
        when_away(n, lambda: rows_from(n).wait_recv())
        for g in range(3):
            gathered[:, g * span + n * HD:g * span + (n + 1) * HD] = raw_in[n, :, g * HD:(g + 1) * HD]

    rows = total.shape[0]
    half = rows // 2
    chunk = half // 2
    my_half = core * half
    other_half = (1 - core) * half
    piece = lambda c: pl.ds(c * chunk, chunk)
    at = lambda base, c: pl.ds(pl.multiple_of(base + c * chunk, chunk), chunk)

    def pair(kind, c, source, target, where):
        return remote(source, target, pair_send.at[kind, c], pair_recv.at[kind, c], where)

    def multiply(part):
        return (dot_nt(part[:, :span], wq_ref[...]) + dot_nt(part[:, span:2 * span], wk_ref[...])
                + dot_nt(part[:, 2 * span:], wv_ref[...]))

    first = [pair(0, c, out_half.at[piece(c)], in_half.at[piece(c)], twin) for c in range(2)]
    second = [pair(1, c, held.at[piece(c)], from_x.at[piece(c)], across) for c in range(2)]
    third = [pair(2, c, total.at[at(my_half, c)], total.at[at(my_half, c)], twin) for c in range(2)]
    for c in range(2):
        out_half[piece(c)] = multiply(gathered[at(other_half, c)]).astype(bf16)
        first[c].start()
    for c in range(2):
        kept = multiply(gathered[at(my_half, c)])
        first[c].wait_recv()
        held[piece(c)] = (kept + in_half[piece(c)].astype(f32)).astype(bf16)
        second[c].start()

    term_stage(0)
    sums.stage_core(3, True)
    sums.stage_core(3, False)
    sums.stage_z(0)
    term_stage(1)
    for c in range(2):
        second[c].wait_recv()
        total[at(my_half, c)] = (held[piece(c)].astype(f32) + from_x[piece(c)].astype(f32)).astype(bf16)
        third[c].start()

    step = 32

    def norm_rows(base):
        def body(i, norm_part):
            part = pl.ds(pl.multiple_of(base + i * step, step), step)
            e = total[part].astype(f32)
            v = hidden_ref[part].astype(f32)
            factor = norm_factor(v)
            n = v * factor
            norm_part = norm_part + jnp.sum(e * n, 0, keepdims=True)
            e = e * gain_ref[...]
            grad_ref[part] = middle_ref[part] + factor * (e - n * jnp.mean(e * n, -1, keepdims=True))
            return norm_part
        return body

    nothing = jnp.zeros((1, total.shape[1]), f32)
    mine_part = lax.fori_loop(0, half // step, norm_rows(my_half), nothing)
    for c in range(2):
        pair(2, c, total.at[at(my_half, c)], total.at[at(other_half, c)], twin).wait_recv()
    other_part = lax.fori_loop(0, half // step, norm_rows(other_half), nothing)
    norm_part = mine_part + other_part
    for t in range(norm_in.shape[1]):
        norm_in[me, t:t + 1] = norm_part[:, t * 128:(t + 1) * 128]

    def norm_to(b):
        return remote(norm_in.at[me], norm_in.at[me], n_send.at[b], n_recv.at[me], device(b // 2, b % 2, x, core))

    def norm_from(b):
        return remote(norm_in.at[b], norm_in.at[b], n_send.at[b], n_recv.at[b], device(b // 2, b % 2, x, core))

    for b in range(8):
        pl.when(me != b)(lambda: norm_to(b).start())
    sums.stage_y(3)
    sums.stage_x(3)
    sums.stage_z(1)
    term_stage(2)
    sums.stage_z(2)
    term_pair(z).wait_recv()
    wout_ref[...] = paired(z)

    @pl.when(z > 0)
    def _():
        term_up(z).wait_recv()
        wout_ref[...] += from_below[z].astype(f32)

    @pl.when(z < 3)
    def _():
        term_down(z).wait_recv()
        wout_ref[...] += from_above[z].astype(f32)

    for n in range(4):
        when_away(n, lambda: small_arriving(n).wait_recv())
    small_out[:, own_lanes] = (small_z[0] + small_z[1]) + (small_z[2] + small_z[3])
    for i in range(3):
        small_spread(i).start()
    for n in range(4):
        when_away(n, lambda: gains_from(n).wait_recv())
        gains_out[:, n * HD:(n + 1) * HD] = gains_in[n]
    sums.own_sum()
    for n in range(4):
        when_away(n, lambda: products_from(n).wait_recv())
    for n in range(4):
        for g in range(3):
            (weights_q, weights_k, weights_v)[g][:, n * HD:(n + 1) * HD] = from_z[n, :, g * HD:(g + 1) * HD].astype(f32)
    sums.own_end()
    for b in range(8):
        pl.when(me != b)(lambda: norm_from(b).wait_recv())
    norms = [norm_in[b] for b in range(8)]
    norm_sum = ((norms[0] + norms[1]) + (norms[2] + norms[3])) + ((norms[4] + norms[5]) + (norms[6] + norms[7]))
    for t in range(norm_in.shape[1]):
        norm_ref[:, t * 128:(t + 1) * 128] = norm_sum[t:t + 1]

    sums.finish()
    for i in range(3):
        small_spread_in(i).wait_recv()
        small_spread(i).wait_send()
    small_pair.wait_send()
    for c in range(2):
        first[c].wait_send()
        second[c].wait_send()
        third[c].wait_send()
    for b in range(8):
        pl.when(me != b)(lambda: norm_to(b).wait_send())
    for n in range(4):
        when_away(n, lambda: g_to(n).wait_send())
        g_over(n).wait_send()
        term_pair(n).wait_send()
        pl.when(n > z)(lambda: term_up(n).wait_send())
        pl.when(n < z)(lambda: term_down(n).wait_send())
        when_away(n, lambda: small_along(n).wait_send())
        when_away(n, lambda: rows_to(n).wait_send())
        when_away(n, lambda: products_to(n).wait_send())
        when_away(n, lambda: gains_to(n).wait_send())


def backward_all(ga, segc, segr, qg, kg, small, gain, w, ctx, q, k, v, qr, kr, cosine, sine, wq, wk, wv, a, hidden, middle, parts, number):
    T, D = a.shape
    rows, half = BLOCK, BLOCK // 2
    span = 4 * HD
    S = small.shape[0]
    sd = jax.ShapeDtypeStruct
    dma = pltpu.SemaphoreType.DMA
    vm = pltpu.VMEM
    like = lambda m: vm(m.shape, m.dtype)
    return pl.pallas_call(
        backward_kernel, in_specs=[VM] * 7 + [ANY, VM] + [ANY] * 14, out_specs=[VM] * 9,
        out_shape=[sd((rows, D), f32), sd((BLOCK, span), f32), sd((BLOCK, span), f32), sd((BLOCK, span), f32), sd((1, D), f32), sd((2, span), f32),
                   sd((span, BLOCK), f32), sd((S, D), f32), sd((rows, D), bf16)],
        scratch_shapes=[like(m) for m in (w, q, k, v, qr, kr, cosine, sine, wq, wk, wv)] + [
            vm((2, T, BLOCK), bf16), like(hidden), like(middle),
            vm((8, BLOCK, 3 * HD), bf16), vm((4, BLOCK, HD), bf16), vm((8, BLOCK, HD), bf16), vm((T, HD), f32), vm((T, HD), f32),
            vm((8, span, BLOCK), bf16)] + [vm((4, span, BLOCK), bf16)] * 4 + [
            vm((S, D // 4), f32), vm((S, D // 4), f32), vm((4, S, D // 4), f32),
            vm((4, BLOCK, 3 * HD), bf16), vm((rows, 3 * span), bf16), vm((4, BLOCK, 3 * HD), bf16), vm((4, BLOCK, 3 * HD), bf16)] + [vm((half, D), bf16)] * 4 + [
            vm((rows, D), bf16), vm((2, HD), f32), vm((4, 2, HD), f32), vm((8, D // 128, 128), f32),
            dma((15,)), dma((4,)), dma((4,)), dma((4,)), dma((4,)), dma((3, 4)), dma((3, 4)), dma((8,)), dma((8,)),
            dma((4,)), dma((4,)), dma((4,)), dma((4,)), dma((3, 2)), dma((3, 2)), dma((4,)), dma((4,)), dma((8,)), dma((8,)),
        ] + scatter_buffers(rows, D) + SCATTER_SEMS,
        compiler_params=pltpu.CompilerParams(collective_id=number, has_side_effects=True, vmem_limit_bytes=63 * 2**20),
    )(ga, segc, segr, qg, kg, small, gain, w, ctx, q, k, v, qr, kr, cosine, sine, wq, wk, wv, a, hidden, middle, parts)


def on_device(
    hidden_in,
    norm1_gain,
    w_query,
    w_key,
    w_value,
    w_out,
    query_gain,
    key_gain,
    norm2_gain,
    w_router,
    w_gate,
    w_up,
    w_down,
    routes,
    segments,
    cotangent,
):
    seq_len, width = hidden_in.shape
    local_width = w_query.shape[1]
    head_count = local_width // HEAD_DIM
    expert_devs = lax.axis_size("expert")
    local_experts = w_gate.shape[0]
    expert_total = w_router.shape[1]
    capacity = 2 * seq_len * TOP // expert_total
    slab_rows = local_experts * capacity
    my_index = lax.axis_index("expert")
    group = SEQ // seq_len
    rank = my_index % group
    f32 = jnp.float32
    bf16 = jnp.bfloat16

    def split_heads(values):
        return values.reshape(seq_len, head_count, HEAD_DIM)

    inputs = hidden_in.astype(f32)
    inverse_attn = inverse_rms(inputs)
    normed_attn = inputs * inverse_attn
    attn_input = (normed_attn * norm1_gain).astype(bf16)
    q_raw = split_heads(jnp.dot(attn_input, w_query, preferred_element_type=f32))
    k_raw = split_heads(jnp.dot(attn_input, w_key, preferred_element_type=f32))
    v_heads = split_heads(jnp.dot(attn_input, w_value, preferred_element_type=f32).astype(bf16))
    q_gains = query_gain.reshape(head_count, HEAD_DIM)
    k_gains = key_gain.reshape(head_count, HEAD_DIM)
    q_inverse = inverse_rms(q_raw)
    q_normed = q_raw * q_inverse
    k_inverse = inverse_rms(k_raw)
    k_normed = k_raw * k_inverse
    local_places = lax.iota(jnp.int32, seq_len)
    query_places = rank * seq_len + local_places
    cosine, sine_part = rope_tables(query_places.astype(f32), HEAD_DIM // 2)
    queries = rotate(q_normed * q_gains, cosine, sine_part, 1.0).astype(bf16)
    key_rot = rotate(k_normed * k_gains, cosine, sine_part, 1.0).astype(bf16)
    score_scale = HEAD_DIM ** (-0.5)
    keys_values = jnp.stack([key_rot, v_heads])
    pieces = [keys_values]
    for offset in range(1, group):
        keys_values = from_behind(keys_values, "expert", 1)
        pieces.append(keys_values)
    stacked = jnp.stack(pieces, 1).reshape(2, group * seq_len, head_count, HEAD_DIM)
    keys_all = stacked[0]
    values_all = stacked[1]
    query_segs = lax.dynamic_slice_in_dim(segments, my_index * seq_len, seq_len, 0)
    key_segs = jnp.concatenate(
        [
            lax.dynamic_slice_in_dim(
                segments, jnp.maximum(my_index - offset, 0) * seq_len, seq_len, 0
            )
            for offset in range(group)
        ],
        0,
    )
    offsets = lax.iota(jnp.int32, group)
    key_places = ((rank - offsets)[:, None] * seq_len + local_places[None, :]).reshape(-1)
    key_valid = jnp.repeat(rank - offsets >= 0, seq_len)
    allowed = (
        key_valid[None, :]
        & (query_places[:, None] >= key_places[None, :])
        & (query_segs[:, None] == key_segs[None, :])
    )

    def scores_of():
        raw_scores = (
            jnp.einsum("thd,shd->hts", queries, keys_all, preferred_element_type=f32) * score_scale
        )
        return jnp.where(allowed[None], raw_scores, MASKED)

    scores = scores_of()
    row_max = jnp.max(scores, -1, keepdims=True)
    raised = jnp.exp(scores - row_max)
    exp_total = jnp.sum(raised, -1, keepdims=True)
    log_total = row_max + jnp.log(exp_total)
    attn_probs = (raised / exp_total).astype(bf16)
    context = (
        jnp.einsum("hts,shd->thd", attn_probs, values_all, preferred_element_type=f32)
        .reshape(seq_len, local_width)
        .astype(bf16)
    )
    attn_part = jnp.dot(context, w_out, preferred_element_type=f32)
    middle = inputs + lax.psum(attn_part, "head")
    inverse_moe = inverse_rms(middle)
    normed_moe = middle * inverse_moe
    moe_input = (normed_moe * norm2_gain).astype(bf16)
    logits = jnp.dot(moe_input, w_router, preferred_element_type=f32)
    chosen = jnp.take_along_axis(logits, routes, 1)
    raised_gate = jnp.exp(chosen - jnp.max(chosen, -1, keepdims=True))
    gate_weights = raised_gate / jnp.sum(raised_gate, -1, keepdims=True)
    catalog = lax.iota(jnp.int32, expert_total)
    route_hot = (routes[:, :, None] == catalog).astype(jnp.int32)
    token_hot = jnp.sum(route_hot, 1, dtype=jnp.int32)
    earlier = jnp.cumsum(token_hot, 0, dtype=jnp.int32) - token_hot
    position = routes * capacity + jnp.take_along_axis(earlier, routes, 1)
    flat_pos = position.reshape(-1)
    owners = (
        jnp.full((expert_total * capacity,), seq_len, jnp.int32)
        .at[flat_pos]
        .set(jnp.repeat(lax.iota(jnp.int32, seq_len), TOP))
    )
    padded = jnp.concatenate([moe_input, jnp.zeros((1, width), bf16)], 0)
    outgoing = padded[owners].reshape(expert_devs, slab_rows, width)
    arrived = lax.all_to_all(outgoing, "expert", split_axis=0, concat_axis=0, tiled=True)
    rows_in = arrived.reshape(expert_devs, local_experts, capacity, width)
    gate_act = jnp.einsum("sjcd,jdf->sjcf", rows_in, w_gate, preferred_element_type=f32)
    up_act = jnp.einsum("sjcd,jdf->sjcf", rows_in, w_up, preferred_element_type=f32)
    hidden = (jax.nn.silu(gate_act) * up_act).astype(bf16)
    partial_out = jnp.einsum("sjcf,jfd->sjcd", hidden, w_down, preferred_element_type=f32).reshape(
        expert_devs, slab_rows, width
    )
    rows_out = (
        lax.psum_scatter(partial_out.astype(jnp.bfloat16), "head", scatter_dimension=2, tiled=True)
        .astype(jnp.float32)
        .astype(bf16)
    )
    leaving = lax.all_gather(rows_out, "head", axis=2, tiled=True)
    returned = lax.all_to_all(leaving, "expert", split_axis=0, concat_axis=0, tiled=True)
    picked = returned.reshape(expert_total * capacity, width)[position]
    moe_out = jnp.einsum("tk,tkd->td", gate_weights, picked, preferred_element_type=f32)
    output = (middle + moe_out).astype(bf16)
    grad_final = cotangent.astype(f32)
    grad_gates = jnp.einsum("td,tkd->tk", grad_final, picked, preferred_element_type=f32)
    grad_chosen = gate_weights * (
        grad_gates - jnp.sum(grad_gates * gate_weights, -1, keepdims=True)
    )
    grad_logits = jnp.einsum("tk,tke->te", grad_chosen, route_hot.astype(f32)).astype(bf16)
    grad_router = jnp.dot(moe_input.T, grad_logits, preferred_element_type=f32)
    grad_moe_input = jnp.dot(grad_logits, w_router.T, preferred_element_type=f32)
    grad_expert_out = (gate_weights[:, :, None] * grad_final[:, None, :]).astype(bf16)
    grad_slab = (
        jnp.zeros((expert_total * capacity, width), bf16)
        .at[flat_pos]
        .set(grad_expert_out.reshape(seq_len * TOP, width))
    )
    grad_slab = grad_slab.reshape(expert_devs, slab_rows, width)
    grad_arrived = lax.all_to_all(grad_slab, "expert", split_axis=0, concat_axis=0, tiled=True)
    grad_rows_out = grad_arrived.reshape(expert_devs, local_experts, capacity, width)
    grad_hidden = jnp.einsum("sjcd,jfd->sjcf", grad_rows_out, w_down, preferred_element_type=f32)
    grad_down = jnp.einsum("sjcf,sjcd->jfd", hidden, grad_rows_out, preferred_element_type=f32)
    sigmoid = jax.nn.sigmoid(gate_act)
    grad_up_act = (grad_hidden * gate_act * sigmoid).astype(bf16)
    grad_gate_act = (grad_hidden * up_act * sigmoid * (1.0 + gate_act * (1.0 - sigmoid))).astype(
        bf16
    )
    grad_gate = jnp.einsum("sjcd,sjcf->jdf", rows_in, grad_gate_act, preferred_element_type=f32)
    grad_up = jnp.einsum("sjcd,sjcf->jdf", rows_in, grad_up_act, preferred_element_type=f32)
    grad_rows_in = jnp.einsum("sjcf,jdf->sjcd", grad_gate_act, w_gate, preferred_element_type=f32)
    grad_rows_in = grad_rows_in + jnp.einsum(
        "sjcf,jdf->sjcd", grad_up_act, w_up, preferred_element_type=f32
    )
    grad_back = (
        lax.psum_scatter(
            grad_rows_in.reshape(expert_devs, slab_rows, width).astype(jnp.bfloat16),
            "head",
            scatter_dimension=2,
            tiled=True,
        )
        .astype(jnp.float32)
        .astype(bf16)
    )
    leaving_grad = lax.all_gather(grad_back, "head", axis=2, tiled=True)
    grad_home = lax.all_to_all(leaving_grad, "expert", split_axis=0, concat_axis=0, tiled=True)
    grad_moe_input = grad_moe_input + jnp.sum(
        grad_home.reshape(expert_total * capacity, width)[position], 1, dtype=f32
    )
    grad_norm2 = jnp.sum(grad_moe_input * normed_moe, 0)
    grad_middle = grad_final + norm_back(grad_moe_input * norm2_gain, normed_moe, inverse_moe)
    grad_attn = grad_middle.astype(bf16)
    grad_out_turned = jnp.dot(grad_attn.T, context, preferred_element_type=f32)
    grad_context = split_heads(jnp.dot(grad_attn, w_out.T, preferred_element_type=f32).astype(bf16))
    attn_full = jnp.exp(scores_of() - log_total)
    attn_low = attn_full.astype(bf16)
    grad_values_all = jnp.einsum("hts,thd->shd", attn_low, grad_context, preferred_element_type=f32)
    grad_probs = jnp.einsum("thd,shd->hts", grad_context, values_all, preferred_element_type=f32)
    grad_scores = (
        attn_full * (grad_probs - jnp.sum(grad_probs * attn_full, -1, keepdims=True))
    ).astype(bf16)
    grad_queries = (
        jnp.einsum("hts,shd->thd", grad_scores, keys_all, preferred_element_type=f32) * score_scale
    )
    grad_keys_all = (
        jnp.einsum("hts,thd->shd", grad_scores, queries, preferred_element_type=f32) * score_scale
    )
    kv_terms = jnp.stack([grad_keys_all, grad_values_all]).reshape(
        2, group, seq_len, head_count, HEAD_DIM
    )
    kv_total = kv_terms[:, 0]
    for offset in range(1, group):
        kv_total = kv_total + from_behind(
            kv_terms[:, offset].astype(jnp.bfloat16), "expert", -offset
        ).astype(jnp.float32)
    grad_keys = kv_total[0]
    grad_values = kv_total[1]
    grad_q_normed = rotate(grad_queries, cosine, sine_part, -1.0)
    grad_k_normed = rotate(grad_keys, cosine, sine_part, -1.0)
    grad_query_gain = jnp.sum(grad_q_normed * q_normed, 0).reshape(local_width)
    grad_key_gain = jnp.sum(grad_k_normed * k_normed, 0).reshape(local_width)
    grad_q_raw = (
        norm_back(grad_q_normed * q_gains, q_normed, q_inverse)
        .reshape(seq_len, local_width)
        .astype(bf16)
    )
    grad_k_raw = (
        norm_back(grad_k_normed * k_gains, k_normed, k_inverse)
        .reshape(seq_len, local_width)
        .astype(bf16)
    )
    grad_v_raw = grad_values.reshape(seq_len, local_width).astype(bf16)
    grad_query = jnp.dot(attn_input.T, grad_q_raw, preferred_element_type=f32)
    grad_key = jnp.dot(attn_input.T, grad_k_raw, preferred_element_type=f32)
    grad_value = jnp.dot(attn_input.T, grad_v_raw, preferred_element_type=f32)
    input_part = jnp.dot(grad_q_raw, w_query.T, preferred_element_type=f32)
    input_part = input_part + jnp.dot(grad_k_raw, w_key.T, preferred_element_type=f32)
    input_part = input_part + jnp.dot(grad_v_raw, w_value.T, preferred_element_type=f32)
    grad_attn_input = lax.psum(input_part.astype(jnp.bfloat16), "head").astype(jnp.float32)
    grad_norm1 = jnp.sum(grad_attn_input * normed_attn, 0)
    grad_input = grad_middle + norm_back(grad_attn_input * norm1_gain, normed_attn, inverse_attn)
    grad_query, grad_key, grad_value, grad_out_turned = (
        lax.psum_scatter(
            grad_query.astype(jnp.bfloat16), "expert", scatter_dimension=0, tiled=True
        ).astype(jnp.float32),
        lax.psum_scatter(
            grad_key.astype(jnp.bfloat16), "expert", scatter_dimension=0, tiled=True
        ).astype(jnp.float32),
        lax.psum_scatter(
            grad_value.astype(jnp.bfloat16), "expert", scatter_dimension=0, tiled=True
        ).astype(jnp.float32),
        lax.psum_scatter(
            grad_out_turned.astype(jnp.bfloat16), "expert", scatter_dimension=0, tiled=True
        ).astype(jnp.float32),
    )
    grad_router, grad_norm1, grad_norm2, grad_query_gain, grad_key_gain = (
        lax.psum(grad_router.astype(jnp.bfloat16), "expert").astype(jnp.float32),
        lax.psum(grad_norm1.astype(jnp.bfloat16), "expert").astype(jnp.float32),
        lax.psum(grad_norm2.astype(jnp.bfloat16), "expert").astype(jnp.float32),
        lax.psum(grad_query_gain.astype(jnp.bfloat16), "expert").astype(jnp.float32),
        lax.psum(grad_key_gain.astype(jnp.bfloat16), "expert").astype(jnp.float32),
    )
    return (
        output,
        grad_input,
        grad_norm1,
        grad_query,
        grad_key,
        grad_value,
        grad_out_turned.T,
        grad_query_gain,
        grad_key_gain,
        grad_norm2,
        grad_router,
        grad_gate,
        grad_up,
        grad_down,
    )


def full_tables(tokens):
    half_dim = HEAD_DIM // 2
    fine_cos, fine_sin = rope_tables(lax.iota(jnp.int32, 64).astype(f32), half_dim)
    coarse = (64 * lax.iota(jnp.int32, tokens // 64)).astype(f32)
    coarse_cos, coarse_sin = rope_tables(coarse, half_dim)
    fine_cos, fine_sin = fine_cos.reshape(1, 64, half_dim), fine_sin.reshape(1, 64, half_dim)
    cosine = (coarse_cos * fine_cos - coarse_sin * fine_sin).reshape(tokens, half_dim)
    sine = (coarse_sin * fine_cos + coarse_cos * fine_sin).reshape(tokens, half_dim)
    return jnp.concatenate([cosine, cosine], 1), jnp.concatenate([-sine, sine], 1)


def dense_layer(
    hidden_in, norm1_gain, w_query, w_key, w_value, w_out, query_gain, key_gain, norm2_gain, w_router,
    w_gate, w_up, w_down, routes, segments, cotangent,
):
    rows, width = hidden_in.shape
    experts = w_router.shape[1]
    devices = lax.axis_size("expert")
    tokens = devices * rows

    cosine, sine = full_tables(tokens)
    segc, segr = segments[:, None], segments[None]
    own_mask = jnp.sum((routes[:, :, None] == lax.iota(jnp.int32, experts)).astype(f32), 1)
    sent = jnp.concatenate([cotangent, jnp.pad(own_mask.astype(bf16), ((0, 0), (0, 128 - experts)))], 1)
    own_context, middle, moe_input, _, attn_all, queries, keys, values, q_raw, k_raw, grads_all, everyone, weighted, grad_acts, parts = (
        forward_all(
            hidden_in, sent, norm1_gain[None], norm2_gain[None], query_gain[None], key_gain[None], segc, segr, w_router.T,
            w_query, w_key, w_value, cosine, sine, w_out, w_gate, w_up, w_down, 1,
        )
    )
    inverse_moe = inverse_rms(middle)
    normed_moe = middle * inverse_moe
    parts = parts.reshape(devices, rows, 2 * width + 128)
    total_a, total_b, grad_gate, grad_up, grad_down = sums_all(parts, everyone, grad_acts, grads_all, weighted, 2)
    total = jnp.concatenate([total_a, total_b], 1)
    grad_final = cotangent.astype(f32)
    tail = total[:, width:].astype(f32)
    grad_gates = tail[:, :experts] + tail[:, experts : 2 * experts]
    logits = jnp.where(
        own_mask > 0, jnp.dot(moe_input, w_router, preferred_element_type=f32), -jnp.inf
    )
    raised_gate = jnp.exp(logits - jnp.max(logits, -1, keepdims=True))
    gate_weights = raised_gate / jnp.sum(raised_gate, -1, keepdims=True)
    grad_logits = (
        gate_weights * (grad_gates - jnp.sum(grad_gates * gate_weights, -1, keepdims=True))
    ).astype(bf16)
    grad_moe_input = jnp.dot(grad_logits, w_router.T, preferred_element_type=f32)
    grad_moe_input = grad_moe_input + total[:, :width].astype(f32)
    grad_middle = grad_final + norm_back(grad_moe_input * norm2_gain, normed_moe, inverse_moe)
    small = jnp.concatenate(
        [
            lax.dot_general(grad_logits, moe_input, (((0,), (0,)), ((), ())), preferred_element_type=f32),
            jnp.sum(grad_moe_input * normed_moe, 0, keepdims=True),
            jnp.zeros((7, width), f32),
        ],
        0,
    )

    grad_input, grad_query, grad_key, grad_value, grad_norm1, gains, grad_w_out, small, moe_out = backward_all(
        grad_middle.astype(bf16), segc, segr, query_gain[None], key_gain[None], small, norm1_gain[None], w_out, own_context,
        queries, keys, values, q_raw, k_raw, cosine, sine, w_query, w_key, w_value, attn_all, hidden_in, grad_middle, parts, 3,
    )
    output = (middle + moe_out.astype(f32)).astype(bf16)
    return (
        output,
        grad_input,
        grad_norm1[0],
        grad_query,
        grad_key,
        grad_value,
        grad_w_out,
        gains[0],
        gains[1],
        small[experts],
        small[:experts].T,
        grad_gate,
        grad_up,
        grad_down,
    )


def layer(*arrays):
    rows, experts = arrays[0].shape[0], arrays[9].shape[1]
    whole = 2 * rows * TOP // experts >= rows and rows * lax.axis_size("expert") == SEQ
    grid = (lax.axis_size("expert"), lax.axis_size("head")) == (8, 4)
    return dense_layer(*arrays) if whole and grid else on_device(*arrays)


def solution(mesh):
    return jax.shard_map(
        layer,
        mesh=mesh,
        in_specs=(
            P("expert", None),
            P(),
            P(None, "head"),
            P(None, "head"),
            P(None, "head"),
            P("head", None),
            P("head"),
            P("head"),
            P(),
            P(),
            P("expert", None, "head"),
            P("expert", None, "head"),
            P("expert", "head", None),
            P("expert", None),
            P(),
            P("expert", None),
        ),
        out_specs=(
            P("expert", None),
            P("expert", None),
            P(),
            P("expert", "head"),
            P("expert", "head"),
            P("expert", "head"),
            P("head", "expert"),
            P("head"),
            P("head"),
            P(),
            P(),
            P("expert", None, "head"),
            P("expert", None, "head"),
            P("expert", "head", None),
        ),
        check_vma=False,
    )
```
